32 devices in a mesh: dp: 8 (over y, x, core), fsdp: 4 (over z).
Axes of the slice: x: 2, y: 2, z: 4, core: 2. Of those that a mesh axis runs over, the one named last changes fastest.
Arguments:
- tokens: bfloat16 [16384, 768], P(('dp', 'fsdp')), may hold values from -6 to 6
- coarse_view: bfloat16 [4096, 768], P(('dp', 'fsdp')), may hold values from -6 to 6
- segment_ids: int32 [32, 512], P(('dp', 'fsdp')), may hold values from 0 to 2, as said below
- partner_device: int32 [128, 1], P(('dp', 'fsdp')), may hold values from 0 to 7; in each aligned block of 4 rows (0 to 3, 4 to 7, ...) at most 2 rows name the same one
- partner_slot: int32 [128], P(('dp', 'fsdp')), may hold values from 0 to 3
- mix_weight: float32 [128], P(('dp', 'fsdp')), may hold values from 0.25 to 0.75
- ln1_gain: bfloat16 [768], P(('dp', 'fsdp')), may hold values from 0.5 to 1.5
- w_qkv: bfloat16 [768, 2304], P(None, ('dp', 'fsdp')), may hold values from -0.21875 to 0.21875
- w_out: bfloat16 [768, 768], P(('dp', 'fsdp')), may hold values from -3.5 to 3.5
- lnx_gain: bfloat16 [768], P(('dp', 'fsdp')), may hold values from 0.5 to 1.5
- w_cq: bfloat16 [768, 768], P(('dp', 'fsdp')), may hold values from -0.21875 to 0.21875
- w_ckv: bfloat16 [768, 1536], P(None, ('dp', 'fsdp')), may hold values from -0.21875 to 0.21875
- w_cout: bfloat16 [768, 768], P(('dp', 'fsdp')), may hold values from -3.5 to 3.5
- ln2_gain: bfloat16 [768], P(('dp', 'fsdp')), may hold values from 0.5 to 1.5
- w_up: bfloat16 [768, 3072], P(None, ('dp', 'fsdp')), may hold values from -0.21875 to 0.21875
- w_down: bfloat16 [3072, 768], P(('dp', 'fsdp')), may hold values from -0.109375 to 0.109375
- cotangent: bfloat16 [16384, 768], P(('dp', 'fsdp')), may hold values from -6 to 6
Outputs:
- output: bfloat16 [16384, 768], P(('dp', 'fsdp'))
- token_grad: float32 [16384, 768], P(('dp', 'fsdp'))
- coarse_grad: float32 [4096, 768], P(('dp', 'fsdp'))
- ln1_grad: float32 [768], P(('dp', 'fsdp'))
- qkv_grad: float32 [768, 2304], P(None, ('dp', 'fsdp'))
- out_grad: float32 [768, 768], P(('dp', 'fsdp'))
- lnx_grad: float32 [768], P(('dp', 'fsdp'))
- cq_grad: float32 [768, 768], P(('dp', 'fsdp'))
- ckv_grad: float32 [768, 1536], P(None, ('dp', 'fsdp'))
- cout_grad: float32 [768, 768], P(('dp', 'fsdp'))
- ln2_grad: float32 [768], P(('dp', 'fsdp'))
- up_grad: float32 [768, 3072], P(None, ('dp', 'fsdp'))
- down_grad: float32 [3072, 768], P(('dp', 'fsdp'))
The draws below stay inside these ranges and needn't reach their ends.
Inputs may be any that keep to these rules, and one draw needn't show every extreme that they name: `partner_device`: among the 4 blocks of one device no value appears more than 2 times, and some device has a value exactly 2 times. `segment_ids`: ids never fall along a device's row; each device holds three videos, each a whole number of mixup blocks of 128 tokens, the longest exactly 256 tokens.
All inputs are finite; a program needn't handle non-finite values.
Results may differ from the reference program's by a relative error of at most 0.02.
Values may be sent and summed in bfloat16 or wider, within the bound.
No kernel may reach another device: no remote copies, remote signals or barrier semaphores. Data moves between devices by JAX's collectives and lax.ppermute only.
A program may use at most 256 MiB of HBM per device.

```python
import math
from functools import partial
import jax
import jax.numpy as jnp
import numpy as np
from jax import lax

D = 768
HEADS = 12
HEAD = 64
FF = 3072
CLIP = 128
CLIP_DEV = 4
CAP = 2
TOK_DEV = 512
TOK_C = 128
TOKENS = 16384
COARSE = 4096
BLOCKS = 128
N_DP = 8
N_FSDP = 4
DEVICES = 32


def draw_segment_ids(key, part):
    key = jax.random.fold_in(key, 7)
    long_key, split_key = jax.random.split(key)
    long_blocks = CLIP_DEV * 2 // 3
    rest_blocks = CLIP_DEV - long_blocks
    long_at = jax.random.randint(long_key, (DEVICES, 1), 0, 3)
    first_short = jax.random.randint(split_key, (DEVICES, 1), 1, rest_blocks)
    slot = jnp.arange(3, dtype=jnp.int32)[None, :]
    rank = slot - (slot > long_at).astype(jnp.int32)
    lengths = jnp.where(slot == long_at, long_blocks, jnp.where(rank == 0, first_short, rest_blocks - first_short))
    first_end = lengths[:, 0:1]
    second_end = first_end + lengths[:, 1:2]
    block = jnp.arange(CLIP_DEV, dtype=jnp.int32)[None, :]
    block_seg = (block >= first_end).astype(jnp.int32) + (block >= second_end).astype(jnp.int32)
    return jnp.repeat(block_seg, CLIP, axis=1).astype(jnp.int32)


def set_ends(values, rng, low, top_value):
    longest = values.shape.index(max(values.shape))
    spots = []
    for shift in (0, 1):
        where = [jax.random.randint(jax.random.fold_in(rng, axis), (), 0, length) for axis, length in enumerate(values.shape)]
        where[longest] = (where[longest] + shift) % values.shape[longest]
        spots.append(tuple(where))
    return values.at[spots[0]].set(low).at[spots[1]].set(top_value)


def level_of(stream_key, dims, shards, low, high):
    level = 1.0
    for position, shards_of in shards:
        steps = jax.random.uniform(jax.random.fold_in(jax.random.fold_in(stream_key, 6), position), (shards_of,), jnp.float32, low / len(shards), high / len(shards))
        level = level * jnp.repeat(jnp.exp(steps), dims[position] // shards_of).reshape((-1,) + (1,) * (len(dims) - 1 - position))
    return level


def deal_out(rng, own, number, rows, number_of, top, bound, skew):
    sequence = jax.random.permutation(rng, number_of)
    packed, common = portions_of(number_of, rows * top, bound, skew, True), portions_of(number_of, rows * top, bound, skew, False)
    places = jnp.arange(number_of)

    def named(tallies, rotation):
        used = int((tallies > 0).sum())
        fixed = max(1, used // 4)
        moved = fixed + (places - fixed + rotation * (used - fixed)) % max(1, number_of - fixed)
        return jnp.zeros((number_of,), jnp.int32).at[sequence[jnp.where(places < fixed, places, moved)]].set(jnp.asarray(tallies, jnp.int32))

    tallies = jnp.where(number % 4 == 0, named(packed, number // 4), named(common, number - number // 4 - 1))
    mixed = jax.random.permutation(jax.random.fold_in(own, 3), number_of)
    giver, sink = mixed[0:number_of // 2 * 2:2], mixed[1:number_of // 2 * 2:2]
    slack = jnp.minimum(tallies[giver] - 1, bound - tallies[sink]) // 2
    slack = jnp.where((giver == sequence[0]) | (sink == sequence[0]) | (tallies[sink] == 0), 0, jnp.maximum(slack, 0))
    moved = jax.random.randint(jax.random.fold_in(own, 4), (number_of // 2,), 0, 1 << 20) % (slack + 1)
    tallies = tallies.at[giver].add(-moved).at[sink].add(moved)
    items = jnp.searchsorted(jnp.cumsum(tallies), jnp.arange(rows * top), side="right").astype(jnp.int32)
    table = items.reshape(top, rows).T
    table = table[jax.random.permutation(jax.random.fold_in(own, 1), rows)]
    rotation = jax.random.randint(jax.random.fold_in(own, 2), (rows, 1), 0, top)
    return jnp.take_along_axis(table, (jnp.arange(top)[None, :] + rotation) % top, axis=1)


def portions_of(amount, total, limit, skew, full):
    loads = [(1 << 20) // math.isqrt(grade ** skew) + 1 for grade in range(1, amount + 1)]
    largest = limit if full else min(limit, max(-(-total // amount), total * loads[0] // sum(loads)))
    least = 1 if total - largest >= amount - 1 else 0
    counts, spare = [largest] + [least] * (amount - 1), total - largest - least * (amount - 1)
    while spare > 0:
        movable = [i for i in range(1, amount) if counts[i] < largest] or [i for i in range(1, amount) if counts[i] < limit]
        pool, budget = sum([loads[i] for i in movable]), spare
        for i in movable:
            more = min(limit - counts[i], max(1, budget * loads[i] // pool), spare)
            counts[i] = counts[i] + more
            spare = spare - more
    return np.array(counts)


def scatter_about(rng, dims, scale, bound, cuts=(), kind=jnp.bfloat16):
    result = scale * jax.random.normal(rng, dims, jnp.float32)
    if cuts:
        result = result * level_of(rng, dims, cuts, -0.22, 0.18)
    return jnp.clip(result, -bound, bound).astype(kind)


def setup_inputs(seed: int = 0) -> dict:
    streams_of = jax.random.split(jax.random.key(seed), 18)
    tokens = scatter_about(streams_of[0], (TOKENS, D), 1.0, 6.0, ((0, 32),))
    coarse_view = scatter_about(streams_of[1], (COARSE, D), 1.0, 6.0, ((0, 32),))
    segment_ids = draw_segment_ids(jax.random.fold_in(streams_of[17], 71), 0)
    partner_device_keys = jax.random.split(jax.random.fold_in(streams_of[3], 1), BLOCKS // CLIP_DEV)
    partner_device_turns = jax.random.permutation(jax.random.fold_in(streams_of[3], 3), BLOCKS // CLIP_DEV)
    partner_device = jax.vmap(lambda own, number: deal_out(jax.random.fold_in(streams_of[3], 2), own, number, CLIP_DEV, N_DP, 1, CAP, 1))(partner_device_keys, partner_device_turns).reshape((BLOCKS, 1))
    partner_slot = set_ends(jax.random.randint(streams_of[4], (BLOCKS,), 0, CLIP_DEV), jax.random.fold_in(streams_of[4], 1), 0, CLIP_DEV - 1).astype(jnp.int32)
    mix_weight = jnp.clip(0.25 + 0.5 * jax.random.uniform(streams_of[5], (BLOCKS,), jnp.float32) ** level_of(streams_of[5], (BLOCKS,), ((0, 32),), -0.2, 0.2), 0.25, 0.75)
    ln1_gain = jnp.clip(1.0 + 0.1 * jax.random.normal(streams_of[6], (D,), jnp.float32), 0.5, 1.5).astype(jnp.bfloat16)
    w_qkv = scatter_about(streams_of[7], (D, 3 * D), D ** -0.5, 0.21875, ((1, 32),))
    w_out = scatter_about(streams_of[8], (D, D), (max(D // 256, 1)) ** -0.5, 3.5, ((0, 32),))
    lnx_gain = jnp.clip(1.0 + 0.1 * jax.random.normal(streams_of[9], (D,), jnp.float32), 0.5, 1.5).astype(jnp.bfloat16)
    w_cq = scatter_about(streams_of[10], (D, D), D ** -0.5, 0.21875, ((0, 32),))
    w_ckv = scatter_about(streams_of[11], (D, 2 * D), D ** -0.5, 0.21875, ((1, 32),))
    w_cout = scatter_about(streams_of[12], (D, D), (max(D // 256, 1)) ** -0.5, 3.5, ((0, 32),))
    ln2_gain = jnp.clip(1.0 + 0.1 * jax.random.normal(streams_of[13], (D,), jnp.float32), 0.5, 1.5).astype(jnp.bfloat16)
    w_up = scatter_about(streams_of[14], (D, FF), D ** -0.5, 0.21875, ((1, 32),))
    w_down = scatter_about(streams_of[15], (FF, D), FF ** -0.5, 0.109375, ((0, 32),))
    cotangent = scatter_about(streams_of[16], (TOKENS, D), 1.0, 6.0, ((0, 32),))
    return dict(tokens=tokens, coarse_view=coarse_view, segment_ids=segment_ids, partner_device=partner_device, partner_slot=partner_slot, mix_weight=mix_weight, ln1_gain=ln1_gain, w_qkv=w_qkv, w_out=w_out, lnx_gain=lnx_gain, w_cq=w_cq, w_ckv=w_ckv, w_cout=w_cout, ln2_gain=ln2_gain, w_up=w_up, w_down=w_down, cotangent=cotangent)


@jax.custom_vjp
def low(v):
    return lax.optimization_barrier(v.astype(jnp.bfloat16)).astype(jnp.float32)

@jax.custom_vjp
def low_back(v):
    return v

def low_keep(v):
    return (low(v), None)

def low_pass(kept, grad):
    return (grad,)

def back_keep(v):
    return (v, None)

def back_low(kept, grad):
    return (low(grad),)
low.defvjp(low_keep, low_pass)
low_back.defvjp(back_keep, back_low)
highest = lax.Precision.HIGHEST

def norm_rows(values, gain):
    centre = lax.optimization_barrier(jnp.mean(values, axis=-1, keepdims=True))
    shifted = values - centre
    spread = lax.optimization_barrier(jnp.mean(shifted * shifted, axis=-1, keepdims=True))
    return shifted * lax.rsqrt(spread + 1e-06) * gain

def attention_rows(queries, keys_all, values_all, query_seg, key_seg):
    scores = low_back(jnp.einsum('qhd,khd->hqk', queries, keys_all, precision=highest))
    same_video = query_seg[:, None] == key_seg[None, :]
    scores = jnp.where(same_video[None, :, :], scores, -1e+30)
    largest = lax.optimization_barrier(jnp.max(scores, axis=-1, keepdims=True))
    raised = jnp.exp(scores - largest)
    soft_weights = raised / lax.optimization_barrier(jnp.sum(raised, axis=-1, keepdims=True))
    attended = jnp.einsum('hqk,khd->qhd', low(soft_weights), values_all, precision=highest)
    return low(low_back(attended.reshape(queries.shape[0], HEADS * HEAD)))

def layer_rows(weights, carried):
    gain_one, qkv_weight, out_weight, gain_cross, cq_weight, ckv_weight, cout_weight, gain_two, up_weight, down_weight = weights
    blended, coarse, segments = carried
    model_width = HEADS * HEAD
    normed = low(norm_rows(blended, gain_one))
    projected = jnp.dot(normed, qkv_weight, precision=highest)
    queries = low(low_back(projected[:, :model_width] * 0.125)).reshape(TOK_DEV, HEADS, HEAD)
    keys_all = low(low_back(projected[:, model_width:2 * model_width])).reshape(TOK_DEV, HEADS, HEAD)
    values_all = low(low_back(projected[:, 2 * model_width:])).reshape(TOK_DEV, HEADS, HEAD)
    attended = attention_rows(queries, keys_all, values_all, segments, segments)
    residual = blended + low_back(jnp.dot(attended, out_weight, precision=highest))
    crossed_in = low(norm_rows(residual, gain_cross))
    cross_q = low(low_back(jnp.dot(crossed_in, cq_weight, precision=highest) * 0.125)).reshape(TOK_DEV, HEADS, HEAD)
    coarse_proj = jnp.dot(coarse, ckv_weight, precision=highest)
    cross_k = low(low_back(coarse_proj[:, :model_width])).reshape(TOK_C, HEADS, HEAD)
    cross_v = low(low_back(coarse_proj[:, model_width:])).reshape(TOK_C, HEADS, HEAD)
    coarse_seg = segments.reshape(TOK_C, TOK_DEV // TOK_C)[:, 0]
    crossed = attention_rows(cross_q, cross_k, cross_v, segments, coarse_seg)
    joined = residual + low_back(jnp.dot(crossed, cout_weight, precision=highest))
    second = low(norm_rows(joined, gain_two))
    pre_act = low_back(jnp.dot(second, up_weight, precision=highest))
    hidden = low(jax.nn.gelu(pre_act, approximate=False))
    return joined + jnp.dot(hidden, down_weight, precision=highest)

def reference(tokens, coarse_view, segment_ids, partner_device, partner_slot, mix_weight, ln1_gain, w_qkv, w_out, lnx_gain, w_cq, w_ckv, w_cout, ln2_gain, w_up, w_down, cotangent):
    block_index = jnp.arange(BLOCKS, dtype=jnp.int32)
    fsdp_index = block_index // CLIP_DEV % N_FSDP
    partner = ((partner_device[:, 0] * N_FSDP + fsdp_index) * CLIP_DEV + partner_slot).astype(jnp.int32)
    mixing = mix_weight[:, None]

    def forward(inputs, coarse, gain_one, qkv_weight, out_weight, gain_cross, cq_weight, ckv_weight, cout_weight, gain_two, up_weight, down_weight):
        pieces = inputs.reshape(BLOCKS, CLIP * D)
        blended = mixing * pieces + (1.0 - mixing) * pieces[partner]
        blended = blended.reshape(DEVICES, TOK_DEV, D)
        coarse_rows = coarse.reshape(DEVICES, TOK_C, D)
        weights = (gain_one, qkv_weight, out_weight, gain_cross, cq_weight, ckv_weight, cout_weight, gain_two, up_weight, down_weight)
        outputs = lax.map(jax.checkpoint(partial(layer_rows, weights)), (blended, coarse_rows, segment_ids))
        return outputs.reshape(TOKENS, D)
    primals = [array_in.astype(jnp.float32) for array_in in (tokens, coarse_view, ln1_gain, w_qkv, w_out, lnx_gain, w_cq, w_ckv, w_cout, ln2_gain, w_up, w_down)]
    output, pullback = jax.vjp(forward, *primals)
    grads = pullback(cotangent.astype(jnp.float32))
    return (output.astype(jnp.bfloat16), grads[0], grads[1], grads[2], grads[3], grads[4], grads[5], grads[6], grads[7], grads[8], grads[9], grads[10], grads[11])
```

```python
import jax
import jax.numpy as jnp
from jax import lax
from jax.sharding import PartitionSpec as P

HEADS = 12
HEAD = 64
CORE = 1
f32 = jnp.float32
bf16 = jnp.bfloat16


def norm_rows(values, gain):
    centre = jnp.mean(values, axis=-1, keepdims=True)
    shifted = values - centre
    spread = jnp.mean(shifted * shifted, axis=-1, keepdims=True)
    return shifted * lax.rsqrt(spread + 1e-06) * gain


def exact_gelu(values):
    return jax.nn.gelu(values, approximate=False)


def swap(values, mask):
    count = lax.axis_size("dp")
    return lax.ppermute(values, "dp", [(i, i ^ mask) for i in range(count)])


def shift(values, step):
    count = lax.axis_size("fsdp")
    return lax.ppermute(values, "fsdp", [(i, (i + step) % count) for i in range(count)])


def link_masks(first):
    masks = []
    mask = 2
    while mask < lax.axis_size("dp"):
        masks.append(mask)
        mask *= 2
    return masks if first else masks[::-1]


def gather_inner(shard):
    count = lax.axis_size("fsdp")
    me = lax.axis_index("fsdp")
    came = [shard] + [shift(shard, step) for step in range(1, count)]
    line = [came[count - 1 - k] for k in range(count)] + [came[count - k] for k in range(1, count)]
    stacked = jnp.stack(line)
    part = lax.dynamic_slice_in_dim(stacked, count - 1 - me, count, 0)
    return part.reshape((count * shard.shape[0],) + shard.shape[1:])


def gather_outer(block, first):
    pieces = {0: block}
    for mask in link_masks(first):
        for e in list(pieces):
            pieces[e | mask] = swap(pieces[e], mask)
    for e in list(pieces):
        pieces[e | CORE] = swap(pieces[e], CORE)
    return pieces


def scatter_outer(pieces, first):
    now = dict(pieces)
    for e in list(now):
        if e & CORE:
            gone = now.pop(e)
            now[e ^ CORE] = now[e ^ CORE].astype(f32) + swap(gone.astype(bf16), CORE).astype(f32)
    for mask in link_masks(first)[::-1]:
        for e in list(now):
            if e & mask:
                gone = now.pop(e)
                now[e ^ mask] = now[e ^ mask].astype(f32) + swap(gone.astype(bf16), mask).astype(f32)
    return now[0]


def scatter_inner(block):
    count = lax.axis_size("fsdp")
    me = lax.axis_index("fsdp")
    parts = block.reshape((count, block.shape[0] // count) + block.shape[1:])
    low = parts.astype(bf16)
    total = lax.dynamic_index_in_dim(parts, me, 0, keepdims=False)
    for step in range(1, count):
        going = lax.dynamic_index_in_dim(low, (me + step) % count, 0, keepdims=False)
        total = total + shift(going, step).astype(f32)
    return total


def true_order(pieces):
    me = lax.axis_index("dp")
    stacked = jnp.stack([pieces[e] for e in range(len(pieces))])
    return jnp.concatenate(
        [lax.dynamic_index_in_dim(stacked, me ^ d, 0, keepdims=False) for d in range(len(pieces))]
    )


def relative_parts(values):
    count = lax.axis_size("dp")
    me = lax.axis_index("dp")
    rows = values.shape[0] // count
    return {e: lax.dynamic_slice_in_dim(values, (me ^ e) * rows, rows, 0) for e in range(count)}


def all_sum(values):
    mask = 1
    while mask < lax.axis_size("dp"):
        values = values + swap(values, mask)
        mask *= 2
    count = lax.axis_size("fsdp")
    mask = 1
    while mask < count:
        values = values + lax.ppermute(values, "fsdp", [(i, i ^ mask) for i in range(count)])
        mask *= 2
    return values


def masked_scores(query_rows, keys_all, same_video):
    scores = jnp.einsum("qhd,khd->hqk", query_rows, keys_all, preferred_element_type=f32)
    return jnp.where(same_video[None, :, :], scores, -1e30)


def attend_rows(queries, keys_all, values_all, same_video):
    row_count = queries.shape[0]
    model_width = queries.shape[1] * queries.shape[2]
    scores = masked_scores(queries, keys_all, same_video)
    largest = jnp.max(scores, axis=-1, keepdims=True)
    raised = jnp.exp(scores - largest)
    total_sum = jnp.sum(raised, axis=-1, keepdims=True)
    soft_low = (raised / total_sum).astype(bf16)
    rows = jnp.einsum("hqk,khd->qhd", soft_low, values_all, preferred_element_type=f32)
    return rows.reshape(row_count, model_width).astype(bf16), largest + jnp.log(total_sum)


def attend_grads(queries, keys_all, values_all, same_video, log_sums, grad_attended):
    row_count = queries.shape[0]
    key_count = keys_all.shape[0]
    model_width = queries.shape[1] * queries.shape[2]
    grad_heads = grad_attended.reshape(queries.shape)
    scores = masked_scores(queries, keys_all, same_video)
    soft_rows = jnp.exp(scores - log_sums)
    soft_low = soft_rows.astype(bf16)
    value_sum = jnp.einsum("hqk,qhd->khd", soft_low, grad_heads, preferred_element_type=f32)
    grad_soft = jnp.einsum("qhd,khd->hqk", grad_heads, values_all, preferred_element_type=f32)
    inner_sum = jnp.sum(soft_rows * grad_soft, axis=-1, keepdims=True)
    grad_scores = (soft_rows * (grad_soft - inner_sum)).astype(bf16)
    query_part = jnp.einsum("hqk,khd->qhd", grad_scores, keys_all, preferred_element_type=f32)
    key_sum = jnp.einsum("hqk,qhd->khd", grad_scores, queries, preferred_element_type=f32)
    return (
        query_part.astype(bf16).reshape(row_count, model_width),
        key_sum.reshape(key_count, model_width).astype(bf16),
        value_sum.reshape(key_count, model_width).astype(bf16),
    )


def dot_nn(a, b):
    return jnp.einsum("td,de->te", a, b, preferred_element_type=f32)


def dot_nt(a, b):
    return jnp.einsum("td,ed->te", a, b, preferred_element_type=f32)


def dot_tn(a, b):
    return jnp.einsum("td,te->de", a, b, preferred_element_type=f32)


def shards(
    tokens,
    coarse_view,
    segment_ids,
    partner_device,
    partner_slot,
    mix_weight,
    ln1_gain,
    w_qkv,
    w_out,
    lnx_gain,
    w_cq,
    w_ckv,
    w_cout,
    ln2_gain,
    w_up,
    w_down,
    cotangent,
):
    row_count, width = tokens.shape
    coarse_rows = coarse_view.shape[0]
    block_count = mix_weight.shape[0]
    clip_rows = row_count // block_count
    dp_count, fsdp_count = lax.axis_size("dp"), lax.axis_size("fsdp")
    dp_me, fsdp_me = lax.axis_index("dp"), lax.axis_index("fsdp")
    part = ln1_gain.shape[0]
    device_me = dp_me * fsdp_count + fsdp_me

    first_rows = (w_qkv.T, w_cq, w_out, w_ckv.T, w_cout)
    sizes = [w.shape[0] for w in first_rows]
    group_a1 = jnp.concatenate([w_qkv.T])
    group_a2 = jnp.concatenate([w_out, w_cq, w_ckv.T, w_cout])
    gains = jnp.stack([ln1_gain, lnx_gain, ln2_gain])
    gains_mine = lax.dynamic_update_slice(
        jnp.zeros((3, width), f32), gains.astype(f32), (0, device_me * part)
    )

    target = partner_device[:, 0]
    own = tokens
    masks = link_masks(True)
    token_pieces = gather_outer(own, True)
    token_stack = jnp.stack(
        [token_pieces[e].reshape(block_count, clip_rows, width) for e in range(dp_count)]
    ).reshape(dp_count * block_count, clip_rows, width)
    partner_at = (target ^ dp_me) * block_count + partner_slot
    partner_rows = jnp.stack(
        [
            lax.dynamic_index_in_dim(token_stack, partner_at[b], 0, keepdims=False)
            for b in range(block_count)
        ]
    ).astype(f32)
    mixing = mix_weight[:, None, None]
    own_blocks = own.reshape(block_count, clip_rows, width).astype(f32)
    blended = (mixing * own_blocks + (1.0 - mixing) * partner_rows).reshape(row_count, width)

    gain_one, gain_cross, gain_two = all_sum(gains_mine)

    qkv_t = true_order(gather_outer(gather_inner(w_qkv.T), True))
    out_full = true_order(gather_outer(gather_inner(w_out), False))
    cq_full = true_order(gather_outer(gather_inner(w_cq), True))
    ckv_t = true_order(gather_outer(gather_inner(w_ckv.T), False))
    cout_full = true_order(gather_outer(gather_inner(w_cout), True))
    up_pieces = gather_outer(gather_inner(w_up.T), True)
    down_pieces = gather_outer(gather_inner(w_down), False)
    up_t = jnp.concatenate([up_pieces[e] for e in range(dp_count)])
    down_full = jnp.concatenate([down_pieces[e] for e in range(dp_count)])

    segments = segment_ids[0]
    coarse_seg = segments.reshape(coarse_rows, row_count // coarse_rows)[:, 0]
    self_same = segments[:, None] == segments[None, :]
    cross_same = segments[:, None] == coarse_seg[None, :]

    normed = norm_rows(blended, gain_one).astype(bf16)
    projected = dot_nt(normed, qkv_t)
    queries = (projected[:, :width] * 0.125).astype(bf16).reshape(row_count, HEADS, HEAD)
    keys_all = projected[:, width : 2 * width].astype(bf16).reshape(row_count, HEADS, HEAD)
    values_all = projected[:, 2 * width :].astype(bf16).reshape(row_count, HEADS, HEAD)
    attended, self_lse = attend_rows(queries, keys_all, values_all, self_same)
    residual = blended + dot_nn(attended, out_full)
    crossed_in = norm_rows(residual, gain_cross).astype(bf16)
    cross_q = (dot_nn(crossed_in, cq_full) * 0.125).astype(bf16).reshape(row_count, HEADS, HEAD)
    coarse_proj = dot_nt(coarse_view, ckv_t)
    cross_k = coarse_proj[:, :width].astype(bf16).reshape(coarse_rows, HEADS, HEAD)
    cross_v = coarse_proj[:, width:].astype(bf16).reshape(coarse_rows, HEADS, HEAD)
    crossed, cross_lse = attend_rows(cross_q, cross_k, cross_v, cross_same)
    joined = residual + dot_nn(crossed, cout_full)
    second = norm_rows(joined, gain_two).astype(bf16)
    pre_act = dot_nt(second, up_t)
    hidden = exact_gelu(pre_act).astype(bf16)
    output = (joined + dot_nn(hidden, down_full)).astype(bf16)

    grad_hidden = dot_nt(cotangent, down_full)
    gelu_value, gelu_pull = jax.vjp(exact_gelu, pre_act)
    grad_pre = gelu_pull(grad_hidden)[0].astype(bf16)
    down_grad = dot_tn(hidden, cotangent)
    up_grad = dot_tn(grad_pre, second)
    grad_second = dot_nn(grad_pre, up_t)
    norm_value, norm_pull = jax.vjp(norm_rows, joined, gain_two)
    grad_joined_norm, ln2_piece = norm_pull(grad_second)
    grad_joined = cotangent.astype(f32) + grad_joined_norm

    rows = up_grad.shape[0] // dp_count
    up_shard = scatter_inner(
        scatter_outer({e: up_grad[e * rows : (e + 1) * rows] for e in range(dp_count)}, True)
    ).T
    down_shard = scatter_inner(
        scatter_outer({e: down_grad[e * rows : (e + 1) * rows] for e in range(dp_count)}, False)
    )

    grad_joined_low = grad_joined.astype(bf16)
    cout_grad = dot_tn(crossed, grad_joined_low)
    grad_crossed = dot_nt(grad_joined_low, cout_full).astype(bf16)
    cq_part, ck_part, cv_part = attend_grads(
        cross_q, cross_k, cross_v, cross_same, cross_lse, grad_crossed
    )
    grad_cq = cq_part * 0.125
    cq_grad = dot_tn(crossed_in, grad_cq)
    grad_crossed_in = dot_nt(grad_cq, cq_full)
    grad_ckv = jnp.concatenate([ck_part, cv_part], axis=1)
    ckv_grad = dot_tn(grad_ckv, coarse_view)
    coarse_grad = dot_nn(grad_ckv, ckv_t)
    cross_value, cross_pull = jax.vjp(norm_rows, residual, gain_cross)
    grad_res_norm, lnx_piece = cross_pull(grad_crossed_in)
    grad_residual = grad_joined + grad_res_norm
    grad_res_low = grad_residual.astype(bf16)
    out_grad = dot_tn(attended, grad_res_low)
    grad_attended = dot_nt(grad_res_low, out_full).astype(bf16)
    query_part, key_part, value_part = attend_grads(
        queries, keys_all, values_all, self_same, self_lse, grad_attended
    )
    grad_projected = jnp.concatenate([query_part * 0.125, key_part, value_part], axis=1)
    qkv_grad = dot_tn(grad_projected, normed)
    grad_normed = dot_nn(grad_projected, qkv_t)
    first_value, first_pull = jax.vjp(norm_rows, blended, gain_one)
    grad_blend_norm, ln1_piece = first_pull(grad_normed)
    grad_blended = grad_residual + grad_blend_norm

    def reduce_shard(values, first):
        return scatter_inner(scatter_outer(relative_parts(values), first))

    cout_shard = reduce_shard(cout_grad, True)
    cq_shard = reduce_shard(cq_grad, True)
    ckv_shard = reduce_shard(ckv_grad, False).T
    out_shard = reduce_shard(out_grad, False)
    qkv_shard = reduce_shard(qkv_grad, True).T

    gain_sums = all_sum(jnp.stack([ln1_piece, lnx_piece, ln2_piece]))
    gain_mine = lax.dynamic_slice(gain_sums, (0, device_me * part), (3, part))

    grad_blocks = grad_blended.reshape(block_count, clip_rows, width)
    send_blocks = ((1.0 - mixing) * grad_blocks).reshape(block_count, clip_rows * width)
    places = jnp.arange(dp_count * block_count, dtype=jnp.int32)
    chosen = (places[:, None] == partner_at[None, :]).astype(bf16)
    outgoing = jnp.dot(chosen, send_blocks.astype(bf16), preferred_element_type=f32)
    outgoing = outgoing.reshape(dp_count, row_count, width)
    incoming = scatter_outer({e: outgoing[e] for e in range(dp_count)}, True)
    token_grad = (mixing * grad_blocks).reshape(row_count, width) + incoming
    return (
        output,
        token_grad,
        coarse_grad,
        gain_mine[0],
        qkv_shard,
        out_shard,
        gain_mine[1],
        cq_shard,
        ckv_shard,
        cout_shard,
        gain_mine[2],
        up_shard,
        down_shard,
    )


def solution(mesh):
    rows = P(("dp", "fsdp"), None)
    columns = P(None, ("dp", "fsdp"))
    line = P(("dp", "fsdp"))
    in_specs = (
        rows, rows, rows, rows, line, line, line, columns, rows,
        line, rows, columns, rows, line, columns, rows, rows,
    )
    out_specs = (
        rows, rows, rows, line, columns, rows, line, rows, columns, rows, line, columns, rows,
    )
    return jax.shard_map(shards, mesh=mesh, in_specs=in_specs, out_specs=out_specs, check_vma=False)
```

```python
import functools

import jax
import jax.numpy as jnp
from jax import lax
from jax.experimental import pallas as pl
from jax.experimental.pallas import tpu as pltpu
from jax.sharding import PartitionSpec as P

HEADS = 12
HEAD = 64
PAIR = 2 * HEAD
CORE = 1
CLIP = 128
WINDOW = 256
TILE = 256
VMEM_BYTES = 56 * 1024 * 1024
f32 = jnp.float32
bf16 = jnp.bfloat16
fence = lax.optimization_barrier


def swap(values, mask):
    count = lax.axis_size("dp")
    return lax.ppermute(values, "dp", [(i, i ^ mask) for i in range(count)])


def shift(values, step):
    count = lax.axis_size("fsdp")
    return lax.ppermute(values, "fsdp", [(i, (i + step) % count) for i in range(count)])


def link_masks():
    masks = []
    mask = 2
    while mask < lax.axis_size("dp"):
        masks.append(mask)
        mask *= 2
    return masks


def relays():
    found = []
    for e in range(2, lax.axis_size("dp"), 2):
        if e & (e - 1):
            found.append((bin(e).count("1"), e, 1 << (e.bit_length() - 1), e & -e))
    return [item[1:] for item in sorted(found)]


def inner_order(came):
    count = len(came)
    me = lax.axis_index("fsdp")
    line = [came[count - 1 - k] for k in range(count)] + [came[count - k] for k in range(1, count)]
    return lax.dynamic_slice_in_dim(jnp.stack(line), count - 1 - me, count, 0)


def inner_start(shard):
    return [shard] + [shift(shard, step) for step in range(1, lax.axis_size("fsdp"))]


def single_steps(block):
    return {mask: swap(block, mask) for mask in link_masks()}


def relay_steps(held, cut):
    def half_of(e, which):
        block = held[e]
        if isinstance(block, tuple):
            return block[which]
        return block[:cut] if which == 0 else block[cut:]

    for e, top, low in relays():
        held[e] = (swap(half_of(e ^ top, 0), top), swap(half_of(e ^ low, 1), low))


def parts_of(pieces, total, cut):
    arrays, places = [], []
    for e in sorted(pieces):
        block = pieces[e]
        if isinstance(block, tuple):
            arrays += [block[0], block[1]]
            places += [(e, 0, cut), (e, cut, total - cut)]
        else:
            arrays.append(block)
            places.append((e, 0, total))
    return arrays, tuple(places)


def core_steps(held):
    out = dict(held)
    for e, block in held.items():
        if isinstance(block, tuple):
            out[e | CORE] = tuple(swap(half, CORE) for half in block)
        else:
            out[e | CORE] = swap(block, CORE)
    return out


def add_low(a, b):
    return (a.astype(f32) + b.astype(f32)).astype(bf16)


def outer_sum(total, cut):
    held = {2 * g: total[g] for g in range(total.shape[0])}
    extra = {e: {0: [], 1: []} for e in held}

    def half_sum(e, which):
        part = held[e][:cut] if which == 0 else held[e][cut:]
        for came in extra[e][which]:
            part = add_low(part, came)
        return part

    for e, top, low in relays()[::-1]:
        extra[e ^ top][0].append(swap(half_sum(e, 0), top))
        extra[e ^ low][1].append(swap(half_sum(e, 1), low))
    came = []
    for mask in link_masks():
        came.append(swap(jnp.concatenate([half_sum(mask, 0), half_sum(mask, 1)]), mask))
    result = held[0].astype(f32)
    for block in came:
        result = result + block.astype(f32)
    return result


def inner_sum(parts):
    count = parts.shape[0]
    me = lax.axis_index("fsdp")
    low = parts.astype(bf16)
    total = lax.dynamic_index_in_dim(parts, me, 0, keepdims=False)
    for step in range(1, count):
        going = lax.dynamic_index_in_dim(low, (me + step) % count, 0, keepdims=False)
        total = total + shift(going, step).astype(f32)
    return total


def nn(a, b):
    return jnp.dot(a, b, preferred_element_type=f32)


def nt(a, b):
    return lax.dot_general(a, b, (((1,), (1,)), ((), ())), preferred_element_type=f32)


def tn(a, b):
    return lax.dot_general(a, b, (((0,), (0,)), ((), ())), preferred_element_type=f32)


def tiles(size):
    step = TILE if size % TILE == 0 else size
    return [(at, step) for at in range(0, size, step)]


def centred(values):
    centre = jnp.mean(values, axis=-1, keepdims=True)
    shifted = values - centre
    spread = jnp.mean(shifted * shifted, axis=-1, keepdims=True)
    r = lax.rsqrt(spread + 1e-06)
    return shifted * r, r


def norm_back(xhat, r, gain, grad):
    c = grad * gain
    first = jnp.mean(c, axis=-1, keepdims=True)
    second = jnp.mean(c * xhat, axis=-1, keepdims=True)
    return r * (c - first - xhat * second), jnp.sum(grad * xhat, axis=0, keepdims=True)


def lower_half(rows):
    return lax.broadcasted_iota(jnp.int32, (rows, PAIR), 1) < HEAD


def two_heads(rows):
    keep = lower_half(rows.shape[0])
    zero = jnp.zeros_like(rows)
    return jnp.concatenate([jnp.where(keep, rows, zero), jnp.where(keep, zero, rows)], axis=0)


def side_by_side(stacked):
    rows = stacked.shape[0] // 2
    return jnp.where(lower_half(rows), stacked[:rows], stacked[rows:])


def softmax_rows(scores):
    raised = jnp.exp(scores - jnp.max(scores, axis=-1, keepdims=True))
    return raised / jnp.sum(raised, axis=-1, keepdims=True)


def bias_of(key_seg, own_seg):
    return jnp.where(key_seg == own_seg, 0.0, -1e30).astype(f32)


def copies(jobs, sems, at):
    made = [pltpu.make_async_copy(src, dst, sems.at[at + i]) for i, (src, dst) in enumerate(jobs)]
    for job in made:
        job.start()
    return made


def whole(shape, dtype):
    return jax.ShapeDtypeStruct(shape, dtype)


VMEM = pl.BlockSpec(memory_space=pltpu.VMEM)
SMEM = pl.BlockSpec(memory_space=pltpu.SMEM)
ANY = pl.BlockSpec(memory_space=pl.ANY)


def params():
    return pltpu.CompilerParams(vmem_limit_bytes=VMEM_BYTES)


def cost(flops, moved, exps=0):
    return pl.CostEstimate(flops=int(flops), bytes_accessed=int(moved), transcendentals=int(exps))


def first_kernel(
    geometry, ints, mix, seg_row, tokens, *refs
):
    dp_count, blocks, token_places, qkv_places, qkv_rows = geometry
    n_tok, n_qkv = len(token_places), len(qkv_places)
    token_refs, qkv_refs = refs[:n_tok], refs[n_tok : n_tok + n_qkv]
    blended_ref, qkv_ref, attended_ref, gains_ref, partner, weight, gain_parts, sems = refs[n_tok + n_qkv :]
    me = ints[0]
    width = tokens.shape[1]

    for b in range(blocks):
        rel, slot = ints[1 + b], ints[1 + blocks + b]
        for ref, (e, start, rows) in zip(token_refs, token_places):
            inside = (rel == e) & (slot * CLIP >= start) & (slot * CLIP < start + rows)

            @pl.when(inside)
            def _(ref=ref, start=start, rows=rows, b=b, slot=slot):
                at = pl.multiple_of(jnp.clip(slot * CLIP - start, 0, rows - CLIP), CLIP)
                pltpu.make_async_copy(ref.at[pl.ds(at, CLIP)], partner.at[b], sems.at[b]).start()

    jobs = []
    for ref, (e, start, rows) in zip(qkv_refs, qkv_places):
        take = min(rows, qkv_rows - start)
        at = pl.multiple_of((me ^ e) * qkv_rows + start, 16)
        jobs.append((ref.at[pl.ds(0, take)], weight.at[pl.ds(at, take)]))
        if start + rows > qkv_rows:
            jobs.append((ref.at[pl.ds(take, rows - take)], gain_parts.at[e]))
    made = copies(jobs, sems, blocks)
    for b in range(blocks):
        pltpu.make_async_copy(tokens.at[pl.ds(0, CLIP)], partner.at[b], sems.at[b]).wait()
    for b in range(blocks):
        rows = slice(b * CLIP, (b + 1) * CLIP)
        share = mix[b]
        blended_ref[rows, :] = share * tokens[rows, :].astype(f32) + (1.0 - share) * partner[b].astype(f32)
    for job in made:
        job.wait()
    gains = gain_parts[0].astype(f32)
    for e in range(1, dp_count):
        gains = gains + gain_parts[e].astype(f32)
    gains_ref[...] = gains[:8]
    xhat, _ = centred(blended_ref[...])
    normed = (xhat * gains[0:1]).astype(bf16)
    for at, step in tiles(3 * width):
        tile = nt(normed, weight[at : at + step, :])
        if at + step <= width:
            tile = tile * 0.125
        qkv_ref[:, at : at + step] = tile.astype(bf16)

    @pl.loop(0, blocks)
    def _(i):
        window = pl.multiple_of(ints[1 + 2 * blocks + i] * CLIP, CLIP)
        bias = bias_of(seg_row[:, pl.ds(window, WINDOW)], ints[1 + 3 * blocks + i])
        rows = pl.ds(pl.multiple_of(i * CLIP, CLIP), CLIP)
        keys = pl.ds(window, WINDOW)
        for at in range(0, width, PAIR):
            queries = two_heads(qkv_ref[rows, at : at + PAIR])
            probs = softmax_rows(nt(queries, qkv_ref[keys, width + at : width + at + PAIR]) + bias).astype(bf16)
            out = nn(probs, qkv_ref[keys, 2 * width + at : 2 * width + at + PAIR])
            attended_ref[rows, at : at + PAIR] = side_by_side(out).astype(bf16)


def load_cross(me, refs, places, layout, weights, sems):
    jobs = []
    for ref, (e, start, rows) in zip(refs, places):
        for (first, size), weight in zip(layout, weights):
            if first >= start and first + size <= start + rows:
                at = pl.multiple_of((me ^ e) * size, 16)
                jobs.append((ref.at[pl.ds(first - start, size)], weight.at[pl.ds(at, size)]))
    return copies(jobs, sems, 0)


def second_kernel(geometry, ints, coarse_seg, coarse, blended, attended, gains, *refs):
    blocks, places, layout = geometry
    weight_refs = refs[: len(places)]
    residual_ref, cq_ref, ckv_ref, crossed_ref, joined_ref, second_ref = refs[len(places) : len(places) + 6]
    w_ckv, w_out, w_cq, w_cout, sems = refs[len(places) + 6 :]
    made = load_cross(ints[0], weight_refs, places, layout, (w_ckv, w_out, w_cq, w_cout), sems)
    for job in made:
        job.wait()
    width = blended.shape[1]
    for at, step in tiles(2 * width):
        ckv_ref[:, at : at + step] = nt(coarse[...], w_ckv[at : at + step, :]).astype(bf16)
    for at, step in tiles(width):
        residual_ref[:, at : at + step] = blended[:, at : at + step] + nn(attended[...], w_out[:, at : at + step])
    xhat, _ = centred(residual_ref[...])
    crossed_in = (xhat * gains[1:2]).astype(bf16)
    for at, step in tiles(width):
        cq_ref[:, at : at + step] = (nn(crossed_in, w_cq[:, at : at + step]) * 0.125).astype(bf16)

    @pl.loop(0, blocks)
    def _(i):
        bias = bias_of(coarse_seg[...], ints[1 + 3 * blocks + i])
        rows = pl.ds(pl.multiple_of(i * CLIP, CLIP), CLIP)
        for at in range(0, width, PAIR):
            queries = two_heads(cq_ref[rows, at : at + PAIR])
            probs = softmax_rows(nt(queries, ckv_ref[:, at : at + PAIR]) + bias).astype(bf16)
            out = nn(probs, ckv_ref[:, width + at : width + at + PAIR])
            crossed_ref[rows, at : at + PAIR] = side_by_side(out).astype(bf16)

    for at, step in tiles(width):
        joined_ref[:, at : at + step] = residual_ref[:, at : at + step] + nn(crossed_ref[...], w_cout[:, at : at + step])
    xhat, _ = centred(joined_ref[...])
    second_ref[...] = (xhat * gains[2:3]).astype(bf16)


def mlp_kernel(geometry, second, cotangent, *refs):
    groups, places, rows, carried = geometry
    weight_refs = refs[: len(places)]
    refs = refs[len(places) :]
    if carried:
        out_in, grad_in = refs[:2]
        refs = refs[2:]
    keep_ref, send_ref, out_ref, grad_ref, w_up, w_down, hidden, grad_pre, sems = refs
    step = pl.program_id(0)

    def jobs_of(group):
        jobs = []
        for ref, (e, which, start) in zip(weight_refs, places):
            if e // 2 == groups[group]:
                for part, weight in ((0, w_up), (1, w_down)):
                    if which is None or which == part:
                        first = part * rows if which is None else 0
                        dst = weight.at[group, pl.ds((e & 1) * rows, rows)]
                        jobs.append((ref.at[pl.ds(first, rows)], dst))
        return jobs

    at = 0
    for group in range(len(groups)):
        jobs = jobs_of(group)
        made = [pltpu.make_async_copy(s, d, sems.at[at + i]) for i, (s, d) in enumerate(jobs)]
        at += len(jobs)

        @pl.when(step == 0)
        def _(made=made):
            for job in made:
                job.start()

        @pl.when(step == group)
        def _(made=made):
            for job in made:
                job.wait()

    @pl.when(step == 0)
    def _():
        if carried:
            out_ref[...] = out_in[...]
            grad_ref[...] = grad_in[...]
        else:
            out_ref[...] = jnp.zeros_like(out_ref)
            grad_ref[...] = jnp.zeros_like(grad_ref)

    up, down = w_up.at[step], w_down.at[step]
    both = 2 * rows
    for first, size in tiles(both):
        pre = nt(second[...], up[first : first + size, :])
        grad_hidden = nt(cotangent[...], down[first : first + size, :])
        cdf = 0.5 * (1.0 + lax.erf(pre * 0.7071067811865476))
        slope = cdf + pre * (jnp.exp(-0.5 * pre * pre) * 0.3989422804014327)
        hidden[:, first : first + size] = (pre * cdf).astype(bf16)
        grad_pre[:, first : first + size] = (grad_hidden * slope).astype(bf16)
    for first, target in ((0, keep_ref), (rows, send_ref)):
        target[0, 0] = tn(grad_pre[:, first : first + rows], second[...]).astype(bf16)
        target[0, 1] = tn(hidden[:, first : first + rows], cotangent[...]).astype(bf16)
    for first, size in tiles(second.shape[1]):
        out_ref[:, first : first + size] += nn(hidden[...], down[:, first : first + size])
        grad_ref[:, first : first + size] += nn(grad_pre[...], up[:, first : first + size])


def grads_out(me, dp_count, layout, sources, keep_ref, send_ref, sems, at):
    jobs = []
    for e in range(dp_count):
        target = send_ref if e & CORE else keep_ref
        for (first, size), source in zip(layout, sources):
            row = pl.multiple_of((me ^ e) * size, 16)
            jobs.append((source.at[pl.ds(row, size)], target.at[e // 2, pl.ds(first, size)]))
    return copies(jobs, sems, at)


def third_kernel(
    geometry, ints, coarse_seg, coarse, gains, mlp_out, grad_second, joined, cotangent, residual, attended, crossed, cq, ckv, *refs
):
    blocks, places, layout, dp_count = geometry
    weight_refs = refs[: len(places)]
    refs = refs[len(places) :]
    output_ref, coarse_ref, grad_res_ref, grad_att_ref, gain_grads_ref, keep_ref, send_ref = refs[:7]
    w_ckv, w_out, w_cq, w_cout, g_ckv, g_out, g_cq, g_cout, crossed_in, grad_cross, grad_cq, key_sum, value_sum, grad_joined, sems = refs[7:]
    me = ints[0]
    width = joined.shape[1]
    made = load_cross(me, weight_refs, places, layout, (w_ckv, w_out, w_cq, w_cout), sems)
    output_ref[...] = (joined[...] + mlp_out[...]).astype(bf16)
    xhat, r = centred(joined[...])
    grad_in, gain_two = norm_back(xhat, r, gains[2:3], grad_second[...])
    grad_joined[...] = cotangent[...].astype(f32) + grad_in
    low = grad_joined[...].astype(bf16)
    for job in made:
        job.wait()
    for at, step in tiles(width):
        grad_cross[:, at : at + step] = nt(low, w_cout[at : at + step, :]).astype(bf16)
    for at, step in tiles(width):
        g_cout[at : at + step, :] = tn(crossed[:, at : at + step], low).astype(bf16)
    key_sum[...] = jnp.zeros_like(key_sum)
    value_sum[...] = jnp.zeros_like(value_sum)

    @pl.loop(0, blocks)
    def _(i):
        bias = bias_of(coarse_seg[...], ints[1 + 3 * blocks + i])
        rows = pl.ds(pl.multiple_of(i * CLIP, CLIP), CLIP)
        for at in range(0, width, PAIR):
            lanes = slice(at, at + PAIR)
            queries = two_heads(cq[rows, lanes])
            grads = two_heads(grad_cross[rows, lanes])
            keys = ckv[:, lanes]
            values = ckv[:, width + at : width + at + PAIR]
            probs = softmax_rows(nt(queries, keys) + bias)
            value_sum[:, lanes] += tn(probs.astype(bf16), grads)
            grad_probs = nt(grads, values)
            inner = jnp.sum(probs * grad_probs, axis=-1, keepdims=True)
            scores = (probs * (grad_probs - inner)).astype(bf16)
            part = side_by_side(nn(scores, keys)).astype(bf16)
            grad_cq[rows, lanes] = part * jnp.asarray(0.125, bf16)
            key_sum[:, lanes] += tn(scores, queries)

    xhat, r = centred(residual[...])
    crossed_in[...] = (xhat * gains[1:2]).astype(bf16)
    for at, step in tiles(width):
        g_cq[at : at + step, :] = tn(crossed_in[:, at : at + step], grad_cq[...]).astype(bf16)
    dk, dv = key_sum[...].astype(bf16), value_sum[...].astype(bf16)
    for at, step in tiles(width):
        g_ckv[at : at + step, :] = tn(dk[:, at : at + step], coarse[...]).astype(bf16)
        g_ckv[width + at : width + at + step, :] = tn(dv[:, at : at + step], coarse[...]).astype(bf16)
        coarse_ref[:, at : at + step] = nn(dk, w_ckv[0:width, at : at + step]) + nn(dv, w_ckv[width : 2 * width, at : at + step])
    pieces = [nt(grad_cq[...], w_cq[at : at + step, :]) for at, step in tiles(width)]
    grad_in, gain_cross = norm_back(xhat, r, gains[1:2], jnp.concatenate(pieces, axis=1))
    grad_res = grad_joined[...] + grad_in
    grad_res_ref[...] = grad_res
    low = grad_res.astype(bf16)
    for at, step in tiles(width):
        g_out[at : at + step, :] = tn(attended[:, at : at + step], low).astype(bf16)
    going = grads_out(me, dp_count, layout, (g_ckv, g_out, g_cq, g_cout), keep_ref, send_ref, sems, sems.shape[0] - 4 * dp_count)
    for at, step in tiles(width):
        grad_att_ref[:, at : at + step] = nt(low, w_out[at : at + step, :]).astype(bf16)
    zero = jnp.zeros_like(gain_two)
    gain_grads_ref[...] = jnp.concatenate([zero, gain_cross, gain_two] + [zero] * 5, axis=0)
    for job in going:
        job.wait()


def fourth_kernel(geometry, ints, mix, seg_row, gains, gain_grads, blended, grad_res, grad_att, qkv, *refs):
    dp_count, blocks, qkv_places, qkv_rows = geometry
    weight_refs = refs[: len(qkv_places)]
    refs = refs[len(qkv_places) :]
    base_ref, keep_ref, send_ref, mix_keep_ref, mix_send_ref = refs[:5]
    weight, grad_w, grad_proj, key_sum, value_sum, going_back, gain_rows, sems = refs[5:]
    me = ints[0]
    width = blended.shape[1]
    jobs = []
    for ref, (e, start, rows) in zip(weight_refs, qkv_places):
        take = min(rows, qkv_rows - start)
        at = pl.multiple_of((me ^ e) * qkv_rows + start, 16)
        jobs.append((ref.at[pl.ds(0, take)], weight.at[pl.ds(at, take)]))
    made = copies(jobs, sems, 0)
    going_back[...] = jnp.zeros_like(going_back)
    key_sum[...] = jnp.zeros_like(key_sum)
    value_sum[...] = jnp.zeros_like(value_sum)

    @pl.loop(0, blocks)
    def _(i):
        window = pl.multiple_of(ints[1 + 2 * blocks + i] * CLIP, CLIP)
        bias = bias_of(seg_row[:, pl.ds(window, WINDOW)], ints[1 + 3 * blocks + i])
        rows = pl.ds(pl.multiple_of(i * CLIP, CLIP), CLIP)
        near = pl.ds(window, WINDOW)
        for at in range(0, width, PAIR):
            lanes = slice(at, at + PAIR)
            queries = two_heads(qkv[rows, lanes])
            grads = two_heads(grad_att[rows, lanes])
            keys = qkv[near, width + at : width + at + PAIR]
            values = qkv[near, 2 * width + at : 2 * width + at + PAIR]
            probs = softmax_rows(nt(queries, keys) + bias)
            value_sum[near, lanes] += tn(probs.astype(bf16), grads)
            grad_probs = nt(grads, values)
            inner = jnp.sum(probs * grad_probs, axis=-1, keepdims=True)
            scores = (probs * (grad_probs - inner)).astype(bf16)
            part = side_by_side(nn(scores, keys)).astype(bf16)
            grad_proj[rows, lanes] = part * jnp.asarray(0.125, bf16)
            key_sum[near, lanes] += tn(scores, queries)

    grad_proj[:, width : 2 * width] = key_sum[...].astype(bf16)
    grad_proj[:, 2 * width : 3 * width] = value_sum[...].astype(bf16)
    xhat, r = centred(blended[...])
    normed = (xhat * gains[0:1]).astype(bf16)
    for at, step in tiles(3 * width):
        grad_w[at : at + step, :] = tn(grad_proj[:, at : at + step], normed).astype(bf16)
    sent = grads_out(me, dp_count, ((0, qkv_rows),), (grad_w,), keep_ref, send_ref, sems, len(jobs))
    for job in made:
        job.wait()
    pieces = [nn(grad_proj[...], weight[:, at : at + step]) for at, step in tiles(width)]
    grad_in, gain_one = norm_back(xhat, r, gains[0:1], jnp.concatenate(pieces, axis=1))
    all_gains = jnp.concatenate([gain_one, gain_grads[1:8], jnp.zeros((8, width), f32)], axis=0)
    gain_rows[...] = all_gains.astype(bf16)
    at = len(jobs) + dp_count
    last = []
    for e in range(dp_count):
        target = send_ref if e & CORE else keep_ref
        last.append((gain_rows, target.at[e // 2, pl.ds(qkv_rows, 16)]))
    sent += copies(last, sems, at)
    at += dp_count
    grad_blend = grad_res[...] + grad_in
    for b in range(blocks):
        rows = slice(b * CLIP, (b + 1) * CLIP)
        share = mix[b]
        part = grad_blend[rows, :]
        base_ref[rows, :] = share * part
        place = ints[1 + b] * blocks + ints[1 + blocks + b]
        going_back[place] = (going_back[place].astype(f32) + (1.0 - share) * part).astype(bf16)
    mixed = []
    for e in range(dp_count):
        target = mix_send_ref if e & CORE else mix_keep_ref
        for s in range(blocks):
            mixed.append((going_back.at[e * blocks + s], target.at[e // 2, pl.ds(s * CLIP, CLIP)]))
    sent += copies(mixed, sems, at)
    for job in sent:
        job.wait()


def shards(
    tokens,
    coarse_view,
    segment_ids,
    partner_device,
    partner_slot,
    mix_weight,
    ln1_gain,
    w_qkv,
    w_out,
    lnx_gain,
    w_cq,
    w_ckv,
    w_cout,
    ln2_gain,
    w_up,
    w_down,
    cotangent,
):
    row_count, width = tokens.shape
    coarse_rows = coarse_view.shape[0]
    blocks = mix_weight.shape[0]
    dp_count, fsdp_count = lax.axis_size("dp"), lax.axis_size("fsdp")
    dp_me, fsdp_me = lax.axis_index("dp"), lax.axis_index("fsdp")
    part = ln1_gain.shape[0]
    device_me = dp_me * fsdp_count + fsdp_me
    pairs = dp_count // 2

    target = partner_device[:, 0]
    segments = segment_ids[0]
    videos = segments.reshape(blocks, row_count // blocks)[:, 0]
    following = jnp.concatenate([videos[1:] == videos[:-1], jnp.zeros((1,), bool)])
    before = jnp.concatenate([jnp.zeros((1,), bool), videos[1:] == videos[:-1]])
    index = jnp.arange(blocks, dtype=jnp.int32)
    window = jnp.where(following, index, jnp.where(before, index - 1, jnp.minimum(index, blocks - 2)))
    ints = jnp.concatenate(
        [dp_me[None].astype(jnp.int32), (target ^ dp_me).astype(jnp.int32), partner_slot, window, videos]
    )
    seg_row = segments[None, :]
    coarse_seg = segments.reshape(coarse_rows, row_count // coarse_rows)[:, 0][None, :]

    gain_rows = lax.dynamic_update_slice(
        jnp.zeros((8, width), bf16), jnp.stack([ln1_gain, lnx_gain, ln2_gain]), (0, device_me * part)
    )
    shard_one = jnp.concatenate([w_qkv.T, gain_rows])
    shard_two = jnp.concatenate([w_ckv.T, w_out, w_cq, w_cout])
    shard_mlp = jnp.concatenate([w_up.T, w_down])
    sizes_two = (w_ckv.shape[1], w_out.shape[0], w_cq.shape[0], w_cout.shape[0])
    qkv_part, up_part = w_qkv.shape[1], w_up.shape[1]
    qkv_rows, up_rows = qkv_part * fsdp_count, up_part * fsdp_count
    layout = []
    at = 0
    for size in sizes_two:
        layout.append((at * fsdp_count, size * fsdp_count))
        at += size
    layout = tuple(layout)
    rows_two = at * fsdp_count

    held_tok = {0: tokens, **single_steps(tokens)}
    held_tok_core = swap(tokens, CORE)
    came_attn = inner_start(jnp.concatenate([shard_one, shard_two]))
    held_tok, held_tok_core, came_attn = fence((held_tok, held_tok_core, came_attn))

    attn = inner_order(came_attn)
    one_rows = qkv_part + 8
    ones, twos = attn[:, :one_rows], attn[:, one_rows:]
    gain_block = jnp.sum(ones[:, qkv_part:].astype(f32), axis=0).astype(bf16)
    block_one = jnp.concatenate(
        [ones[:, :qkv_part].reshape(qkv_rows, width), gain_block, jnp.zeros((8, width), bf16)]
    )
    split = []
    at = 0
    for size in sizes_two:
        split.append(twos[:, at : at + size].reshape(size * fsdp_count, width))
        at += size
    block_two = jnp.concatenate(split)
    cut_tok, cut_one, cut_two, cut_mlp = row_count // 2, qkv_rows // 2, layout[0][1], up_rows

    relay_steps(held_tok, cut_tok)
    core_tok = core_steps({e: b for e, b in held_tok.items() if e and not isinstance(b, tuple)})
    held_one = {0: block_one, **single_steps(block_one)}
    held_tok, core_tok, held_one, shard_mlp, block_two = fence(
        (held_tok, core_tok, held_one, shard_mlp, block_two)
    )
    core_tok.update({1: held_tok_core})
    core_tok.update(core_steps({e: b for e, b in held_tok.items() if isinstance(b, tuple)}))
    pieces_tok = {**held_tok, **core_tok}

    came_mlp = inner_start(shard_mlp)
    relay_steps(held_one, cut_one)
    pieces_one = core_steps(held_one)
    pieces_tok, pieces_one, came_mlp, block_two = fence((pieces_tok, pieces_one, came_mlp, block_two))

    held_two = {0: block_two, **single_steps(block_two)}
    mlp = inner_order(came_mlp)
    block_mlp = jnp.concatenate(
        [mlp[:, :up_part].reshape(up_rows, width), mlp[:, up_part:].reshape(up_rows, width)]
    )
    arrays_tok, places_tok = parts_of(pieces_tok, row_count, cut_tok)
    arrays_one, places_one = parts_of(pieces_one, qkv_rows + 16, cut_one)
    blended, qkv, attended, gains = pl.pallas_call(
        functools.partial(first_kernel, (dp_count, blocks, places_tok, places_one, qkv_rows)),
        out_shape=(
            whole((row_count, width), f32),
            whole((row_count, 3 * width), bf16),
            whole((row_count, width), bf16),
            whole((8, width), f32),
        ),
        in_specs=[SMEM, SMEM, VMEM, VMEM] + [ANY] * (len(arrays_tok) + len(arrays_one)),
        out_specs=(VMEM,) * 4,
        scratch_shapes=[
            pltpu.VMEM((blocks, CLIP, width), bf16),
            pltpu.VMEM((3 * width, width), bf16),
            pltpu.VMEM((dp_count, 16, width), bf16),
            pltpu.SemaphoreType.DMA((blocks + len(arrays_one) + dp_count,)),
        ],
        compiler_params=params(),
        cost_estimate=cost(2e9 * 10, 12e6),
        name="mix_self_attention",
    )(ints, mix_weight, seg_row, tokens, *arrays_tok, *arrays_one)
    held_two, block_mlp = fence((held_two, block_mlp))

    relay_steps(held_two, cut_two)
    pieces_two = core_steps(held_two)
    held_mlp = {0: block_mlp, **single_steps(block_mlp)}
    arrays_two, places_two = parts_of(pieces_two, rows_two, cut_two)
    wide = [pltpu.VMEM((sizes * fsdp_count * dp_count, width), bf16) for sizes in sizes_two]
    n_two = 4 * dp_count
    residual, cq, ckv, crossed, joined, second = pl.pallas_call(
        functools.partial(second_kernel, (blocks, places_two, layout)),
        out_shape=(
            whole((row_count, width), f32),
            whole((row_count, width), bf16),
            whole((coarse_rows, 2 * width), bf16),
            whole((row_count, width), bf16),
            whole((row_count, width), f32),
            whole((row_count, width), bf16),
        ),
        in_specs=[SMEM] + [VMEM] * 5 + [ANY] * len(arrays_two),
        out_specs=(VMEM,) * 6,
        scratch_shapes=wide + [pltpu.SemaphoreType.DMA((n_two,))],
        compiler_params=params(),
        cost_estimate=cost(2e9 * 10, 12e6),
        name="cross_attention",
    )(ints, coarse_seg, coarse_view, blended, attended, gains, *arrays_two)
    held_mlp = fence(held_mlp)

    singles = dict(held_mlp)
    pieces_mlp = core_steps(singles)
    relay_steps(held_mlp, cut_mlp)
    late = core_steps({e: b for e, b in held_mlp.items() if isinstance(b, tuple)})

    def mlp_call(pieces, carried):
        groups = tuple(sorted({e // 2 for e in pieces}))
        arrays, places = [], []
        for e in sorted(pieces):
            block = pieces[e]
            if isinstance(block, tuple):
                arrays += list(block)
                places += [(e, 0, 0), (e, 1, 0)]
            else:
                arrays.append(block)
                places.append((e, None, 0))
        count = len(groups)
        fixed = pl.BlockSpec((row_count, width), lambda g: (0, 0))
        moving = pl.BlockSpec((1, 2, up_rows, width), lambda g: (g, 0, 0, 0))
        keep, send, out, grad = pl.pallas_call(
            functools.partial(mlp_kernel, (groups, tuple(places), up_rows, bool(carried))),
            grid=(count,),
            out_shape=(
                whole((count, 2, up_rows, width), bf16),
                whole((count, 2, up_rows, width), bf16),
                whole((row_count, width), f32),
                whole((row_count, width), f32),
            ),
            in_specs=[fixed, fixed] + [ANY] * len(arrays) + [fixed] * len(carried),
            out_specs=(moving, moving, fixed, fixed),
            scratch_shapes=[
                pltpu.VMEM((count, 2 * up_rows, width), bf16),
                pltpu.VMEM((count, 2 * up_rows, width), bf16),
                pltpu.VMEM((row_count, 2 * up_rows), bf16),
                pltpu.VMEM((row_count, 2 * up_rows), bf16),
                pltpu.SemaphoreType.DMA((4 * count,)),
            ],
            compiler_params=params(),
            cost_estimate=cost(7.2e9 * count, 8e6 * count),
            name="feed_forward",
        )(second, cotangent, *arrays, *carried)
        flat = (count, 2 * up_rows, width)
        return groups, keep.reshape(flat), send.reshape(flat), out, grad

    groups_a, keep_a, send_a, out_a, grad_a = mlp_call(pieces_mlp, ())
    groups_b, keep_b, send_b, mlp_out, grad_second = mlp_call(late, (out_a, grad_a))

    total_b = add_low(keep_b, swap(send_b, CORE))
    total_a = add_low(keep_a, swap(send_a, CORE))
    where = {g: total_a[i] for i, g in enumerate(groups_a)}
    where.update({g: total_b[i] for i, g in enumerate(groups_b)})

    output, coarse_grad, grad_res, grad_att, gain_grads, keep_two, send_two = pl.pallas_call(
        functools.partial(third_kernel, (blocks, places_two, layout, dp_count)),
        out_shape=(
            whole((row_count, width), bf16),
            whole((coarse_rows, width), f32),
            whole((row_count, width), f32),
            whole((row_count, width), bf16),
            whole((8, width), f32),
            whole((pairs, rows_two, width), bf16),
            whole((pairs, rows_two, width), bf16),
        ),
        in_specs=[SMEM] + [VMEM] * 12 + [ANY] * len(arrays_two),
        out_specs=(VMEM,) * 5 + (ANY,) * 2,
        scratch_shapes=wide
        + wide
        + [
            pltpu.VMEM((row_count, width), bf16),
            pltpu.VMEM((row_count, width), bf16),
            pltpu.VMEM((row_count, width), bf16),
            pltpu.VMEM((coarse_rows, width), f32),
            pltpu.VMEM((coarse_rows, width), f32),
            pltpu.VMEM((row_count, width), f32),
            pltpu.SemaphoreType.DMA((n_two + 4 * dp_count,)),
        ],
        compiler_params=params(),
        cost_estimate=cost(2e9 * 12, 30e6),
        name="cross_attention_backward",
    )(
        ints, coarse_seg, coarse_view, gains, mlp_out, grad_second, joined, cotangent, residual, attended, crossed, cq, ckv,
        *arrays_two,
    )

    base, keep_one, send_one, keep_tok, send_tok = pl.pallas_call(
        functools.partial(fourth_kernel, (dp_count, blocks, places_one, qkv_rows)),
        out_shape=(
            whole((row_count, width), f32),
            whole((pairs, qkv_rows + 16, width), bf16),
            whole((pairs, qkv_rows + 16, width), bf16),
            whole((pairs, row_count, width), bf16),
            whole((pairs, row_count, width), bf16),
        ),
        in_specs=[SMEM, SMEM] + [VMEM] * 7 + [ANY] * len(arrays_one),
        out_specs=(VMEM,) + (ANY,) * 4,
        scratch_shapes=[
            pltpu.VMEM((3 * width, width), bf16),
            pltpu.VMEM((3 * width, width), bf16),
            pltpu.VMEM((row_count, 3 * width), bf16),
            pltpu.VMEM((row_count, width), f32),
            pltpu.VMEM((row_count, width), f32),
            pltpu.VMEM((dp_count * blocks, CLIP, width), bf16),
            pltpu.VMEM((16, width), bf16),
            pltpu.SemaphoreType.DMA((len(arrays_one) + 2 * dp_count + dp_count * blocks,)),
        ],
        compiler_params=params(),
        cost_estimate=cost(2e9 * 12, 30e6),
        name="self_attention_backward",
    )(ints, mix_weight, seg_row, gains, gain_grads, blended, grad_res, grad_att, qkv, *arrays_one)

    mlp_sum = outer_sum(jnp.stack([where[g] for g in range(pairs)]), cut_mlp)
    mlp_parts = jnp.concatenate(
        [mlp_sum[:up_rows].reshape(fsdp_count, up_part, width), mlp_sum[up_rows:].reshape(fsdp_count, up_part, width)], axis=1
    )
    mlp_mine = inner_sum(mlp_parts)
    up_shard, down_shard = mlp_mine[:up_part].T, mlp_mine[up_part:]

    two_sum = outer_sum(add_low(keep_two, swap(send_two, CORE)), cut_two)
    two_parts = jnp.concatenate(
        [two_sum[first : first + size].reshape(fsdp_count, size // fsdp_count, width) for first, size in layout], axis=1
    )
    two_mine = inner_sum(two_parts)
    found = []
    at = 0
    for size in sizes_two:
        found.append(two_mine[at : at + size])
        at += size
    ckv_shard, out_shard, cq_shard, cout_shard = found[0].T, found[1], found[2], found[3]

    one_sum = outer_sum(add_low(keep_one, swap(send_one, CORE)), cut_one)
    gain_sum = jnp.broadcast_to(one_sum[qkv_rows : qkv_rows + 8][None], (fsdp_count, 8, width))
    one_parts = jnp.concatenate([one_sum[:qkv_rows].reshape(fsdp_count, qkv_part, width), gain_sum], axis=1)
    one_mine = inner_sum(one_parts)
    qkv_shard = one_mine[:qkv_part].T
    gain_mine = lax.dynamic_slice(one_mine[qkv_part:], (0, device_me * part), (3, part))

    token_grad = base + outer_sum(add_low(keep_tok, swap(send_tok, CORE)), cut_tok)
    return (
        output,
        token_grad,
        coarse_grad,
        gain_mine[0],
        qkv_shard,
        out_shard,
        gain_mine[1],
        cq_shard,
        ckv_shard,
        cout_shard,
        gain_mine[2],
        up_shard,
        down_shard,
    )


def solution(mesh):
    rows = P(("dp", "fsdp"), None)
    columns = P(None, ("dp", "fsdp"))
    line = P(("dp", "fsdp"))
    in_specs = (
        rows, rows, rows, rows, line, line, line, columns, rows,
        line, rows, columns, rows, line, columns, rows, rows,
    )
    out_specs = (
        rows, rows, rows, line, columns, rows, line, rows, columns, rows, line, columns, rows,
    )
    return jax.shard_map(shards, mesh=mesh, in_specs=in_specs, out_specs=out_specs, check_vma=False)
```

```python
import functools

import jax
import jax.numpy as jnp
from jax import lax
from jax.experimental import pallas as pl
from jax.experimental.pallas import tpu as pltpu
from jax.sharding import PartitionSpec as P

HEADS = 12
HEAD = 64
PAIR = 2 * HEAD
CORE = 1
CLIP = 128
WINDOW = 256
TILE = 256
VMEM_BYTES = 56 * 1024 * 1024
f32 = jnp.float32
bf16 = jnp.bfloat16
fence = lax.optimization_barrier


def swap(values, mask):
    count = lax.axis_size("dp")
    return lax.ppermute(values, "dp", [(i, i ^ mask) for i in range(count)])


def shift(values, step):
    count = lax.axis_size("fsdp")
    return lax.ppermute(values, "fsdp", [(i, (i + step) % count) for i in range(count)])


def link_masks():
    masks = []
    mask = 2
    while mask < lax.axis_size("dp"):
        masks.append(mask)
        mask *= 2
    return masks


def relays():
    found = []
    for e in range(2, lax.axis_size("dp"), 2):
        if e & (e - 1):
            found.append((bin(e).count("1"), e, 1 << (e.bit_length() - 1), e & -e))
    return [item[1:] for item in sorted(found)]


def inner_gather(shard):
    count = lax.axis_size("fsdp")
    me = lax.axis_index("fsdp")
    held = shard[None]
    mask = 1
    while mask < count:
        came = lax.ppermute(held, "fsdp", [(i, i ^ mask) for i in range(count)])
        high = (me & mask) != 0
        held = jnp.concatenate([jnp.where(high, came, held), jnp.where(high, held, came)])
        mask *= 2
    return held


def inner_start(shard):
    return [shard] + [shift(shard, step) for step in range(1, lax.axis_size("fsdp"))]


def inner_order(came):
    count = len(came)
    me = lax.axis_index("fsdp")
    line = [came[count - 1 - k] for k in range(count)] + [came[count - k] for k in range(1, count)]
    return lax.dynamic_slice_in_dim(jnp.stack(line), count - 1 - me, count, 0)


def single_steps(block):
    return {mask: swap(block, mask) for mask in link_masks()}


def relay_steps(held, cut):
    def half_of(e, which):
        block = held[e]
        if isinstance(block, tuple):
            return block[which]
        return block[:cut] if which == 0 else block[cut:]

    for e, top, low in relays():
        held[e] = (swap(half_of(e ^ top, 0), top), swap(half_of(e ^ low, 1), low))


def parts_of(pieces, total, cut):
    arrays, places = [], []
    for e in sorted(pieces):
        block = pieces[e]
        if isinstance(block, tuple):
            arrays += [block[0], block[1]]
            places += [(e, 0, cut), (e, cut, total - cut)]
        else:
            arrays.append(block)
            places.append((e, 0, total))
    return arrays, tuple(places)


def core_steps(held):
    out = dict(held)
    for e, block in held.items():
        if isinstance(block, tuple):
            out[e | CORE] = tuple(swap(half, CORE) for half in block)
        else:
            out[e | CORE] = swap(block, CORE)
    return out


def add_low(a, b):
    return (a.astype(f32) + b.astype(f32)).astype(bf16)


class OuterSum:
    def __init__(self, total, cut):
        self.held = {2 * g: block for g, block in enumerate(total)}
        self.cut = cut
        self.extra = {e: {0: [], 1: []} for e in self.held}
        self.came = []

    def half(self, e, which):
        part = self.held[e][: self.cut] if which == 0 else self.held[e][self.cut :]
        for came in self.extra[e][which]:
            part = add_low(part, came)
        return part

    def relays(self):
        for e, top, low in relays()[::-1]:
            self.extra[e ^ top][0].append(swap(self.half(e, 0), top))
            self.extra[e ^ low][1].append(swap(self.half(e, 1), low))

    def singles(self):
        self.came = [
            swap(jnp.concatenate([self.half(mask, 0), self.half(mask, 1)]), mask) for mask in link_masks()
        ]

    def result(self):
        total = self.held[0].astype(f32)
        for block in self.came:
            total = total + block.astype(f32)
        return total

    def state(self):
        return (self.held, self.extra, self.came)

    def put(self, state):
        self.held, self.extra, self.came = state


class InnerSum:
    def __init__(self, parts):
        count = parts.shape[0]
        me = lax.axis_index("fsdp")
        low = parts.astype(bf16)
        self.own = lax.dynamic_index_in_dim(parts, me, 0, keepdims=False)
        self.came = [
            shift(lax.dynamic_index_in_dim(low, (me + step) % count, 0, keepdims=False), step) for step in range(1, count)
        ]

    def result(self):
        total = self.own
        for block in self.came:
            total = total + block.astype(f32)
        return total


def nn(a, b):
    return jnp.dot(a, b, preferred_element_type=f32)


def nt(a, b):
    return lax.dot_general(a, b, (((1,), (1,)), ((), ())), preferred_element_type=f32)


def tn(a, b):
    return lax.dot_general(a, b, (((0,), (0,)), ((), ())), preferred_element_type=f32)


def tiles(size):
    step = TILE if size % TILE == 0 else size
    return [(at, step) for at in range(0, size, step)]


def centred(values):
    centre = jnp.mean(values, axis=-1, keepdims=True)
    shifted = values - centre
    spread = jnp.mean(shifted * shifted, axis=-1, keepdims=True)
    r = lax.rsqrt(spread + 1e-06)
    return shifted * r, r


def norm_back(xhat, r, gain, grad):
    c = grad * gain
    first = jnp.mean(c, axis=-1, keepdims=True)
    second = jnp.mean(c * xhat, axis=-1, keepdims=True)
    return r * (c - first - xhat * second), jnp.sum(grad * xhat, axis=0, keepdims=True)


def lower_half(rows):
    return lax.broadcasted_iota(jnp.int32, (rows, PAIR), 1) < HEAD


def two_heads(rows):
    keep = lower_half(rows.shape[0])
    zero = jnp.zeros_like(rows)
    return jnp.concatenate([jnp.where(keep, rows, zero), jnp.where(keep, zero, rows)], axis=0)


def side_by_side(stacked):
    rows = stacked.shape[0] // 2
    return jnp.where(lower_half(rows), stacked[:rows], stacked[rows:])


def softmax_rows(scores):
    raised = jnp.exp(scores - jnp.max(scores, axis=-1, keepdims=True))
    return raised / jnp.sum(raised, axis=-1, keepdims=True)


def bias_of(key_seg, own_seg):
    return jnp.where(key_seg == own_seg, 0.0, -1e30).astype(f32)


def block_bias(key_seg, ints, blocks):
    return jnp.stack([bias_of(key_seg[...], ints[1 + 3 * blocks + i]) for i in range(blocks)])


def biased(scores, bias):
    blocks, _, keys = bias.shape
    rows = scores.shape[0] // (2 * blocks)
    return (scores.reshape(2, blocks, rows, keys) + bias[None]).reshape(scores.shape)


def copies(jobs, sems, at):
    made = [pltpu.make_async_copy(src, dst, sems.at[at + i]) for i, (src, dst) in enumerate(jobs)]
    for job in made:
        job.start()
    return made


def whole(shape, dtype):
    return jax.ShapeDtypeStruct(shape, dtype)


VMEM = pl.BlockSpec(memory_space=pltpu.VMEM)
SMEM = pl.BlockSpec(memory_space=pltpu.SMEM)
ANY = pl.BlockSpec(memory_space=pl.ANY)


def params():
    return pltpu.CompilerParams(vmem_limit_bytes=VMEM_BYTES)


def cost(flops, moved, exps=0):
    return pl.CostEstimate(flops=int(flops), bytes_accessed=int(moved), transcendentals=int(exps))


def first_kernel(
    geometry, ints, mix, seg_row, tokens, *refs
):
    dp_count, blocks, token_places, qkv_places, qkv_rows = geometry
    n_tok, n_qkv = len(token_places), len(qkv_places)
    token_refs, qkv_refs = refs[:n_tok], refs[n_tok : n_tok + n_qkv]
    blended_ref, qkv_ref, attended_ref, gains_ref, partner, weight, gain_parts, sems = refs[n_tok + n_qkv :]
    me = ints[0]
    width = tokens.shape[1]

    for b in range(blocks):
        rel, slot = ints[1 + b], ints[1 + blocks + b]
        for ref, (e, start, rows) in zip(token_refs, token_places):
            inside = (rel == e) & (slot * CLIP >= start) & (slot * CLIP < start + rows)

            @pl.when(inside)
            def _(ref=ref, start=start, rows=rows, b=b, slot=slot):
                at = pl.multiple_of(jnp.clip(slot * CLIP - start, 0, rows - CLIP), CLIP)
                pltpu.make_async_copy(ref.at[pl.ds(at, CLIP)], partner.at[b], sems.at[b]).start()

    jobs = []
    for ref, (e, start, rows) in zip(qkv_refs, qkv_places):
        take = min(rows, qkv_rows - start)
        at = pl.multiple_of((me ^ e) * qkv_rows + start, 16)
        jobs.append((ref.at[pl.ds(0, take)], weight.at[pl.ds(at, take)]))
        if start + rows > qkv_rows:
            jobs.append((ref.at[pl.ds(take, rows - take)], gain_parts.at[e]))
    made = copies(jobs, sems, blocks)
    for b in range(blocks):
        pltpu.make_async_copy(tokens.at[pl.ds(0, CLIP)], partner.at[b], sems.at[b]).wait()
    for b in range(blocks):
        rows = slice(b * CLIP, (b + 1) * CLIP)
        share = mix[b]
        blended_ref[rows, :] = share * tokens[rows, :].astype(f32) + (1.0 - share) * partner[b].astype(f32)
    for job in made:
        job.wait()
    gains = gain_parts[0].astype(f32)
    for e in range(1, dp_count):
        gains = gains + gain_parts[e].astype(f32)
    gains_ref[...] = gains[:8]
    xhat, _ = centred(blended_ref[...])
    normed = (xhat * gains[0:1]).astype(bf16)
    for at, step in tiles(3 * width):
        tile = nt(normed, weight[at : at + step, :])
        if at + step <= width:
            tile = tile * 0.125
        qkv_ref[:, at : at + step] = tile.astype(bf16)

    @pl.loop(0, blocks)
    def _(i):
        window = pl.multiple_of(ints[1 + 2 * blocks + i] * CLIP, CLIP)
        bias = bias_of(seg_row[:, pl.ds(window, WINDOW)], ints[1 + 3 * blocks + i])
        rows = pl.ds(pl.multiple_of(i * CLIP, CLIP), CLIP)
        keys = pl.ds(window, WINDOW)
        for at in range(0, width, PAIR):
            queries = two_heads(qkv_ref[rows, at : at + PAIR])
            probs = softmax_rows(nt(queries, qkv_ref[keys, width + at : width + at + PAIR]) + bias).astype(bf16)
            out = nn(probs, qkv_ref[keys, 2 * width + at : 2 * width + at + PAIR])
            attended_ref[rows, at : at + PAIR] = side_by_side(out).astype(bf16)


def load_cross(me, refs, places, layout, weights, sems):
    jobs = []
    for ref, (e, start, rows) in zip(refs, places):
        for (first, size), weight in zip(layout, weights):
            if weight is not None and first >= start and first + size <= start + rows:
                at = pl.multiple_of((me ^ e) * size, 16)
                jobs.append((ref.at[pl.ds(first - start, size)], weight.at[pl.ds(at, size)]))
    return copies(jobs, sems, 0)


def second_kernel(geometry, ints, coarse_seg, coarse, blended, attended, gains, *refs):
    blocks, places, layout = geometry
    weight_refs = refs[: len(places)]
    residual_ref, cq_ref, ckv_ref, crossed_ref, joined_ref, second_ref = refs[len(places) : len(places) + 6]
    w_ckv, w_out, w_cq, w_cout, sems = refs[len(places) + 6 :]
    made = load_cross(ints[0], weight_refs, places, layout, (w_ckv, w_out, w_cq, w_cout), sems)
    for job in made:
        job.wait()
    width = blended.shape[1]
    for at, step in tiles(2 * width):
        ckv_ref[:, at : at + step] = nt(coarse[...], w_ckv[at : at + step, :]).astype(bf16)
    for at, step in tiles(width):
        residual_ref[:, at : at + step] = blended[:, at : at + step] + nn(attended[...], w_out[:, at : at + step])
    xhat, _ = centred(residual_ref[...])
    crossed_in = (xhat * gains[1:2]).astype(bf16)
    for at, step in tiles(width):
        cq_ref[:, at : at + step] = (nn(crossed_in, w_cq[:, at : at + step]) * 0.125).astype(bf16)

    bias = block_bias(coarse_seg, ints, blocks)
    for at in range(0, width, PAIR):
        queries = two_heads(cq_ref[:, at : at + PAIR])
        probs = softmax_rows(biased(nt(queries, ckv_ref[:, at : at + PAIR]), bias)).astype(bf16)
        out = nn(probs, ckv_ref[:, width + at : width + at + PAIR])
        crossed_ref[:, at : at + PAIR] = side_by_side(out).astype(bf16)

    for at, step in tiles(width):
        joined_ref[:, at : at + step] = residual_ref[:, at : at + step] + nn(crossed_ref[...], w_cout[:, at : at + step])
    xhat, _ = centred(joined_ref[...])
    second_ref[...] = (xhat * gains[2:3]).astype(bf16)


def mlp_kernel(geometry, second, cotangent, *refs):
    groups, places, rows, carried = geometry
    weight_refs = refs[: len(places)]
    refs = refs[len(places) :]
    if carried:
        out_in, grad_in = refs[:2]
        refs = refs[2:]
    keep_ref, send_ref, out_ref, grad_ref, w_up, w_down, hidden, grad_pre, sems = refs
    step = pl.program_id(0)

    def jobs_of(group):
        jobs = []
        for ref, (e, which, start) in zip(weight_refs, places):
            if e // 2 == groups[group]:
                for part, weight in ((0, w_up), (1, w_down)):
                    if which is None or which == part:
                        first = part * rows if which is None else 0
                        dst = weight.at[group, pl.ds((e & 1) * rows, rows)]
                        jobs.append((ref.at[pl.ds(first, rows)], dst))
        return jobs

    at = 0
    for group in range(len(groups)):
        jobs = jobs_of(group)
        made = [pltpu.make_async_copy(s, d, sems.at[at + i]) for i, (s, d) in enumerate(jobs)]
        at += len(jobs)

        @pl.when(step == 0)
        def _(made=made):
            for job in made:
                job.start()

        @pl.when(step == group)
        def _(made=made):
            for job in made:
                job.wait()

    @pl.when(step == 0)
    def _():
        if carried:
            out_ref[...] = out_in[...]
            grad_ref[...] = grad_in[...]
        else:
            out_ref[...] = jnp.zeros_like(out_ref)
            grad_ref[...] = jnp.zeros_like(grad_ref)

    up, down = w_up.at[step], w_down.at[step]
    both = 2 * rows
    for first, size in tiles(both):
        pre = nt(second[...], up[first : first + size, :])
        grad_hidden = nt(cotangent[...], down[first : first + size, :])
        cdf = 0.5 * (1.0 + lax.erf(pre * 0.7071067811865476))
        slope = cdf + pre * (jnp.exp(-0.5 * pre * pre) * 0.3989422804014327)
        hidden[:, first : first + size] = (pre * cdf).astype(bf16)
        grad_pre[:, first : first + size] = (grad_hidden * slope).astype(bf16)
    for first, target in ((0, keep_ref), (rows, send_ref)):
        target[0, 0] = tn(grad_pre[:, first : first + rows], second[...]).astype(bf16)
        target[0, 1] = tn(hidden[:, first : first + rows], cotangent[...]).astype(bf16)
    for first, size in tiles(second.shape[1]):
        out_ref[:, first : first + size] += nn(hidden[...], down[:, first : first + size])
        grad_ref[:, first : first + size] += nn(grad_pre[...], up[:, first : first + size])


def grads_out(me, dp_count, layout, sources, keep_ref, send_ref, sems, at):
    jobs = []
    for e in range(dp_count):
        target = send_ref if e & CORE else keep_ref
        for (first, size), source in zip(layout, sources):
            if source is None:
                continue
            row = pl.multiple_of((me ^ e) * size, 16)
            jobs.append((source.at[pl.ds(row, size)], target.at[e // 2, pl.ds(first, size)]))
    return copies(jobs, sems, at)


def third_kernel(
    geometry, ints, coarse_seg, gains, mlp_out, grad_second, joined, cotangent, crossed, cq, ckv, *refs
):
    blocks, places, layout, dp_count = geometry
    weight_refs = refs[: len(places)]
    refs = refs[len(places) :]
    output_ref, grad_joined_ref, grad_cq_ref, grad_ckv_ref, gain_grads_ref, keep_ref, send_ref = refs[:7]
    w_cout, g_cout, grad_cross, sems = refs[7:]
    me = ints[0]
    width = joined.shape[1]
    made = load_cross(me, weight_refs, places, layout, (None, None, None, w_cout), sems)
    output_ref[...] = (joined[...] + mlp_out[...]).astype(bf16)
    xhat, r = centred(joined[...])
    grad_in, gain_two = norm_back(xhat, r, gains[2:3], grad_second[...])
    grad_joined_ref[...] = cotangent[...].astype(f32) + grad_in
    low = grad_joined_ref[...].astype(bf16)
    for job in made:
        job.wait()
    for at, step in tiles(width):
        grad_cross[:, at : at + step] = nt(low, w_cout[at : at + step, :]).astype(bf16)
    for at, step in tiles(width):
        g_cout[at : at + step, :] = tn(crossed[:, at : at + step], low).astype(bf16)
    going = grads_out(me, dp_count, layout, (None, None, None, g_cout), keep_ref, send_ref, sems, len(made))
    bias = block_bias(coarse_seg, ints, blocks)
    for at in range(0, width, PAIR):
        lanes = slice(at, at + PAIR)
        queries = two_heads(cq[:, lanes])
        grads = two_heads(grad_cross[:, lanes])
        keys = ckv[:, lanes]
        values = ckv[:, width + at : width + at + PAIR]
        probs = softmax_rows(biased(nt(queries, keys), bias))
        grad_ckv_ref[:, width + at : width + at + PAIR] = tn(probs.astype(bf16), grads).astype(bf16)
        grad_probs = nt(grads, values)
        inner = jnp.sum(probs * grad_probs, axis=-1, keepdims=True)
        scores = (probs * (grad_probs - inner)).astype(bf16)
        part = side_by_side(nn(scores, keys)).astype(bf16)
        grad_cq_ref[:, lanes] = part * jnp.asarray(0.125, bf16)
        grad_ckv_ref[:, lanes] = tn(scores, queries).astype(bf16)

    gain_grads_ref[...] = jnp.concatenate([gain_two] * 8, axis=0)
    for job in going:
        job.wait()


def third_part(geometry, ints, coarse, gains, gain_two, grad_joined, residual, attended, grad_cq, grad_ckv, keep_in, send_in, *refs):
    places, layout, dp_count = geometry
    weight_refs = refs[: len(places)]
    refs = refs[len(places) :]
    coarse_ref, grad_res_ref, grad_att_ref, gain_grads_ref, keep_ref, send_ref = refs[:6]
    w_ckv, w_out, w_cq, g_ckv, g_out, g_cq, crossed_in, sems = refs[6:]
    me = ints[0]
    width = residual.shape[1]
    made = load_cross(me, weight_refs, places, layout, (w_ckv, w_out, w_cq, None), sems)
    xhat, r = centred(residual[...])
    crossed_in[...] = (xhat * gains[1:2]).astype(bf16)
    for at, step in tiles(width):
        g_cq[at : at + step, :] = tn(crossed_in[:, at : at + step], grad_cq[...]).astype(bf16)
    for at, step in tiles(2 * width):
        g_ckv[at : at + step, :] = tn(grad_ckv[:, at : at + step], coarse[...]).astype(bf16)
    for job in made:
        job.wait()
    going = grads_out(me, dp_count, layout, (g_ckv, None, g_cq, None), keep_ref, send_ref, sems, 0)
    for at, step in tiles(width):
        coarse_ref[:, at : at + step] = nn(grad_ckv[:, 0:width], w_ckv[0:width, at : at + step]) + nn(
            grad_ckv[:, width : 2 * width], w_ckv[width : 2 * width, at : at + step]
        )
    pieces = [nt(grad_cq[...], w_cq[at : at + step, :]) for at, step in tiles(width)]
    grad_in, gain_cross = norm_back(xhat, r, gains[1:2], jnp.concatenate(pieces, axis=1))
    grad_res = grad_joined[...] + grad_in
    grad_res_ref[...] = grad_res
    low = grad_res.astype(bf16)
    for at, step in tiles(width):
        g_out[at : at + step, :] = tn(attended[:, at : at + step], low).astype(bf16)
    going += grads_out(me, dp_count, layout, (None, g_out, None, None), keep_ref, send_ref, sems, len(going))
    for at, step in tiles(width):
        grad_att_ref[:, at : at + step] = nt(low, w_out[at : at + step, :]).astype(bf16)
    zero = jnp.zeros_like(gain_cross)
    gain_grads_ref[...] = jnp.concatenate([zero, gain_cross, gain_two[0:1]] + [zero] * 5, axis=0)
    for job in going:
        job.wait()


def fourth_kernel(geometry, ints, seg_row, grad_att, qkv, grad_proj, key_sum, value_sum):
    (blocks,) = geometry
    width = grad_att.shape[1]
    key_sum[...] = jnp.zeros_like(key_sum)
    value_sum[...] = jnp.zeros_like(value_sum)

    @pl.loop(0, blocks)
    def _(i):
        window = pl.multiple_of(ints[1 + 2 * blocks + i] * CLIP, CLIP)
        bias = bias_of(seg_row[:, pl.ds(window, WINDOW)], ints[1 + 3 * blocks + i])
        rows = pl.ds(pl.multiple_of(i * CLIP, CLIP), CLIP)
        near = pl.ds(window, WINDOW)
        for at in range(0, width, PAIR):
            lanes = slice(at, at + PAIR)
            queries = two_heads(qkv[rows, lanes])
            grads = two_heads(grad_att[rows, lanes])
            keys = qkv[near, width + at : width + at + PAIR]
            values = qkv[near, 2 * width + at : 2 * width + at + PAIR]
            probs = softmax_rows(nt(queries, keys) + bias)
            value_sum[near, lanes] += tn(probs.astype(bf16), grads)
            grad_probs = nt(grads, values)
            inner = jnp.sum(probs * grad_probs, axis=-1, keepdims=True)
            scores = (probs * (grad_probs - inner)).astype(bf16)
            part = side_by_side(nn(scores, keys)).astype(bf16)
            grad_proj[rows, lanes] = part * jnp.asarray(0.125, bf16)
            key_sum[near, lanes] += tn(scores, queries)

    grad_proj[:, width : 2 * width] = key_sum[...].astype(bf16)
    grad_proj[:, 2 * width : 3 * width] = value_sum[...].astype(bf16)


def fifth_kernel(geometry, ints, mix, gains, blended, grad_res, grad_proj, *refs):
    dp_count, blocks, qkv_places, qkv_rows = geometry
    weight_refs = refs[: len(qkv_places)]
    refs = refs[len(qkv_places) :]
    base_ref, gain_ref, mix_keep_ref, mix_send_ref = refs[:4]
    weight, going_back, sems = refs[4:]
    me = ints[0]
    width = blended.shape[1]
    jobs = []
    for ref, (e, start, rows) in zip(weight_refs, qkv_places):
        take = min(rows, qkv_rows - start)
        at = pl.multiple_of((me ^ e) * qkv_rows + start, 16)
        jobs.append((ref.at[pl.ds(0, take)], weight.at[pl.ds(at, take)]))
    made = copies(jobs, sems, 0)
    going_back[...] = jnp.zeros_like(going_back)
    xhat, r = centred(blended[...])
    for job in made:
        job.wait()
    pieces = [nn(grad_proj[...], weight[:, at : at + step]) for at, step in tiles(width)]
    grad_in, gain_one = norm_back(xhat, r, gains[0:1], jnp.concatenate(pieces, axis=1))
    gain_ref[...] = jnp.concatenate([gain_one] * 8, axis=0)
    grad_blend = grad_res[...] + grad_in
    for b in range(blocks):
        rows = slice(b * CLIP, (b + 1) * CLIP)
        share = mix[b]
        part = grad_blend[rows, :]
        base_ref[rows, :] = share * part
        place = ints[1 + b] * blocks + ints[1 + blocks + b]
        going_back[place] = (going_back[place].astype(f32) + (1.0 - share) * part).astype(bf16)
    mixed = []
    for e in range(dp_count):
        target = mix_send_ref if e & CORE else mix_keep_ref
        for s in range(blocks):
            mixed.append((going_back.at[e * blocks + s], target.at[e // 2, pl.ds(s * CLIP, CLIP)]))
    for job in copies(mixed, sems, len(jobs)):
        job.wait()


def sixth_kernel(geometry, ints, gains, gain_grads, gain_one, blended, grad_proj, keep_ref, send_ref, grad_w, gain_rows, sems):
    dp_count, qkv_rows = geometry
    me = ints[0]
    width = blended.shape[1]
    xhat, _ = centred(blended[...])
    normed = (xhat * gains[0:1]).astype(bf16)
    all_gains = jnp.concatenate([gain_one[0:1], gain_grads[1:8], jnp.zeros((8, width), f32)], axis=0)
    gain_rows[...] = all_gains.astype(bf16)
    last = []
    for e in range(dp_count):
        target = send_ref if e & CORE else keep_ref
        last.append((gain_rows, target.at[e // 2, pl.ds(qkv_rows, 16)]))
    sent = copies(last, sems, 0)
    for at, step in tiles(3 * width):
        grad_w[at : at + step, :] = tn(grad_proj[:, at : at + step], normed).astype(bf16)
    sent += grads_out(me, dp_count, ((0, qkv_rows),), (grad_w,), keep_ref, send_ref, sems, dp_count)
    for job in sent:
        job.wait()


def shards(
    tokens,
    coarse_view,
    segment_ids,
    partner_device,
    partner_slot,
    mix_weight,
    ln1_gain,
    w_qkv,
    w_out,
    lnx_gain,
    w_cq,
    w_ckv,
    w_cout,
    ln2_gain,
    w_up,
    w_down,
    cotangent,
):
    row_count, width = tokens.shape
    coarse_rows = coarse_view.shape[0]
    blocks = mix_weight.shape[0]
    dp_count, fsdp_count = lax.axis_size("dp"), lax.axis_size("fsdp")
    dp_me, fsdp_me = lax.axis_index("dp"), lax.axis_index("fsdp")
    part = ln1_gain.shape[0]
    device_me = dp_me * fsdp_count + fsdp_me
    pairs = dp_count // 2

    target = partner_device[:, 0]
    segments = segment_ids[0]
    videos = segments.reshape(blocks, row_count // blocks)[:, 0]
    following = jnp.concatenate([videos[1:] == videos[:-1], jnp.zeros((1,), bool)])
    before = jnp.concatenate([jnp.zeros((1,), bool), videos[1:] == videos[:-1]])
    index = jnp.arange(blocks, dtype=jnp.int32)
    window = jnp.where(following, index, jnp.where(before, index - 1, jnp.minimum(index, blocks - 2)))
    ints = jnp.concatenate(
        [dp_me[None].astype(jnp.int32), (target ^ dp_me).astype(jnp.int32), partner_slot, window, videos]
    )
    seg_row = segments[None, :]
    coarse_seg = segments.reshape(coarse_rows, row_count // coarse_rows)[:, 0][None, :]

    gain_rows = lax.dynamic_update_slice(
        jnp.zeros((8, width), bf16), jnp.stack([ln1_gain, lnx_gain, ln2_gain]), (0, device_me * part)
    )
    shard_one = jnp.concatenate([w_qkv.T, gain_rows])
    shard_two = jnp.concatenate([w_ckv.T, w_out, w_cq, w_cout])
    shard_mlp = jnp.concatenate([w_up.T, w_down])
    sizes_two = (w_ckv.shape[1], w_out.shape[0], w_cq.shape[0], w_cout.shape[0])
    qkv_part, up_part = w_qkv.shape[1], w_up.shape[1]
    qkv_rows, up_rows = qkv_part * fsdp_count, up_part * fsdp_count
    layout = []
    at = 0
    for size in sizes_two:
        layout.append((at * fsdp_count, size * fsdp_count))
        at += size
    layout = tuple(layout)
    rows_two = at * fsdp_count

    cut_tok, cut_one, cut_two, cut_mlp = row_count // 2, qkv_rows // 2, layout[0][1], up_rows

    held_tok = {0: tokens, **single_steps(tokens)}
    came_one = inner_start(shard_one)
    held_tok, came_one, shard_two = fence((held_tok, came_one, shard_two))

    ones = inner_order(came_one)
    gain_block = jnp.sum(ones[:, qkv_part:].astype(f32), axis=0).astype(bf16)
    block_one = jnp.concatenate(
        [ones[:, :qkv_part].reshape(qkv_rows, width), gain_block, jnp.zeros((8, width), bf16)]
    )
    held_one = {0: block_one, **single_steps(block_one)}
    came_two = inner_start(shard_two)
    held_tok, held_one, came_two, shard_mlp = fence((held_tok, held_one, came_two, shard_mlp))

    mlp = inner_gather(shard_mlp)
    core_tok = core_steps({e: b for e, b in held_tok.items()})
    relay_steps(held_tok, cut_tok)
    twos = inner_order(came_two)
    split = []
    at = 0
    for size in sizes_two:
        split.append(twos[:, at : at + size].reshape(size * fsdp_count, width))
        at += size
    block_two = jnp.concatenate(split)
    held_one, core_tok, held_tok, block_two = fence((held_one, core_tok, held_tok, block_two))

    core_one = core_steps({e: b for e, b in held_one.items()})
    relay_steps(held_one, cut_one)
    late_tok = core_steps({e: b for e, b in held_tok.items() if isinstance(b, tuple)})
    held_one, core_one, late_tok, block_two = fence((held_one, core_one, late_tok, block_two))

    held_two = {0: block_two, **single_steps(block_two)}
    late_one = core_steps({e: b for e, b in held_one.items() if isinstance(b, tuple)})
    pieces_tok = {**core_tok, **late_tok}
    pieces_one = {**core_one, **late_one}
    arrays_tok, places_tok = parts_of(pieces_tok, row_count, cut_tok)
    arrays_one, places_one = parts_of(pieces_one, qkv_rows + 16, cut_one)
    blended, qkv, attended, gains = pl.pallas_call(
        functools.partial(first_kernel, (dp_count, blocks, places_tok, places_one, qkv_rows)),
        out_shape=(
            whole((row_count, width), f32),
            whole((row_count, 3 * width), bf16),
            whole((row_count, width), bf16),
            whole((8, width), f32),
        ),
        in_specs=[SMEM, SMEM, VMEM, VMEM] + [ANY] * (len(arrays_tok) + len(arrays_one)),
        out_specs=(VMEM,) * 4,
        scratch_shapes=[
            pltpu.VMEM((blocks, CLIP, width), bf16),
            pltpu.VMEM((3 * width, width), bf16),
            pltpu.VMEM((dp_count, 16, width), bf16),
            pltpu.SemaphoreType.DMA((blocks + len(arrays_one) + dp_count,)),
        ],
        compiler_params=params(),
        cost_estimate=cost(1e9, 1e6),
        name="mix_self_attention",
    )(ints, mix_weight, seg_row, tokens, *arrays_tok, *arrays_one)
    held_two, attended = fence((held_two, attended))

    core_two = core_steps({e: b for e, b in held_two.items()})
    relay_steps(held_two, cut_two)
    held_two, core_two, mlp = fence((held_two, core_two, mlp))

    block_mlp = jnp.concatenate(
        [mlp[:, :up_part].reshape(up_rows, width), mlp[:, up_part:].reshape(up_rows, width)]
    )
    held_mlp = {0: block_mlp, **single_steps(block_mlp)}
    late_two = core_steps({e: b for e, b in held_two.items() if isinstance(b, tuple)})
    pieces_two = {**core_two, **late_two}
    wide = [pltpu.VMEM((sizes * fsdp_count * dp_count, width), bf16) for sizes in sizes_two]
    n_two = 4 * dp_count
    arrays_two, places_two = parts_of(pieces_two, rows_two, cut_two)
    wide = [pltpu.VMEM((sizes * fsdp_count * dp_count, width), bf16) for sizes in sizes_two]
    n_two = 4 * dp_count
    residual, cq, ckv, crossed, joined, second = pl.pallas_call(
        functools.partial(second_kernel, (blocks, places_two, layout)),
        out_shape=(
            whole((row_count, width), f32),
            whole((row_count, width), bf16),
            whole((coarse_rows, 2 * width), bf16),
            whole((row_count, width), bf16),
            whole((row_count, width), f32),
            whole((row_count, width), bf16),
        ),
        in_specs=[SMEM] + [VMEM] * 5 + [ANY] * len(arrays_two),
        out_specs=(VMEM,) * 6,
        scratch_shapes=wide + [pltpu.SemaphoreType.DMA((n_two,))],
        compiler_params=params(),
        cost_estimate=cost(1e9, 1e6),
        name="cross_attention",
    )(ints, coarse_seg, coarse_view, blended, attended, gains, *arrays_two)
    held_mlp, second = fence((held_mlp, second))

    core_mlp = core_steps(dict(held_mlp))
    order = sorted({e & ~CORE for e in core_mlp})
    early, middle = order[:-1], order[-1:]
    pieces_early = {e: core_mlp[e] for g in early for e in (g, g | CORE)}
    pieces_middle = {e: core_mlp[e] for g in middle for e in (g, g | CORE)}
    relay_steps(held_mlp, cut_mlp)

    def mlp_call(pieces, carried):
        groups = tuple(sorted({e // 2 for e in pieces}))
        arrays, places = [], []
        for e in sorted(pieces):
            block = pieces[e]
            if isinstance(block, tuple):
                arrays += list(block)
                places += [(e, 0, 0), (e, 1, 0)]
            else:
                arrays.append(block)
                places.append((e, None, 0))
        count = len(groups)
        fixed = pl.BlockSpec((row_count, width), lambda g: (0, 0))
        moving = pl.BlockSpec((1, 2, up_rows, width), lambda g: (g, 0, 0, 0))
        keep, send, out, grad = pl.pallas_call(
            functools.partial(mlp_kernel, (groups, tuple(places), up_rows, bool(carried))),
            grid=(count,),
            out_shape=(
                whole((count, 2, up_rows, width), bf16),
                whole((count, 2, up_rows, width), bf16),
                whole((row_count, width), f32),
                whole((row_count, width), f32),
            ),
            in_specs=[fixed, fixed] + [ANY] * len(arrays) + [fixed] * len(carried),
            out_specs=(moving, moving, fixed, fixed),
            scratch_shapes=[
                pltpu.VMEM((count, 2 * up_rows, width), bf16),
                pltpu.VMEM((count, 2 * up_rows, width), bf16),
                pltpu.VMEM((row_count, 2 * up_rows), bf16),
                pltpu.VMEM((row_count, 2 * up_rows), bf16),
                pltpu.SemaphoreType.DMA((4 * count,)),
            ],
            compiler_params=params(),
            cost_estimate=cost(1e9, 1e6),
            name="feed_forward",
        )(second, cotangent, *arrays, *carried)
        flat = (count, 2 * up_rows, width)
        return groups, keep.reshape(flat), send.reshape(flat), out, grad

    groups_a, keep_a, send_a, out_a, grad_a = mlp_call(pieces_early, ())
    held_mlp, pieces_middle, keep_a, send_a, out_a, grad_a = fence((held_mlp, pieces_middle, keep_a, send_a, out_a, grad_a))

    late = core_steps({e: b for e, b in held_mlp.items() if isinstance(b, tuple)})
    came_a = swap(send_a, CORE)
    groups_m, keep_m, send_m, out_m, grad_m = mlp_call(pieces_middle, (out_a, grad_a))
    late, came_a, keep_m, send_m, out_m, grad_m = fence((late, came_a, keep_m, send_m, out_m, grad_m))

    came_m = swap(send_m, CORE)
    groups_b, keep_b, send_b, mlp_out, grad_second = mlp_call(late, (out_m, grad_m))
    came_m, keep_b, send_b, mlp_out, grad_second = fence((came_m, keep_b, send_b, mlp_out, grad_second))

    total_b = add_low(keep_b, swap(send_b, CORE))
    total_a = add_low(keep_a, came_a)
    total_m = add_low(keep_m, came_m)
    totals = [None] * pairs
    for groups, total in ((groups_a, total_a), (groups_m, total_m), (groups_b, total_b)):
        for i, g in enumerate(groups):
            totals[g] = total[i]
    totals, mlp_out = fence((totals, mlp_out))

    sum_mlp = OuterSum(totals, cut_mlp)
    sum_mlp.relays()
    output, grad_joined, grad_cq, grad_ckv, gain_two, keep_two, send_two = pl.pallas_call(
        functools.partial(third_kernel, (blocks, places_two, layout, dp_count)),
        out_shape=(
            whole((row_count, width), bf16),
            whole((row_count, width), f32),
            whole((row_count, width), bf16),
            whole((coarse_rows, 2 * width), bf16),
            whole((8, width), f32),
            whole((pairs, rows_two, width), bf16),
            whole((pairs, rows_two, width), bf16),
        ),
        in_specs=[SMEM] + [VMEM] * 9 + [ANY] * len(arrays_two),
        out_specs=(VMEM,) * 5 + (ANY,) * 2,
        scratch_shapes=[
            wide[3],
            wide[3],
            pltpu.VMEM((row_count, width), bf16),
            pltpu.SemaphoreType.DMA((n_two + dp_count,)),
        ],
        compiler_params=params(),
        cost_estimate=cost(1e9, 1e6),
        name="cross_attention_backward",
    )(ints, coarse_seg, gains, mlp_out, grad_second, joined, cotangent, crossed, cq, ckv, *arrays_two)
    state, grad_joined = fence((sum_mlp.state(), grad_joined))
    sum_mlp.put(state)

    sum_mlp.singles()
    coarse_grad, grad_res, grad_att, gain_grads, keep_two, send_two = pl.pallas_call(
        functools.partial(third_part, (places_two, layout, dp_count)),
        out_shape=(
            whole((coarse_rows, width), f32),
            whole((row_count, width), f32),
            whole((row_count, width), bf16),
            whole((8, width), f32),
            whole((pairs, rows_two, width), bf16),
            whole((pairs, rows_two, width), bf16),
        ),
        in_specs=[SMEM] + [VMEM] * 8 + [ANY] * (2 + len(arrays_two)),
        out_specs=(VMEM,) * 4 + (ANY,) * 2,
        scratch_shapes=[
            wide[0],
            wide[1],
            wide[2],
            wide[0],
            wide[1],
            wide[2],
            pltpu.VMEM((row_count, width), bf16),
            pltpu.SemaphoreType.DMA((n_two,)),
        ],
        input_output_aliases={9: 4, 10: 5},
        compiler_params=params(),
        cost_estimate=cost(1e9, 1e6),
        name="cross_attention_weights",
    )(
        ints, coarse_view, gains, gain_two, grad_joined, residual, attended, grad_cq, grad_ckv, keep_two, send_two, *arrays_two
    )

    (grad_proj,) = pl.pallas_call(
        functools.partial(fourth_kernel, (blocks,)),
        out_shape=(whole((row_count, 3 * width), bf16),),
        in_specs=[SMEM] + [VMEM] * 3,
        out_specs=(VMEM,),
        scratch_shapes=[pltpu.VMEM((row_count, width), f32), pltpu.VMEM((row_count, width), f32)],
        compiler_params=params(),
        cost_estimate=cost(1e9, 1e6),
        name="self_attention_backward",
    )(ints, seg_row, grad_att, qkv)
    state, grad_proj, keep_two, send_two = fence((sum_mlp.state(), grad_proj, keep_two, send_two))
    sum_mlp.put(state)

    came_two = swap(send_two, CORE)
    mlp_sum = sum_mlp.result()
    mlp_parts = jnp.concatenate(
        [mlp_sum[:up_rows].reshape(fsdp_count, up_part, width), mlp_sum[up_rows:].reshape(fsdp_count, up_part, width)], axis=1
    )
    inner_mlp = InnerSum(mlp_parts)
    base, gain_one, keep_tok, send_tok = pl.pallas_call(
        functools.partial(fifth_kernel, (dp_count, blocks, places_one, qkv_rows)),
        out_shape=(
            whole((row_count, width), f32),
            whole((8, width), f32),
            whole((pairs, row_count, width), bf16),
            whole((pairs, row_count, width), bf16),
        ),
        in_specs=[SMEM, SMEM] + [VMEM] * 4 + [ANY] * len(arrays_one),
        out_specs=(VMEM,) * 2 + (ANY,) * 2,
        scratch_shapes=[
            pltpu.VMEM((3 * width, width), bf16),
            pltpu.VMEM((dp_count * blocks, CLIP, width), bf16),
            pltpu.SemaphoreType.DMA((len(arrays_one) + dp_count * blocks,)),
        ],
        compiler_params=params(),
        cost_estimate=cost(1e9, 1e6),
        name="self_attention_input",
    )(ints, mix_weight, gains, blended, grad_res, grad_proj, *arrays_one)
    came_two, keep_tok, send_tok, gain_one = fence((came_two, keep_tok, send_tok, gain_one))

    sum_two = OuterSum(add_low(keep_two, came_two), cut_two)
    sum_two.relays()
    came_tok = swap(send_tok, CORE)
    keep_one, send_one = pl.pallas_call(
        functools.partial(sixth_kernel, (dp_count, qkv_rows)),
        out_shape=(
            whole((pairs, qkv_rows + 16, width), bf16),
            whole((pairs, qkv_rows + 16, width), bf16),
        ),
        in_specs=[SMEM] + [VMEM] * 5,
        out_specs=(ANY,) * 2,
        scratch_shapes=[
            pltpu.VMEM((3 * width, width), bf16),
            pltpu.VMEM((16, width), bf16),
            pltpu.SemaphoreType.DMA((2 * dp_count,)),
        ],
        compiler_params=params(),
        cost_estimate=cost(1e9, 1e6),
        name="self_attention_weights",
    )(ints, gains, gain_grads, gain_one, blended, grad_proj)
    state, came_tok, keep_one, send_one, mlp_came = fence((sum_two.state(), came_tok, keep_one, send_one, inner_mlp.came))
    sum_two.put(state)
    inner_mlp.came = mlp_came

    sum_two.singles()
    came_one = swap(send_one, CORE)
    total_tok = add_low(keep_tok, came_tok)
    state, came_one, total_tok = fence((sum_two.state(), came_one, total_tok))
    sum_two.put(state)

    sum_one, sum_tok = OuterSum(add_low(keep_one, came_one), cut_one), OuterSum(total_tok, cut_tok)
    sum_one.relays()
    sum_tok.relays()
    two_sum = sum_two.result()
    two_parts = jnp.concatenate(
        [two_sum[first : first + size].reshape(fsdp_count, size // fsdp_count, width) for first, size in layout], axis=1
    )
    inner_two = InnerSum(two_parts)
    state, state_tok, two_came = fence((sum_one.state(), sum_tok.state(), inner_two.came))
    sum_one.put(state)
    sum_tok.put(state_tok)
    inner_two.came = two_came

    sum_one.singles()
    state = fence(sum_one.state())
    sum_one.put(state)
    sum_tok.singles()
    one_sum = sum_one.result()
    gain_sum = jnp.broadcast_to(one_sum[qkv_rows : qkv_rows + 8][None], (fsdp_count, 8, width))
    one_parts = jnp.concatenate([one_sum[:qkv_rows].reshape(fsdp_count, qkv_part, width), gain_sum], axis=1)
    one_mine = InnerSum(one_parts).result()

    mlp_mine = inner_mlp.result()
    up_shard, down_shard = mlp_mine[:up_part].T, mlp_mine[up_part:]
    two_mine = inner_two.result()
    found = []
    at = 0
    for size in sizes_two:
        found.append(two_mine[at : at + size])
        at += size
    ckv_shard, out_shard, cq_shard, cout_shard = found[0].T, found[1], found[2], found[3]
    qkv_shard = one_mine[:qkv_part].T
    gain_mine = lax.dynamic_slice(one_mine[qkv_part:], (0, device_me * part), (3, part))
    token_grad = base + sum_tok.result()
    return (
        output,
        token_grad,
        coarse_grad,
        gain_mine[0],
        qkv_shard,
        out_shard,
        gain_mine[1],
        cq_shard,
        ckv_shard,
        cout_shard,
        gain_mine[2],
        up_shard,
        down_shard,
    )


def solution(mesh):
    rows = P(("dp", "fsdp"), None)
    columns = P(None, ("dp", "fsdp"))
    line = P(("dp", "fsdp"))
    in_specs = (
        rows, rows, rows, rows, line, line, line, columns, rows,
        line, rows, columns, rows, line, columns, rows, rows,
    )
    out_specs = (
        rows, rows, rows, line, columns, rows, line, rows, columns, rows, line, columns, rows,
    )
    return jax.shard_map(shards, mesh=mesh, in_specs=in_specs, out_specs=out_specs, check_vma=False)
```

```python
import functools

import jax
import jax.numpy as jnp
from jax import lax
from jax.experimental import pallas as pl
from jax.experimental.pallas import tpu as pltpu
from jax.sharding import PartitionSpec as P

HEADS = 12
HEAD = 64
PAIR = 2 * HEAD
CORE = 1
CLIP = 128
WINDOW = 256
TILE = 256
VMEM_BYTES = 56 * 1024 * 1024
f32 = jnp.float32
bf16 = jnp.bfloat16
fence = lax.optimization_barrier


def swap(values, mask):
    count = lax.axis_size("dp")
    return lax.ppermute(values, "dp", [(i, i ^ mask) for i in range(count)])


def shift(values, step):
    count = lax.axis_size("fsdp")
    return lax.ppermute(values, "fsdp", [(i, (i + step) % count) for i in range(count)])


def link_masks():
    masks = []
    mask = 2
    while mask < lax.axis_size("dp"):
        masks.append(mask)
        mask *= 2
    return masks


def relays():
    found = []
    for e in range(2, lax.axis_size("dp"), 2):
        if e & (e - 1):
            found.append((bin(e).count("1"), e, 1 << (e.bit_length() - 1), e & -e))
    return [item[1:] for item in sorted(found)]


def inner_gather(shard):
    count = lax.axis_size("fsdp")
    me = lax.axis_index("fsdp")
    held = shard[None]
    mask = 1
    while mask < count:
        came = lax.ppermute(held, "fsdp", [(i, i ^ mask) for i in range(count)])
        high = (me & mask) != 0
        held = jnp.concatenate([jnp.where(high, came, held), jnp.where(high, held, came)])
        mask *= 2
    return held


def inner_start(shard):
    return [shard] + [shift(shard, step) for step in range(1, lax.axis_size("fsdp"))]


def inner_order(came):
    count = len(came)
    me = lax.axis_index("fsdp")
    line = [came[count - 1 - k] for k in range(count)] + [came[count - k] for k in range(1, count)]
    return lax.dynamic_slice_in_dim(jnp.stack(line), count - 1 - me, count, 0)


def single_steps(block):
    return {mask: swap(block, mask) for mask in link_masks()}


def relay_steps(held, cut):
    def half_of(e, which):
        block = held[e]
        if isinstance(block, tuple):
            return block[which]
        return block[:cut] if which == 0 else block[cut:]

    for e, top, low in relays():
        held[e] = (swap(half_of(e ^ top, 0), top), swap(half_of(e ^ low, 1), low))


def parts_of(pieces, total, cut):
    arrays, places = [], []
    for e in sorted(pieces):
        block = pieces[e]
        if isinstance(block, tuple):
            arrays += [block[0], block[1]]
            places += [(e, 0, cut), (e, cut, total - cut)]
        else:
            arrays.append(block)
            places.append((e, 0, total))
    return arrays, tuple(places)


def core_steps(held):
    out = dict(held)
    for e, block in held.items():
        if isinstance(block, tuple):
            out[e | CORE] = tuple(swap(half, CORE) for half in block)
        else:
            out[e | CORE] = swap(block, CORE)
    return out


def add_low(a, b):
    return (a.astype(f32) + b.astype(f32)).astype(bf16)


class OuterSum:
    def __init__(self, total, cut):
        self.held = {2 * g: block for g, block in enumerate(total)}
        self.cut = cut
        self.extra = {e: {0: [], 1: []} for e in self.held}
        self.came = []
        self.halves = [[], []]

    def half(self, e, which):
        part = self.held[e][: self.cut] if which == 0 else self.held[e][self.cut :]
        for came in self.extra[e][which]:
            part = add_low(part, came)
        return part

    def relays(self):
        for e, top, low in relays()[::-1]:
            self.extra[e ^ top][0].append(swap(self.half(e, 0), top))
            self.extra[e ^ low][1].append(swap(self.half(e, 1), low))

    def singles(self):
        self.came += [
            swap(jnp.concatenate([self.half(mask, 0), self.half(mask, 1)]), mask) for mask in link_masks()
        ]

    def singles_half(self, which):
        self.halves[which] = [swap(self.half(mask, which), mask) for mask in link_masks()]

    def result(self):
        total = self.held[0].astype(f32)
        for block in self.came:
            total = total + block.astype(f32)
        for first, second in zip(self.halves[0], self.halves[1]):
            total = total + jnp.concatenate([first, second]).astype(f32)
        return total

    def state(self):
        return (self.held, self.extra, self.came, self.halves)

    def put(self, state):
        self.held, self.extra, self.came, self.halves = state


class InnerSum:
    def __init__(self, parts):
        count = parts.shape[0]
        me = lax.axis_index("fsdp")
        low = parts.astype(bf16)
        self.own = lax.dynamic_index_in_dim(parts, me, 0, keepdims=False)
        self.came = [
            shift(lax.dynamic_index_in_dim(low, (me + step) % count, 0, keepdims=False), step) for step in range(1, count)
        ]

    def result(self):
        total = self.own
        for block in self.came:
            total = total + block.astype(f32)
        return total


def nn(a, b):
    return jnp.dot(a, b, preferred_element_type=f32)


def nt(a, b):
    return lax.dot_general(a, b, (((1,), (1,)), ((), ())), preferred_element_type=f32)


def tn(a, b):
    return lax.dot_general(a, b, (((0,), (0,)), ((), ())), preferred_element_type=f32)


def tiles(size):
    step = TILE if size % TILE == 0 else size
    return [(at, step) for at in range(0, size, step)]


def centred(values):
    centre = jnp.mean(values, axis=-1, keepdims=True)
    shifted = values - centre
    spread = jnp.mean(shifted * shifted, axis=-1, keepdims=True)
    r = lax.rsqrt(spread + 1e-06)
    return shifted * r, r


def norm_back(xhat, r, gain, grad):
    c = grad * gain
    first = jnp.mean(c, axis=-1, keepdims=True)
    second = jnp.mean(c * xhat, axis=-1, keepdims=True)
    return r * (c - first - xhat * second), jnp.sum(grad * xhat, axis=0, keepdims=True)


def lower_half(rows):
    return lax.broadcasted_iota(jnp.int32, (rows, PAIR), 1) < HEAD


def two_heads(rows):
    keep = lower_half(rows.shape[0])
    zero = jnp.zeros_like(rows)
    return jnp.concatenate([jnp.where(keep, rows, zero), jnp.where(keep, zero, rows)], axis=0)


def side_by_side(stacked):
    rows = stacked.shape[0] // 2
    return jnp.where(lower_half(rows), stacked[:rows], stacked[rows:])


def softmax_rows(scores):
    raised = jnp.exp(scores - jnp.max(scores, axis=-1, keepdims=True))
    return raised / jnp.sum(raised, axis=-1, keepdims=True)


def bias_of(key_seg, own_seg):
    return jnp.where(key_seg == own_seg, 0.0, -1e30).astype(f32)


def block_bias(key_seg, ints, blocks):
    return jnp.stack([bias_of(key_seg[...], ints[1 + 3 * blocks + i]) for i in range(blocks)])


def biased(scores, bias):
    blocks, _, keys = bias.shape
    rows = scores.shape[0] // (2 * blocks)
    return (scores.reshape(2, blocks, rows, keys) + bias[None]).reshape(scores.shape)


def copies(jobs, sems, at):
    made = [pltpu.make_async_copy(src, dst, sems.at[at + i]) for i, (src, dst) in enumerate(jobs)]
    for job in made:
        job.start()
    return made


def whole(shape, dtype):
    return jax.ShapeDtypeStruct(shape, dtype)


VMEM = pl.BlockSpec(memory_space=pltpu.VMEM)
SMEM = pl.BlockSpec(memory_space=pltpu.SMEM)
ANY = pl.BlockSpec(memory_space=pl.ANY)


def params():
    return pltpu.CompilerParams(vmem_limit_bytes=VMEM_BYTES)


def cost(flops, moved, exps=0):
    return pl.CostEstimate(flops=int(flops), bytes_accessed=int(moved), transcendentals=int(exps))


def first_kernel(
    geometry, ints, mix, seg_row, tokens, *refs
):
    dp_count, blocks, token_places, qkv_places, qkv_rows = geometry
    n_tok, n_qkv = len(token_places), len(qkv_places)
    token_refs, qkv_refs = refs[:n_tok], refs[n_tok : n_tok + n_qkv]
    blended_ref, qkv_ref, attended_ref, gains_ref, partner, weight, gain_parts, sems = refs[n_tok + n_qkv :]
    me = ints[0]
    width = tokens.shape[1]

    for b in range(blocks):
        rel, slot = ints[1 + b], ints[1 + blocks + b]
        for ref, (e, start, rows) in zip(token_refs, token_places):
            inside = (rel == e) & (slot * CLIP >= start) & (slot * CLIP < start + rows)

            @pl.when(inside)
            def _(ref=ref, start=start, rows=rows, b=b, slot=slot):
                at = pl.multiple_of(jnp.clip(slot * CLIP - start, 0, rows - CLIP), CLIP)
                pltpu.make_async_copy(ref.at[pl.ds(at, CLIP)], partner.at[b], sems.at[b]).start()

    jobs = []
    for ref, (e, start, rows) in zip(qkv_refs, qkv_places):
        take = min(rows, qkv_rows - start)
        at = pl.multiple_of((me ^ e) * qkv_rows + start, 16)
        jobs.append((ref.at[pl.ds(0, take)], weight.at[pl.ds(at, take)]))
        if start + rows > qkv_rows:
            jobs.append((ref.at[pl.ds(take, rows - take)], gain_parts.at[e]))
    made = copies(jobs, sems, blocks)
    for b in range(blocks):
        pltpu.make_async_copy(tokens.at[pl.ds(0, CLIP)], partner.at[b], sems.at[b]).wait()
    for b in range(blocks):
        rows = slice(b * CLIP, (b + 1) * CLIP)
        share = mix[b]
        blended_ref[rows, :] = share * tokens[rows, :].astype(f32) + (1.0 - share) * partner[b].astype(f32)
    for job in made:
        job.wait()
    gains = gain_parts[0].astype(f32)
    for e in range(1, dp_count):
        gains = gains + gain_parts[e].astype(f32)
    gains_ref[...] = gains[:8]
    xhat, _ = centred(blended_ref[...])
    normed = (xhat * gains[0:1]).astype(bf16)
    for at, step in tiles(3 * width):
        tile = nt(normed, weight[at : at + step, :])
        if at + step <= width:
            tile = tile * 0.125
        qkv_ref[:, at : at + step] = tile.astype(bf16)

    @pl.loop(0, blocks)
    def _(i):
        window = pl.multiple_of(ints[1 + 2 * blocks + i] * CLIP, CLIP)
        bias = bias_of(seg_row[:, pl.ds(window, WINDOW)], ints[1 + 3 * blocks + i])
        rows = pl.ds(pl.multiple_of(i * CLIP, CLIP), CLIP)
        keys = pl.ds(window, WINDOW)
        for at in range(0, width, PAIR):
            queries = two_heads(qkv_ref[rows, at : at + PAIR])
            probs = softmax_rows(nt(queries, qkv_ref[keys, width + at : width + at + PAIR]) + bias).astype(bf16)
            out = nn(probs, qkv_ref[keys, 2 * width + at : 2 * width + at + PAIR])
            attended_ref[rows, at : at + PAIR] = side_by_side(out).astype(bf16)


def load_cross(me, refs, places, layout, weights, sems):
    jobs = []
    for ref, (e, start, rows) in zip(refs, places):
        for (first, size), weight in zip(layout, weights):
            if weight is not None and first >= start and first + size <= start + rows:
                at = pl.multiple_of((me ^ e) * size, 16)
                jobs.append((ref.at[pl.ds(first - start, size)], weight.at[pl.ds(at, size)]))
    return copies(jobs, sems, 0)


def second_kernel(geometry, ints, coarse_seg, coarse, blended, attended, gains, *refs):
    blocks, places, layout = geometry
    weight_refs = refs[: len(places)]
    residual_ref, cq_ref, ckv_ref, crossed_ref, joined_ref, second_ref = refs[len(places) : len(places) + 6]
    w_ckv, w_out, w_cq, w_cout, sems = refs[len(places) + 6 :]
    made = load_cross(ints[0], weight_refs, places, layout, (w_ckv, w_out, w_cq, w_cout), sems)
    for job in made:
        job.wait()
    width = blended.shape[1]
    for at, step in tiles(2 * width):
        ckv_ref[:, at : at + step] = nt(coarse[...], w_ckv[at : at + step, :]).astype(bf16)
    for at, step in tiles(width):
        residual_ref[:, at : at + step] = blended[:, at : at + step] + nn(attended[...], w_out[:, at : at + step])
    xhat, _ = centred(residual_ref[...])
    crossed_in = (xhat * gains[1:2]).astype(bf16)
    for at, step in tiles(width):
        cq_ref[:, at : at + step] = (nn(crossed_in, w_cq[:, at : at + step]) * 0.125).astype(bf16)

    bias = block_bias(coarse_seg, ints, blocks)
    for at in range(0, width, PAIR):
        queries = two_heads(cq_ref[:, at : at + PAIR])
        probs = softmax_rows(biased(nt(queries, ckv_ref[:, at : at + PAIR]), bias)).astype(bf16)
        out = nn(probs, ckv_ref[:, width + at : width + at + PAIR])
        crossed_ref[:, at : at + PAIR] = side_by_side(out).astype(bf16)

    for at, step in tiles(width):
        joined_ref[:, at : at + step] = residual_ref[:, at : at + step] + nn(crossed_ref[...], w_cout[:, at : at + step])
    xhat, _ = centred(joined_ref[...])
    second_ref[...] = (xhat * gains[2:3]).astype(bf16)


def mlp_kernel(geometry, second, second_near, cotangent, cotangent_near, *refs):
    groups, places, rows, carried, last = geometry
    weight_refs = refs[: len(places)]
    refs = refs[len(places) :]
    if carried:
        held = refs[:4]
        refs = refs[4:]
    keep_ref = refs[0]
    if last:
        going_ref, out_near, grad_near = refs[3:6]
        sums = (refs[1], refs[2], out_near, grad_near)
        refs = refs[6:]
    else:
        sums = refs[1:5]
        refs = refs[5:]
    w_up, w_down, hidden, grad_pre, sems = refs
    step = pl.program_id(0)

    def jobs_of(group):
        jobs = []
        for ref, (e, which) in zip(weight_refs, places):
            if e == groups[group]:
                for part, weight in ((0, w_up), (1, w_down)):
                    if which is None or which == part:
                        first = part * rows if which is None else 0
                        jobs.append((ref.at[pl.ds(first, rows)], weight.at[group]))
        return jobs

    at = 0
    for group in range(len(groups)):
        jobs = jobs_of(group)
        made = [pltpu.make_async_copy(s, d, sems.at[at + i]) for i, (s, d) in enumerate(jobs)]
        at += len(jobs)

        @pl.when(step == 0)
        def _(made=made):
            for job in made:
                job.start()

        @pl.when(step == group)
        def _(made=made):
            for job in made:
                job.wait()

    @pl.when(step == 0)
    def _():
        for i, ref in enumerate(sums):
            ref[...] = held[i][...] if carried else jnp.zeros_like(ref)

    up, down = w_up.at[step], w_down.at[step]
    for half, (inputs, upstream) in enumerate(((second, cotangent), (second_near, cotangent_near))):
        pre = nt(inputs[...], up[...])
        grad_hidden = nt(upstream[...], down[...])
        cdf = 0.5 * (1.0 + lax.erf(pre * 0.7071067811865476))
        slope = cdf + pre * (jnp.exp(-0.5 * pre * pre) * 0.3989422804014327)
        hidden[half] = (pre * cdf).astype(bf16)
        grad_pre[half] = (grad_hidden * slope).astype(bf16)
        for first, size in tiles(second.shape[1]):
            columns = slice(first, first + size)
            sums[2 * half][:, columns] += nn(hidden[half], down[:, columns])
            sums[2 * half + 1][:, columns] += nn(grad_pre[half], up[:, columns])
    keep_ref[0, 0] = (tn(grad_pre[0], second[...]) + tn(grad_pre[1], second_near[...])).astype(bf16)
    keep_ref[0, 1] = (tn(hidden[0], cotangent[...]) + tn(hidden[1], cotangent_near[...])).astype(bf16)
    if last:

        @pl.when(step == len(groups) - 1)
        def _():
            going_ref[0] = out_near[...].astype(bf16)
            going_ref[1] = grad_near[...].astype(bf16)


def grads_out(me, dp_count, layout, sources, keep_ref, send_ref, sems, at):
    jobs = []
    for e in range(dp_count):
        target = send_ref if e & CORE else keep_ref
        for (first, size), source in zip(layout, sources):
            if source is None:
                continue
            row = pl.multiple_of((me ^ e) * size, 16)
            jobs.append((source.at[pl.ds(row, size)], target.at[e // 2, pl.ds(first, size)]))
    return copies(jobs, sems, at)


def third_kernel(
    geometry, ints, coarse_seg, gains, mlp_out, grad_second, mlp_came, joined, cotangent, crossed, cq, ckv, *refs
):
    blocks, places, layout, dp_count = geometry
    weight_refs = refs[: len(places)]
    refs = refs[len(places) :]
    output_ref, grad_joined_ref, grad_cq_ref, grad_ckv_ref, gain_grads_ref, keep_ref, send_ref = refs[:7]
    w_cout, g_cout, grad_cross, sems = refs[7:]
    me = ints[0]
    width = joined.shape[1]
    made = load_cross(me, weight_refs, places, layout, (None, None, None, w_cout), sems)
    output_ref[...] = (joined[...] + (mlp_out[...] + mlp_came[0].astype(f32))).astype(bf16)
    xhat, r = centred(joined[...])
    grad_in, gain_two = norm_back(xhat, r, gains[2:3], grad_second[...] + mlp_came[1].astype(f32))
    grad_joined_ref[...] = cotangent[...].astype(f32) + grad_in
    low = grad_joined_ref[...].astype(bf16)
    for job in made:
        job.wait()
    for at, step in tiles(width):
        grad_cross[:, at : at + step] = nt(low, w_cout[at : at + step, :]).astype(bf16)
    for at, step in tiles(width):
        g_cout[at : at + step, :] = tn(crossed[:, at : at + step], low).astype(bf16)
    going = grads_out(me, dp_count, layout, (None, None, None, g_cout), keep_ref, send_ref, sems, len(made))
    bias = block_bias(coarse_seg, ints, blocks)
    for at in range(0, width, PAIR):
        lanes = slice(at, at + PAIR)
        queries = two_heads(cq[:, lanes])
        grads = two_heads(grad_cross[:, lanes])
        keys = ckv[:, lanes]
        values = ckv[:, width + at : width + at + PAIR]
        probs = softmax_rows(biased(nt(queries, keys), bias))
        grad_ckv_ref[:, width + at : width + at + PAIR] = tn(probs.astype(bf16), grads).astype(bf16)
        grad_probs = nt(grads, values)
        inner = jnp.sum(probs * grad_probs, axis=-1, keepdims=True)
        scores = (probs * (grad_probs - inner)).astype(bf16)
        part = side_by_side(nn(scores, keys)).astype(bf16)
        grad_cq_ref[:, lanes] = part * jnp.asarray(0.125, bf16)
        grad_ckv_ref[:, lanes] = tn(scores, queries).astype(bf16)

    gain_grads_ref[...] = jnp.concatenate([gain_two] * 8, axis=0)
    for job in going:
        job.wait()


def third_part(geometry, ints, coarse, gains, gain_two, grad_joined, residual, attended, grad_cq, grad_ckv, keep_in, send_in, *refs):
    places, layout, dp_count = geometry
    weight_refs = refs[: len(places)]
    refs = refs[len(places) :]
    coarse_ref, grad_res_ref, grad_att_ref, gain_grads_ref, keep_ref, send_ref = refs[:6]
    w_ckv, w_out, w_cq, g_ckv, g_out, g_cq, crossed_in, sems = refs[6:]
    me = ints[0]
    width = residual.shape[1]
    made = load_cross(me, weight_refs, places, layout, (w_ckv, w_out, w_cq, None), sems)
    xhat, r = centred(residual[...])
    crossed_in[...] = (xhat * gains[1:2]).astype(bf16)
    for at, step in tiles(width):
        g_cq[at : at + step, :] = tn(crossed_in[:, at : at + step], grad_cq[...]).astype(bf16)
    for at, step in tiles(2 * width):
        g_ckv[at : at + step, :] = tn(grad_ckv[:, at : at + step], coarse[...]).astype(bf16)
    for job in made:
        job.wait()
    going = grads_out(me, dp_count, layout, (g_ckv, None, g_cq, None), keep_ref, send_ref, sems, 0)
    for at, step in tiles(width):
        coarse_ref[:, at : at + step] = nn(grad_ckv[:, 0:width], w_ckv[0:width, at : at + step]) + nn(
            grad_ckv[:, width : 2 * width], w_ckv[width : 2 * width, at : at + step]
        )
    pieces = [nt(grad_cq[...], w_cq[at : at + step, :]) for at, step in tiles(width)]
    grad_in, gain_cross = norm_back(xhat, r, gains[1:2], jnp.concatenate(pieces, axis=1))
    grad_res = grad_joined[...] + grad_in
    grad_res_ref[...] = grad_res
    low = grad_res.astype(bf16)
    for at, step in tiles(width):
        g_out[at : at + step, :] = tn(attended[:, at : at + step], low).astype(bf16)
    going += grads_out(me, dp_count, layout, (None, g_out, None, None), keep_ref, send_ref, sems, len(going))
    for at, step in tiles(width):
        grad_att_ref[:, at : at + step] = nt(low, w_out[at : at + step, :]).astype(bf16)
    zero = jnp.zeros_like(gain_cross)
    gain_grads_ref[...] = jnp.concatenate([zero, gain_cross, gain_two[0:1]] + [zero] * 5, axis=0)
    for job in going:
        job.wait()


def fourth_kernel(geometry, ints, seg_row, grad_att, qkv, grad_proj, key_sum, value_sum):
    (blocks,) = geometry
    width = grad_att.shape[1]
    key_sum[...] = jnp.zeros_like(key_sum)
    value_sum[...] = jnp.zeros_like(value_sum)

    @pl.loop(0, blocks)
    def _(i):
        window = pl.multiple_of(ints[1 + 2 * blocks + i] * CLIP, CLIP)
        bias = bias_of(seg_row[:, pl.ds(window, WINDOW)], ints[1 + 3 * blocks + i])
        rows = pl.ds(pl.multiple_of(i * CLIP, CLIP), CLIP)
        near = pl.ds(window, WINDOW)
        for at in range(0, width, PAIR):
            lanes = slice(at, at + PAIR)
            queries = two_heads(qkv[rows, lanes])
            grads = two_heads(grad_att[rows, lanes])
            keys = qkv[near, width + at : width + at + PAIR]
            values = qkv[near, 2 * width + at : 2 * width + at + PAIR]
            probs = softmax_rows(nt(queries, keys) + bias)
            value_sum[near, lanes] += tn(probs.astype(bf16), grads)
            grad_probs = nt(grads, values)
            inner = jnp.sum(probs * grad_probs, axis=-1, keepdims=True)
            scores = (probs * (grad_probs - inner)).astype(bf16)
            part = side_by_side(nn(scores, keys)).astype(bf16)
            grad_proj[rows, lanes] = part * jnp.asarray(0.125, bf16)
            key_sum[near, lanes] += tn(scores, queries)

    grad_proj[:, width : 2 * width] = key_sum[...].astype(bf16)
    grad_proj[:, 2 * width : 3 * width] = value_sum[...].astype(bf16)


def fifth_kernel(geometry, ints, mix, gains, blended, grad_res, grad_proj, *refs):
    dp_count, blocks, qkv_places, qkv_rows = geometry
    weight_refs = refs[: len(qkv_places)]
    refs = refs[len(qkv_places) :]
    base_ref, gain_ref, mix_keep_ref, mix_send_ref = refs[:4]
    weight, going_back, sems = refs[4:]
    me = ints[0]
    width = blended.shape[1]
    jobs = []
    for ref, (e, start, rows) in zip(weight_refs, qkv_places):
        take = min(rows, qkv_rows - start)
        at = pl.multiple_of((me ^ e) * qkv_rows + start, 16)
        jobs.append((ref.at[pl.ds(0, take)], weight.at[pl.ds(at, take)]))
    made = copies(jobs, sems, 0)
    going_back[...] = jnp.zeros_like(going_back)
    xhat, r = centred(blended[...])
    for job in made:
        job.wait()
    pieces = [nn(grad_proj[...], weight[:, at : at + step]) for at, step in tiles(width)]
    grad_in, gain_one = norm_back(xhat, r, gains[0:1], jnp.concatenate(pieces, axis=1))
    gain_ref[...] = jnp.concatenate([gain_one] * 8, axis=0)
    grad_blend = grad_res[...] + grad_in
    for b in range(blocks):
        rows = slice(b * CLIP, (b + 1) * CLIP)
        share = mix[b]
        part = grad_blend[rows, :]
        base_ref[rows, :] = share * part
        place = ints[1 + b] * blocks + ints[1 + blocks + b]
        going_back[place] = (going_back[place].astype(f32) + (1.0 - share) * part).astype(bf16)
    mixed = []
    for e in range(dp_count):
        target = mix_send_ref if e & CORE else mix_keep_ref
        for s in range(blocks):
            mixed.append((going_back.at[e * blocks + s], target.at[e // 2, pl.ds(s * CLIP, CLIP)]))
    for job in copies(mixed, sems, len(jobs)):
        job.wait()


def sixth_kernel(geometry, ints, gains, gain_grads, gain_one, blended, grad_proj, keep_ref, send_ref, grad_w, gain_rows, sems):
    dp_count, qkv_rows = geometry
    me = ints[0]
    width = blended.shape[1]
    xhat, _ = centred(blended[...])
    normed = (xhat * gains[0:1]).astype(bf16)
    all_gains = jnp.concatenate([gain_one[0:1], gain_grads[1:8], jnp.zeros((8, width), f32)], axis=0)
    gain_rows[...] = all_gains.astype(bf16)
    last = []
    for e in range(dp_count):
        target = send_ref if e & CORE else keep_ref
        last.append((gain_rows, target.at[e // 2, pl.ds(qkv_rows, 16)]))
    sent = copies(last, sems, 0)
    for at, step in tiles(3 * width):
        grad_w[at : at + step, :] = tn(grad_proj[:, at : at + step], normed).astype(bf16)
    sent += grads_out(me, dp_count, ((0, qkv_rows),), (grad_w,), keep_ref, send_ref, sems, dp_count)
    for job in sent:
        job.wait()


def shards(
    tokens,
    coarse_view,
    segment_ids,
    partner_device,
    partner_slot,
    mix_weight,
    ln1_gain,
    w_qkv,
    w_out,
    lnx_gain,
    w_cq,
    w_ckv,
    w_cout,
    ln2_gain,
    w_up,
    w_down,
    cotangent,
):
    row_count, width = tokens.shape
    coarse_rows = coarse_view.shape[0]
    blocks = mix_weight.shape[0]
    dp_count, fsdp_count = lax.axis_size("dp"), lax.axis_size("fsdp")
    dp_me, fsdp_me = lax.axis_index("dp"), lax.axis_index("fsdp")
    part = ln1_gain.shape[0]
    device_me = dp_me * fsdp_count + fsdp_me
    pairs = dp_count // 2

    target = partner_device[:, 0]
    segments = segment_ids[0]
    videos = segments.reshape(blocks, row_count // blocks)[:, 0]
    following = jnp.concatenate([videos[1:] == videos[:-1], jnp.zeros((1,), bool)])
    before = jnp.concatenate([jnp.zeros((1,), bool), videos[1:] == videos[:-1]])
    index = jnp.arange(blocks, dtype=jnp.int32)
    window = jnp.where(following, index, jnp.where(before, index - 1, jnp.minimum(index, blocks - 2)))
    ints = jnp.concatenate(
        [dp_me[None].astype(jnp.int32), (target ^ dp_me).astype(jnp.int32), partner_slot, window, videos]
    )
    seg_row = segments[None, :]
    coarse_seg = segments.reshape(coarse_rows, row_count // coarse_rows)[:, 0][None, :]

    gain_rows = lax.dynamic_update_slice(
        jnp.zeros((8, width), bf16), jnp.stack([ln1_gain, lnx_gain, ln2_gain]), (0, device_me * part)
    )
    shard_one = jnp.concatenate([w_qkv.T, gain_rows])
    shard_two = jnp.concatenate([w_ckv.T, w_out, w_cq, w_cout])
    shard_mlp = jnp.concatenate([w_up.T, w_down])
    sizes_two = (w_ckv.shape[1], w_out.shape[0], w_cq.shape[0], w_cout.shape[0])
    qkv_part, up_part = w_qkv.shape[1], w_up.shape[1]
    qkv_rows, up_rows = qkv_part * fsdp_count, up_part * fsdp_count
    layout = []
    at = 0
    for size in sizes_two:
        layout.append((at * fsdp_count, size * fsdp_count))
        at += size
    layout = tuple(layout)
    rows_two = at * fsdp_count

    cut_tok, cut_one, cut_two, cut_mlp = row_count // 2, qkv_rows // 2, layout[0][1], up_rows

    held_tok = {0: tokens, **single_steps(tokens)}
    came_one = inner_start(shard_one)
    cotangent_near = swap(cotangent, CORE)
    held_tok, came_one, shard_two, cotangent_near = fence((held_tok, came_one, shard_two, cotangent_near))

    ones = inner_order(came_one)
    gain_block = jnp.sum(ones[:, qkv_part:].astype(f32), axis=0).astype(bf16)
    block_one = jnp.concatenate(
        [ones[:, :qkv_part].reshape(qkv_rows, width), gain_block, jnp.zeros((8, width), bf16)]
    )
    held_one = {0: block_one, **single_steps(block_one)}
    came_two = inner_start(shard_two)
    held_tok, held_one, came_two, shard_mlp = fence((held_tok, held_one, came_two, shard_mlp))

    mlp = lax.all_gather(shard_mlp, "fsdp", axis=0, tiled=False)
    core_tok = core_steps({e: b for e, b in held_tok.items()})
    relay_steps(held_tok, cut_tok)
    twos = inner_order(came_two)
    split = []
    at = 0
    for size in sizes_two:
        split.append(twos[:, at : at + size].reshape(size * fsdp_count, width))
        at += size
    block_two = jnp.concatenate(split)
    held_one, core_tok, held_tok, block_two = fence((held_one, core_tok, held_tok, block_two))

    core_one = core_steps({e: b for e, b in held_one.items()})
    relay_steps(held_one, cut_one)
    late_tok = core_steps({e: b for e, b in held_tok.items() if isinstance(b, tuple)})
    held_one, core_one, late_tok, block_two = fence((held_one, core_one, late_tok, block_two))

    held_two = {0: block_two, **single_steps(block_two)}
    late_one = core_steps({e: b for e, b in held_one.items() if isinstance(b, tuple)})
    pieces_tok = {**core_tok, **late_tok}
    pieces_one = {**core_one, **late_one}
    arrays_tok, places_tok = parts_of(pieces_tok, row_count, cut_tok)
    arrays_one, places_one = parts_of(pieces_one, qkv_rows + 16, cut_one)
    blended, qkv, attended, gains = pl.pallas_call(
        functools.partial(first_kernel, (dp_count, blocks, places_tok, places_one, qkv_rows)),
        out_shape=(
            whole((row_count, width), f32),
            whole((row_count, 3 * width), bf16),
            whole((row_count, width), bf16),
            whole((8, width), f32),
        ),
        in_specs=[SMEM, SMEM, VMEM, VMEM] + [ANY] * (len(arrays_tok) + len(arrays_one)),
        out_specs=(VMEM,) * 4,
        scratch_shapes=[
            pltpu.VMEM((blocks, CLIP, width), bf16),
            pltpu.VMEM((3 * width, width), bf16),
            pltpu.VMEM((dp_count, 16, width), bf16),
            pltpu.SemaphoreType.DMA((blocks + len(arrays_one) + dp_count,)),
        ],
        compiler_params=params(),
        cost_estimate=cost(1e9, 1e6),
        name="mix_self_attention",
    )(ints, mix_weight, seg_row, tokens, *arrays_tok, *arrays_one)
    held_two, attended = fence((held_two, attended))

    core_two = core_steps({e: b for e, b in held_two.items()})
    relay_steps(held_two, cut_two)
    held_two, core_two, mlp = fence((held_two, core_two, mlp))

    block_mlp = jnp.concatenate(
        [mlp[:, :up_part].reshape(up_rows, width), mlp[:, up_part:].reshape(up_rows, width)]
    )
    held_mlp = {0: block_mlp, **single_steps(block_mlp)}
    late_two = core_steps({e: b for e, b in held_two.items() if isinstance(b, tuple)})
    pieces_two = {**core_two, **late_two}
    wide = [pltpu.VMEM((sizes * fsdp_count * dp_count, width), bf16) for sizes in sizes_two]
    n_two = 4 * dp_count
    arrays_two, places_two = parts_of(pieces_two, rows_two, cut_two)
    wide = [pltpu.VMEM((sizes * fsdp_count * dp_count, width), bf16) for sizes in sizes_two]
    n_two = 4 * dp_count
    residual, cq, ckv, crossed, joined, second = pl.pallas_call(
        functools.partial(second_kernel, (blocks, places_two, layout)),
        out_shape=(
            whole((row_count, width), f32),
            whole((row_count, width), bf16),
            whole((coarse_rows, 2 * width), bf16),
            whole((row_count, width), bf16),
            whole((row_count, width), f32),
            whole((row_count, width), bf16),
        ),
        in_specs=[SMEM] + [VMEM] * 5 + [ANY] * len(arrays_two),
        out_specs=(VMEM,) * 6,
        scratch_shapes=wide + [pltpu.SemaphoreType.DMA((n_two,))],
        compiler_params=params(),
        cost_estimate=cost(1e9, 1e6),
        name="cross_attention",
    )(ints, coarse_seg, coarse_view, blended, attended, gains, *arrays_two)
    second_near = swap(second, CORE)
    held_mlp, second, second_near = fence((held_mlp, second, second_near))

    early = {e: b for e, b in held_mlp.items()}
    relay_steps(held_mlp, cut_mlp)

    def mlp_call(pieces, carried, last):
        groups = tuple(sorted(pieces))
        arrays, places = [], []
        for e in groups:
            block = pieces[e]
            if isinstance(block, tuple):
                arrays += list(block)
                places += [(e, 0), (e, 1)]
            else:
                arrays.append(block)
                places.append((e, None))
        count = len(groups)
        fixed = pl.BlockSpec((row_count, width), lambda g: (0, 0))
        moving = pl.BlockSpec((1, 2, up_rows, width), lambda g: (g, 0, 0, 0))
        table = whole((row_count, width), f32)
        out_shape = [whole((count, 2, up_rows, width), bf16), table, table]
        out_specs = [moving, fixed, fixed]
        scratch = []
        if last:
            out_shape.append(whole((2, row_count, width), bf16))
            out_specs.append(pl.BlockSpec((2, row_count, width), lambda g: (0, 0, 0)))
            scratch += [pltpu.VMEM((row_count, width), f32)] * 2
        else:
            out_shape += [table, table]
            out_specs += [fixed, fixed]
        made = pl.pallas_call(
            functools.partial(mlp_kernel, (groups, tuple(places), up_rows, bool(carried), last)),
            grid=(count,),
            out_shape=tuple(out_shape),
            in_specs=[fixed] * 4 + [ANY] * len(arrays) + [fixed] * len(carried),
            out_specs=tuple(out_specs),
            scratch_shapes=scratch
            + [
                pltpu.VMEM((count, up_rows, width), bf16),
                pltpu.VMEM((count, up_rows, width), bf16),
                pltpu.VMEM((2, row_count, up_rows), bf16),
                pltpu.VMEM((2, row_count, up_rows), bf16),
                pltpu.SemaphoreType.DMA((2 * count,)),
            ],
            compiler_params=params(),
            cost_estimate=cost(1e9, 1e6),
            name="feed_forward",
        )(second, second_near, cotangent, cotangent_near, *arrays, *carried)
        return groups, made[0].reshape(count, 2 * up_rows, width), made[1:]

    groups_a, keep_a, sums = mlp_call(early, (), False)
    late, keep_a, sums = fence(({e: b for e, b in held_mlp.items() if isinstance(b, tuple)}, keep_a, sums))
    groups_b, keep_b, (mlp_out, grad_second, mlp_going) = mlp_call(late, sums, True)
    mlp_came = swap(mlp_going, CORE)
    totals = [None] * pairs
    for groups, keep in ((groups_a, keep_a), (groups_b, keep_b)):
        for i, e in enumerate(groups):
            totals[e // 2] = keep[i]
    totals, mlp_came = fence((totals, mlp_came))

    sum_mlp = OuterSum(totals, cut_mlp)
    sum_mlp.relays()
    output, grad_joined, grad_cq, grad_ckv, gain_two, keep_two, send_two = pl.pallas_call(
        functools.partial(third_kernel, (blocks, places_two, layout, dp_count)),
        out_shape=(
            whole((row_count, width), bf16),
            whole((row_count, width), f32),
            whole((row_count, width), bf16),
            whole((coarse_rows, 2 * width), bf16),
            whole((8, width), f32),
            whole((pairs, rows_two, width), bf16),
            whole((pairs, rows_two, width), bf16),
        ),
        in_specs=[SMEM] + [VMEM] * 10 + [ANY] * len(arrays_two),
        out_specs=(VMEM,) * 5 + (ANY,) * 2,
        scratch_shapes=[
            wide[3],
            wide[3],
            pltpu.VMEM((row_count, width), bf16),
            pltpu.SemaphoreType.DMA((n_two + dp_count,)),
        ],
        compiler_params=params(),
        cost_estimate=cost(1e9, 1e6),
        name="cross_attention_backward",
    )(ints, coarse_seg, gains, mlp_out, grad_second, mlp_came, joined, cotangent, crossed, cq, ckv, *arrays_two)
    state, grad_joined = fence((sum_mlp.state(), grad_joined))
    sum_mlp.put(state)

    sum_mlp.singles_half(0)
    coarse_grad, grad_res, grad_att, gain_grads, keep_two, send_two = pl.pallas_call(
        functools.partial(third_part, (places_two, layout, dp_count)),
        out_shape=(
            whole((coarse_rows, width), f32),
            whole((row_count, width), f32),
            whole((row_count, width), bf16),
            whole((8, width), f32),
            whole((pairs, rows_two, width), bf16),
            whole((pairs, rows_two, width), bf16),
        ),
        in_specs=[SMEM] + [VMEM] * 8 + [ANY] * (2 + len(arrays_two)),
        out_specs=(VMEM,) * 4 + (ANY,) * 2,
        scratch_shapes=[
            wide[0],
            wide[1],
            wide[2],
            wide[0],
            wide[1],
            wide[2],
            pltpu.VMEM((row_count, width), bf16),
            pltpu.SemaphoreType.DMA((n_two,)),
        ],
        input_output_aliases={9: 4, 10: 5},
        compiler_params=params(),
        cost_estimate=cost(1e9, 1e6),
        name="cross_attention_weights",
    )(
        ints, coarse_view, gains, gain_two, grad_joined, residual, attended, grad_cq, grad_ckv, keep_two, send_two, *arrays_two
    )

    state, grad_att, keep_two, send_two = fence((sum_mlp.state(), grad_att, keep_two, send_two))
    sum_mlp.put(state)

    sum_mlp.singles_half(1)
    came_two = swap(send_two, CORE)
    (grad_proj,) = pl.pallas_call(
        functools.partial(fourth_kernel, (blocks,)),
        out_shape=(whole((row_count, 3 * width), bf16),),
        in_specs=[SMEM] + [VMEM] * 3,
        out_specs=(VMEM,),
        scratch_shapes=[pltpu.VMEM((row_count, width), f32), pltpu.VMEM((row_count, width), f32)],
        compiler_params=params(),
        cost_estimate=cost(1e9, 1e6),
        name="self_attention_backward",
    )(ints, seg_row, grad_att, qkv)
    state, grad_proj, came_two = fence((sum_mlp.state(), grad_proj, came_two))
    sum_mlp.put(state)

    sum_two = OuterSum(add_low(keep_two, came_two), cut_two)
    sum_two.relays()
    mlp_sum = sum_mlp.result()
    mlp_parts = jnp.concatenate(
        [mlp_sum[:up_rows].reshape(fsdp_count, up_part, width), mlp_sum[up_rows:].reshape(fsdp_count, up_part, width)], axis=1
    )
    inner_mlp = InnerSum(mlp_parts)
    base, gain_one, keep_tok, send_tok = pl.pallas_call(
        functools.partial(fifth_kernel, (dp_count, blocks, places_one, qkv_rows)),
        out_shape=(
            whole((row_count, width), f32),
            whole((8, width), f32),
            whole((pairs, row_count, width), bf16),
            whole((pairs, row_count, width), bf16),
        ),
        in_specs=[SMEM, SMEM] + [VMEM] * 4 + [ANY] * len(arrays_one),
        out_specs=(VMEM,) * 2 + (ANY,) * 2,
        scratch_shapes=[
            pltpu.VMEM((3 * width, width), bf16),
            pltpu.VMEM((dp_count * blocks, CLIP, width), bf16),
            pltpu.SemaphoreType.DMA((len(arrays_one) + dp_count * blocks,)),
        ],
        compiler_params=params(),
        cost_estimate=cost(1e9, 1e6),
        name="self_attention_input",
    )(ints, mix_weight, gains, blended, grad_res, grad_proj, *arrays_one)
    state, keep_tok, send_tok, gain_one = fence((sum_two.state(), keep_tok, send_tok, gain_one))
    sum_two.put(state)

    sum_two.singles()
    came_tok = swap(send_tok, CORE)
    keep_one, send_one = pl.pallas_call(
        functools.partial(sixth_kernel, (dp_count, qkv_rows)),
        out_shape=(
            whole((pairs, qkv_rows + 16, width), bf16),
            whole((pairs, qkv_rows + 16, width), bf16),
        ),
        in_specs=[SMEM] + [VMEM] * 5,
        out_specs=(ANY,) * 2,
        scratch_shapes=[
            pltpu.VMEM((3 * width, width), bf16),
            pltpu.VMEM((16, width), bf16),
            pltpu.SemaphoreType.DMA((2 * dp_count,)),
        ],
        compiler_params=params(),
        cost_estimate=cost(1e9, 1e6),
        name="self_attention_weights",
    )(ints, gains, gain_grads, gain_one, blended, grad_proj)
    state, came_tok, keep_one, send_one, mlp_came = fence((sum_two.state(), came_tok, keep_one, send_one, inner_mlp.came))
    sum_two.put(state)
    inner_mlp.came = mlp_came

    sum_tok = OuterSum(add_low(keep_tok, came_tok), cut_tok)
    sum_tok.relays()
    came_one = swap(send_one, CORE)
    two_sum = sum_two.result()
    two_parts = jnp.concatenate(
        [two_sum[first : first + size].reshape(fsdp_count, size // fsdp_count, width) for first, size in layout], axis=1
    )
    state, came_one, two_parts = fence((sum_tok.state(), came_one, two_parts))
    sum_tok.put(state)

    sum_one = OuterSum(add_low(keep_one, came_one), cut_one)
    sum_one.relays()
    inner_two = InnerSum(two_parts)
    state = fence(sum_one.state())
    sum_one.put(state)
    sum_one.singles()
    state, two_came = fence((sum_one.state(), inner_two.came))
    sum_one.put(state)
    inner_two.came = two_came
    sum_tok.singles()
    one_sum = sum_one.result()
    gain_sum = jnp.broadcast_to(one_sum[qkv_rows : qkv_rows + 8][None], (fsdp_count, 8, width))
    one_parts = jnp.concatenate([one_sum[:qkv_rows].reshape(fsdp_count, qkv_part, width), gain_sum], axis=1)
    one_mine = InnerSum(one_parts).result()

    mlp_mine = inner_mlp.result()
    up_shard, down_shard = mlp_mine[:up_part].T, mlp_mine[up_part:]
    two_mine = inner_two.result()
    found = []
    at = 0
    for size in sizes_two:
        found.append(two_mine[at : at + size])
        at += size
    ckv_shard, out_shard, cq_shard, cout_shard = found[0].T, found[1], found[2], found[3]
    qkv_shard = one_mine[:qkv_part].T
    gain_mine = lax.dynamic_slice(one_mine[qkv_part:], (0, device_me * part), (3, part))
    token_grad = base + sum_tok.result()
    return (
        output,
        token_grad,
        coarse_grad,
        gain_mine[0],
        qkv_shard,
        out_shard,
        gain_mine[1],
        cq_shard,
        ckv_shard,
        cout_shard,
        gain_mine[2],
        up_shard,
        down_shard,
    )


def solution(mesh):
    rows = P(("dp", "fsdp"), None)
    columns = P(None, ("dp", "fsdp"))
    line = P(("dp", "fsdp"))
    in_specs = (
        rows, rows, rows, rows, line, line, line, columns, rows,
        line, rows, columns, rows, line, columns, rows, rows,
    )
    out_specs = (
        rows, rows, rows, line, columns, rows, line, rows, columns, rows, line, columns, rows,
    )
    return jax.shard_map(shards, mesh=mesh, in_specs=in_specs, out_specs=out_specs, check_vma=False)
```

```python
import functools

import jax
import jax.numpy as jnp
from jax import lax
from jax.experimental import pallas as pl
from jax.experimental.pallas import tpu as pltpu
from jax.sharding import PartitionSpec as P

HEADS = 12
HEAD = 64
PAIR = 2 * HEAD
CORE = 1
CLIP = 128
WINDOW = 256
TILE = 256
VMEM_BYTES = 56 * 1024 * 1024
f32 = jnp.float32
bf16 = jnp.bfloat16
fence = lax.optimization_barrier


def swap(values, mask):
    count = lax.axis_size("dp")
    return lax.ppermute(values, "dp", [(i, i ^ mask) for i in range(count)])


def shift(values, step):
    count = lax.axis_size("fsdp")
    return lax.ppermute(values, "fsdp", [(i, (i + step) % count) for i in range(count)])


def link_masks():
    masks = []
    mask = 2
    while mask < lax.axis_size("dp"):
        masks.append(mask)
        mask *= 2
    return masks


def inner_swap(values, mask):
    count = lax.axis_size("fsdp")
    return lax.ppermute(values, "fsdp", [(i, i ^ mask) for i in range(count)])


def inner_double(held, mask):
    return inner_join(held, inner_swap(held, mask), mask)


def inner_join(held, came, mask):
    high = (lax.axis_index("fsdp") & mask) != 0
    return jnp.concatenate([jnp.where(high, came, held), jnp.where(high, held, came)])


def inner_rest(held):
    while held.shape[0] < lax.axis_size("fsdp"):
        held = inner_double(held, held.shape[0])
    return held


def inner_start(shard):
    return [shard] + [shift(shard, step) for step in range(1, lax.axis_size("fsdp"))]


def inner_order(came):
    count = len(came)
    me = lax.axis_index("fsdp")
    line = [came[count - 1 - k] for k in range(count)] + [came[count - k] for k in range(1, count)]
    return lax.dynamic_slice_in_dim(jnp.stack(line), count - 1 - me, count, 0)


def mirrored(role):
    masks = link_masks()
    return sum(masks[len(masks) - 1 - i] for i, mask in enumerate(masks) if role & mask)


def step_along(values, mask):
    count = lax.axis_size("dp")
    return lax.ppermute(values, "dp", [(i, i ^ (mirrored(mask) if i & CORE else mask)) for i in range(count)])


def top_bit(role):
    return 1 << (role.bit_length() - 1)


def relayed_roles():
    found = [role for role in range(2, lax.axis_size("dp"), 2) if role & (role - 1)]
    return sorted(found, key=lambda role: bin(role).count("1"))


def device_of(me, role, mirrors):
    holder = me ^ (role & CORE)
    link = role & ~CORE
    return holder ^ (link + lax.rem(holder, 2) * (mirrors[link] - link))


def mirror_table():
    return {role: mirrored(role) for role in range(0, lax.axis_size("dp"), 2)}


def single_steps(block):
    return {mask: step_along(block, mask) for mask in link_masks()}


def relay_steps(held):
    for role in relayed_roles():
        held[role] = step_along(held[role ^ top_bit(role)], top_bit(role))


def parts_of(pieces, total):
    return [pieces[e] for e in sorted(pieces)], tuple((e, 0, total) for e in sorted(pieces))


def core_steps(held):
    return {**held, **{e | CORE: swap(block, CORE) for e, block in held.items()}}


def inner_parts(inner):
    inner.add()
    return inner.parts


def add_low(a, b):
    return (a.astype(f32) + b.astype(f32)).astype(bf16)


class OuterSum:
    def __init__(self, *parts):
        self.parts = {2 * g: [part[g] for part in parts] for g in range(lax.axis_size("dp") // 2)}
        self.came = []

    def value(self, role, rows=slice(None)):
        total = self.parts[role][0][rows].astype(f32)
        for part in self.parts[role][1:]:
            total = total + part[rows].astype(f32)
        return total

    def relays(self):
        for role in relayed_roles()[::-1]:
            came = step_along(self.value(role).astype(bf16), top_bit(role))
            self.parts[role ^ top_bit(role)].append(came)

    def singles(self, rows=slice(None)):
        self.came.append((rows, [step_along(self.value(mask, rows).astype(bf16), mask) for mask in link_masks()]))

    def result(self, index=None):
        chosen = self.came if index is None else [self.came[index]]
        sums = []
        for rows, blocks in chosen:
            total = self.value(0, rows)
            for block in blocks:
                total = total + block.astype(f32)
            sums.append(total)
        return sums[0] if len(sums) == 1 else jnp.concatenate(sums)

    def state(self):
        return (self.parts, [blocks for _, blocks in self.came])

    def put(self, state):
        self.parts = state[0]
        self.came = [(rows, blocks) for (rows, _), blocks in zip(self.came, state[1])]


class InnerSum:
    def __init__(self, parts):
        self.parts = parts
        self.came = None
        self.mask = parts.shape[0]

    def step(self):
        self.add()
        self.mask //= 2
        bit = ((lax.axis_index("fsdp") & self.mask) != 0).astype(jnp.int32)
        halves = self.parts.reshape((2, self.mask) + self.parts.shape[1:])
        self.parts = lax.dynamic_index_in_dim(halves, bit, 0, keepdims=False)
        going = lax.dynamic_index_in_dim(halves, 1 - bit, 0, keepdims=False).astype(bf16)
        self.came = inner_swap(going, self.mask)

    def finish(self, steps=None):
        while self.mask > 1:
            self.step()

    def add(self):
        if self.came is not None:
            self.parts = self.parts + self.came.astype(f32)
            self.came = None

    def result(self):
        self.finish()
        self.add()
        return self.parts[0]


def nn(a, b):
    return jnp.dot(a, b, preferred_element_type=f32)


def nt(a, b):
    return lax.dot_general(a, b, (((1,), (1,)), ((), ())), preferred_element_type=f32)


def tn(a, b):
    return lax.dot_general(a, b, (((0,), (0,)), ((), ())), preferred_element_type=f32)


def tiles(size):
    step = TILE if size % TILE == 0 else size
    return [(at, step) for at in range(0, size, step)]


def centred(values):
    centre = jnp.mean(values, axis=-1, keepdims=True)
    shifted = values - centre
    spread = jnp.mean(shifted * shifted, axis=-1, keepdims=True)
    r = lax.rsqrt(spread + 1e-06)
    return shifted * r, r


def norm_back(xhat, r, gain, grad):
    c = grad * gain
    first = jnp.mean(c, axis=-1, keepdims=True)
    second = jnp.mean(c * xhat, axis=-1, keepdims=True)
    return r * (c - first - xhat * second), jnp.sum(grad * xhat, axis=0, keepdims=True)


def lower_half(rows):
    return lax.broadcasted_iota(jnp.int32, (rows, PAIR), 1) < HEAD


def two_heads(rows):
    keep = lower_half(rows.shape[0])
    zero = jnp.zeros_like(rows)
    return jnp.concatenate([jnp.where(keep, rows, zero), jnp.where(keep, zero, rows)], axis=0)


def side_by_side(stacked):
    rows = stacked.shape[0] // 2
    return jnp.where(lower_half(rows), stacked[:rows], stacked[rows:])


def softmax_rows(scores):
    raised = jnp.exp(scores - jnp.max(scores, axis=-1, keepdims=True))
    return raised / jnp.sum(raised, axis=-1, keepdims=True)


def bias_of(key_seg, own_seg):
    return jnp.where(key_seg == own_seg, 0.0, -1e30).astype(f32)


def block_bias(key_seg, ints, blocks):
    return jnp.stack([bias_of(key_seg[...], ints[1 + 3 * blocks + i]) for i in range(blocks)])


def biased(scores, bias):
    blocks, _, keys = bias.shape
    rows = scores.shape[0] // (2 * blocks)
    return (scores.reshape(2, blocks, rows, keys) + bias[None]).reshape(scores.shape)


def copies(jobs, sems, at):
    made = [pltpu.make_async_copy(src, dst, sems.at[at + i]) for i, (src, dst) in enumerate(jobs)]
    for job in made:
        job.start()
    return made


def whole(shape, dtype):
    return jax.ShapeDtypeStruct(shape, dtype)


VMEM = pl.BlockSpec(memory_space=pltpu.VMEM)
SMEM = pl.BlockSpec(memory_space=pltpu.SMEM)
ANY = pl.BlockSpec(memory_space=pl.ANY)


def params():
    return pltpu.CompilerParams(vmem_limit_bytes=VMEM_BYTES)


def cost(flops, moved, exps=0):
    return pl.CostEstimate(flops=int(flops), bytes_accessed=int(moved), transcendentals=int(exps))


def first_kernel(
    geometry, ints, mix, seg_row, tokens, *refs
):
    dp_count, blocks, token_places, qkv_places, qkv_rows, mirrors = geometry
    n_tok, n_qkv = len(token_places), len(qkv_places)
    token_refs, qkv_refs = refs[:n_tok], refs[n_tok : n_tok + n_qkv]
    blended_ref, qkv_ref, attended_ref, gains_ref, partner, weight, gain_parts, sems = refs[n_tok + n_qkv :]
    me = ints[0]
    width = tokens.shape[1]

    for b in range(blocks):
        holder, slot = ints[1 + b], ints[1 + blocks + b]
        for ref, (role, _, rows) in zip(token_refs, token_places):

            @pl.when(holder == device_of(me, role, mirrors))
            def _(ref=ref, rows=rows, b=b, slot=slot):
                at = pl.multiple_of(slot * CLIP, CLIP)
                pltpu.make_async_copy(ref.at[pl.ds(at, CLIP)], partner.at[b], sems.at[b]).start()

    jobs = []
    for ref, (e, start, rows) in zip(qkv_refs, qkv_places):
        take = min(rows, qkv_rows - start)
        at = pl.multiple_of(device_of(me, e, mirrors) * qkv_rows + start, 16)
        jobs.append((ref.at[pl.ds(0, take)], weight.at[pl.ds(at, take)]))
        if start + rows > qkv_rows:
            jobs.append((ref.at[pl.ds(take, rows - take)], gain_parts.at[e]))
    made = copies(jobs, sems, blocks)
    for b in range(blocks):
        pltpu.make_async_copy(tokens.at[pl.ds(0, CLIP)], partner.at[b], sems.at[b]).wait()
    for b in range(blocks):
        rows = slice(b * CLIP, (b + 1) * CLIP)
        share = mix[b]
        blended_ref[rows, :] = share * tokens[rows, :].astype(f32) + (1.0 - share) * partner[b].astype(f32)
    for job in made:
        job.wait()
    gains = gain_parts[0].astype(f32)
    for e in range(1, dp_count):
        gains = gains + gain_parts[e].astype(f32)
    gains_ref[...] = gains[:8]
    xhat, _ = centred(blended_ref[...])
    normed = (xhat * gains[0:1]).astype(bf16)
    for at, step in tiles(3 * width):
        tile = nt(normed, weight[at : at + step, :])
        if at + step <= width:
            tile = tile * 0.125
        qkv_ref[:, at : at + step] = tile.astype(bf16)

    @pl.loop(0, blocks)
    def _(i):
        window = pl.multiple_of(ints[1 + 2 * blocks + i] * CLIP, CLIP)
        bias = bias_of(seg_row[:, pl.ds(window, WINDOW)], ints[1 + 3 * blocks + i])
        rows = pl.ds(pl.multiple_of(i * CLIP, CLIP), CLIP)
        keys = pl.ds(window, WINDOW)
        for at in range(0, width, PAIR):
            queries = two_heads(qkv_ref[rows, at : at + PAIR])
            probs = softmax_rows(nt(queries, qkv_ref[keys, width + at : width + at + PAIR]) + bias).astype(bf16)
            out = nn(probs, qkv_ref[keys, 2 * width + at : 2 * width + at + PAIR])
            attended_ref[rows, at : at + PAIR] = side_by_side(out).astype(bf16)


def load_cross(me, refs, places, layout, weights, sems, mirrors):
    jobs = []
    for ref, (e, start, rows) in zip(refs, places):
        for (first, size), weight in zip(layout, weights):
            if weight is not None and first >= start and first + size <= start + rows:
                at = pl.multiple_of(device_of(me, e, mirrors) * size, 16)
                jobs.append((ref.at[pl.ds(first - start, size)], weight.at[pl.ds(at, size)]))
    return copies(jobs, sems, 0)


def second_kernel(geometry, ints, coarse_seg, coarse, blended, attended, gains, *refs):
    blocks, places, layout, mirrors = geometry
    weight_refs = refs[: len(places)]
    residual_ref, cq_ref, ckv_ref, crossed_ref, joined_ref, second_ref = refs[len(places) : len(places) + 6]
    w_ckv, w_out, w_cq, w_cout, sems = refs[len(places) + 6 :]
    made = load_cross(ints[0], weight_refs, places, layout, (w_ckv, w_out, w_cq, w_cout), sems, mirrors)
    for job in made:
        job.wait()
    width = blended.shape[1]
    for at, step in tiles(2 * width):
        ckv_ref[:, at : at + step] = nt(coarse[...], w_ckv[at : at + step, :]).astype(bf16)
    for at, step in tiles(width):
        residual_ref[:, at : at + step] = blended[:, at : at + step] + nn(attended[...], w_out[:, at : at + step])
    xhat, _ = centred(residual_ref[...])
    crossed_in = (xhat * gains[1:2]).astype(bf16)
    for at, step in tiles(width):
        cq_ref[:, at : at + step] = (nn(crossed_in, w_cq[:, at : at + step]) * 0.125).astype(bf16)

    bias = block_bias(coarse_seg, ints, blocks)
    for at in range(0, width, PAIR):
        queries = two_heads(cq_ref[:, at : at + PAIR])
        probs = softmax_rows(biased(nt(queries, ckv_ref[:, at : at + PAIR]), bias)).astype(bf16)
        out = nn(probs, ckv_ref[:, width + at : width + at + PAIR])
        crossed_ref[:, at : at + PAIR] = side_by_side(out).astype(bf16)

    for at, step in tiles(width):
        joined_ref[:, at : at + step] = residual_ref[:, at : at + step] + nn(crossed_ref[...], w_cout[:, at : at + step])
    xhat, _ = centred(joined_ref[...])
    second_ref[...] = (xhat * gains[2:3]).astype(bf16)


def mlp_kernel(geometry, second, second_near, cotangent, cotangent_near, *refs):
    groups, places, rows, last = geometry
    weight_refs = refs[: len(places)]
    refs = refs[len(places) :]
    keep_ref, going_ref = refs[:2]
    if last:
        own_ref = refs[2]
        sums = refs[3:7]
        refs = refs[7:]
    else:
        sums = refs[2:6]
        refs = refs[6:]
    w_up, w_down, hidden, grad_pre, sems = refs
    step = pl.program_id(0)

    def jobs_of(group):
        jobs = []
        for ref, (e, which) in zip(weight_refs, places):
            if e == groups[group]:
                for part, weight in ((0, w_up), (1, w_down)):
                    if which is None or which == part:
                        first = part * rows if which is None else 0
                        jobs.append((ref.at[pl.ds(first, rows)], weight.at[group]))
        return jobs

    at = 0
    for group in range(len(groups)):
        jobs = jobs_of(group)
        made = [pltpu.make_async_copy(s, d, sems.at[at + i]) for i, (s, d) in enumerate(jobs)]
        at += len(jobs)

        @pl.when(step == 0)
        def _(made=made):
            for job in made:
                job.start()

        @pl.when(step == group)
        def _(made=made):
            for job in made:
                job.wait()

    @pl.when(step == 0)
    def _():
        for ref in sums:
            ref[...] = jnp.zeros_like(ref)

    up, down = w_up.at[step], w_down.at[step]
    for half, (inputs, upstream) in enumerate(((second, cotangent), (second_near, cotangent_near))):
        pre = nt(inputs[...], up[...])
        grad_hidden = nt(upstream[...], down[...])
        cdf = 0.5 * (1.0 + lax.erf(pre * 0.7071067811865476))
        slope = cdf + pre * (jnp.exp(-0.5 * pre * pre) * 0.3989422804014327)
        hidden[half] = (pre * cdf).astype(bf16)
        grad_pre[half] = (grad_hidden * slope).astype(bf16)
        for first, size in tiles(second.shape[1]):
            columns = slice(first, first + size)
            sums[2 * half][:, columns] += nn(hidden[half], down[:, columns])
            sums[2 * half + 1][:, columns] += nn(grad_pre[half], up[:, columns])
    keep_ref[0, 0] = (tn(grad_pre[0], second[...]) + tn(grad_pre[1], second_near[...])).astype(bf16)
    keep_ref[0, 1] = (tn(hidden[0], cotangent[...]) + tn(hidden[1], cotangent_near[...])).astype(bf16)

    @pl.when(step == len(groups) - 1)
    def _():
        going_ref[0] = sums[2][...].astype(bf16)
        going_ref[1] = sums[3][...].astype(bf16)
        if last:
            own_ref[0] = sums[0][...].astype(bf16)
            own_ref[1] = sums[1][...].astype(bf16)


def grads_out(me, dp_count, layout, sources, keep_ref, send_ref, sems, at, mirrors):
    jobs = []
    for e in range(dp_count):
        target = send_ref if e & CORE else keep_ref
        for (first, size), source in zip(layout, sources):
            if source is None:
                continue
            row = pl.multiple_of(device_of(me, e, mirrors) * size, 16)
            jobs.append((source.at[pl.ds(row, size)], target.at[e // 2, pl.ds(first, size)]))
    return copies(jobs, sems, at)


def third_kernel(
    geometry, ints, coarse_seg, gains, mlp_out, grad_second, own_b, came_a, came_b, joined, cotangent, crossed, cq, ckv, *refs
):
    blocks, places, layout, dp_count, mirrors = geometry
    weight_refs = refs[: len(places)]
    refs = refs[len(places) :]
    output_ref, grad_joined_ref, grad_cq_ref, grad_ckv_ref, gain_grads_ref, keep_ref, send_ref = refs[:7]
    w_cout, g_cout, grad_cross, sems = refs[7:]
    me = ints[0]
    width = joined.shape[1]
    made = load_cross(me, weight_refs, places, layout, (None, None, None, w_cout), sems, mirrors)
    rest = [own_b[i].astype(f32) + came_a[i].astype(f32) + came_b[i].astype(f32) for i in range(2)]
    output_ref[...] = (joined[...] + (mlp_out[...] + rest[0])).astype(bf16)
    xhat, r = centred(joined[...])
    grad_in, gain_two = norm_back(xhat, r, gains[2:3], grad_second[...] + rest[1])
    grad_joined_ref[...] = cotangent[...].astype(f32) + grad_in
    low = grad_joined_ref[...].astype(bf16)
    for job in made:
        job.wait()
    for at, step in tiles(width):
        grad_cross[:, at : at + step] = nt(low, w_cout[at : at + step, :]).astype(bf16)
    for at, step in tiles(width):
        g_cout[at : at + step, :] = tn(crossed[:, at : at + step], low).astype(bf16)
    going = grads_out(me, dp_count, layout, (None, None, None, g_cout), keep_ref, send_ref, sems, len(made), mirrors)
    bias = block_bias(coarse_seg, ints, blocks)
    for at in range(0, width, PAIR):
        lanes = slice(at, at + PAIR)
        queries = two_heads(cq[:, lanes])
        grads = two_heads(grad_cross[:, lanes])
        keys = ckv[:, lanes]
        values = ckv[:, width + at : width + at + PAIR]
        probs = softmax_rows(biased(nt(queries, keys), bias))
        grad_ckv_ref[:, width + at : width + at + PAIR] = tn(probs.astype(bf16), grads).astype(bf16)
        grad_probs = nt(grads, values)
        inner = jnp.sum(probs * grad_probs, axis=-1, keepdims=True)
        scores = (probs * (grad_probs - inner)).astype(bf16)
        part = side_by_side(nn(scores, keys)).astype(bf16)
        grad_cq_ref[:, lanes] = part * jnp.asarray(0.125, bf16)
        grad_ckv_ref[:, lanes] = tn(scores, queries).astype(bf16)

    gain_grads_ref[...] = jnp.concatenate([gain_two] * 8, axis=0)
    for job in going:
        job.wait()


def third_part(geometry, ints, coarse, gains, gain_two, grad_joined, residual, attended, grad_cq, grad_ckv, keep_in, send_in, *refs):
    places, layout, dp_count, mirrors = geometry
    weight_refs = refs[: len(places)]
    refs = refs[len(places) :]
    coarse_ref, grad_res_ref, grad_att_ref, gain_grads_ref, keep_ref, send_ref = refs[:6]
    w_ckv, w_out, w_cq, g_ckv, g_out, g_cq, crossed_in, sems = refs[6:]
    me = ints[0]
    width = residual.shape[1]
    made = load_cross(me, weight_refs, places, layout, (w_ckv, w_out, w_cq, None), sems, mirrors)
    xhat, r = centred(residual[...])
    crossed_in[...] = (xhat * gains[1:2]).astype(bf16)
    for at, step in tiles(width):
        g_cq[at : at + step, :] = tn(crossed_in[:, at : at + step], grad_cq[...]).astype(bf16)
    for at, step in tiles(2 * width):
        g_ckv[at : at + step, :] = tn(grad_ckv[:, at : at + step], coarse[...]).astype(bf16)
    for job in made:
        job.wait()
    going = grads_out(me, dp_count, layout, (g_ckv, None, g_cq, None), keep_ref, send_ref, sems, 0, mirrors)
    for at, step in tiles(width):
        coarse_ref[:, at : at + step] = nn(grad_ckv[:, 0:width], w_ckv[0:width, at : at + step]) + nn(
            grad_ckv[:, width : 2 * width], w_ckv[width : 2 * width, at : at + step]
        )
    pieces = [nt(grad_cq[...], w_cq[at : at + step, :]) for at, step in tiles(width)]
    grad_in, gain_cross = norm_back(xhat, r, gains[1:2], jnp.concatenate(pieces, axis=1))
    grad_res = grad_joined[...] + grad_in
    grad_res_ref[...] = grad_res
    low = grad_res.astype(bf16)
    for at, step in tiles(width):
        g_out[at : at + step, :] = tn(attended[:, at : at + step], low).astype(bf16)
    going += grads_out(me, dp_count, layout, (None, g_out, None, None), keep_ref, send_ref, sems, len(going), mirrors)
    for at, step in tiles(width):
        grad_att_ref[:, at : at + step] = nt(low, w_out[at : at + step, :]).astype(bf16)
    zero = jnp.zeros_like(gain_cross)
    gain_grads_ref[...] = jnp.concatenate([zero, gain_cross, gain_two[0:1]] + [zero] * 5, axis=0)
    for job in going:
        job.wait()


def fourth_kernel(geometry, ints, seg_row, grad_att, qkv, *refs):
    blocks, first, last = geometry
    grad_proj, query_part, key_part, value_part, key_sum, value_sum, sems = refs[-7:]
    width = grad_att.shape[1]
    low, high = first * PAIR, last * PAIR
    key_sum[...] = jnp.zeros_like(key_sum)
    value_sum[...] = jnp.zeros_like(value_sum)

    @pl.loop(0, blocks)
    def _(i):
        window = pl.multiple_of(ints[1 + 2 * blocks + i] * CLIP, CLIP)
        bias = bias_of(seg_row[:, pl.ds(window, WINDOW)], ints[1 + 3 * blocks + i])
        rows = pl.ds(pl.multiple_of(i * CLIP, CLIP), CLIP)
        near = pl.ds(window, WINDOW)
        for at in range(low, high, PAIR):
            lanes = slice(at - low, at - low + PAIR)
            queries = two_heads(qkv[rows, at : at + PAIR])
            grads = two_heads(grad_att[rows, at : at + PAIR])
            keys = qkv[near, width + at : width + at + PAIR]
            values = qkv[near, 2 * width + at : 2 * width + at + PAIR]
            probs = softmax_rows(nt(queries, keys) + bias)
            value_sum[near, lanes] += tn(probs.astype(bf16), grads)
            grad_probs = nt(grads, values)
            inner = jnp.sum(probs * grad_probs, axis=-1, keepdims=True)
            scores = (probs * (grad_probs - inner)).astype(bf16)
            part = side_by_side(nn(scores, keys)).astype(bf16)
            query_part[rows, lanes] = part * jnp.asarray(0.125, bf16)
            key_sum[near, lanes] += tn(scores, queries)

    key_part[...] = key_sum[...].astype(bf16)
    value_part[...] = value_sum[...].astype(bf16)
    jobs = [
        (part, grad_proj.at[:, pl.ds(i * width + low, high - low)])
        for i, part in enumerate((query_part, key_part, value_part))
    ]
    for job in copies(jobs, sems, 0):
        job.wait()


def fifth_kernel(geometry, ints, mix, gains, blended, grad_res, grad_proj, *refs):
    dp_count, blocks, qkv_places, qkv_rows, mirrors = geometry
    weight_refs = refs[: len(qkv_places)]
    refs = refs[len(qkv_places) :]
    base_ref, going_ref = refs[:2]
    weight, sems = refs[2:]
    me = ints[0]
    width = blended.shape[1]
    jobs = []
    for ref, (e, start, rows) in zip(weight_refs, qkv_places):
        take = min(rows, qkv_rows - start)
        at = pl.multiple_of(device_of(me, e, mirrors) * qkv_rows + start, 16)
        jobs.append((ref.at[pl.ds(0, take)], weight.at[pl.ds(at, take)]))
    made = copies(jobs, sems, 0)
    xhat, r = centred(blended[...])
    for job in made:
        job.wait()
    pieces = [nn(grad_proj[...], weight[:, at : at + step]) for at, step in tiles(width)]
    grad_in, _ = norm_back(xhat, r, gains[0:1], jnp.concatenate(pieces, axis=1))
    grad_blend = grad_res[...] + grad_in
    for b in range(blocks):
        rows = slice(b * CLIP, (b + 1) * CLIP)
        share = mix[b]
        part = grad_blend[rows, :]
        base_ref[rows, :] = share * part
        going_ref[rows, :] = ((1.0 - share) * part).astype(bf16)


def place_kernel(geometry, ints, ints_near, blocks_own, blocks_near, out_ref):
    blocks, mirrors = geometry
    me = ints[0]
    out_ref[...] = jnp.zeros_like(out_ref)
    for table, first, source in ((ints, 1, blocks_own), (ints_near, 0, blocks_near)):
        for b in range(blocks):
            holder, slot = table[first + b], table[first + blocks + b]
            group = jnp.int32(0)
            for role in mirrors:
                group = group + jnp.where(device_of(me, role, mirrors) == holder, role // 2, 0)

            @pl.when(lax.rem(holder, 2) == lax.rem(me, 2))
            def _(group=group, slot=slot, source=source, b=b):
                rows = pl.ds(pl.multiple_of(slot * CLIP, CLIP), CLIP)
                part = source[b * CLIP : (b + 1) * CLIP, :].astype(f32)
                out_ref[group, rows, :] = (out_ref[group, rows, :].astype(f32) + part).astype(bf16)


def sixth_kernel(geometry, ints, gains, gain_grads, blended, grad_proj, *refs):
    dp_count, qkv_places, qkv_rows, mirrors = geometry
    weight_refs = refs[: len(qkv_places)]
    keep_ref, send_ref, weight, grad_w, gain_rows, sems = refs[len(qkv_places) :]
    me = ints[0]
    width = blended.shape[1]
    jobs = []
    for ref, (e, start, rows) in zip(weight_refs, qkv_places):
        take = min(rows, qkv_rows - start)
        at = pl.multiple_of(device_of(me, e, mirrors) * qkv_rows + start, 16)
        jobs.append((ref.at[pl.ds(0, take)], weight.at[pl.ds(at, take)]))
    made = copies(jobs, sems, 0)
    xhat, _ = centred(blended[...])
    normed = (xhat * gains[0:1]).astype(bf16)
    for job in made:
        job.wait()
    gain_one = jnp.zeros((1, width), f32)
    for at, step in tiles(3 * width):
        part = tn(grad_proj[:, at : at + step], normed)
        gain_one = gain_one + jnp.sum(part * weight[at : at + step, :].astype(f32), axis=0, keepdims=True)
        grad_w[at : at + step, :] = part.astype(bf16)
    sent = grads_out(me, dp_count, ((0, qkv_rows),), (grad_w,), keep_ref, send_ref, sems, len(jobs), mirrors)
    all_gains = jnp.concatenate([gain_one / gains[0:1], gain_grads[1:8], jnp.zeros((8, width), f32)], axis=0)
    gain_rows[...] = all_gains.astype(bf16)
    last = []
    for e in range(dp_count):
        target = send_ref if e & CORE else keep_ref
        last.append((gain_rows, target.at[e // 2, pl.ds(qkv_rows, 16)]))
    for job in sent + copies(last, sems, len(jobs) + dp_count):
        job.wait()


def shards(
    tokens,
    coarse_view,
    segment_ids,
    partner_device,
    partner_slot,
    mix_weight,
    ln1_gain,
    w_qkv,
    w_out,
    lnx_gain,
    w_cq,
    w_ckv,
    w_cout,
    ln2_gain,
    w_up,
    w_down,
    cotangent,
):
    row_count, width = tokens.shape
    coarse_rows = coarse_view.shape[0]
    blocks = mix_weight.shape[0]
    dp_count, fsdp_count = lax.axis_size("dp"), lax.axis_size("fsdp")
    dp_me, fsdp_me = lax.axis_index("dp"), lax.axis_index("fsdp")
    part = ln1_gain.shape[0]
    device_me = dp_me * fsdp_count + fsdp_me
    pairs = dp_count // 2
    mirrors = mirror_table()

    target = partner_device[:, 0]
    segments = segment_ids[0]
    videos = segments.reshape(blocks, row_count // blocks)[:, 0]
    following = jnp.concatenate([videos[1:] == videos[:-1], jnp.zeros((1,), bool)])
    before = jnp.concatenate([jnp.zeros((1,), bool), videos[1:] == videos[:-1]])
    index = jnp.arange(blocks, dtype=jnp.int32)
    window = jnp.where(following, index, jnp.where(before, index - 1, jnp.minimum(index, blocks - 2)))
    ints = jnp.concatenate(
        [dp_me[None].astype(jnp.int32), target, partner_slot, window, videos]
    )
    ints_near = swap(ints[1 : 1 + 2 * blocks], CORE)
    seg_row = segments[None, :]
    coarse_seg = segments.reshape(coarse_rows, row_count // coarse_rows)[:, 0][None, :]

    gain_rows = lax.dynamic_update_slice(
        jnp.zeros((8, width), bf16), jnp.stack([ln1_gain, lnx_gain, ln2_gain]), (0, device_me * part)
    )
    shard_one = jnp.concatenate([w_qkv.T, gain_rows])
    shard_two = jnp.concatenate([w_ckv.T, w_out, w_cq, w_cout])
    shard_mlp = jnp.concatenate([w_up.T, w_down])
    sizes_two = (w_ckv.shape[1], w_out.shape[0], w_cq.shape[0], w_cout.shape[0])
    qkv_part, up_part = w_qkv.shape[1], w_up.shape[1]
    qkv_rows, up_rows = qkv_part * fsdp_count, up_part * fsdp_count
    layout = []
    at = 0
    for size in sizes_two:
        layout.append((at * fsdp_count, size * fsdp_count))
        at += size
    layout = tuple(layout)
    rows_two = at * fsdp_count

    held_tok = {0: tokens, **single_steps(tokens)}
    came_one = inner_start(shard_one)
    held_tok, came_one, shard_two = fence((held_tok, came_one, shard_two))

    ones = inner_order(came_one)
    gain_block = jnp.sum(ones[:, qkv_part:].astype(f32), axis=0).astype(bf16)
    block_one = jnp.concatenate(
        [ones[:, :qkv_part].reshape(qkv_rows, width), gain_block, jnp.zeros((8, width), bf16)]
    )
    held_one = {0: block_one, **single_steps(block_one)}
    came_two = inner_start(shard_two)
    held_tok, held_one, came_two, shard_mlp = fence((held_tok, held_one, came_two, shard_mlp))

    mlp = inner_double(shard_mlp[None], 1)
    core_tok = core_steps(dict(held_tok))
    near_tok = set(held_tok)
    relay_steps(held_tok)
    twos = inner_order(came_two)
    split = []
    at = 0
    for size in sizes_two:
        split.append(twos[:, at : at + size].reshape(size * fsdp_count, width))
        at += size
    block_two = jnp.concatenate(split)
    held_one, core_tok, held_tok, block_two, mlp = fence((held_one, core_tok, held_tok, block_two, mlp))

    cuts = (0, 2 * up_part // 3, 5 * up_part // 3, 2 * up_part)
    mlp_cut = [mlp[:, first:last] for first, last in zip(cuts, cuts[1:])]
    mlp_came = [inner_swap(mlp_cut[0], 2)]
    core_one = core_steps(dict(held_one))
    relay_steps(held_one)
    late_tok = core_steps({e: b for e, b in held_tok.items() if e not in near_tok})
    held_one, core_one, late_tok, block_two, mlp_cut, mlp_came = fence(
        (held_one, core_one, late_tok, block_two, mlp_cut, mlp_came)
    )

    held_two = {0: block_two, **single_steps(block_two)}
    cotangent_near = swap(cotangent, CORE)
    mlp_came.append(inner_swap(mlp_cut[1], 2))
    late_one = core_steps({e: b for e, b in held_one.items() if e not in near_tok})
    pieces_tok = {**core_tok, **late_tok}
    pieces_one = {**core_one, **late_one}
    arrays_tok, places_tok = parts_of(pieces_tok, row_count)
    arrays_one, places_one = parts_of(pieces_one, qkv_rows + 16)
    blended, qkv, attended, gains = pl.pallas_call(
        functools.partial(first_kernel, (dp_count, blocks, places_tok, places_one, qkv_rows, mirrors)),
        out_shape=(
            whole((row_count, width), f32),
            whole((row_count, 3 * width), bf16),
            whole((row_count, width), bf16),
            whole((8, width), f32),
        ),
        in_specs=[SMEM, SMEM, VMEM, VMEM] + [ANY] * (len(arrays_tok) + len(arrays_one)),
        out_specs=(VMEM,) * 4,
        scratch_shapes=[
            pltpu.VMEM((blocks, CLIP, width), bf16),
            pltpu.VMEM((3 * width, width), bf16),
            pltpu.VMEM((dp_count, 16, width), bf16),
            pltpu.SemaphoreType.DMA((blocks + len(arrays_one) + dp_count,)),
        ],
        compiler_params=params(),
        cost_estimate=cost(1e9, 1e6),
        name="mix_self_attention",
    )(ints, mix_weight, seg_row, tokens, *arrays_tok, *arrays_one)
    held_two, attended, mlp_came, cotangent_near, mlp_cut = fence((held_two, attended, mlp_came, cotangent_near, mlp_cut))

    core_two = core_steps(dict(held_two))
    relay_steps(held_two)
    mlp_came.append(inner_swap(mlp_cut[2], 2))
    held_two, core_two, mlp_came, ints_near = fence((held_two, core_two, mlp_came, ints_near))

    mlp = jnp.concatenate([inner_rest(inner_join(cut, came, 2)) for cut, came in zip(mlp_cut, mlp_came)], axis=1)
    block_mlp = jnp.concatenate([mlp[:, :up_part].reshape(up_rows, width), mlp[:, up_part:].reshape(up_rows, width)])
    held_mlp = {0: block_mlp, **single_steps(block_mlp)}
    late_two = core_steps({e: b for e, b in held_two.items() if e not in near_tok})
    pieces_two = {**core_two, **late_two}
    wide = [pltpu.VMEM((sizes * fsdp_count * dp_count, width), bf16) for sizes in sizes_two]
    n_two = 4 * dp_count
    arrays_two, places_two = parts_of(pieces_two, rows_two)
    wide = [pltpu.VMEM((sizes * fsdp_count * dp_count, width), bf16) for sizes in sizes_two]
    n_two = 4 * dp_count
    residual, cq, ckv, crossed, joined, second = pl.pallas_call(
        functools.partial(second_kernel, (blocks, places_two, layout, mirrors)),
        out_shape=(
            whole((row_count, width), f32),
            whole((row_count, width), bf16),
            whole((coarse_rows, 2 * width), bf16),
            whole((row_count, width), bf16),
            whole((row_count, width), f32),
            whole((row_count, width), bf16),
        ),
        in_specs=[SMEM] + [VMEM] * 5 + [ANY] * len(arrays_two),
        out_specs=(VMEM,) * 6,
        scratch_shapes=wide + [pltpu.SemaphoreType.DMA((n_two,))],
        compiler_params=params(),
        cost_estimate=cost(1e9, 1e6),
        name="cross_attention",
    )(ints, coarse_seg, coarse_view, blended, attended, gains, *arrays_two)
    second_near = swap(second, CORE)
    held_mlp, second, second_near = fence((held_mlp, second, second_near))

    early = dict(held_mlp)
    relay_steps(held_mlp)

    def mlp_call(pieces, last):
        groups = tuple(sorted(pieces))
        count = len(groups)
        fixed = pl.BlockSpec((row_count, width), lambda g: (0, 0))
        moving = pl.BlockSpec((1, 2, up_rows, width), lambda g: (g, 0, 0, 0))
        both = pl.BlockSpec((2, row_count, width), lambda g: (0, 0, 0))
        table = whole((row_count, width), f32)
        out_shape = [whole((count, 2, up_rows, width), bf16), whole((2, row_count, width), bf16)]
        out_specs = [moving, both]
        scratch = [pltpu.VMEM((row_count, width), f32)] * (4 if last else 2)
        if last:
            out_shape.append(whole((2, row_count, width), bf16))
            out_specs.append(both)
        else:
            out_shape += [table, table]
            out_specs += [fixed, fixed]
        made = pl.pallas_call(
            functools.partial(mlp_kernel, (groups, tuple((e, None) for e in groups), up_rows, last)),
            grid=(count,),
            out_shape=tuple(out_shape),
            in_specs=[fixed] * 4 + [ANY] * count,
            out_specs=tuple(out_specs),
            scratch_shapes=scratch
            + [
                pltpu.VMEM((count, up_rows, width), bf16),
                pltpu.VMEM((count, up_rows, width), bf16),
                pltpu.VMEM((2, row_count, up_rows), bf16),
                pltpu.VMEM((2, row_count, up_rows), bf16),
                pltpu.SemaphoreType.DMA((2 * count,)),
            ],
            compiler_params=params(),
            cost_estimate=cost(1e9, 1e6),
            name="feed_forward",
        )(second, second_near, cotangent, cotangent_near, *[pieces[e] for e in groups])
        return groups, made[0].reshape(count, 2 * up_rows, width), made[1], made[2:]

    groups_a, keep_a, going_a, (mlp_out, grad_second) = mlp_call(early, False)
    late = {e: b for e, b in held_mlp.items() if e not in near_tok}
    late, keep_a, going_a, mlp_out, grad_second = fence((late, keep_a, going_a, mlp_out, grad_second))
    came_a = swap(going_a, CORE)
    groups_b, keep_b, going_b, (own_b,) = mlp_call(late, True)
    came_a, keep_b, going_b, own_b = fence((came_a, keep_b, going_b, own_b))
    came_b = swap(going_b, CORE)
    totals = [None] * pairs
    for groups, keep in ((groups_a, keep_a), (groups_b, keep_b)):
        for i, e in enumerate(groups):
            totals[e // 2] = keep[i]
    totals, came_b = fence((totals, came_b))

    sum_mlp = OuterSum(totals)
    sum_mlp.relays()
    output, grad_joined, grad_cq, grad_ckv, gain_two, keep_two, send_two = pl.pallas_call(
        functools.partial(third_kernel, (blocks, places_two, layout, dp_count, mirrors)),
        out_shape=(
            whole((row_count, width), bf16),
            whole((row_count, width), f32),
            whole((row_count, width), bf16),
            whole((coarse_rows, 2 * width), bf16),
            whole((8, width), f32),
            whole((pairs, rows_two, width), bf16),
            whole((pairs, rows_two, width), bf16),
        ),
        in_specs=[SMEM] + [VMEM] * 12 + [ANY] * len(arrays_two),
        out_specs=(VMEM,) * 5 + (ANY,) * 2,
        scratch_shapes=[
            wide[3],
            wide[3],
            pltpu.VMEM((row_count, width), bf16),
            pltpu.SemaphoreType.DMA((n_two + dp_count,)),
        ],
        compiler_params=params(),
        cost_estimate=cost(1e9, 1e6),
        name="cross_attention_backward",
    )(ints, coarse_seg, gains, mlp_out, grad_second, own_b, came_a, came_b, joined, cotangent, crossed, cq, ckv, *arrays_two)
    state, grad_joined = fence((sum_mlp.state(), grad_joined))
    sum_mlp.put(state)

    sum_mlp.singles(slice(0, up_rows))
    coarse_grad, grad_res, grad_att, gain_grads, keep_two, send_two = pl.pallas_call(
        functools.partial(third_part, (places_two, layout, dp_count, mirrors)),
        out_shape=(
            whole((coarse_rows, width), f32),
            whole((row_count, width), f32),
            whole((row_count, width), bf16),
            whole((8, width), f32),
            whole((pairs, rows_two, width), bf16),
            whole((pairs, rows_two, width), bf16),
        ),
        in_specs=[SMEM] + [VMEM] * 8 + [ANY] * (2 + len(arrays_two)),
        out_specs=(VMEM,) * 4 + (ANY,) * 2,
        scratch_shapes=[
            wide[0],
            wide[1],
            wide[2],
            wide[0],
            wide[1],
            wide[2],
            pltpu.VMEM((row_count, width), bf16),
            pltpu.SemaphoreType.DMA((n_two,)),
        ],
        input_output_aliases={9: 4, 10: 5},
        compiler_params=params(),
        cost_estimate=cost(1e9, 1e6),
        name="cross_attention_weights",
    )(
        ints, coarse_view, gains, gain_two, grad_joined, residual, attended, grad_cq, grad_ckv, keep_two, send_two, *arrays_two
    )

    state, grad_att, keep_two, send_two = fence((sum_mlp.state(), grad_att, keep_two, send_two))
    sum_mlp.put(state)

    sum_mlp.singles(slice(up_rows, 2 * up_rows))
    came_two = swap(send_two, CORE)
    def attention_back(first, last, held):
        columns = (last - first) * PAIR
        return pl.pallas_call(
            functools.partial(fourth_kernel, (blocks, first, last)),
            out_shape=whole((row_count, 3 * width), bf16),
            in_specs=[SMEM] + [VMEM] * 3 + [ANY] * len(held),
            out_specs=ANY,
            scratch_shapes=[pltpu.VMEM((row_count, columns), bf16)] * 3
            + [pltpu.VMEM((row_count, columns), f32)] * 2
            + [pltpu.SemaphoreType.DMA((3,))],
            input_output_aliases={4: 0} if held else {},
            compiler_params=params(),
            cost_estimate=cost(1e9, 1e6),
            name="self_attention_backward",
        )(ints, seg_row, grad_att, qkv, *held)

    grad_proj = attention_back(0, HEADS // 2, ())
    state, came_two, grad_proj = fence((sum_mlp.state(), came_two, grad_proj))
    sum_mlp.put(state)

    sum_two = OuterSum(keep_two, came_two)
    sum_two.relays()
    inner_up = InnerSum(sum_mlp.result(0).reshape(fsdp_count, up_part, width))
    inner_up.step()
    keep_one, send_one = pl.pallas_call(
        functools.partial(sixth_kernel, (dp_count, places_one, qkv_rows, mirrors)),
        out_shape=(
            whole((pairs, qkv_rows + 16, width), bf16),
            whole((pairs, qkv_rows + 16, width), bf16),
        ),
        in_specs=[SMEM] + [VMEM] * 4 + [ANY] * len(arrays_one),
        out_specs=(ANY,) * 2,
        scratch_shapes=[
            pltpu.VMEM((3 * width, width), bf16),
            pltpu.VMEM((3 * width, width), bf16),
            pltpu.VMEM((16, width), bf16),
            pltpu.SemaphoreType.DMA((len(arrays_one) + 2 * dp_count,)),
        ],
        compiler_params=params(),
        cost_estimate=cost(1e9, 1e6),
        name="self_attention_weights",
    )(ints, gains, gain_grads, blended, grad_proj, *arrays_one)
    state, keep_one, send_one, up_came = fence((sum_two.state(), keep_one, send_one, inner_up.came))
    sum_two.put(state)
    inner_up.came = up_came

    sum_two.singles()
    inner_down = InnerSum(sum_mlp.result(1).reshape(fsdp_count, up_part, width))
    inner_down.step()
    came_one = swap(send_one, CORE)
    base, going_tok = pl.pallas_call(
        functools.partial(fifth_kernel, (dp_count, blocks, places_one, qkv_rows, mirrors)),
        out_shape=(
            whole((row_count, width), f32),
            whole((row_count, width), bf16),
        ),
        in_specs=[SMEM, SMEM] + [VMEM] * 4 + [ANY] * len(arrays_one),
        out_specs=(VMEM,) * 2,
        scratch_shapes=[
            pltpu.VMEM((3 * width, width), bf16),
            pltpu.SemaphoreType.DMA((len(arrays_one),)),
        ],
        compiler_params=params(),
        cost_estimate=cost(1e9, 1e6),
        name="self_attention_input",
    )(ints, mix_weight, gains, blended, grad_res, grad_proj, *arrays_one)
    state, came_one, going_tok, down_came = fence((sum_two.state(), came_one, going_tok, inner_down.came))
    sum_two.put(state)
    inner_down.came = down_came

    sum_one = OuterSum(keep_one, came_one)
    sum_one.relays()
    came_tok = swap(going_tok, CORE)
    placed = pl.pallas_call(
        functools.partial(place_kernel, (blocks, mirrors)),
        out_shape=whole((pairs, row_count, width), bf16),
        in_specs=[SMEM, SMEM] + [VMEM] * 2,
        out_specs=VMEM,
        compiler_params=params(),
        cost_estimate=cost(1e9, 1e6),
        name="place_partner_gradients",
    )(ints, ints_near, going_tok, came_tok)
    mlp_parts = jnp.concatenate([inner_parts(inner_up), inner_parts(inner_down)], axis=1)
    inner_mlp = InnerSum(mlp_parts)
    inner_mlp.finish()
    state, placed, mlp_came = fence((sum_one.state(), placed, inner_mlp.came))
    sum_one.put(state)
    inner_mlp.came = mlp_came

    sum_one.singles()
    sum_tok = OuterSum(placed)
    sum_tok.relays()
    two_sum = sum_two.result()
    two_parts = jnp.concatenate(
        [two_sum[first : first + size].reshape(fsdp_count, size // fsdp_count, width) for first, size in layout], axis=1
    )
    inner_two = InnerSum(two_parts)
    inner_two.step()
    state, state_tok, two_came = fence((sum_one.state(), sum_tok.state(), inner_two.came))
    sum_one.put(state)
    sum_tok.put(state_tok)
    inner_two.came = two_came

    sum_tok.singles()
    one_sum = sum_one.result()
    gain_sum = jnp.broadcast_to(one_sum[qkv_rows : qkv_rows + 8][None], (fsdp_count, 8, width))
    one_parts = jnp.concatenate([one_sum[:qkv_rows].reshape(fsdp_count, qkv_part, width), gain_sum], axis=1)
    inner_one = InnerSum(one_parts)
    inner_one.step()
    one_mine = inner_one.result()
    mlp_mine = inner_mlp.result()
    up_shard, down_shard = mlp_mine[:up_part].T, mlp_mine[up_part:]
    two_mine = inner_two.result()
    found = []
    at = 0
    for size in sizes_two:
        found.append(two_mine[at : at + size])
        at += size
    ckv_shard, out_shard, cq_shard, cout_shard = found[0].T, found[1], found[2], found[3]
    qkv_shard = one_mine[:qkv_part].T
    gain_mine = lax.dynamic_slice(one_mine[qkv_part:], (0, device_me * part), (3, part))
    token_grad = base + sum_tok.result()
    return (
        output,
        token_grad,
        coarse_grad,
        gain_mine[0],
        qkv_shard,
        out_shard,
        gain_mine[1],
        cq_shard,
        ckv_shard,
        cout_shard,
        gain_mine[2],
        up_shard,
        down_shard,
    )


def solution(mesh):
    rows = P(("dp", "fsdp"), None)
    columns = P(None, ("dp", "fsdp"))
    line = P(("dp", "fsdp"))
    in_specs = (
        rows, rows, rows, rows, line, line, line, columns, rows,
        line, rows, columns, rows, line, columns, rows, rows,
    )
    out_specs = (
        rows, rows, rows, line, columns, rows, line, rows, columns, rows, line, columns, rows,
    )
    return jax.shard_map(shards, mesh=mesh, in_specs=in_specs, out_specs=out_specs, check_vma=False)
```

```python
import functools

import jax
import jax.numpy as jnp
from jax import lax
from jax.experimental import pallas as pl
from jax.experimental.pallas import tpu as pltpu
from jax.sharding import PartitionSpec as P

HEADS = 12
HEAD = 64
PAIR = 2 * HEAD
CORE = 1
CLIP = 128
WINDOW = 256
TILE = 256
f32 = jnp.float32
bf16 = jnp.bfloat16
fence = lax.optimization_barrier


def swap(values, mask):
    count = lax.axis_size("dp")
    return lax.ppermute(values, "dp", [(i, i ^ mask) for i in range(count)])


def shift(values, step):
    count = lax.axis_size("fsdp")
    return lax.ppermute(values, "fsdp", [(i, (i + step) % count) for i in range(count)])


def link_masks():
    masks = []
    mask = 2
    while mask < lax.axis_size("dp"):
        masks.append(mask)
        mask *= 2
    return masks


def inner_swap(values, mask):
    count = lax.axis_size("fsdp")
    return lax.ppermute(values, "fsdp", [(i, i ^ mask) for i in range(count)])


def inner_double(held, mask):
    return inner_join(held, inner_swap(held, mask), mask)


def inner_join(held, came, mask):
    high = (lax.axis_index("fsdp") & mask) != 0
    return jnp.concatenate([jnp.where(high, came, held), jnp.where(high, held, came)])


def inner_rest(held):
    while held.shape[0] < lax.axis_size("fsdp"):
        held = inner_double(held, held.shape[0])
    return held


def inner_start(shard):
    return [shard] + [shift(shard, step) for step in range(1, lax.axis_size("fsdp"))]


def inner_order(came):
    count = len(came)
    me = lax.axis_index("fsdp")
    line = [came[count - 1 - k] for k in range(count)] + [came[count - k] for k in range(1, count)]
    return lax.dynamic_slice_in_dim(jnp.stack(line), count - 1 - me, count, 0)


def mirrored(role):
    masks = link_masks()
    return sum(masks[len(masks) - 1 - i] for i, mask in enumerate(masks) if role & mask)


def step_along(values, mask):
    count = lax.axis_size("dp")
    return lax.ppermute(values, "dp", [(i, i ^ (mirrored(mask) if i & CORE else mask)) for i in range(count)])


def top_bit(role):
    return 1 << (role.bit_length() - 1)


def relayed_roles():
    found = [role for role in range(2, lax.axis_size("dp"), 2) if role & (role - 1)]
    return sorted(found, key=lambda role: bin(role).count("1"))


def device_of(me, role, mirrors):
    holder = me ^ (role & CORE)
    link = role & ~CORE
    return holder ^ (link + lax.rem(holder, 2) * (mirrors[link] - link))


def mirror_table():
    return {role: mirrored(role) for role in range(0, lax.axis_size("dp"), 2)}


def single_steps(block):
    return {mask: step_along(block, mask) for mask in link_masks()}


def relay_steps(held):
    for role in relayed_roles():
        held[role] = step_along(held[role ^ top_bit(role)], top_bit(role))


def parts_of(pieces, total):
    return [pieces[e] for e in sorted(pieces)], tuple((e, 0, total) for e in sorted(pieces))


def core_steps(held):
    return {**held, **{e | CORE: swap(block, CORE) for e, block in held.items()}}


def inner_parts(inner):
    inner.add()
    return inner.parts


def add_low(a, b):
    return (a.astype(f32) + b.astype(f32)).astype(bf16)


class OuterSum:
    def __init__(self, *parts):
        self.parts = {2 * g: [part[g] for part in parts] for g in range(lax.axis_size("dp") // 2)}
        self.came = []

    def value(self, role, rows=slice(None)):
        total = self.parts[role][0][rows].astype(f32)
        for part in self.parts[role][1:]:
            total = total + part[rows].astype(f32)
        return total

    def relays(self):
        for role in relayed_roles()[::-1]:
            came = step_along(self.value(role).astype(bf16), top_bit(role))
            self.parts[role ^ top_bit(role)].append(came)

    def singles(self, rows=slice(None)):
        self.came.append((rows, [step_along(self.value(mask, rows).astype(bf16), mask) for mask in link_masks()]))

    def result(self, index=None):
        chosen = self.came if index is None else [self.came[index]]
        sums = []
        for rows, blocks in chosen:
            total = self.value(0, rows)
            for block in blocks:
                total = total + block.astype(f32)
            sums.append(total)
        return sums[0] if len(sums) == 1 else jnp.concatenate(sums)

    def state(self):
        return (self.parts, [blocks for _, blocks in self.came])

    def put(self, state):
        self.parts = state[0]
        self.came = [(rows, blocks) for (rows, _), blocks in zip(self.came, state[1])]


class InnerSum:
    def __init__(self, parts):
        self.parts = parts
        self.came = None
        self.mask = parts.shape[0]

    def step(self):
        self.add()
        self.mask //= 2
        bit = ((lax.axis_index("fsdp") & self.mask) != 0).astype(jnp.int32)
        halves = self.parts.reshape((2, self.mask) + self.parts.shape[1:])
        self.parts = lax.dynamic_index_in_dim(halves, bit, 0, keepdims=False)
        going = lax.dynamic_index_in_dim(halves, 1 - bit, 0, keepdims=False).astype(bf16)
        self.came = inner_swap(going, self.mask)

    def finish(self, steps=None):
        while self.mask > 1:
            self.step()

    def add(self):
        if self.came is not None:
            self.parts = self.parts + self.came.astype(f32)
            self.came = None

    def result(self):
        self.finish()
        self.add()
        return self.parts[0]


def nn(a, b):
    return jnp.dot(a, b, preferred_element_type=f32)


def nt(a, b):
    return lax.dot_general(a, b, (((1,), (1,)), ((), ())), preferred_element_type=f32)


def tn(a, b):
    return lax.dot_general(a, b, (((0,), (0,)), ((), ())), preferred_element_type=f32)


def tiles(size):
    step = TILE if size % TILE == 0 else size
    return [(at, step) for at in range(0, size, step)]


def centred(values):
    centre = jnp.mean(values, axis=-1, keepdims=True)
    shifted = values - centre
    spread = jnp.mean(shifted * shifted, axis=-1, keepdims=True)
    r = lax.rsqrt(spread + 1e-06)
    return shifted * r, r


def norm_back(xhat, r, gain, grad):
    c = grad * gain
    first = jnp.mean(c, axis=-1, keepdims=True)
    second = jnp.mean(c * xhat, axis=-1, keepdims=True)
    return r * (c - first - xhat * second), jnp.sum(grad * xhat, axis=0, keepdims=True)


def lower_half(rows):
    return lax.broadcasted_iota(jnp.int32, (rows, PAIR), 1) < HEAD


def two_heads(rows):
    keep = lower_half(rows.shape[0])
    zero = jnp.zeros_like(rows)
    return jnp.concatenate([jnp.where(keep, rows, zero), jnp.where(keep, zero, rows)], axis=0)


def side_by_side(stacked):
    rows = stacked.shape[0] // 2
    return jnp.where(lower_half(rows), stacked[:rows], stacked[rows:])


def softmax_rows(scores):
    raised = jnp.exp(scores - jnp.max(scores, axis=-1, keepdims=True))
    return raised / jnp.sum(raised, axis=-1, keepdims=True)


def bias_of(key_seg, own_seg):
    return jnp.where(key_seg == own_seg, 0.0, -1e30).astype(f32)


def block_bias(key_seg, ints, blocks):
    return jnp.stack([bias_of(key_seg[...], ints[1 + 3 * blocks + i]) for i in range(blocks)])


def biased(scores, bias):
    blocks, _, keys = bias.shape
    rows = scores.shape[0] // (2 * blocks)
    return (scores.reshape(2, blocks, rows, keys) + bias[None]).reshape(scores.shape)


def copies(jobs, sems, at):
    made = [pltpu.make_async_copy(src, dst, sems.at[at + i]) for i, (src, dst) in enumerate(jobs)]
    for job in made:
        job.start()
    return made


def whole(shape, dtype):
    return jax.ShapeDtypeStruct(shape, dtype)


VMEM = pl.BlockSpec(memory_space=pltpu.VMEM)
SMEM = pl.BlockSpec(memory_space=pltpu.SMEM)
ANY = pl.BlockSpec(memory_space=pl.ANY)


def params(mib=56):
    return pltpu.CompilerParams(vmem_limit_bytes=mib * 1024 * 1024)


def cost(flops, moved, exps=0):
    return pl.CostEstimate(flops=int(flops), bytes_accessed=int(moved), transcendentals=int(exps))


def first_kernel(
    geometry, ints, mix, seg_row, tokens, *refs
):
    dp_count, blocks, token_places, qkv_places, qkv_rows, mirrors = geometry
    n_tok, n_qkv = len(token_places), len(qkv_places)
    token_refs, qkv_refs = refs[:n_tok], refs[n_tok : n_tok + n_qkv]
    blended_ref, qkv_ref, attended_ref, gains_ref, partner, weight, gain_parts, sems = refs[n_tok + n_qkv :]
    me = ints[0]
    width = tokens.shape[1]

    for b in range(blocks):
        holder, slot = ints[1 + b], ints[1 + blocks + b]
        for ref, (role, _, rows) in zip(token_refs, token_places):

            @pl.when(holder == device_of(me, role, mirrors))
            def _(ref=ref, rows=rows, b=b, slot=slot):
                at = pl.multiple_of(slot * CLIP, CLIP)
                pltpu.make_async_copy(ref.at[pl.ds(at, CLIP)], partner.at[b], sems.at[b]).start()

    jobs = []
    for ref, (e, start, rows) in zip(qkv_refs, qkv_places):
        take = min(rows, qkv_rows - start)
        at = pl.multiple_of(device_of(me, e, mirrors) * qkv_rows + start, 16)
        jobs.append((ref.at[pl.ds(0, take)], weight.at[pl.ds(at, take)]))
        if start + rows > qkv_rows:
            jobs.append((ref.at[pl.ds(take, rows - take)], gain_parts.at[e]))
    made = copies(jobs, sems, blocks)
    for b in range(blocks):
        pltpu.make_async_copy(tokens.at[pl.ds(0, CLIP)], partner.at[b], sems.at[b]).wait()
    for b in range(blocks):
        rows = slice(b * CLIP, (b + 1) * CLIP)
        share = mix[b]
        blended_ref[rows, :] = share * tokens[rows, :].astype(f32) + (1.0 - share) * partner[b].astype(f32)
    for job in made:
        job.wait()
    gains = gain_parts[0].astype(f32)
    for e in range(1, dp_count):
        gains = gains + gain_parts[e].astype(f32)
    gains_ref[...] = gains[:8]
    xhat, _ = centred(blended_ref[...])
    normed = (xhat * gains[0:1]).astype(bf16)
    for at, step in tiles(3 * width):
        tile = nt(normed, weight[at : at + step, :])
        if at + step <= width:
            tile = tile * 0.125
        qkv_ref[:, at : at + step] = tile.astype(bf16)

    @pl.loop(0, blocks)
    def _(i):
        window = pl.multiple_of(ints[1 + 2 * blocks + i] * CLIP, CLIP)
        bias = bias_of(seg_row[:, pl.ds(window, WINDOW)], ints[1 + 3 * blocks + i])
        rows = pl.ds(pl.multiple_of(i * CLIP, CLIP), CLIP)
        keys = pl.ds(window, WINDOW)
        for at in range(0, width, PAIR):
            queries = two_heads(qkv_ref[rows, at : at + PAIR])
            probs = softmax_rows(nt(queries, qkv_ref[keys, width + at : width + at + PAIR]) + bias).astype(bf16)
            out = nn(probs, qkv_ref[keys, 2 * width + at : 2 * width + at + PAIR])
            attended_ref[rows, at : at + PAIR] = side_by_side(out).astype(bf16)


def load_cross(me, refs, places, layout, weights, sems, mirrors):
    jobs = []
    for ref, (e, start, rows) in zip(refs, places):
        for (first, size), weight in zip(layout, weights):
            if weight is not None and first >= start and first + size <= start + rows:
                at = pl.multiple_of(device_of(me, e, mirrors) * size, 16)
                jobs.append((ref.at[pl.ds(first - start, size)], weight.at[pl.ds(at, size)]))
    return copies(jobs, sems, 0)


def second_kernel(geometry, ints, coarse_seg, coarse, blended, attended, gains, *refs):
    blocks, places, layout, mirrors = geometry
    weight_refs = refs[: len(places)]
    residual_ref, cq_ref, ckv_ref, crossed_ref, joined_ref, second_ref = refs[len(places) : len(places) + 6]
    w_ckv, w_out, w_cq, w_cout, sems = refs[len(places) + 6 :]
    made = load_cross(ints[0], weight_refs, places, layout, (w_ckv, w_out, w_cq, w_cout), sems, mirrors)
    for job in made:
        job.wait()
    width = blended.shape[1]
    for at, step in tiles(2 * width):
        ckv_ref[:, at : at + step] = nt(coarse[...], w_ckv[at : at + step, :]).astype(bf16)
    for at, step in tiles(width):
        residual_ref[:, at : at + step] = blended[:, at : at + step] + nn(attended[...], w_out[:, at : at + step])
    xhat, _ = centred(residual_ref[...])
    crossed_in = (xhat * gains[1:2]).astype(bf16)
    for at, step in tiles(width):
        cq_ref[:, at : at + step] = (nn(crossed_in, w_cq[:, at : at + step]) * 0.125).astype(bf16)

    bias = block_bias(coarse_seg, ints, blocks)
    for at in range(0, width, PAIR):
        queries = two_heads(cq_ref[:, at : at + PAIR])
        probs = softmax_rows(biased(nt(queries, ckv_ref[:, at : at + PAIR]), bias)).astype(bf16)
        out = nn(probs, ckv_ref[:, width + at : width + at + PAIR])
        crossed_ref[:, at : at + PAIR] = side_by_side(out).astype(bf16)

    for at, step in tiles(width):
        joined_ref[:, at : at + step] = residual_ref[:, at : at + step] + nn(crossed_ref[...], w_cout[:, at : at + step])
    xhat, _ = centred(joined_ref[...])
    second_ref[...] = (xhat * gains[2:3]).astype(bf16)


def mlp_kernel(geometry, second, second_near, cotangent, cotangent_near, *refs):
    groups, places, rows, last = geometry
    weight_refs = refs[: len(places)]
    refs = refs[len(places) :]
    keep_ref, going_ref = refs[:2]
    if last:
        own_ref = refs[2]
        sums = refs[3:7]
        refs = refs[7:]
    else:
        sums = refs[2:6]
        refs = refs[6:]
    w_up, w_down, hidden, grad_pre, sems = refs
    step = pl.program_id(0)

    def jobs_of(group):
        jobs = []
        for ref, (e, which) in zip(weight_refs, places):
            if e == groups[group]:
                for part, weight in ((0, w_up), (1, w_down)):
                    if which is None or which == part:
                        first = part * rows if which is None else 0
                        jobs.append((ref.at[pl.ds(first, rows)], weight.at[group]))
        return jobs

    at = 0
    for group in range(len(groups)):
        jobs = jobs_of(group)
        made = [pltpu.make_async_copy(s, d, sems.at[at + i]) for i, (s, d) in enumerate(jobs)]
        at += len(jobs)

        @pl.when(step == 0)
        def _(made=made):
            for job in made:
                job.start()

        @pl.when(step == group)
        def _(made=made):
            for job in made:
                job.wait()

    @pl.when(step == 0)
    def _():
        for ref in sums:
            ref[...] = jnp.zeros_like(ref)

    up, down = w_up.at[step], w_down.at[step]
    for half, (inputs, upstream) in enumerate(((second, cotangent), (second_near, cotangent_near))):
        pre = nt(inputs[...], up[...])
        grad_hidden = nt(upstream[...], down[...])
        cdf = 0.5 * (1.0 + lax.erf(pre * 0.7071067811865476))
        slope = cdf + pre * (jnp.exp(-0.5 * pre * pre) * 0.3989422804014327)
        hidden[half] = (pre * cdf).astype(bf16)
        grad_pre[half] = (grad_hidden * slope).astype(bf16)
        for first, size in tiles(second.shape[1]):
            columns = slice(first, first + size)
            sums[2 * half][:, columns] += nn(hidden[half], down[:, columns])
            sums[2 * half + 1][:, columns] += nn(grad_pre[half], up[:, columns])
    keep_ref[0, 0] = (tn(grad_pre[0], second[...]) + tn(grad_pre[1], second_near[...])).astype(bf16)
    keep_ref[0, 1] = (tn(hidden[0], cotangent[...]) + tn(hidden[1], cotangent_near[...])).astype(bf16)

    @pl.when(step == len(groups) - 1)
    def _():
        going_ref[0] = sums[2][...].astype(bf16)
        going_ref[1] = sums[3][...].astype(bf16)
        if last:
            own_ref[0] = sums[0][...].astype(bf16)
            own_ref[1] = sums[1][...].astype(bf16)


def grads_out(me, dp_count, layout, sources, keep_ref, send_ref, sems, at, mirrors):
    jobs = []
    for e in range(dp_count):
        target = send_ref if e & CORE else keep_ref
        for (first, size), source in zip(layout, sources):
            if source is None:
                continue
            row = pl.multiple_of(device_of(me, e, mirrors) * size, 16)
            jobs.append((source.at[pl.ds(row, size)], target.at[e // 2, pl.ds(first, size)]))
    return copies(jobs, sems, at)


def third_kernel(
    geometry, ints, coarse_seg, gains, mlp_out, grad_second, own_b, came_a, came_b, joined, cotangent, crossed, cq, ckv, *refs
):
    blocks, places, layout, dp_count, mirrors = geometry
    weight_refs = refs[: len(places)]
    refs = refs[len(places) :]
    output_ref, grad_joined_ref, grad_cq_ref, grad_ckv_ref, gain_grads_ref, keep_ref, send_ref = refs[:7]
    w_cout, g_cout, grad_cross, sems = refs[7:]
    me = ints[0]
    width = joined.shape[1]
    made = load_cross(me, weight_refs, places, layout, (None, None, None, w_cout), sems, mirrors)
    rest = [own_b[i].astype(f32) + came_a[i].astype(f32) + came_b[i].astype(f32) for i in range(2)]
    output_ref[...] = (joined[...] + (mlp_out[...] + rest[0])).astype(bf16)
    xhat, r = centred(joined[...])
    grad_in, gain_two = norm_back(xhat, r, gains[2:3], grad_second[...] + rest[1])
    grad_joined_ref[...] = cotangent[...].astype(f32) + grad_in
    low = grad_joined_ref[...].astype(bf16)
    for job in made:
        job.wait()
    for at, step in tiles(width):
        grad_cross[:, at : at + step] = nt(low, w_cout[at : at + step, :]).astype(bf16)
    for at, step in tiles(width):
        g_cout[at : at + step, :] = tn(crossed[:, at : at + step], low).astype(bf16)
    going = grads_out(me, dp_count, layout, (None, None, None, g_cout), keep_ref, send_ref, sems, len(made), mirrors)
    bias = block_bias(coarse_seg, ints, blocks)
    for at in range(0, width, PAIR):
        lanes = slice(at, at + PAIR)
        queries = two_heads(cq[:, lanes])
        grads = two_heads(grad_cross[:, lanes])
        keys = ckv[:, lanes]
        values = ckv[:, width + at : width + at + PAIR]
        probs = softmax_rows(biased(nt(queries, keys), bias))
        grad_ckv_ref[:, width + at : width + at + PAIR] = tn(probs.astype(bf16), grads).astype(bf16)
        grad_probs = nt(grads, values)
        inner = jnp.sum(probs * grad_probs, axis=-1, keepdims=True)
        scores = (probs * (grad_probs - inner)).astype(bf16)
        part = side_by_side(nn(scores, keys)).astype(bf16)
        grad_cq_ref[:, lanes] = part * jnp.asarray(0.125, bf16)
        grad_ckv_ref[:, lanes] = tn(scores, queries).astype(bf16)

    gain_grads_ref[...] = jnp.concatenate([gain_two] * 8, axis=0)
    for job in going:
        job.wait()


def third_part(geometry, ints, coarse, gains, gain_two, grad_joined, residual, attended, grad_cq, grad_ckv, keep_in, send_in, *refs):
    places, layout, dp_count, mirrors = geometry
    weight_refs = refs[: len(places)]
    refs = refs[len(places) :]
    coarse_ref, grad_res_ref, grad_att_ref, gain_grads_ref, keep_ref, send_ref = refs[:6]
    w_ckv, w_out, w_cq, g_ckv, g_out, g_cq, crossed_in, sems = refs[6:]
    me = ints[0]
    width = residual.shape[1]
    made = load_cross(me, weight_refs, places, layout, (w_ckv, w_out, w_cq, None), sems, mirrors)
    xhat, r = centred(residual[...])
    crossed_in[...] = (xhat * gains[1:2]).astype(bf16)
    for at, step in tiles(width):
        g_cq[at : at + step, :] = tn(crossed_in[:, at : at + step], grad_cq[...]).astype(bf16)
    for at, step in tiles(2 * width):
        g_ckv[at : at + step, :] = tn(grad_ckv[:, at : at + step], coarse[...]).astype(bf16)
    for job in made:
        job.wait()
    going = grads_out(me, dp_count, layout, (g_ckv, None, g_cq, None), keep_ref, send_ref, sems, 0, mirrors)
    for at, step in tiles(width):
        coarse_ref[:, at : at + step] = nn(grad_ckv[:, 0:width], w_ckv[0:width, at : at + step]) + nn(
            grad_ckv[:, width : 2 * width], w_ckv[width : 2 * width, at : at + step]
        )
    pieces = [nt(grad_cq[...], w_cq[at : at + step, :]) for at, step in tiles(width)]
    grad_in, gain_cross = norm_back(xhat, r, gains[1:2], jnp.concatenate(pieces, axis=1))
    grad_res = grad_joined[...] + grad_in
    grad_res_ref[...] = grad_res
    low = grad_res.astype(bf16)
    for at, step in tiles(width):
        g_out[at : at + step, :] = tn(attended[:, at : at + step], low).astype(bf16)
    going += grads_out(me, dp_count, layout, (None, g_out, None, None), keep_ref, send_ref, sems, len(going), mirrors)
    for at, step in tiles(width):
        grad_att_ref[:, at : at + step] = nt(low, w_out[at : at + step, :]).astype(bf16)
    zero = jnp.zeros_like(gain_cross)
    gain_grads_ref[...] = jnp.concatenate([zero, gain_cross, gain_two[0:1]] + [zero] * 5, axis=0)
    for job in going:
        job.wait()


def fourth_kernel(geometry, ints, seg_row, grad_att, qkv, *refs):
    blocks, first, last = geometry
    grad_proj, query_part, key_part, value_part, key_sum, value_sum, sems = refs[-7:]
    width = grad_att.shape[1]
    low, high = first * PAIR, last * PAIR
    key_sum[...] = jnp.zeros_like(key_sum)
    value_sum[...] = jnp.zeros_like(value_sum)

    @pl.loop(0, blocks)
    def _(i):
        window = pl.multiple_of(ints[1 + 2 * blocks + i] * CLIP, CLIP)
        bias = bias_of(seg_row[:, pl.ds(window, WINDOW)], ints[1 + 3 * blocks + i])
        rows = pl.ds(pl.multiple_of(i * CLIP, CLIP), CLIP)
        near = pl.ds(window, WINDOW)
        for at in range(low, high, PAIR):
            lanes = slice(at - low, at - low + PAIR)
            queries = two_heads(qkv[rows, at : at + PAIR])
            grads = two_heads(grad_att[rows, at : at + PAIR])
            keys = qkv[near, width + at : width + at + PAIR]
            values = qkv[near, 2 * width + at : 2 * width + at + PAIR]
            probs = softmax_rows(nt(queries, keys) + bias)
            value_sum[near, lanes] += tn(probs.astype(bf16), grads)
            grad_probs = nt(grads, values)
            inner = jnp.sum(probs * grad_probs, axis=-1, keepdims=True)
            scores = (probs * (grad_probs - inner)).astype(bf16)
            part = side_by_side(nn(scores, keys)).astype(bf16)
            query_part[rows, lanes] = part * jnp.asarray(0.125, bf16)
            key_sum[near, lanes] += tn(scores, queries)

    key_part[...] = key_sum[...].astype(bf16)
    value_part[...] = value_sum[...].astype(bf16)
    jobs = [
        (part, grad_proj.at[:, pl.ds(i * width + low, high - low)])
        for i, part in enumerate((query_part, key_part, value_part))
    ]
    for job in copies(jobs, sems, 0):
        job.wait()


def fifth_kernel(geometry, ints, mix, gains, blended, grad_res, grad_proj, *refs):
    dp_count, blocks, qkv_places, qkv_rows, mirrors = geometry
    weight_refs = refs[: len(qkv_places)]
    refs = refs[len(qkv_places) :]
    base_ref, going_ref = refs[:2]
    weight, sems = refs[2:]
    me = ints[0]
    width = blended.shape[1]
    jobs = []
    for ref, (e, start, rows) in zip(weight_refs, qkv_places):
        take = min(rows, qkv_rows - start)
        at = pl.multiple_of(device_of(me, e, mirrors) * qkv_rows + start, 16)
        jobs.append((ref.at[pl.ds(0, take)], weight.at[pl.ds(at, take)]))
    made = copies(jobs, sems, 0)
    xhat, r = centred(blended[...])
    for job in made:
        job.wait()
    pieces = [nn(grad_proj[...], weight[:, at : at + step]) for at, step in tiles(width)]
    grad_in, _ = norm_back(xhat, r, gains[0:1], jnp.concatenate(pieces, axis=1))
    grad_blend = grad_res[...] + grad_in
    for b in range(blocks):
        rows = slice(b * CLIP, (b + 1) * CLIP)
        share = mix[b]
        part = grad_blend[rows, :]
        base_ref[rows, :] = share * part
        going_ref[rows, :] = ((1.0 - share) * part).astype(bf16)


def place_kernel(geometry, ints, ints_near, blocks_own, blocks_near, out_ref):
    blocks, mirrors = geometry
    me = ints[0]
    out_ref[...] = jnp.zeros_like(out_ref)
    for table, first, source in ((ints, 1, blocks_own), (ints_near, 0, blocks_near)):
        for b in range(blocks):
            holder, slot = table[first + b], table[first + blocks + b]
            group = jnp.int32(0)
            for role in mirrors:
                group = group + jnp.where(device_of(me, role, mirrors) == holder, role // 2, 0)

            @pl.when(lax.rem(holder, 2) == lax.rem(me, 2))
            def _(group=group, slot=slot, source=source, b=b):
                rows = pl.ds(pl.multiple_of(slot * CLIP, CLIP), CLIP)
                part = source[b * CLIP : (b + 1) * CLIP, :].astype(f32)
                out_ref[group, rows, :] = (out_ref[group, rows, :].astype(f32) + part).astype(bf16)


def sixth_kernel(geometry, ints, gains, gain_grads, blended, grad_proj, *refs):
    dp_count, qkv_places, qkv_rows, mirrors = geometry
    weight_refs = refs[: len(qkv_places)]
    keep_ref, send_ref, weight, grad_w, gain_rows, sems = refs[len(qkv_places) :]
    me = ints[0]
    width = blended.shape[1]
    jobs = []
    for ref, (e, start, rows) in zip(weight_refs, qkv_places):
        take = min(rows, qkv_rows - start)
        at = pl.multiple_of(device_of(me, e, mirrors) * qkv_rows + start, 16)
        jobs.append((ref.at[pl.ds(0, take)], weight.at[pl.ds(at, take)]))
    made = copies(jobs, sems, 0)
    xhat, _ = centred(blended[...])
    normed = (xhat * gains[0:1]).astype(bf16)
    for job in made:
        job.wait()
    gain_one = jnp.zeros((1, width), f32)
    for at, step in tiles(3 * width):
        part = tn(grad_proj[:, at : at + step], normed)
        gain_one = gain_one + jnp.sum(part * weight[at : at + step, :].astype(f32), axis=0, keepdims=True)
        grad_w[at : at + step, :] = part.astype(bf16)
    sent = grads_out(me, dp_count, ((0, qkv_rows),), (grad_w,), keep_ref, send_ref, sems, len(jobs), mirrors)
    all_gains = jnp.concatenate([gain_one / gains[0:1], gain_grads[1:8], jnp.zeros((8, width), f32)], axis=0)
    gain_rows[...] = all_gains.astype(bf16)
    last = []
    for e in range(dp_count):
        target = send_ref if e & CORE else keep_ref
        last.append((gain_rows, target.at[e // 2, pl.ds(qkv_rows, 16)]))
    for job in sent + copies(last, sems, len(jobs) + dp_count):
        job.wait()


def shards(
    tokens,
    coarse_view,
    segment_ids,
    partner_device,
    partner_slot,
    mix_weight,
    ln1_gain,
    w_qkv,
    w_out,
    lnx_gain,
    w_cq,
    w_ckv,
    w_cout,
    ln2_gain,
    w_up,
    w_down,
    cotangent,
):
    row_count, width = tokens.shape
    coarse_rows = coarse_view.shape[0]
    blocks = mix_weight.shape[0]
    dp_count, fsdp_count = lax.axis_size("dp"), lax.axis_size("fsdp")
    dp_me, fsdp_me = lax.axis_index("dp"), lax.axis_index("fsdp")
    part = ln1_gain.shape[0]
    device_me = dp_me * fsdp_count + fsdp_me
    pairs = dp_count // 2
    mirrors = mirror_table()

    target = partner_device[:, 0]
    segments = segment_ids[0]
    videos = segments.reshape(blocks, row_count // blocks)[:, 0]
    following = jnp.concatenate([videos[1:] == videos[:-1], jnp.zeros((1,), bool)])
    before = jnp.concatenate([jnp.zeros((1,), bool), videos[1:] == videos[:-1]])
    index = jnp.arange(blocks, dtype=jnp.int32)
    window = jnp.where(following, index, jnp.where(before, index - 1, jnp.minimum(index, blocks - 2)))
    ints = jnp.concatenate(
        [dp_me[None].astype(jnp.int32), target, partner_slot, window, videos]
    )
    ints_near = swap(ints[1 : 1 + 2 * blocks], CORE)
    seg_row = segments[None, :]
    coarse_seg = segments.reshape(coarse_rows, row_count // coarse_rows)[:, 0][None, :]

    gain_rows = lax.dynamic_update_slice(
        jnp.zeros((8, width), bf16), jnp.stack([ln1_gain, lnx_gain, ln2_gain]), (0, device_me * part)
    )
    shard_one = jnp.concatenate([w_qkv.T, gain_rows])
    shard_first = jnp.concatenate([shard_one, w_ckv.T])
    shard_rest = jnp.concatenate([w_out, w_cq, w_cout])
    shard_mlp = jnp.concatenate([w_up.T, w_down])
    sizes_two = (w_ckv.shape[1], w_out.shape[0], w_cq.shape[0], w_cout.shape[0])
    qkv_part, up_part = w_qkv.shape[1], w_up.shape[1]
    qkv_rows, up_rows = qkv_part * fsdp_count, up_part * fsdp_count
    layout = []
    at = 0
    for size in sizes_two:
        layout.append((at * fsdp_count, size * fsdp_count))
        at += size
    layout = tuple(layout)
    rows_two = at * fsdp_count

    held_tok = {0: tokens, **single_steps(tokens)}
    came_first = inner_start(shard_first)
    held_tok, came_first, shard_rest = fence((held_tok, came_first, shard_rest))

    firsts = inner_order(came_first)
    ones = firsts[:, : qkv_part + 8]
    gain_block = jnp.sum(ones[:, qkv_part:].astype(f32), axis=0).astype(bf16)
    block_one = jnp.concatenate(
        [ones[:, :qkv_part].reshape(qkv_rows, width), gain_block, jnp.zeros((8, width), bf16)]
    )
    held_one = {0: block_one, **single_steps(block_one)}
    came_rest = inner_start(shard_rest)
    held_tok, held_one, came_rest, shard_mlp, firsts = fence((held_tok, held_one, came_rest, shard_mlp, firsts))

    near_mlp = inner_swap(shard_mlp, 1)
    core_tok = core_steps(dict(held_tok))
    near_tok = set(held_tok)
    relay_steps(held_tok)
    rests = inner_order(came_rest)
    split = [firsts[:, qkv_part + 8 :].reshape(sizes_two[0] * fsdp_count, width)]
    at = 0
    for size in sizes_two[1:]:
        split.append(rests[:, at : at + size].reshape(size * fsdp_count, width))
        at += size
    block_two = jnp.concatenate(split)
    held_one, core_tok, held_tok, block_two, near_mlp = fence((held_one, core_tok, held_tok, block_two, near_mlp))

    cuts = (0, up_part // 3, 3 * up_part // 2, 2 * up_part)
    mlp_cut = [
        inner_join(shard_mlp[None, first:last], near_mlp[None, first:last], 1) for first, last in zip(cuts, cuts[1:])
    ]
    mlp_came = [inner_swap(mlp_cut[0], 2)]
    core_one = core_steps(dict(held_one))
    relay_steps(held_one)
    late_tok = core_steps({e: b for e, b in held_tok.items() if e not in near_tok})
    held_one, core_one, late_tok, block_two, mlp_cut, mlp_came = fence(
        (held_one, core_one, late_tok, block_two, mlp_cut, mlp_came)
    )

    held_two = {0: block_two, **single_steps(block_two)}
    cotangent_near = swap(cotangent, CORE)
    mlp_came.append(inner_swap(mlp_cut[1], 2))
    mlp_joined = [inner_rest(inner_join(mlp_cut[0], mlp_came[0], 2))]
    late_one = core_steps({e: b for e, b in held_one.items() if e not in near_tok})
    pieces_tok = {**core_tok, **late_tok}
    pieces_one = {**core_one, **late_one}
    arrays_tok, places_tok = parts_of(pieces_tok, row_count)
    arrays_one, places_one = parts_of(pieces_one, qkv_rows + 16)
    blended, qkv, attended, gains = pl.pallas_call(
        functools.partial(first_kernel, (dp_count, blocks, places_tok, places_one, qkv_rows, mirrors)),
        out_shape=(
            whole((row_count, width), f32),
            whole((row_count, 3 * width), bf16),
            whole((row_count, width), bf16),
            whole((8, width), f32),
        ),
        in_specs=[SMEM, SMEM, VMEM, VMEM] + [ANY] * (len(arrays_tok) + len(arrays_one)),
        out_specs=(VMEM,) * 4,
        scratch_shapes=[
            pltpu.VMEM((blocks, CLIP, width), bf16),
            pltpu.VMEM((3 * width, width), bf16),
            pltpu.VMEM((dp_count, 16, width), bf16),
            pltpu.SemaphoreType.DMA((blocks + len(arrays_one) + dp_count,)),
        ],
        compiler_params=params(),
        cost_estimate=cost(1e9, 1e6),
        name="mix_self_attention",
    )(ints, mix_weight, seg_row, tokens, *arrays_tok, *arrays_one)
    held_two, attended, mlp_came, cotangent_near, mlp_cut, mlp_joined = fence(
        (held_two, attended, mlp_came, cotangent_near, mlp_cut, mlp_joined)
    )

    core_two = core_steps(dict(held_two))
    relay_steps(held_two)
    mlp_came.append(inner_swap(mlp_cut[2], 2))
    mlp_joined.append(inner_rest(inner_join(mlp_cut[1], mlp_came[1], 2)))
    held_two, core_two, mlp_came, mlp_joined = fence((held_two, core_two, mlp_came, mlp_joined))

    mlp_joined.append(inner_rest(inner_join(mlp_cut[2], mlp_came[2], 2)))
    mlp = jnp.concatenate(mlp_joined, axis=1)
    block_mlp = jnp.concatenate([mlp[:, :up_part].reshape(up_rows, width), mlp[:, up_part:].reshape(up_rows, width)])
    held_mlp = {0: block_mlp, **single_steps(block_mlp)}
    late_two = core_steps({e: b for e, b in held_two.items() if e not in near_tok})
    pieces_two = {**core_two, **late_two}
    wide = [pltpu.VMEM((sizes * fsdp_count * dp_count, width), bf16) for sizes in sizes_two]
    n_two = 4 * dp_count
    arrays_two, places_two = parts_of(pieces_two, rows_two)
    wide = [pltpu.VMEM((sizes * fsdp_count * dp_count, width), bf16) for sizes in sizes_two]
    n_two = 4 * dp_count
    residual, cq, ckv, crossed, joined, second = pl.pallas_call(
        functools.partial(second_kernel, (blocks, places_two, layout, mirrors)),
        out_shape=(
            whole((row_count, width), f32),
            whole((row_count, width), bf16),
            whole((coarse_rows, 2 * width), bf16),
            whole((row_count, width), bf16),
            whole((row_count, width), f32),
            whole((row_count, width), bf16),
        ),
        in_specs=[SMEM] + [VMEM] * 5 + [ANY] * len(arrays_two),
        out_specs=(VMEM,) * 6,
        scratch_shapes=wide + [pltpu.SemaphoreType.DMA((n_two,))],
        compiler_params=params(),
        cost_estimate=cost(1e9, 1e6),
        name="cross_attention",
    )(ints, coarse_seg, coarse_view, blended, attended, gains, *arrays_two)
    second_near = swap(second, CORE)
    held_mlp, second, second_near, ints_near = fence((held_mlp, second, second_near, ints_near))

    early = dict(held_mlp)
    relay_steps(held_mlp)

    def mlp_call(pieces, last):
        groups = tuple(sorted(pieces))
        count = len(groups)
        fixed = pl.BlockSpec((row_count, width), lambda g: (0, 0))
        moving = pl.BlockSpec((1, 2, up_rows, width), lambda g: (g, 0, 0, 0))
        both = pl.BlockSpec((2, row_count, width), lambda g: (0, 0, 0))
        table = whole((row_count, width), f32)
        out_shape = [whole((count, 2, up_rows, width), bf16), whole((2, row_count, width), bf16)]
        out_specs = [moving, both]
        scratch = [pltpu.VMEM((row_count, width), f32)] * (4 if last else 2)
        if last:
            out_shape.append(whole((2, row_count, width), bf16))
            out_specs.append(both)
        else:
            out_shape += [table, table]
            out_specs += [fixed, fixed]
        made = pl.pallas_call(
            functools.partial(mlp_kernel, (groups, tuple((e, None) for e in groups), up_rows, last)),
            grid=(count,),
            out_shape=tuple(out_shape),
            in_specs=[fixed] * 4 + [ANY] * count,
            out_specs=tuple(out_specs),
            scratch_shapes=scratch
            + [
                pltpu.VMEM((count, up_rows, width), bf16),
                pltpu.VMEM((count, up_rows, width), bf16),
                pltpu.VMEM((2, row_count, up_rows), bf16),
                pltpu.VMEM((2, row_count, up_rows), bf16),
                pltpu.SemaphoreType.DMA((2 * count,)),
            ],
            compiler_params=params(32),
            cost_estimate=cost(1e9, 1e6),
            name="feed_forward",
        )(second, second_near, cotangent, cotangent_near, *[pieces[e] for e in groups])
        return groups, made[0].reshape(count, 2 * up_rows, width), made[1], made[2:]

    groups_a, keep_a, going_a, (mlp_out, grad_second) = mlp_call(early, False)
    late = {e: b for e, b in held_mlp.items() if e not in near_tok}
    late, keep_a, going_a, mlp_out, grad_second = fence((late, keep_a, going_a, mlp_out, grad_second))
    came_a = swap(going_a, CORE)
    groups_b, keep_b, going_b, (own_b,) = mlp_call(late, True)
    came_a, keep_b, going_b, own_b = fence((came_a, keep_b, going_b, own_b))
    came_b = swap(going_b, CORE)
    totals = [None] * pairs
    for groups, keep in ((groups_a, keep_a), (groups_b, keep_b)):
        for i, e in enumerate(groups):
            totals[e // 2] = keep[i]
    totals, came_b = fence((totals, came_b))

    sum_mlp = OuterSum(totals)
    sum_mlp.relays()
    output, grad_joined, grad_cq, grad_ckv, gain_two, keep_two, send_two = pl.pallas_call(
        functools.partial(third_kernel, (blocks, places_two, layout, dp_count, mirrors)),
        out_shape=(
            whole((row_count, width), bf16),
            whole((row_count, width), f32),
            whole((row_count, width), bf16),
            whole((coarse_rows, 2 * width), bf16),
            whole((8, width), f32),
            whole((pairs, rows_two, width), bf16),
            whole((pairs, rows_two, width), bf16),
        ),
        in_specs=[SMEM] + [VMEM] * 12 + [ANY] * len(arrays_two),
        out_specs=(VMEM,) * 5 + (ANY,) * 2,
        scratch_shapes=[
            wide[3],
            wide[3],
            pltpu.VMEM((row_count, width), bf16),
            pltpu.SemaphoreType.DMA((n_two + dp_count,)),
        ],
        compiler_params=params(32),
        cost_estimate=cost(1e9, 1e6),
        name="cross_attention_backward",
    )(ints, coarse_seg, gains, mlp_out, grad_second, own_b, came_a, came_b, joined, cotangent, crossed, cq, ckv, *arrays_two)
    state, grad_joined = fence((sum_mlp.state(), grad_joined))
    sum_mlp.put(state)

    sum_mlp.singles(slice(0, up_rows))
    coarse_grad, grad_res, grad_att, gain_grads, keep_two, send_two = pl.pallas_call(
        functools.partial(third_part, (places_two, layout, dp_count, mirrors)),
        out_shape=(
            whole((coarse_rows, width), f32),
            whole((row_count, width), f32),
            whole((row_count, width), bf16),
            whole((8, width), f32),
            whole((pairs, rows_two, width), bf16),
            whole((pairs, rows_two, width), bf16),
        ),
        in_specs=[SMEM] + [VMEM] * 8 + [ANY] * (2 + len(arrays_two)),
        out_specs=(VMEM,) * 4 + (ANY,) * 2,
        scratch_shapes=[
            wide[0],
            wide[1],
            wide[2],
            wide[0],
            wide[1],
            wide[2],
            pltpu.VMEM((row_count, width), bf16),
            pltpu.SemaphoreType.DMA((n_two,)),
        ],
        input_output_aliases={9: 4, 10: 5},
        compiler_params=params(),
        cost_estimate=cost(1e9, 1e6),
        name="cross_attention_weights",
    )(
        ints, coarse_view, gains, gain_two, grad_joined, residual, attended, grad_cq, grad_ckv, keep_two, send_two, *arrays_two
    )

    state, grad_att, keep_two, send_two = fence((sum_mlp.state(), grad_att, keep_two, send_two))
    sum_mlp.put(state)

    sum_mlp.singles(slice(up_rows, 2 * up_rows))
    came_two = swap(send_two, CORE)
    def attention_back(first, last, held):
        columns = (last - first) * PAIR
        return pl.pallas_call(
            functools.partial(fourth_kernel, (blocks, first, last)),
            out_shape=whole((row_count, 3 * width), bf16),
            in_specs=[SMEM] + [VMEM] * 3 + [ANY] * len(held),
            out_specs=ANY,
            scratch_shapes=[pltpu.VMEM((row_count, columns), bf16)] * 3
            + [pltpu.VMEM((row_count, columns), f32)] * 2
            + [pltpu.SemaphoreType.DMA((3,))],
            input_output_aliases={4: 0} if held else {},
            compiler_params=params(32),
            cost_estimate=cost(1e9, 1e6),
            name="self_attention_backward",
        )(ints, seg_row, grad_att, qkv, *held)

    inner_mlp = [InnerSum(sum_mlp.result(0).reshape(fsdp_count, up_part, width))]
    inner_mlp[0].step()
    grad_proj = attention_back(0, HEADS // 2, ())
    state, came_two, grad_proj, inner_mlp[0].came = fence((sum_mlp.state(), came_two, grad_proj, inner_mlp[0].came))
    sum_mlp.put(state)

    sum_two = OuterSum(keep_two, came_two)
    sum_two.relays()
    inner_mlp.append(InnerSum(sum_mlp.result(1).reshape(fsdp_count, up_part, width)))
    inner_mlp[1].step()
    keep_one, send_one = pl.pallas_call(
        functools.partial(sixth_kernel, (dp_count, places_one, qkv_rows, mirrors)),
        out_shape=(
            whole((pairs, qkv_rows + 16, width), bf16),
            whole((pairs, qkv_rows + 16, width), bf16),
        ),
        in_specs=[SMEM] + [VMEM] * 4 + [ANY] * len(arrays_one),
        out_specs=(ANY,) * 2,
        scratch_shapes=[
            pltpu.VMEM((3 * width, width), bf16),
            pltpu.VMEM((3 * width, width), bf16),
            pltpu.VMEM((16, width), bf16),
            pltpu.SemaphoreType.DMA((len(arrays_one) + 2 * dp_count,)),
        ],
        compiler_params=params(),
        cost_estimate=cost(1e9, 1e6),
        name="self_attention_weights",
    )(ints, gains, gain_grads, blended, grad_proj, *arrays_one)
    state, keep_one, send_one, inner_mlp[1].came = fence((sum_two.state(), keep_one, send_one, inner_mlp[1].came))
    sum_two.put(state)

    sum_two.singles()
    came_one = swap(send_one, CORE)
    base, going_tok = pl.pallas_call(
        functools.partial(fifth_kernel, (dp_count, blocks, places_one, qkv_rows, mirrors)),
        out_shape=(
            whole((row_count, width), f32),
            whole((row_count, width), bf16),
        ),
        in_specs=[SMEM, SMEM] + [VMEM] * 4 + [ANY] * len(arrays_one),
        out_specs=(VMEM,) * 2,
        scratch_shapes=[
            pltpu.VMEM((3 * width, width), bf16),
            pltpu.SemaphoreType.DMA((len(arrays_one),)),
        ],
        compiler_params=params(),
        cost_estimate=cost(1e9, 1e6),
        name="self_attention_input",
    )(ints, mix_weight, gains, blended, grad_res, grad_proj, *arrays_one)
    state, came_one, going_tok = fence((sum_two.state(), came_one, going_tok))
    sum_two.put(state)

    sum_one = OuterSum(keep_one, came_one)
    sum_one.relays()
    came_tok = swap(going_tok, CORE)
    placed = pl.pallas_call(
        functools.partial(place_kernel, (blocks, mirrors)),
        out_shape=whole((pairs, row_count, width), bf16),
        in_specs=[SMEM, SMEM] + [VMEM] * 2,
        out_specs=VMEM,
        compiler_params=params(32),
        cost_estimate=cost(1e9, 1e6),
        name="place_partner_gradients",
    )(ints, ints_near, going_tok, came_tok)
    mlp_parts = jnp.concatenate([inner_parts(inner) for inner in inner_mlp], axis=1)
    inner_mlp = InnerSum(mlp_parts)
    inner_mlp.finish()
    state, placed, mlp_came = fence((sum_one.state(), placed, inner_mlp.came))
    sum_one.put(state)
    inner_mlp.came = mlp_came

    sum_one.singles()
    sum_tok = OuterSum(placed)
    sum_tok.relays()
    two_sum = sum_two.result()
    two_parts = jnp.concatenate(
        [two_sum[first : first + size].reshape(fsdp_count, size // fsdp_count, width) for first, size in layout], axis=1
    )
    inner_two = InnerSum(two_parts)
    inner_two.step()
    state, state_tok, two_came = fence((sum_one.state(), sum_tok.state(), inner_two.came))
    sum_one.put(state)
    sum_tok.put(state_tok)
    inner_two.came = two_came

    sum_tok.singles()
    one_sum = sum_one.result()
    gain_sum = jnp.broadcast_to(one_sum[qkv_rows : qkv_rows + 8][None], (fsdp_count, 8, width))
    one_parts = jnp.concatenate([one_sum[:qkv_rows].reshape(fsdp_count, qkv_part, width), gain_sum], axis=1)
    inner_one = InnerSum(one_parts)
    inner_one.step()
    one_mine = inner_one.result()
    mlp_mine = inner_mlp.result()
    up_shard, down_shard = mlp_mine[:up_part].T, mlp_mine[up_part:]
    two_mine = inner_two.result()
    found = []
    at = 0
    for size in sizes_two:
        found.append(two_mine[at : at + size])
        at += size
    ckv_shard, out_shard, cq_shard, cout_shard = found[0].T, found[1], found[2], found[3]
    qkv_shard = one_mine[:qkv_part].T
    gain_mine = lax.dynamic_slice(one_mine[qkv_part:], (0, device_me * part), (3, part))
    token_grad = base + sum_tok.result()
    return (
        output,
        token_grad,
        coarse_grad,
        gain_mine[0],
        qkv_shard,
        out_shard,
        gain_mine[1],
        cq_shard,
        ckv_shard,
        cout_shard,
        gain_mine[2],
        up_shard,
        down_shard,
    )


def solution(mesh):
    rows = P(("dp", "fsdp"), None)
    columns = P(None, ("dp", "fsdp"))
    line = P(("dp", "fsdp"))
    in_specs = (
        rows, rows, rows, rows, line, line, line, columns, rows,
        line, rows, columns, rows, line, columns, rows, rows,
    )
    out_specs = (
        rows, rows, rows, line, columns, rows, line, rows, columns, rows, line, columns, rows,
    )
    return jax.shard_map(shards, mesh=mesh, in_specs=in_specs, out_specs=out_specs, check_vma=False)
```

```python
import functools

import jax
import jax.numpy as jnp
from jax import lax
from jax.experimental import pallas as pl
from jax.experimental.pallas import tpu as pltpu
from jax.sharding import PartitionSpec as P

HEADS = 12
HEAD = 64
PAIR = 2 * HEAD
CORE = 1
CLIP = 128
WINDOW = 256
TILE = 256
f32 = jnp.float32
bf16 = jnp.bfloat16
fence = lax.optimization_barrier


def swap(values, mask):
    count = lax.axis_size("dp")
    return lax.ppermute(values, "dp", [(i, i ^ mask) for i in range(count)])


def shift(values, step):
    count = lax.axis_size("fsdp")
    return lax.ppermute(values, "fsdp", [(i, (i + step) % count) for i in range(count)])


def link_masks():
    masks = []
    mask = 2
    while mask < lax.axis_size("dp"):
        masks.append(mask)
        mask *= 2
    return masks


def inner_swap(values, mask):
    count = lax.axis_size("fsdp")
    return lax.ppermute(values, "fsdp", [(i, i ^ mask) for i in range(count)])


def inner_double(held, mask):
    return inner_join(held, inner_swap(held, mask), mask)


def inner_join(held, came, mask):
    high = (lax.axis_index("fsdp") & mask) != 0
    return jnp.concatenate([jnp.where(high, came, held), jnp.where(high, held, came)])


def inner_rest(held):
    while held.shape[0] < lax.axis_size("fsdp"):
        held = inner_double(held, held.shape[0])
    return held


def inner_start(shard):
    return [shard] + [shift(shard, step) for step in range(1, lax.axis_size("fsdp"))]


def inner_order(came):
    count = len(came)
    me = lax.axis_index("fsdp")
    line = [came[count - 1 - k] for k in range(count)] + [came[count - k] for k in range(1, count)]
    return lax.dynamic_slice_in_dim(jnp.stack(line), count - 1 - me, count, 0)


def mirrored(role):
    masks = link_masks()
    return sum(masks[len(masks) - 1 - i] for i, mask in enumerate(masks) if role & mask)


def step_along(values, mask):
    count = lax.axis_size("dp")
    return lax.ppermute(values, "dp", [(i, i ^ (mirrored(mask) if i & CORE else mask)) for i in range(count)])


def top_bit(role):
    return 1 << (role.bit_length() - 1)


def relayed_roles():
    found = [role for role in range(2, lax.axis_size("dp"), 2) if role & (role - 1)]
    return sorted(found, key=lambda role: bin(role).count("1"))


def device_of(me, role, mirrors):
    holder = me ^ (role & CORE)
    link = role & ~CORE
    return holder ^ (link + lax.rem(holder, 2) * (mirrors[link] - link))


def mirror_table():
    return {role: mirrored(role) for role in range(0, lax.axis_size("dp"), 2)}


def single_steps(block):
    return {mask: step_along(block, mask) for mask in link_masks()}


def relay_steps(held):
    for role in relayed_roles():
        held[role] = step_along(held[role ^ top_bit(role)], top_bit(role))


def parts_of(pieces, total):
    return [pieces[e] for e in sorted(pieces)], tuple((e, 0, total) for e in sorted(pieces))


def core_steps(held):
    return {**held, **{e | CORE: swap(block, CORE) for e, block in held.items()}}


def inner_parts(inner):
    inner.add()
    return inner.parts


def add_low(a, b):
    return (a.astype(f32) + b.astype(f32)).astype(bf16)


class OuterSum:
    def __init__(self, *parts):
        self.parts = {2 * g: [part[g] for part in parts] for g in range(lax.axis_size("dp") // 2)}
        self.came = []
        self.ready = {}

    def prepare(self, role, rows=slice(None)):
        self.ready[role, rows.start] = self.value(role, rows).astype(bf16)

    def going(self, role, rows):
        return self.ready[role, rows.start] if (role, rows.start) in self.ready else self.value(role, rows).astype(bf16)

    def value(self, role, rows=slice(None)):
        total = self.parts[role][0][rows].astype(f32)
        for part in self.parts[role][1:]:
            total = total + part[rows].astype(f32)
        return total

    def relays(self):
        for role in relayed_roles()[::-1]:
            came = step_along(self.value(role).astype(bf16), top_bit(role))
            self.parts[role ^ top_bit(role)].append(came)

    def singles(self, rows=slice(None)):
        self.came.append((rows, [step_along(self.going(mask, rows), mask) for mask in link_masks()]))

    def result(self, index=None):
        chosen = self.came if index is None else [self.came[index]]
        sums = []
        for rows, blocks in chosen:
            total = self.value(0, rows)
            for block in blocks:
                total = total + block.astype(f32)
            sums.append(total)
        return sums[0] if len(sums) == 1 else jnp.concatenate(sums)

    def state(self):
        return (self.parts, [blocks for _, blocks in self.came], list(self.ready.values()))

    def put(self, state):
        self.parts = state[0]
        self.ready = dict(zip(self.ready, state[2]))
        self.came = [(rows, blocks) for (rows, _), blocks in zip(self.came, state[1])]


class InnerSum:
    def __init__(self, parts):
        self.parts = parts
        self.came = None
        self.mask = parts.shape[0]

    def step(self):
        self.add()
        self.mask //= 2
        bit = ((lax.axis_index("fsdp") & self.mask) != 0).astype(jnp.int32)
        halves = self.parts.reshape((2, self.mask) + self.parts.shape[1:])
        self.parts = lax.dynamic_index_in_dim(halves, bit, 0, keepdims=False)
        going = lax.dynamic_index_in_dim(halves, 1 - bit, 0, keepdims=False).astype(bf16)
        self.came = inner_swap(going, self.mask)

    def finish(self, steps=None):
        while self.mask > 1:
            self.step()

    def add(self):
        if self.came is not None:
            self.parts = self.parts + self.came.astype(f32)
            self.came = None

    def result(self):
        self.finish()
        self.add()
        return self.parts[0]


def nn(a, b):
    return jnp.dot(a, b, preferred_element_type=f32)


def nt(a, b):
    return lax.dot_general(a, b, (((1,), (1,)), ((), ())), preferred_element_type=f32)


def tn(a, b):
    return lax.dot_general(a, b, (((0,), (0,)), ((), ())), preferred_element_type=f32)


def tiles(size):
    step = TILE if size % TILE == 0 else size
    return [(at, step) for at in range(0, size, step)]


def centred(values):
    centre = jnp.mean(values, axis=-1, keepdims=True)
    shifted = values - centre
    spread = jnp.mean(shifted * shifted, axis=-1, keepdims=True)
    r = lax.rsqrt(spread + 1e-06)
    return shifted * r, r


def norm_back(xhat, r, gain, grad):
    c = grad * gain
    first = jnp.mean(c, axis=-1, keepdims=True)
    second = jnp.mean(c * xhat, axis=-1, keepdims=True)
    return r * (c - first - xhat * second), jnp.sum(grad * xhat, axis=0, keepdims=True)


def lower_half(rows):
    return lax.broadcasted_iota(jnp.int32, (rows, PAIR), 1) < HEAD


def two_heads(rows):
    keep = lower_half(rows.shape[0])
    zero = jnp.zeros_like(rows)
    return jnp.concatenate([jnp.where(keep, rows, zero), jnp.where(keep, zero, rows)], axis=0)


def side_by_side(stacked):
    rows = stacked.shape[0] // 2
    return jnp.where(lower_half(rows), stacked[:rows], stacked[rows:])


def softmax_rows(scores):
    raised = jnp.exp(scores - jnp.max(scores, axis=-1, keepdims=True))
    return raised / jnp.sum(raised, axis=-1, keepdims=True)


def bias_of(key_seg, own_seg):
    return jnp.where(key_seg == own_seg, 0.0, -1e30).astype(f32)


def block_bias(key_seg, ints, blocks):
    return jnp.stack([bias_of(key_seg[...], ints[1 + 3 * blocks + i]) for i in range(blocks)])


def biased(scores, bias):
    blocks, _, keys = bias.shape
    rows = scores.shape[0] // (2 * blocks)
    return (scores.reshape(2, blocks, rows, keys) + bias[None]).reshape(scores.shape)


def copies(jobs, sems, at):
    made = [pltpu.make_async_copy(src, dst, sems.at[at + i]) for i, (src, dst) in enumerate(jobs)]
    for job in made:
        job.start()
    return made


def whole(shape, dtype):
    return jax.ShapeDtypeStruct(shape, dtype)


VMEM = pl.BlockSpec(memory_space=pltpu.VMEM)
SMEM = pl.BlockSpec(memory_space=pltpu.SMEM)
ANY = pl.BlockSpec(memory_space=pl.ANY)


def params(mib=56):
    return pltpu.CompilerParams(vmem_limit_bytes=mib * 1024 * 1024)


def cost(flops, moved, exps=0):
    return pl.CostEstimate(flops=int(flops), bytes_accessed=int(moved), transcendentals=int(exps))


def first_kernel(
    geometry, ints, mix, seg_row, tokens, *refs
):
    dp_count, blocks, token_places, qkv_places, qkv_rows, mirrors = geometry
    n_tok, n_qkv = len(token_places), len(qkv_places)
    token_refs, qkv_refs = refs[:n_tok], refs[n_tok : n_tok + n_qkv]
    blended_ref, qkv_ref, attended_ref, gains_ref, partner, weight, gain_parts, sems = refs[n_tok + n_qkv :]
    me = ints[0]
    width = tokens.shape[1]

    for b in range(blocks):
        holder, slot = ints[1 + b], ints[1 + blocks + b]
        for ref, (role, _, rows) in zip(token_refs, token_places):

            @pl.when(holder == device_of(me, role, mirrors))
            def _(ref=ref, rows=rows, b=b, slot=slot):
                at = pl.multiple_of(slot * CLIP, CLIP)
                pltpu.make_async_copy(ref.at[pl.ds(at, CLIP)], partner.at[b], sems.at[b]).start()

    jobs = []
    for ref, (e, start, rows) in zip(qkv_refs, qkv_places):
        take = min(rows, qkv_rows - start)
        at = pl.multiple_of(device_of(me, e, mirrors) * qkv_rows + start, 16)
        jobs.append((ref.at[pl.ds(0, take)], weight.at[pl.ds(at, take)]))
        if start + rows > qkv_rows:
            jobs.append((ref.at[pl.ds(take, rows - take)], gain_parts.at[e]))
    made = copies(jobs, sems, blocks)
    for b in range(blocks):
        pltpu.make_async_copy(tokens.at[pl.ds(0, CLIP)], partner.at[b], sems.at[b]).wait()
    for b in range(blocks):
        rows = slice(b * CLIP, (b + 1) * CLIP)
        share = mix[b]
        blended_ref[rows, :] = share * tokens[rows, :].astype(f32) + (1.0 - share) * partner[b].astype(f32)
    for job in made:
        job.wait()
    gains = gain_parts[0].astype(f32)
    for e in range(1, dp_count):
        gains = gains + gain_parts[e].astype(f32)
    gains_ref[...] = gains[:8]
    xhat, _ = centred(blended_ref[...])
    normed = (xhat * gains[0:1]).astype(bf16)
    for at, step in tiles(3 * width):
        tile = nt(normed, weight[at : at + step, :])
        if at + step <= width:
            tile = tile * 0.125
        qkv_ref[:, at : at + step] = tile.astype(bf16)

    for i in range(blocks):
        window = pl.multiple_of(ints[1 + 2 * blocks + i] * CLIP, CLIP)
        bias = bias_of(seg_row[:, pl.ds(window, WINDOW)], ints[1 + 3 * blocks + i])
        rows = pl.ds(i * CLIP, CLIP)
        keys = pl.ds(window, WINDOW)
        for at in range(0, width, PAIR):
            queries = two_heads(qkv_ref[rows, at : at + PAIR])
            probs = softmax_rows(nt(queries, qkv_ref[keys, width + at : width + at + PAIR]) + bias).astype(bf16)
            out = nn(probs, qkv_ref[keys, 2 * width + at : 2 * width + at + PAIR])
            attended_ref[rows, at : at + PAIR] = side_by_side(out).astype(bf16)


def load_cross(me, refs, places, layout, weights, sems, mirrors):
    jobs = []
    for ref, (e, start, rows) in zip(refs, places):
        for (first, size), weight in zip(layout, weights):
            if weight is not None and first >= start and first + size <= start + rows:
                at = pl.multiple_of(device_of(me, e, mirrors) * size, 16)
                jobs.append((ref.at[pl.ds(first - start, size)], weight.at[pl.ds(at, size)]))
    return copies(jobs, sems, 0)


def second_kernel(geometry, ints, coarse_seg, coarse, blended, attended, gains, *refs):
    blocks, places, layout, mirrors = geometry
    weight_refs = refs[: len(places)]
    residual_ref, cq_ref, ckv_ref, crossed_ref, joined_ref, second_ref = refs[len(places) : len(places) + 6]
    w_ckv, w_out, w_cq, w_cout, sems = refs[len(places) + 6 :]
    made = load_cross(ints[0], weight_refs, places, layout, (w_ckv, w_out, w_cq, w_cout), sems, mirrors)
    for job in made:
        job.wait()
    width = blended.shape[1]
    for at, step in tiles(2 * width):
        ckv_ref[:, at : at + step] = nt(coarse[...], w_ckv[at : at + step, :]).astype(bf16)
    for at, step in tiles(width):
        residual_ref[:, at : at + step] = blended[:, at : at + step] + nn(attended[...], w_out[:, at : at + step])
    xhat, _ = centred(residual_ref[...])
    crossed_in = (xhat * gains[1:2]).astype(bf16)
    for at, step in tiles(width):
        cq_ref[:, at : at + step] = (nn(crossed_in, w_cq[:, at : at + step]) * 0.125).astype(bf16)

    bias = block_bias(coarse_seg, ints, blocks)
    for at in range(0, width, PAIR):
        queries = two_heads(cq_ref[:, at : at + PAIR])
        probs = softmax_rows(biased(nt(queries, ckv_ref[:, at : at + PAIR]), bias)).astype(bf16)
        out = nn(probs, ckv_ref[:, width + at : width + at + PAIR])
        crossed_ref[:, at : at + PAIR] = side_by_side(out).astype(bf16)

    for at, step in tiles(width):
        joined_ref[:, at : at + step] = residual_ref[:, at : at + step] + nn(crossed_ref[...], w_cout[:, at : at + step])
    xhat, _ = centred(joined_ref[...])
    second_ref[...] = (xhat * gains[2:3]).astype(bf16)


def mlp_kernel(geometry, second, second_near, cotangent, cotangent_near, *refs):
    groups, places, rows, last = geometry
    weight_refs = refs[: len(places)]
    refs = refs[len(places) :]
    keep_ref, going_ref = refs[:2]
    if last:
        own_ref = refs[2]
        sums = refs[3:7]
        refs = refs[7:]
    else:
        sums = refs[2:6]
        refs = refs[6:]
    w_up, w_down, hidden, grad_pre, sems = refs
    step = pl.program_id(0)

    def jobs_of(group):
        jobs = []
        for ref, (e, which) in zip(weight_refs, places):
            if e == groups[group]:
                for part, weight in ((0, w_up), (1, w_down)):
                    if which is None or which == part:
                        first = part * rows if which is None else 0
                        jobs.append((ref.at[pl.ds(first, rows)], weight.at[group]))
        return jobs

    at = 0
    for group in range(len(groups)):
        jobs = jobs_of(group)
        made = [pltpu.make_async_copy(s, d, sems.at[at + i]) for i, (s, d) in enumerate(jobs)]
        at += len(jobs)

        @pl.when(step == 0)
        def _(made=made):
            for job in made:
                job.start()

        @pl.when(step == group)
        def _(made=made):
            for job in made:
                job.wait()

    @pl.when(step == 0)
    def _():
        for ref in sums:
            ref[...] = jnp.zeros_like(ref)

    up, down = w_up.at[step], w_down.at[step]
    for half, (inputs, upstream) in enumerate(((second, cotangent), (second_near, cotangent_near))):
        pre = nt(inputs[...], up[...])
        grad_hidden = nt(upstream[...], down[...])
        cdf = 0.5 * (1.0 + lax.erf(pre * 0.7071067811865476))
        slope = cdf + pre * (jnp.exp(-0.5 * pre * pre) * 0.3989422804014327)
        hidden[half] = (pre * cdf).astype(bf16)
        grad_pre[half] = (grad_hidden * slope).astype(bf16)
        for first, size in tiles(second.shape[1]):
            columns = slice(first, first + size)
            sums[2 * half][:, columns] += nn(hidden[half], down[:, columns])
            sums[2 * half + 1][:, columns] += nn(grad_pre[half], up[:, columns])
    keep_ref[0, 0] = (tn(grad_pre[0], second[...]) + tn(grad_pre[1], second_near[...])).astype(bf16)
    keep_ref[0, 1] = (tn(hidden[0], cotangent[...]) + tn(hidden[1], cotangent_near[...])).astype(bf16)

    @pl.when(step == len(groups) - 1)
    def _():
        going_ref[0] = sums[2][...].astype(bf16)
        going_ref[1] = sums[3][...].astype(bf16)
        if last:
            own_ref[0] = sums[0][...].astype(bf16)
            own_ref[1] = sums[1][...].astype(bf16)


def grads_out(me, dp_count, layout, sources, keep_ref, send_ref, sems, at, mirrors):
    jobs = []
    for e in range(dp_count):
        target = send_ref if e & CORE else keep_ref
        for (first, size), source in zip(layout, sources):
            if source is None:
                continue
            row = pl.multiple_of(device_of(me, e, mirrors) * size, 16)
            jobs.append((source.at[pl.ds(row, size)], target.at[e // 2, pl.ds(first, size)]))
    return copies(jobs, sems, at)


def third_kernel(
    geometry, ints, coarse_seg, gains, mlp_out, grad_second, own_b, came_a, came_b, joined, cotangent, crossed, cq, ckv, *refs
):
    blocks, places, layout, dp_count, mirrors = geometry
    weight_refs = refs[: len(places)]
    refs = refs[len(places) :]
    output_ref, grad_joined_ref, grad_cq_ref, grad_ckv_ref, gain_grads_ref, keep_ref, send_ref = refs[:7]
    w_cout, g_cout, grad_cross, sems = refs[7:]
    me = ints[0]
    width = joined.shape[1]
    made = load_cross(me, weight_refs, places, layout, (None, None, None, w_cout), sems, mirrors)
    rest = [own_b[i].astype(f32) + came_a[i].astype(f32) + came_b[i].astype(f32) for i in range(2)]
    output_ref[...] = (joined[...] + (mlp_out[...] + rest[0])).astype(bf16)
    xhat, r = centred(joined[...])
    grad_in, gain_two = norm_back(xhat, r, gains[2:3], grad_second[...] + rest[1])
    grad_joined_ref[...] = cotangent[...].astype(f32) + grad_in
    low = grad_joined_ref[...].astype(bf16)
    for job in made:
        job.wait()
    for at, step in tiles(width):
        grad_cross[:, at : at + step] = nt(low, w_cout[at : at + step, :]).astype(bf16)
    for at, step in tiles(width):
        g_cout[at : at + step, :] = tn(crossed[:, at : at + step], low).astype(bf16)
    going = grads_out(me, dp_count, layout, (None, None, None, g_cout), keep_ref, send_ref, sems, len(made), mirrors)
    bias = block_bias(coarse_seg, ints, blocks)
    for at in range(0, width, PAIR):
        lanes = slice(at, at + PAIR)
        queries = two_heads(cq[:, lanes])
        grads = two_heads(grad_cross[:, lanes])
        keys = ckv[:, lanes]
        values = ckv[:, width + at : width + at + PAIR]
        probs = softmax_rows(biased(nt(queries, keys), bias))
        grad_ckv_ref[:, width + at : width + at + PAIR] = tn(probs.astype(bf16), grads).astype(bf16)
        grad_probs = nt(grads, values)
        inner = jnp.sum(probs * grad_probs, axis=-1, keepdims=True)
        scores = (probs * (grad_probs - inner)).astype(bf16)
        part = side_by_side(nn(scores, keys)).astype(bf16)
        grad_cq_ref[:, lanes] = part * jnp.asarray(0.125, bf16)
        grad_ckv_ref[:, lanes] = tn(scores, queries).astype(bf16)

    gain_grads_ref[...] = jnp.concatenate([gain_two] * 8, axis=0)
    for job in going:
        job.wait()


def third_part(geometry, ints, coarse, gains, gain_two, grad_joined, residual, attended, grad_cq, grad_ckv, keep_in, send_in, *refs):
    places, layout, dp_count, mirrors = geometry
    weight_refs = refs[: len(places)]
    refs = refs[len(places) :]
    coarse_ref, grad_res_ref, grad_att_ref, gain_grads_ref, keep_ref, send_ref = refs[:6]
    w_ckv, w_out, w_cq, g_ckv, g_out, g_cq, crossed_in, sems = refs[6:]
    me = ints[0]
    width = residual.shape[1]
    made = load_cross(me, weight_refs, places, layout, (w_ckv, w_out, w_cq, None), sems, mirrors)
    xhat, r = centred(residual[...])
    crossed_in[...] = (xhat * gains[1:2]).astype(bf16)
    for at, step in tiles(width):
        g_cq[at : at + step, :] = tn(crossed_in[:, at : at + step], grad_cq[...]).astype(bf16)
    for at, step in tiles(2 * width):
        g_ckv[at : at + step, :] = tn(grad_ckv[:, at : at + step], coarse[...]).astype(bf16)
    for job in made:
        job.wait()
    going = grads_out(me, dp_count, layout, (g_ckv, None, g_cq, None), keep_ref, send_ref, sems, 0, mirrors)
    for at, step in tiles(width):
        coarse_ref[:, at : at + step] = nn(grad_ckv[:, 0:width], w_ckv[0:width, at : at + step]) + nn(
            grad_ckv[:, width : 2 * width], w_ckv[width : 2 * width, at : at + step]
        )
    pieces = [nt(grad_cq[...], w_cq[at : at + step, :]) for at, step in tiles(width)]
    grad_in, gain_cross = norm_back(xhat, r, gains[1:2], jnp.concatenate(pieces, axis=1))
    grad_res = grad_joined[...] + grad_in
    grad_res_ref[...] = grad_res
    low = grad_res.astype(bf16)
    for at, step in tiles(width):
        g_out[at : at + step, :] = tn(attended[:, at : at + step], low).astype(bf16)
    going += grads_out(me, dp_count, layout, (None, g_out, None, None), keep_ref, send_ref, sems, len(going), mirrors)
    for at, step in tiles(width):
        grad_att_ref[:, at : at + step] = nt(low, w_out[at : at + step, :]).astype(bf16)
    zero = jnp.zeros_like(gain_cross)
    gain_grads_ref[...] = jnp.concatenate([zero, gain_cross, gain_two[0:1]] + [zero] * 5, axis=0)
    for job in going:
        job.wait()


def fourth_kernel(geometry, ints, seg_row, grad_att, qkv, *refs):
    blocks, first, last = geometry
    count = last - first
    grad_proj, sems = refs[-1 - 5 * count - 1], refs[-1]
    scratch = refs[-1 - 5 * count : -1]
    query_part, key_part, value_part, key_sum, value_sum = [scratch[i * count : (i + 1) * count] for i in range(5)]
    width = grad_att.shape[1]
    for ref in key_sum + value_sum:
        ref[...] = jnp.zeros_like(ref)

    for i in range(blocks):
        window = pl.multiple_of(ints[1 + 2 * blocks + i] * CLIP, CLIP)
        bias = bias_of(seg_row[:, pl.ds(window, WINDOW)], ints[1 + 3 * blocks + i])
        rows = pl.ds(i * CLIP, CLIP)
        near = pl.ds(window, WINDOW)
        for pair in range(count):
            at = (first + pair) * PAIR
            queries = two_heads(qkv[rows, at : at + PAIR])
            grads = two_heads(grad_att[rows, at : at + PAIR])
            keys = qkv[near, width + at : width + at + PAIR]
            values = qkv[near, 2 * width + at : 2 * width + at + PAIR]
            probs = softmax_rows(nt(queries, keys) + bias)
            grad_probs = nt(grads, values)
            inner = jnp.sum(probs * grad_probs, axis=-1, keepdims=True)
            scores = (probs * (grad_probs - inner)).astype(bf16)
            part = side_by_side(nn(scores, keys)).astype(bf16)
            query_part[pair][rows, :] = part * jnp.asarray(0.125, bf16)
            value_sum[pair][near, :] += tn(probs.astype(bf16), grads)
            key_sum[pair][near, :] += tn(scores, queries)

    jobs = []
    for pair in range(count):
        key_part[pair][...] = key_sum[pair][...].astype(bf16)
        value_part[pair][...] = value_sum[pair][...].astype(bf16)
        for i, part in enumerate((query_part, key_part, value_part)):
            jobs.append((part[pair], grad_proj.at[:, pl.ds(i * width + (first + pair) * PAIR, PAIR)]))
    for job in copies(jobs, sems, 0):
        job.wait()


def fifth_kernel(geometry, ints, mix, gains, blended, grad_res, grad_proj, *refs):
    dp_count, blocks, qkv_places, qkv_rows, mirrors = geometry
    weight_refs = refs[: len(qkv_places)]
    refs = refs[len(qkv_places) :]
    base_ref, going_ref = refs[:2]
    weight, sems = refs[2:]
    me = ints[0]
    width = blended.shape[1]
    jobs = []
    for ref, (e, start, rows) in zip(weight_refs, qkv_places):
        take = min(rows, qkv_rows - start)
        at = pl.multiple_of(device_of(me, e, mirrors) * qkv_rows + start, 16)
        jobs.append((ref.at[pl.ds(0, take)], weight.at[pl.ds(at, take)]))
    made = copies(jobs, sems, 0)
    xhat, r = centred(blended[...])
    for job in made:
        job.wait()
    pieces = [nn(grad_proj[...], weight[:, at : at + step]) for at, step in tiles(width)]
    grad_in, _ = norm_back(xhat, r, gains[0:1], jnp.concatenate(pieces, axis=1))
    grad_blend = grad_res[...] + grad_in
    for b in range(blocks):
        rows = slice(b * CLIP, (b + 1) * CLIP)
        share = mix[b]
        part = grad_blend[rows, :]
        base_ref[rows, :] = share * part
        going_ref[rows, :] = ((1.0 - share) * part).astype(bf16)


def place_kernel(geometry, ints, ints_near, blocks_own, blocks_near, out_ref):
    blocks, mirrors = geometry
    me = ints[0]
    out_ref[...] = jnp.zeros_like(out_ref)
    for table, first, source in ((ints, 1, blocks_own), (ints_near, 0, blocks_near)):
        for b in range(blocks):
            holder, slot = table[first + b], table[first + blocks + b]
            group = jnp.int32(0)
            for role in mirrors:
                group = group + jnp.where(device_of(me, role, mirrors) == holder, role // 2, 0)

            @pl.when(lax.rem(holder, 2) == lax.rem(me, 2))
            def _(group=group, slot=slot, source=source, b=b):
                rows = pl.ds(pl.multiple_of(slot * CLIP, CLIP), CLIP)
                part = source[b * CLIP : (b + 1) * CLIP, :].astype(f32)
                out_ref[group, rows, :] = (out_ref[group, rows, :].astype(f32) + part).astype(bf16)


def sixth_kernel(geometry, ints, gains, gain_grads, blended, grad_proj, *refs):
    dp_count, qkv_places, qkv_rows, mirrors = geometry
    weight_refs = refs[: len(qkv_places)]
    keep_ref, send_ref, weight, grad_w, gain_rows, sems = refs[len(qkv_places) :]
    me = ints[0]
    width = blended.shape[1]
    jobs = []
    for ref, (e, start, rows) in zip(weight_refs, qkv_places):
        take = min(rows, qkv_rows - start)
        at = pl.multiple_of(device_of(me, e, mirrors) * qkv_rows + start, 16)
        jobs.append((ref.at[pl.ds(0, take)], weight.at[pl.ds(at, take)]))
    made = copies(jobs, sems, 0)
    xhat, _ = centred(blended[...])
    normed = (xhat * gains[0:1]).astype(bf16)
    for job in made:
        job.wait()
    gain_one = jnp.zeros((1, width), f32)
    for at, step in tiles(3 * width):
        part = tn(grad_proj[:, at : at + step], normed)
        gain_one = gain_one + jnp.sum(part * weight[at : at + step, :].astype(f32), axis=0, keepdims=True)
        grad_w[at : at + step, :] = part.astype(bf16)
    sent = grads_out(me, dp_count, ((0, qkv_rows),), (grad_w,), keep_ref, send_ref, sems, len(jobs), mirrors)
    all_gains = jnp.concatenate([gain_one / gains[0:1], gain_grads[1:8], jnp.zeros((8, width), f32)], axis=0)
    gain_rows[...] = all_gains.astype(bf16)
    last = []
    for e in range(dp_count):
        target = send_ref if e & CORE else keep_ref
        last.append((gain_rows, target.at[e // 2, pl.ds(qkv_rows, 16)]))
    for job in sent + copies(last, sems, len(jobs) + dp_count):
        job.wait()


def shards(
    tokens,
    coarse_view,
    segment_ids,
    partner_device,
    partner_slot,
    mix_weight,
    ln1_gain,
    w_qkv,
    w_out,
    lnx_gain,
    w_cq,
    w_ckv,
    w_cout,
    ln2_gain,
    w_up,
    w_down,
    cotangent,
):
    row_count, width = tokens.shape
    coarse_rows = coarse_view.shape[0]
    blocks = mix_weight.shape[0]
    dp_count, fsdp_count = lax.axis_size("dp"), lax.axis_size("fsdp")
    dp_me, fsdp_me = lax.axis_index("dp"), lax.axis_index("fsdp")
    part = ln1_gain.shape[0]
    device_me = dp_me * fsdp_count + fsdp_me
    pairs = dp_count // 2
    mirrors = mirror_table()

    target = partner_device[:, 0]
    segments = segment_ids[0]
    videos = segments.reshape(blocks, row_count // blocks)[:, 0]
    following = jnp.concatenate([videos[1:] == videos[:-1], jnp.zeros((1,), bool)])
    before = jnp.concatenate([jnp.zeros((1,), bool), videos[1:] == videos[:-1]])
    index = jnp.arange(blocks, dtype=jnp.int32)
    window = jnp.where(following, index, jnp.where(before, index - 1, jnp.minimum(index, blocks - 2)))
    ints = jnp.concatenate(
        [dp_me[None].astype(jnp.int32), target, partner_slot, window, videos]
    )
    ints_near = swap(ints[1 : 1 + 2 * blocks], CORE)
    seg_row = segments[None, :]
    coarse_seg = segments.reshape(coarse_rows, row_count // coarse_rows)[:, 0][None, :]

    gain_rows = lax.dynamic_update_slice(
        jnp.zeros((8, width), bf16), jnp.stack([ln1_gain, lnx_gain, ln2_gain]), (0, device_me * part)
    )
    shard_one = jnp.concatenate([w_qkv.T, gain_rows])
    shard_first = jnp.concatenate([shard_one, w_ckv.T])
    shard_rest = jnp.concatenate([w_out, w_cq, w_cout])
    shard_mlp = jnp.concatenate([w_up.T, w_down])
    sizes_two = (w_ckv.shape[1], w_out.shape[0], w_cq.shape[0], w_cout.shape[0])
    qkv_part, up_part = w_qkv.shape[1], w_up.shape[1]
    qkv_rows, up_rows = qkv_part * fsdp_count, up_part * fsdp_count
    layout = []
    at = 0
    for size in sizes_two:
        layout.append((at * fsdp_count, size * fsdp_count))
        at += size
    layout = tuple(layout)
    rows_two = at * fsdp_count

    held_tok = {0: tokens, **single_steps(tokens)}
    came_first = inner_start(shard_first)
    held_tok, came_first, shard_rest = fence((held_tok, came_first, shard_rest))

    firsts = inner_order(came_first)
    ones = firsts[:, : qkv_part + 8]
    gain_block = jnp.sum(ones[:, qkv_part:].astype(f32), axis=0).astype(bf16)
    block_one = jnp.concatenate(
        [ones[:, :qkv_part].reshape(qkv_rows, width), gain_block, jnp.zeros((8, width), bf16)]
    )
    held_one = {0: block_one, **single_steps(block_one)}
    came_rest = inner_start(shard_rest)
    held_tok, held_one, came_rest, shard_mlp, firsts = fence((held_tok, held_one, came_rest, shard_mlp, firsts))

    near_mlp = inner_swap(shard_mlp, 1)
    core_tok = core_steps(dict(held_tok))
    near_tok = set(held_tok)
    relay_steps(held_tok)
    rests = inner_order(came_rest)
    split = [firsts[:, qkv_part + 8 :].reshape(sizes_two[0] * fsdp_count, width)]
    at = 0
    for size in sizes_two[1:]:
        split.append(rests[:, at : at + size].reshape(size * fsdp_count, width))
        at += size
    block_two = jnp.concatenate(split)
    held_one, core_tok, held_tok, block_two, near_mlp = fence((held_one, core_tok, held_tok, block_two, near_mlp))

    cuts = (0, 5 * up_part // 12, 3 * up_part // 2, 2 * up_part)
    mlp_cut = [
        inner_join(shard_mlp[None, first:last], near_mlp[None, first:last], 1) for first, last in zip(cuts, cuts[1:])
    ]
    mlp_came = [inner_swap(mlp_cut[0], 2)]
    core_one = core_steps(dict(held_one))
    relay_steps(held_one)
    late_tok = core_steps({e: b for e, b in held_tok.items() if e not in near_tok})
    held_one, core_one, late_tok, block_two, mlp_cut, mlp_came = fence(
        (held_one, core_one, late_tok, block_two, mlp_cut, mlp_came)
    )

    held_two = {0: block_two, **single_steps(block_two)}
    cotangent_near = swap(cotangent, CORE)
    mlp_came.append(inner_swap(mlp_cut[1], 2))
    mlp_joined = [inner_rest(inner_join(mlp_cut[0], mlp_came[0], 2))]
    late_one = core_steps({e: b for e, b in held_one.items() if e not in near_tok})
    pieces_tok = {**core_tok, **late_tok}
    pieces_one = {**core_one, **late_one}
    arrays_tok, places_tok = parts_of(pieces_tok, row_count)
    arrays_one, places_one = parts_of(pieces_one, qkv_rows + 16)
    blended, qkv, attended, gains = pl.pallas_call(
        functools.partial(first_kernel, (dp_count, blocks, places_tok, places_one, qkv_rows, mirrors)),
        out_shape=(
            whole((row_count, width), f32),
            whole((row_count, 3 * width), bf16),
            whole((row_count, width), bf16),
            whole((8, width), f32),
        ),
        in_specs=[SMEM, SMEM, VMEM, VMEM] + [ANY] * (len(arrays_tok) + len(arrays_one)),
        out_specs=(VMEM,) * 4,
        scratch_shapes=[
            pltpu.VMEM((blocks, CLIP, width), bf16),
            pltpu.VMEM((3 * width, width), bf16),
            pltpu.VMEM((dp_count, 16, width), bf16),
            pltpu.SemaphoreType.DMA((blocks + len(arrays_one) + dp_count,)),
        ],
        compiler_params=params(),
        cost_estimate=cost(1e9, 1e6),
        name="mix_self_attention",
    )(ints, mix_weight, seg_row, tokens, *arrays_tok, *arrays_one)
    held_two, attended, mlp_came, cotangent_near, mlp_cut, mlp_joined = fence(
        (held_two, attended, mlp_came, cotangent_near, mlp_cut, mlp_joined)
    )

    core_two = core_steps(dict(held_two))
    relay_steps(held_two)
    mlp_came.append(inner_swap(mlp_cut[2], 2))
    mlp_joined.append(inner_rest(inner_join(mlp_cut[1], mlp_came[1], 2)))
    held_two, core_two, mlp_came, mlp_joined = fence((held_two, core_two, mlp_came, mlp_joined))

    mlp_joined.append(inner_rest(inner_join(mlp_cut[2], mlp_came[2], 2)))
    mlp = jnp.concatenate(mlp_joined, axis=1)
    block_mlp = jnp.concatenate([mlp[:, :up_part].reshape(up_rows, width), mlp[:, up_part:].reshape(up_rows, width)])
    held_mlp = {0: block_mlp, **single_steps(block_mlp)}
    late_two = core_steps({e: b for e, b in held_two.items() if e not in near_tok})
    pieces_two = {**core_two, **late_two}
    wide = [pltpu.VMEM((sizes * fsdp_count * dp_count, width), bf16) for sizes in sizes_two]
    n_two = 4 * dp_count
    arrays_two, places_two = parts_of(pieces_two, rows_two)
    wide = [pltpu.VMEM((sizes * fsdp_count * dp_count, width), bf16) for sizes in sizes_two]
    n_two = 4 * dp_count
    residual, cq, ckv, crossed, joined, second = pl.pallas_call(
        functools.partial(second_kernel, (blocks, places_two, layout, mirrors)),
        out_shape=(
            whole((row_count, width), f32),
            whole((row_count, width), bf16),
            whole((coarse_rows, 2 * width), bf16),
            whole((row_count, width), bf16),
            whole((row_count, width), f32),
            whole((row_count, width), bf16),
        ),
        in_specs=[SMEM] + [VMEM] * 5 + [ANY] * len(arrays_two),
        out_specs=(VMEM,) * 6,
        scratch_shapes=wide + [pltpu.SemaphoreType.DMA((n_two,))],
        compiler_params=params(),
        cost_estimate=cost(1e9, 1e6),
        name="cross_attention",
    )(ints, coarse_seg, coarse_view, blended, attended, gains, *arrays_two)
    second_near = swap(second, CORE)
    held_mlp, second, second_near, ints_near = fence((held_mlp, second, second_near, ints_near))

    early = dict(held_mlp)
    relay_steps(held_mlp)

    def mlp_call(pieces, last):
        groups = tuple(sorted(pieces))
        count = len(groups)
        fixed = pl.BlockSpec((row_count, width), lambda g: (0, 0))
        moving = pl.BlockSpec((1, 2, up_rows, width), lambda g: (g, 0, 0, 0))
        both = pl.BlockSpec((2, row_count, width), lambda g: (0, 0, 0))
        table = whole((row_count, width), f32)
        out_shape = [whole((count, 2, up_rows, width), bf16), whole((2, row_count, width), bf16)]
        out_specs = [moving, both]
        scratch = [pltpu.VMEM((row_count, width), f32)] * (4 if last else 2)
        if last:
            out_shape.append(whole((2, row_count, width), bf16))
            out_specs.append(both)
        else:
            out_shape += [table, table]
            out_specs += [fixed, fixed]
        made = pl.pallas_call(
            functools.partial(mlp_kernel, (groups, tuple((e, None) for e in groups), up_rows, last)),
            grid=(count,),
            out_shape=tuple(out_shape),
            in_specs=[fixed] * 4 + [ANY] * count,
            out_specs=tuple(out_specs),
            scratch_shapes=scratch
            + [
                pltpu.VMEM((count, up_rows, width), bf16),
                pltpu.VMEM((count, up_rows, width), bf16),
                pltpu.VMEM((2, row_count, up_rows), bf16),
                pltpu.VMEM((2, row_count, up_rows), bf16),
                pltpu.SemaphoreType.DMA((2 * count,)),
            ],
            compiler_params=params(32),
            cost_estimate=cost(1e9, 1e6),
            name="feed_forward",
        )(second, second_near, cotangent, cotangent_near, *[pieces[e] for e in groups])
        return groups, made[0].reshape(count, 2 * up_rows, width), made[1], made[2:]

    groups_a, keep_a, going_a, (mlp_out, grad_second) = mlp_call(early, False)
    late = {e: b for e, b in held_mlp.items() if e not in near_tok}
    late, keep_a, going_a, mlp_out, grad_second = fence((late, keep_a, going_a, mlp_out, grad_second))
    came_a = swap(going_a, CORE)
    groups_b, keep_b, going_b, (own_b,) = mlp_call(late, True)
    came_a, keep_b, going_b, own_b = fence((came_a, keep_b, going_b, own_b))
    came_b = swap(going_b, CORE)
    totals = [None] * pairs
    for groups, keep in ((groups_a, keep_a), (groups_b, keep_b)):
        for i, e in enumerate(groups):
            totals[e // 2] = keep[i]
    totals, came_b = fence((totals, came_b))

    sum_mlp = OuterSum(totals)
    upper, lower = slice(0, up_rows), slice(up_rows, 2 * up_rows)
    sum_mlp.relays()
    sum_mlp.prepare(link_masks()[-1], upper)
    output, grad_joined, grad_cq, grad_ckv, gain_two, keep_two, send_two = pl.pallas_call(
        functools.partial(third_kernel, (blocks, places_two, layout, dp_count, mirrors)),
        out_shape=(
            whole((row_count, width), bf16),
            whole((row_count, width), f32),
            whole((row_count, width), bf16),
            whole((coarse_rows, 2 * width), bf16),
            whole((8, width), f32),
            whole((pairs, rows_two, width), bf16),
            whole((pairs, rows_two, width), bf16),
        ),
        in_specs=[SMEM] + [VMEM] * 12 + [ANY] * len(arrays_two),
        out_specs=(VMEM,) * 5 + (ANY,) * 2,
        scratch_shapes=[
            wide[3],
            wide[3],
            pltpu.VMEM((row_count, width), bf16),
            pltpu.SemaphoreType.DMA((n_two + dp_count,)),
        ],
        compiler_params=params(32),
        cost_estimate=cost(1e9, 1e6),
        name="cross_attention_backward",
    )(ints, coarse_seg, gains, mlp_out, grad_second, own_b, came_a, came_b, joined, cotangent, crossed, cq, ckv, *arrays_two)
    state, grad_joined = fence((sum_mlp.state(), grad_joined))
    sum_mlp.put(state)

    sum_mlp.singles(upper)
    for mask in link_masks():
        sum_mlp.prepare(mask, lower)
    coarse_grad, grad_res, grad_att, gain_grads, keep_two, send_two = pl.pallas_call(
        functools.partial(third_part, (places_two, layout, dp_count, mirrors)),
        out_shape=(
            whole((coarse_rows, width), f32),
            whole((row_count, width), f32),
            whole((row_count, width), bf16),
            whole((8, width), f32),
            whole((pairs, rows_two, width), bf16),
            whole((pairs, rows_two, width), bf16),
        ),
        in_specs=[SMEM] + [VMEM] * 8 + [ANY] * (2 + len(arrays_two)),
        out_specs=(VMEM,) * 4 + (ANY,) * 2,
        scratch_shapes=[
            wide[0],
            wide[1],
            wide[2],
            wide[0],
            wide[1],
            wide[2],
            pltpu.VMEM((row_count, width), bf16),
            pltpu.SemaphoreType.DMA((n_two,)),
        ],
        input_output_aliases={9: 4, 10: 5},
        compiler_params=params(),
        cost_estimate=cost(1e9, 1e6),
        name="cross_attention_weights",
    )(
        ints, coarse_view, gains, gain_two, grad_joined, residual, attended, grad_cq, grad_ckv, keep_two, send_two, *arrays_two
    )

    state, grad_att, keep_two, send_two = fence((sum_mlp.state(), grad_att, keep_two, send_two))
    sum_mlp.put(state)

    sum_mlp.singles(lower)
    came_two = swap(send_two, CORE)
    def attention_back(first, last, held):
        count = last - first
        return pl.pallas_call(
            functools.partial(fourth_kernel, (blocks, first, last)),
            out_shape=whole((row_count, 3 * width), bf16),
            in_specs=[SMEM] + [VMEM] * 3 + [ANY] * len(held),
            out_specs=ANY,
            scratch_shapes=[pltpu.VMEM((row_count, PAIR), bf16)] * (3 * count)
            + [pltpu.VMEM((row_count, PAIR), f32)] * (2 * count)
            + [pltpu.SemaphoreType.DMA((3 * count,))],
            input_output_aliases={4: 0} if held else {},
            compiler_params=params(32),
            cost_estimate=cost(1e9, 1e6),
            name="self_attention_backward",
        )(ints, seg_row, grad_att, qkv, *held)

    inner_mlp = [InnerSum(sum_mlp.result(0).reshape(fsdp_count, up_part, width))]
    inner_mlp[0].step()
    grad_proj = attention_back(0, HEADS // 2, ())
    state, came_two, grad_proj, inner_mlp[0].came = fence((sum_mlp.state(), came_two, grad_proj, inner_mlp[0].came))
    sum_mlp.put(state)

    sum_two = OuterSum(keep_two, came_two)
    sum_two.relays()
    inner_mlp.append(InnerSum(sum_mlp.result(1).reshape(fsdp_count, up_part, width)))
    inner_mlp[1].step()
    keep_one, send_one = pl.pallas_call(
        functools.partial(sixth_kernel, (dp_count, places_one, qkv_rows, mirrors)),
        out_shape=(
            whole((pairs, qkv_rows + 16, width), bf16),
            whole((pairs, qkv_rows + 16, width), bf16),
        ),
        in_specs=[SMEM] + [VMEM] * 4 + [ANY] * len(arrays_one),
        out_specs=(ANY,) * 2,
        scratch_shapes=[
            pltpu.VMEM((3 * width, width), bf16),
            pltpu.VMEM((3 * width, width), bf16),
            pltpu.VMEM((16, width), bf16),
            pltpu.SemaphoreType.DMA((len(arrays_one) + 2 * dp_count,)),
        ],
        compiler_params=params(),
        cost_estimate=cost(1e9, 1e6),
        name="self_attention_weights",
    )(ints, gains, gain_grads, blended, grad_proj, *arrays_one)
    state, keep_one, send_one, inner_mlp[1].came = fence((sum_two.state(), keep_one, send_one, inner_mlp[1].came))
    sum_two.put(state)

    sum_two.singles()
    came_one = swap(send_one, CORE)
    base, going_tok = pl.pallas_call(
        functools.partial(fifth_kernel, (dp_count, blocks, places_one, qkv_rows, mirrors)),
        out_shape=(
            whole((row_count, width), f32),
            whole((row_count, width), bf16),
        ),
        in_specs=[SMEM, SMEM] + [VMEM] * 4 + [ANY] * len(arrays_one),
        out_specs=(VMEM,) * 2,
        scratch_shapes=[
            pltpu.VMEM((3 * width, width), bf16),
            pltpu.SemaphoreType.DMA((len(arrays_one),)),
        ],
        compiler_params=params(),
        cost_estimate=cost(1e9, 1e6),
        name="self_attention_input",
    )(ints, mix_weight, gains, blended, grad_res, grad_proj, *arrays_one)
    state, came_one, going_tok = fence((sum_two.state(), came_one, going_tok))
    sum_two.put(state)

    sum_one = OuterSum(keep_one, came_one)
    sum_one.relays()
    came_tok = swap(going_tok, CORE)
    placed = pl.pallas_call(
        functools.partial(place_kernel, (blocks, mirrors)),
        out_shape=whole((pairs, row_count, width), bf16),
        in_specs=[SMEM, SMEM] + [VMEM] * 2,
        out_specs=VMEM,
        compiler_params=params(32),
        cost_estimate=cost(1e9, 1e6),
        name="place_partner_gradients",
    )(ints, ints_near, going_tok, came_tok)
    mlp_parts = jnp.concatenate([inner_parts(inner) for inner in inner_mlp], axis=1)
    inner_mlp = InnerSum(mlp_parts)
    inner_mlp.finish()
    state, placed, mlp_came = fence((sum_one.state(), placed, inner_mlp.came))
    sum_one.put(state)
    inner_mlp.came = mlp_came

    sum_one.singles()
    sum_tok = OuterSum(placed)
    sum_tok.relays()
    two_sum = sum_two.result()
    two_parts = jnp.concatenate(
        [two_sum[first : first + size].reshape(fsdp_count, size // fsdp_count, width) for first, size in layout], axis=1
    )
    inner_two = InnerSum(two_parts)
    inner_two.step()
    state, state_tok, two_came = fence((sum_one.state(), sum_tok.state(), inner_two.came))
    sum_one.put(state)
    sum_tok.put(state_tok)
    inner_two.came = two_came

    sum_tok.singles()
    one_sum = sum_one.result()
    gain_sum = jnp.broadcast_to(one_sum[qkv_rows : qkv_rows + 8][None], (fsdp_count, 8, width))
    one_parts = jnp.concatenate([one_sum[:qkv_rows].reshape(fsdp_count, qkv_part, width), gain_sum], axis=1)
    inner_one = InnerSum(one_parts)
    inner_one.step()
    one_mine = inner_one.result()
    mlp_mine = inner_mlp.result()
    up_shard, down_shard = mlp_mine[:up_part].T, mlp_mine[up_part:]
    two_mine = inner_two.result()
    found = []
    at = 0
    for size in sizes_two:
        found.append(two_mine[at : at + size])
        at += size
    ckv_shard, out_shard, cq_shard, cout_shard = found[0].T, found[1], found[2], found[3]
    qkv_shard = one_mine[:qkv_part].T
    gain_mine = lax.dynamic_slice(one_mine[qkv_part:], (0, device_me * part), (3, part))
    token_grad = base + sum_tok.result()
    return (
        output,
        token_grad,
        coarse_grad,
        gain_mine[0],
        qkv_shard,
        out_shard,
        gain_mine[1],
        cq_shard,
        ckv_shard,
        cout_shard,
        gain_mine[2],
        up_shard,
        down_shard,
    )


def solution(mesh):
    rows = P(("dp", "fsdp"), None)
    columns = P(None, ("dp", "fsdp"))
    line = P(("dp", "fsdp"))
    in_specs = (
        rows, rows, rows, rows, line, line, line, columns, rows,
        line, rows, columns, rows, line, columns, rows, rows,
    )
    out_specs = (
        rows, rows, rows, line, columns, rows, line, rows, columns, rows, line, columns, rows,
    )
    return jax.shard_map(shards, mesh=mesh, in_specs=in_specs, out_specs=out_specs, check_vma=False)
```

```python
import functools

import jax
import jax.numpy as jnp
from jax import lax
from jax.experimental import pallas as pl
from jax.experimental.pallas import tpu as pltpu
from jax.sharding import PartitionSpec as P

HEADS = 12
HEAD = 64
PAIR = 2 * HEAD
CORE = 1
CLIP = 128
WINDOW = 256
TILE = 256
f32 = jnp.float32
bf16 = jnp.bfloat16
fence = lax.optimization_barrier


def swap(values, mask):
    count = lax.axis_size("dp")
    return lax.ppermute(values, "dp", [(i, i ^ mask) for i in range(count)])


def shift(values, step):
    count = lax.axis_size("fsdp")
    return lax.ppermute(values, "fsdp", [(i, (i + step) % count) for i in range(count)])


def link_masks():
    masks = []
    mask = 2
    while mask < lax.axis_size("dp"):
        masks.append(mask)
        mask *= 2
    return masks


def inner_swap(values, mask):
    count = lax.axis_size("fsdp")
    return lax.ppermute(values, "fsdp", [(i, i ^ mask) for i in range(count)])


def inner_double(held, mask):
    return inner_join(held, inner_swap(held, mask), mask)


def inner_join(held, came, mask):
    high = (lax.axis_index("fsdp") & mask) != 0
    return jnp.concatenate([jnp.where(high, came, held), jnp.where(high, held, came)])


def inner_rest(held):
    while held.shape[0] < lax.axis_size("fsdp"):
        held = inner_double(held, held.shape[0])
    return held


def inner_start(shard):
    return [shard] + [shift(shard, step) for step in range(1, lax.axis_size("fsdp"))]


def inner_order(came):
    count = len(came)
    me = lax.axis_index("fsdp")
    line = [came[count - 1 - k] for k in range(count)] + [came[count - k] for k in range(1, count)]
    return lax.dynamic_slice_in_dim(jnp.stack(line), count - 1 - me, count, 0)


def mirrored(role):
    masks = link_masks()
    return sum(masks[len(masks) - 1 - i] for i, mask in enumerate(masks) if role & mask)


def step_along(values, mask):
    count = lax.axis_size("dp")
    return lax.ppermute(values, "dp", [(i, i ^ (mirrored(mask) if i & CORE else mask)) for i in range(count)])


def top_bit(role):
    return 1 << (role.bit_length() - 1)


def relayed_roles():
    found = [role for role in range(2, lax.axis_size("dp"), 2) if role & (role - 1)]
    return sorted(found, key=lambda role: bin(role).count("1"))


def device_of(me, role, mirrors):
    holder = me ^ (role & CORE)
    link = role & ~CORE
    return holder ^ (link + lax.rem(holder, 2) * (mirrors[link] - link))


def mirror_table():
    return {role: mirrored(role) for role in range(0, lax.axis_size("dp"), 2)}


def single_steps(block):
    return {mask: step_along(block, mask) for mask in link_masks()}


def relay_steps(held):
    for role in relayed_roles():
        held[role] = step_along(held[role ^ top_bit(role)], top_bit(role))


def parts_of(pieces, total):
    return [pieces[e] for e in sorted(pieces)], tuple((e, 0, total) for e in sorted(pieces))


def core_steps(held):
    return {**held, **{e | CORE: swap(block, CORE) for e, block in held.items()}}


def inner_parts(inner):
    inner.add()
    return inner.parts


def add_low(a, b):
    return (a.astype(f32) + b.astype(f32)).astype(bf16)


class OuterSum:
    def __init__(self, *parts):
        self.parts = {2 * g: [part[g] for part in parts] for g in range(lax.axis_size("dp") // 2)}
        self.came = []
        self.ready = {}

    def prepare(self, role, rows=slice(None)):
        self.ready[role, rows.start] = self.value(role, rows).astype(bf16)

    def going(self, role, rows):
        return self.ready[role, rows.start] if (role, rows.start) in self.ready else self.value(role, rows).astype(bf16)

    def value(self, role, rows=slice(None)):
        total = self.parts[role][0][rows].astype(f32)
        for part in self.parts[role][1:]:
            total = total + part[rows].astype(f32)
        return total

    def relays(self):
        for role in relayed_roles()[::-1]:
            came = step_along(self.value(role).astype(bf16), top_bit(role))
            self.parts[role ^ top_bit(role)].append(came)

    def singles(self, rows=slice(None), masks=None):
        self.came.append((rows, [step_along(self.going(mask, rows), mask) for mask in masks or link_masks()]))

    def result(self, index=None):
        found = {}
        for rows, blocks in self.came:
            found.setdefault(rows.start, (rows, []))[1].extend(blocks)
        chosen = list(found.values())
        sums = []
        for rows, blocks in chosen if index is None else [chosen[index]]:
            total = self.value(0, rows)
            for block in blocks:
                total = total + block.astype(f32)
            sums.append(total)
        return sums[0] if len(sums) == 1 else jnp.concatenate(sums)

    def state(self):
        return (self.parts, [blocks for _, blocks in self.came], list(self.ready.values()))

    def put(self, state):
        self.parts = state[0]
        self.ready = dict(zip(self.ready, state[2]))
        self.came = [(rows, blocks) for (rows, _), blocks in zip(self.came, state[1])]


class InnerSum:
    def __init__(self, parts):
        self.parts = parts
        self.came = None
        self.mask = parts.shape[0]

    def step(self):
        self.add()
        self.mask //= 2
        bit = ((lax.axis_index("fsdp") & self.mask) != 0).astype(jnp.int32)
        halves = self.parts.reshape((2, self.mask) + self.parts.shape[1:])
        self.parts = lax.dynamic_index_in_dim(halves, bit, 0, keepdims=False)
        going = lax.dynamic_index_in_dim(halves, 1 - bit, 0, keepdims=False).astype(bf16)
        self.came = inner_swap(going, self.mask)

    def finish(self, steps=None):
        while self.mask > 1:
            self.step()

    def add(self):
        if self.came is not None:
            self.parts = self.parts + self.came.astype(f32)
            self.came = None

    def result(self):
        self.finish()
        self.add()
        return self.parts[0]


def nn(a, b):
    return jnp.dot(a, b, preferred_element_type=f32)


def nt(a, b):
    return lax.dot_general(a, b, (((1,), (1,)), ((), ())), preferred_element_type=f32)


def tn(a, b):
    return lax.dot_general(a, b, (((0,), (0,)), ((), ())), preferred_element_type=f32)


def tiles(size):
    step = TILE if size % TILE == 0 else size
    return [(at, step) for at in range(0, size, step)]


def centred(values):
    centre = jnp.mean(values, axis=-1, keepdims=True)
    shifted = values - centre
    spread = jnp.mean(shifted * shifted, axis=-1, keepdims=True)
    r = lax.rsqrt(spread + 1e-06)
    return shifted * r, r


def norm_back(xhat, r, gain, grad):
    c = grad * gain
    first = jnp.mean(c, axis=-1, keepdims=True)
    second = jnp.mean(c * xhat, axis=-1, keepdims=True)
    return r * (c - first - xhat * second), jnp.sum(grad * xhat, axis=0, keepdims=True)


def lower_half(rows):
    return lax.broadcasted_iota(jnp.int32, (rows, PAIR), 1) < HEAD


def two_heads(rows):
    keep = lower_half(rows.shape[0])
    zero = jnp.zeros_like(rows)
    return jnp.concatenate([jnp.where(keep, rows, zero), jnp.where(keep, zero, rows)], axis=0)


def side_by_side(stacked):
    rows = stacked.shape[0] // 2
    return jnp.where(lower_half(rows), stacked[:rows], stacked[rows:])


def softmax_rows(scores):
    raised = jnp.exp(scores - jnp.max(scores, axis=-1, keepdims=True))
    return raised / jnp.sum(raised, axis=-1, keepdims=True)


def bias_of(key_seg, own_seg):
    return jnp.where(key_seg == own_seg, 0.0, -1e30).astype(f32)


def block_bias(key_seg, ints, blocks):
    return jnp.stack([bias_of(key_seg[...], ints[1 + 3 * blocks + i]) for i in range(blocks)])


def biased(scores, bias):
    blocks, _, keys = bias.shape
    rows = scores.shape[0] // (2 * blocks)
    return (scores.reshape(2, blocks, rows, keys) + bias[None]).reshape(scores.shape)


def copies(jobs, sems, at):
    made = [pltpu.make_async_copy(src, dst, sems.at[at + i]) for i, (src, dst) in enumerate(jobs)]
    for job in made:
        job.start()
    return made


def whole(shape, dtype):
    return jax.ShapeDtypeStruct(shape, dtype)


VMEM = pl.BlockSpec(memory_space=pltpu.VMEM)
SMEM = pl.BlockSpec(memory_space=pltpu.SMEM)
ANY = pl.BlockSpec(memory_space=pl.ANY)


def params(mib=56):
    return pltpu.CompilerParams(vmem_limit_bytes=mib * 1024 * 1024)


def cost(flops, moved, exps=0):
    return pl.CostEstimate(flops=int(flops), bytes_accessed=int(moved), transcendentals=int(exps))


def first_kernel(
    geometry, ints, mix, seg_row, tokens, *refs
):
    dp_count, blocks, token_places, qkv_places, qkv_rows, mirrors = geometry
    n_tok, n_qkv = len(token_places), len(qkv_places)
    token_refs, qkv_refs = refs[:n_tok], refs[n_tok : n_tok + n_qkv]
    blended_ref, qkv_ref, attended_ref, gains_ref, partner, weight, gain_parts, sems = refs[n_tok + n_qkv :]
    me = ints[0]
    width = tokens.shape[1]

    for b in range(blocks):
        holder, slot = ints[1 + b], ints[1 + blocks + b]
        for ref, (role, _, rows) in zip(token_refs, token_places):

            @pl.when(holder == device_of(me, role, mirrors))
            def _(ref=ref, rows=rows, b=b, slot=slot):
                at = pl.multiple_of(slot * CLIP, CLIP)
                pltpu.make_async_copy(ref.at[pl.ds(at, CLIP)], partner.at[b], sems.at[b]).start()

    jobs = []
    for ref, (e, start, rows) in zip(qkv_refs, qkv_places):
        take = min(rows, qkv_rows - start)
        at = pl.multiple_of(device_of(me, e, mirrors) * qkv_rows + start, 16)
        jobs.append((ref.at[pl.ds(0, take)], weight.at[pl.ds(at, take)]))
        if start + rows > qkv_rows:
            jobs.append((ref.at[pl.ds(take, rows - take)], gain_parts.at[e]))
    made = copies(jobs, sems, blocks)
    for b in range(blocks):
        pltpu.make_async_copy(tokens.at[pl.ds(0, CLIP)], partner.at[b], sems.at[b]).wait()
    for b in range(blocks):
        rows = slice(b * CLIP, (b + 1) * CLIP)
        share = mix[b]
        blended_ref[rows, :] = share * tokens[rows, :].astype(f32) + (1.0 - share) * partner[b].astype(f32)
    for job in made:
        job.wait()
    gains = gain_parts[0].astype(f32)
    for e in range(1, dp_count):
        gains = gains + gain_parts[e].astype(f32)
    gains_ref[...] = gains[:8]
    xhat, _ = centred(blended_ref[...])
    normed = (xhat * gains[0:1]).astype(bf16)
    for at, step in tiles(3 * width):
        tile = nt(normed, weight[at : at + step, :])
        if at + step <= width:
            tile = tile * 0.125
        qkv_ref[:, at : at + step] = tile.astype(bf16)

    for i in range(blocks):
        window = pl.multiple_of(ints[1 + 2 * blocks + i] * CLIP, CLIP)
        bias = bias_of(seg_row[:, pl.ds(window, WINDOW)], ints[1 + 3 * blocks + i])
        rows = pl.ds(i * CLIP, CLIP)
        keys = pl.ds(window, WINDOW)
        for at in range(0, width, PAIR):
            queries = two_heads(qkv_ref[rows, at : at + PAIR])
            probs = softmax_rows(nt(queries, qkv_ref[keys, width + at : width + at + PAIR]) + bias).astype(bf16)
            out = nn(probs, qkv_ref[keys, 2 * width + at : 2 * width + at + PAIR])
            attended_ref[rows, at : at + PAIR] = side_by_side(out).astype(bf16)


def load_cross(me, refs, places, layout, weights, sems, mirrors):
    jobs = []
    for ref, (e, start, rows) in zip(refs, places):
        for (first, size), weight in zip(layout, weights):
            if weight is not None and first >= start and first + size <= start + rows:
                at = pl.multiple_of(device_of(me, e, mirrors) * size, 16)
                jobs.append((ref.at[pl.ds(first - start, size)], weight.at[pl.ds(at, size)]))
    return copies(jobs, sems, 0)


def second_kernel(geometry, ints, coarse_seg, coarse, blended, attended, gains, *refs):
    blocks, places, layout, mirrors = geometry
    weight_refs = refs[: len(places)]
    residual_ref, cq_ref, ckv_ref, crossed_ref, joined_ref, second_ref = refs[len(places) : len(places) + 6]
    w_ckv, w_out, w_cq, w_cout, sems = refs[len(places) + 6 :]
    made = load_cross(ints[0], weight_refs, places, layout, (w_ckv, w_out, w_cq, w_cout), sems, mirrors)
    for job in made:
        job.wait()
    width = blended.shape[1]
    for at, step in tiles(2 * width):
        ckv_ref[:, at : at + step] = nt(coarse[...], w_ckv[at : at + step, :]).astype(bf16)
    for at, step in tiles(width):
        residual_ref[:, at : at + step] = blended[:, at : at + step] + nn(attended[...], w_out[:, at : at + step])
    xhat, _ = centred(residual_ref[...])
    crossed_in = (xhat * gains[1:2]).astype(bf16)
    for at, step in tiles(width):
        cq_ref[:, at : at + step] = (nn(crossed_in, w_cq[:, at : at + step]) * 0.125).astype(bf16)

    bias = block_bias(coarse_seg, ints, blocks)
    for at in range(0, width, PAIR):
        queries = two_heads(cq_ref[:, at : at + PAIR])
        probs = softmax_rows(biased(nt(queries, ckv_ref[:, at : at + PAIR]), bias)).astype(bf16)
        out = nn(probs, ckv_ref[:, width + at : width + at + PAIR])
        crossed_ref[:, at : at + PAIR] = side_by_side(out).astype(bf16)

    for at, step in tiles(width):
        joined_ref[:, at : at + step] = residual_ref[:, at : at + step] + nn(crossed_ref[...], w_cout[:, at : at + step])
    xhat, _ = centred(joined_ref[...])
    second_ref[...] = (xhat * gains[2:3]).astype(bf16)


def mlp_kernel(geometry, second, second_near, cotangent, cotangent_near, *refs):
    groups, places, rows, last = geometry
    weight_refs = refs[: len(places)]
    refs = refs[len(places) :]
    keep_ref, going_ref = refs[:2]
    if last:
        own_ref = refs[2]
        sums = refs[3:7]
        refs = refs[7:]
    else:
        sums = refs[2:6]
        refs = refs[6:]
    w_up, w_down, hidden, grad_pre, sems = refs
    step = pl.program_id(0)

    def jobs_of(group):
        jobs = []
        for ref, (e, which) in zip(weight_refs, places):
            if e == groups[group]:
                for part, weight in ((0, w_up), (1, w_down)):
                    if which is None or which == part:
                        first = part * rows if which is None else 0
                        jobs.append((ref.at[pl.ds(first, rows)], weight.at[group]))
        return jobs

    at = 0
    for group in range(len(groups)):
        jobs = jobs_of(group)
        made = [pltpu.make_async_copy(s, d, sems.at[at + i]) for i, (s, d) in enumerate(jobs)]
        at += len(jobs)

        @pl.when(step == 0)
        def _(made=made):
            for job in made:
                job.start()

        @pl.when(step == group)
        def _(made=made):
            for job in made:
                job.wait()

    @pl.when(step == 0)
    def _():
        for ref in sums:
            ref[...] = jnp.zeros_like(ref)

    up, down = w_up.at[step], w_down.at[step]
    for half, (inputs, upstream) in enumerate(((second, cotangent), (second_near, cotangent_near))):
        pre = nt(inputs[...], up[...])
        grad_hidden = nt(upstream[...], down[...])
        cdf = 0.5 * (1.0 + lax.erf(pre * 0.7071067811865476))
        slope = cdf + pre * (jnp.exp(-0.5 * pre * pre) * 0.3989422804014327)
        hidden[half] = (pre * cdf).astype(bf16)
        grad_pre[half] = (grad_hidden * slope).astype(bf16)
        for first, size in tiles(second.shape[1]):
            columns = slice(first, first + size)
            sums[2 * half][:, columns] += nn(hidden[half], down[:, columns])
            sums[2 * half + 1][:, columns] += nn(grad_pre[half], up[:, columns])
    keep_ref[0, 0] = (tn(grad_pre[0], second[...]) + tn(grad_pre[1], second_near[...])).astype(bf16)
    keep_ref[0, 1] = (tn(hidden[0], cotangent[...]) + tn(hidden[1], cotangent_near[...])).astype(bf16)

    @pl.when(step == len(groups) - 1)
    def _():
        going_ref[0] = sums[2][...].astype(bf16)
        going_ref[1] = sums[3][...].astype(bf16)
        if last:
            own_ref[0] = sums[0][...].astype(bf16)
            own_ref[1] = sums[1][...].astype(bf16)


def grads_out(me, dp_count, layout, sources, keep_ref, send_ref, sems, at, mirrors):
    jobs = []
    for e in range(dp_count):
        target = send_ref if e & CORE else keep_ref
        for (first, size), source in zip(layout, sources):
            if source is None:
                continue
            row = pl.multiple_of(device_of(me, e, mirrors) * size, 16)
            jobs.append((source.at[pl.ds(row, size)], target.at[e // 2, pl.ds(first, size)]))
    return copies(jobs, sems, at)


def third_kernel(
    geometry, ints, coarse_seg, gains, mlp_out, grad_second, own_b, came_a, came_b, joined, cotangent, crossed, cq, ckv, *refs
):
    blocks, places, layout, dp_count, mirrors = geometry
    weight_refs = refs[: len(places)]
    refs = refs[len(places) :]
    output_ref, grad_joined_ref, grad_cq_ref, grad_ckv_ref, gain_grads_ref, keep_ref, send_ref = refs[:7]
    w_cout, g_cout, grad_cross, sems = refs[7:]
    me = ints[0]
    width = joined.shape[1]
    made = load_cross(me, weight_refs, places, layout, (None, None, None, w_cout), sems, mirrors)
    rest = [own_b[i].astype(f32) + came_a[i].astype(f32) + came_b[i].astype(f32) for i in range(2)]
    output_ref[...] = (joined[...] + (mlp_out[...] + rest[0])).astype(bf16)
    xhat, r = centred(joined[...])
    grad_in, gain_two = norm_back(xhat, r, gains[2:3], grad_second[...] + rest[1])
    grad_joined_ref[...] = cotangent[...].astype(f32) + grad_in
    low = grad_joined_ref[...].astype(bf16)
    for job in made:
        job.wait()
    for at, step in tiles(width):
        grad_cross[:, at : at + step] = nt(low, w_cout[at : at + step, :]).astype(bf16)
    for at, step in tiles(width):
        g_cout[at : at + step, :] = tn(crossed[:, at : at + step], low).astype(bf16)
    going = grads_out(me, dp_count, layout, (None, None, None, g_cout), keep_ref, send_ref, sems, len(made), mirrors)
    bias = block_bias(coarse_seg, ints, blocks)
    for at in range(0, width, PAIR):
        lanes = slice(at, at + PAIR)
        queries = two_heads(cq[:, lanes])
        grads = two_heads(grad_cross[:, lanes])
        keys = ckv[:, lanes]
        values = ckv[:, width + at : width + at + PAIR]
        probs = softmax_rows(biased(nt(queries, keys), bias))
        grad_ckv_ref[:, width + at : width + at + PAIR] = tn(probs.astype(bf16), grads).astype(bf16)
        grad_probs = nt(grads, values)
        inner = jnp.sum(probs * grad_probs, axis=-1, keepdims=True)
        scores = (probs * (grad_probs - inner)).astype(bf16)
        part = side_by_side(nn(scores, keys)).astype(bf16)
        grad_cq_ref[:, lanes] = part * jnp.asarray(0.125, bf16)
        grad_ckv_ref[:, lanes] = tn(scores, queries).astype(bf16)

    gain_grads_ref[...] = jnp.concatenate([gain_two] * 8, axis=0)
    for job in going:
        job.wait()


def third_part(geometry, ints, coarse, gains, gain_two, grad_joined, residual, attended, grad_cq, grad_ckv, keep_in, send_in, *refs):
    places, layout, dp_count, mirrors = geometry
    weight_refs = refs[: len(places)]
    refs = refs[len(places) :]
    coarse_ref, grad_res_ref, grad_att_ref, gain_grads_ref, keep_ref, send_ref = refs[:6]
    w_ckv, w_out, w_cq, g_ckv, g_out, g_cq, crossed_in, sems = refs[6:]
    me = ints[0]
    width = residual.shape[1]
    made = load_cross(me, weight_refs, places, layout, (w_ckv, w_out, w_cq, None), sems, mirrors)
    xhat, r = centred(residual[...])
    crossed_in[...] = (xhat * gains[1:2]).astype(bf16)
    for at, step in tiles(width):
        g_cq[at : at + step, :] = tn(crossed_in[:, at : at + step], grad_cq[...]).astype(bf16)
    for at, step in tiles(2 * width):
        g_ckv[at : at + step, :] = tn(grad_ckv[:, at : at + step], coarse[...]).astype(bf16)
    for job in made:
        job.wait()
    going = grads_out(me, dp_count, layout, (g_ckv, None, g_cq, None), keep_ref, send_ref, sems, 0, mirrors)
    for at, step in tiles(width):
        coarse_ref[:, at : at + step] = nn(grad_ckv[:, 0:width], w_ckv[0:width, at : at + step]) + nn(
            grad_ckv[:, width : 2 * width], w_ckv[width : 2 * width, at : at + step]
        )
    pieces = [nt(grad_cq[...], w_cq[at : at + step, :]) for at, step in tiles(width)]
    grad_in, gain_cross = norm_back(xhat, r, gains[1:2], jnp.concatenate(pieces, axis=1))
    grad_res = grad_joined[...] + grad_in
    grad_res_ref[...] = grad_res
    low = grad_res.astype(bf16)
    for at, step in tiles(width):
        g_out[at : at + step, :] = tn(attended[:, at : at + step], low).astype(bf16)
    going += grads_out(me, dp_count, layout, (None, g_out, None, None), keep_ref, send_ref, sems, len(going), mirrors)
    for at, step in tiles(width):
        grad_att_ref[:, at : at + step] = nt(low, w_out[at : at + step, :]).astype(bf16)
    zero = jnp.zeros_like(gain_cross)
    gain_grads_ref[...] = jnp.concatenate([zero, gain_cross, gain_two[0:1]] + [zero] * 5, axis=0)
    for job in going:
        job.wait()


def fourth_kernel(geometry, ints, seg_row, grad_att, qkv, *refs):
    blocks, first, last = geometry
    count = last - first
    grad_proj, sems = refs[-1 - 5 * count - 1], refs[-1]
    scratch = refs[-1 - 5 * count : -1]
    query_part, key_part, value_part, key_sum, value_sum = [scratch[i * count : (i + 1) * count] for i in range(5)]
    width = grad_att.shape[1]
    for ref in key_sum + value_sum:
        ref[...] = jnp.zeros_like(ref)

    for i in range(blocks):
        window = pl.multiple_of(ints[1 + 2 * blocks + i] * CLIP, CLIP)
        bias = bias_of(seg_row[:, pl.ds(window, WINDOW)], ints[1 + 3 * blocks + i])
        rows = pl.ds(i * CLIP, CLIP)
        near = pl.ds(window, WINDOW)
        for pair in range(count):
            at = (first + pair) * PAIR
            queries = two_heads(qkv[rows, at : at + PAIR])
            grads = two_heads(grad_att[rows, at : at + PAIR])
            keys = qkv[near, width + at : width + at + PAIR]
            values = qkv[near, 2 * width + at : 2 * width + at + PAIR]
            probs = softmax_rows(nt(queries, keys) + bias)
            grad_probs = nt(grads, values)
            inner = jnp.sum(probs * grad_probs, axis=-1, keepdims=True)
            scores = (probs * (grad_probs - inner)).astype(bf16)
            part = side_by_side(nn(scores, keys)).astype(bf16)
            query_part[pair][rows, :] = part * jnp.asarray(0.125, bf16)
            value_sum[pair][near, :] += tn(probs.astype(bf16), grads)
            key_sum[pair][near, :] += tn(scores, queries)

    jobs = []
    for pair in range(count):
        key_part[pair][...] = key_sum[pair][...].astype(bf16)
        value_part[pair][...] = value_sum[pair][...].astype(bf16)
        for i, part in enumerate((query_part, key_part, value_part)):
            jobs.append((part[pair], grad_proj.at[:, pl.ds(i * width + (first + pair) * PAIR, PAIR)]))
    for job in copies(jobs, sems, 0):
        job.wait()


def fifth_kernel(geometry, ints, mix, gains, blended, grad_res, grad_proj, *refs):
    dp_count, blocks, qkv_places, qkv_rows, mirrors = geometry
    weight_refs = refs[: len(qkv_places)]
    refs = refs[len(qkv_places) :]
    base_ref, going_ref = refs[:2]
    weight, sems = refs[2:]
    me = ints[0]
    width = blended.shape[1]
    jobs = []
    for ref, (e, start, rows) in zip(weight_refs, qkv_places):
        take = min(rows, qkv_rows - start)
        at = pl.multiple_of(device_of(me, e, mirrors) * qkv_rows + start, 16)
        jobs.append((ref.at[pl.ds(0, take)], weight.at[pl.ds(at, take)]))
    made = copies(jobs, sems, 0)
    xhat, r = centred(blended[...])
    for job in made:
        job.wait()
    pieces = [nn(grad_proj[...], weight[:, at : at + step]) for at, step in tiles(width)]
    grad_in, _ = norm_back(xhat, r, gains[0:1], jnp.concatenate(pieces, axis=1))
    grad_blend = grad_res[...] + grad_in
    for b in range(blocks):
        rows = slice(b * CLIP, (b + 1) * CLIP)
        share = mix[b]
        part = grad_blend[rows, :]
        base_ref[rows, :] = share * part
        going_ref[rows, :] = ((1.0 - share) * part).astype(bf16)


def place_kernel(geometry, ints, ints_near, blocks_own, blocks_near, out_ref):
    blocks, mirrors = geometry
    me = ints[0]
    out_ref[...] = jnp.zeros_like(out_ref)
    for table, first, source in ((ints, 1, blocks_own), (ints_near, 0, blocks_near)):
        for b in range(blocks):
            holder, slot = table[first + b], table[first + blocks + b]
            group = jnp.int32(0)
            for role in mirrors:
                group = group + jnp.where(device_of(me, role, mirrors) == holder, role // 2, 0)

            @pl.when(lax.rem(holder, 2) == lax.rem(me, 2))
            def _(group=group, slot=slot, source=source, b=b):
                rows = pl.ds(pl.multiple_of(slot * CLIP, CLIP), CLIP)
                part = source[b * CLIP : (b + 1) * CLIP, :].astype(f32)
                out_ref[group, rows, :] = (out_ref[group, rows, :].astype(f32) + part).astype(bf16)


def sixth_kernel(geometry, ints, gains, gain_grads, blended, grad_proj, *refs):
    dp_count, qkv_places, qkv_rows, mirrors = geometry
    weight_refs = refs[: len(qkv_places)]
    keep_ref, send_ref, weight, grad_w, gain_rows, sems = refs[len(qkv_places) :]
    me = ints[0]
    width = blended.shape[1]
    jobs = []
    for ref, (e, start, rows) in zip(weight_refs, qkv_places):
        take = min(rows, qkv_rows - start)
        at = pl.multiple_of(device_of(me, e, mirrors) * qkv_rows + start, 16)
        jobs.append((ref.at[pl.ds(0, take)], weight.at[pl.ds(at, take)]))
    made = copies(jobs, sems, 0)
    xhat, _ = centred(blended[...])
    normed = (xhat * gains[0:1]).astype(bf16)
    for job in made:
        job.wait()
    gain_one = jnp.zeros((1, width), f32)
    for at, step in tiles(3 * width):
        part = tn(grad_proj[:, at : at + step], normed)
        gain_one = gain_one + jnp.sum(part * weight[at : at + step, :].astype(f32), axis=0, keepdims=True)
        grad_w[at : at + step, :] = part.astype(bf16)
    sent = grads_out(me, dp_count, ((0, qkv_rows),), (grad_w,), keep_ref, send_ref, sems, len(jobs), mirrors)
    all_gains = jnp.concatenate([gain_one / gains[0:1], gain_grads[1:8], jnp.zeros((8, width), f32)], axis=0)
    gain_rows[...] = all_gains.astype(bf16)
    last = []
    for e in range(dp_count):
        target = send_ref if e & CORE else keep_ref
        last.append((gain_rows, target.at[e // 2, pl.ds(qkv_rows, 16)]))
    for job in sent + copies(last, sems, len(jobs) + dp_count):
        job.wait()


def shards(
    tokens,
    coarse_view,
    segment_ids,
    partner_device,
    partner_slot,
    mix_weight,
    ln1_gain,
    w_qkv,
    w_out,
    lnx_gain,
    w_cq,
    w_ckv,
    w_cout,
    ln2_gain,
    w_up,
    w_down,
    cotangent,
):
    row_count, width = tokens.shape
    coarse_rows = coarse_view.shape[0]
    blocks = mix_weight.shape[0]
    dp_count, fsdp_count = lax.axis_size("dp"), lax.axis_size("fsdp")
    dp_me, fsdp_me = lax.axis_index("dp"), lax.axis_index("fsdp")
    part = ln1_gain.shape[0]
    device_me = dp_me * fsdp_count + fsdp_me
    pairs = dp_count // 2
    mirrors = mirror_table()

    target = partner_device[:, 0]
    segments = segment_ids[0]
    videos = segments.reshape(blocks, row_count // blocks)[:, 0]
    following = jnp.concatenate([videos[1:] == videos[:-1], jnp.zeros((1,), bool)])
    before = jnp.concatenate([jnp.zeros((1,), bool), videos[1:] == videos[:-1]])
    index = jnp.arange(blocks, dtype=jnp.int32)
    window = jnp.where(following, index, jnp.where(before, index - 1, jnp.minimum(index, blocks - 2)))
    ints = jnp.concatenate(
        [dp_me[None].astype(jnp.int32), target, partner_slot, window, videos]
    )
    ints_near = swap(ints[1 : 1 + 2 * blocks], CORE)
    seg_row = segments[None, :]
    coarse_seg = segments.reshape(coarse_rows, row_count // coarse_rows)[:, 0][None, :]

    gain_rows = lax.dynamic_update_slice(
        jnp.zeros((8, width), bf16), jnp.stack([ln1_gain, lnx_gain, ln2_gain]), (0, device_me * part)
    )
    shard_one = jnp.concatenate([w_qkv.T, gain_rows])
    shard_first = jnp.concatenate([shard_one, w_ckv.T])
    shard_rest = jnp.concatenate([w_out, w_cq, w_cout])
    shard_mlp = jnp.concatenate([w_up.T, w_down])
    sizes_two = (w_ckv.shape[1], w_out.shape[0], w_cq.shape[0], w_cout.shape[0])
    qkv_part, up_part = w_qkv.shape[1], w_up.shape[1]
    qkv_rows, up_rows = qkv_part * fsdp_count, up_part * fsdp_count
    layout = []
    at = 0
    for size in sizes_two:
        layout.append((at * fsdp_count, size * fsdp_count))
        at += size
    layout = tuple(layout)
    rows_two = at * fsdp_count

    held_tok = {0: tokens, **single_steps(tokens)}
    came_first = inner_start(shard_first)
    held_tok, came_first, shard_rest = fence((held_tok, came_first, shard_rest))

    firsts = inner_order(came_first)
    ones = firsts[:, : qkv_part + 8]
    gain_block = jnp.sum(ones[:, qkv_part:].astype(f32), axis=0).astype(bf16)
    block_one = jnp.concatenate(
        [ones[:, :qkv_part].reshape(qkv_rows, width), gain_block, jnp.zeros((8, width), bf16)]
    )
    held_one = {0: block_one, **single_steps(block_one)}
    came_rest = inner_start(shard_rest)
    held_tok, held_one, came_rest, shard_mlp, firsts = fence((held_tok, held_one, came_rest, shard_mlp, firsts))

    near_mlp = inner_swap(shard_mlp, 1)
    core_tok = core_steps(dict(held_tok))
    near_tok = set(held_tok)
    relay_steps(held_tok)
    rests = inner_order(came_rest)
    split = [firsts[:, qkv_part + 8 :].reshape(sizes_two[0] * fsdp_count, width)]
    at = 0
    for size in sizes_two[1:]:
        split.append(rests[:, at : at + size].reshape(size * fsdp_count, width))
        at += size
    block_two = jnp.concatenate(split)
    held_one, core_tok, held_tok, block_two, near_mlp = fence((held_one, core_tok, held_tok, block_two, near_mlp))

    cuts = (0, 5 * up_part // 12, 3 * up_part // 2, 2 * up_part)
    mlp_cut = [
        inner_join(shard_mlp[None, first:last], near_mlp[None, first:last], 1) for first, last in zip(cuts, cuts[1:])
    ]
    mlp_came = [inner_swap(mlp_cut[0], 2)]
    core_one = core_steps(dict(held_one))
    relay_steps(held_one)
    late_tok = core_steps({e: b for e, b in held_tok.items() if e not in near_tok})
    held_one, core_one, late_tok, block_two, mlp_cut, mlp_came = fence(
        (held_one, core_one, late_tok, block_two, mlp_cut, mlp_came)
    )

    held_two = {0: block_two, **single_steps(block_two)}
    cotangent_near = swap(cotangent, CORE)
    mlp_came.append(inner_swap(mlp_cut[1], 2))
    mlp_joined = [inner_rest(inner_join(mlp_cut[0], mlp_came[0], 2))]
    late_one = core_steps({e: b for e, b in held_one.items() if e not in near_tok})
    pieces_tok = {**core_tok, **late_tok}
    pieces_one = {**core_one, **late_one}
    arrays_tok, places_tok = parts_of(pieces_tok, row_count)
    arrays_one, places_one = parts_of(pieces_one, qkv_rows + 16)
    blended, qkv, attended, gains = pl.pallas_call(
        functools.partial(first_kernel, (dp_count, blocks, places_tok, places_one, qkv_rows, mirrors)),
        out_shape=(
            whole((row_count, width), f32),
            whole((row_count, 3 * width), bf16),
            whole((row_count, width), bf16),
            whole((8, width), f32),
        ),
        in_specs=[SMEM, SMEM, VMEM, VMEM] + [ANY] * (len(arrays_tok) + len(arrays_one)),
        out_specs=(VMEM,) * 4,
        scratch_shapes=[
            pltpu.VMEM((blocks, CLIP, width), bf16),
            pltpu.VMEM((3 * width, width), bf16),
            pltpu.VMEM((dp_count, 16, width), bf16),
            pltpu.SemaphoreType.DMA((blocks + len(arrays_one) + dp_count,)),
        ],
        compiler_params=params(),
        cost_estimate=cost(1e9, 1e6),
        name="mix_self_attention",
    )(ints, mix_weight, seg_row, tokens, *arrays_tok, *arrays_one)
    held_two, attended, mlp_came, cotangent_near, mlp_cut, mlp_joined = fence(
        (held_two, attended, mlp_came, cotangent_near, mlp_cut, mlp_joined)
    )

    core_two = core_steps(dict(held_two))
    relay_steps(held_two)
    mlp_came.append(inner_swap(mlp_cut[2], 2))
    mlp_joined.append(inner_rest(inner_join(mlp_cut[1], mlp_came[1], 2)))
    held_two, core_two, mlp_came, mlp_joined = fence((held_two, core_two, mlp_came, mlp_joined))

    mlp_joined.append(inner_rest(inner_join(mlp_cut[2], mlp_came[2], 2)))
    mlp = jnp.concatenate(mlp_joined, axis=1)
    block_mlp = jnp.concatenate([mlp[:, :up_part].reshape(up_rows, width), mlp[:, up_part:].reshape(up_rows, width)])
    held_mlp = {0: block_mlp, **single_steps(block_mlp)}
    late_two = core_steps({e: b for e, b in held_two.items() if e not in near_tok})
    pieces_two = {**core_two, **late_two}
    wide = [pltpu.VMEM((sizes * fsdp_count * dp_count, width), bf16) for sizes in sizes_two]
    n_two = 4 * dp_count
    arrays_two, places_two = parts_of(pieces_two, rows_two)
    wide = [pltpu.VMEM((sizes * fsdp_count * dp_count, width), bf16) for sizes in sizes_two]
    n_two = 4 * dp_count
    residual, cq, ckv, crossed, joined, second = pl.pallas_call(
        functools.partial(second_kernel, (blocks, places_two, layout, mirrors)),
        out_shape=(
            whole((row_count, width), f32),
            whole((row_count, width), bf16),
            whole((coarse_rows, 2 * width), bf16),
            whole((row_count, width), bf16),
            whole((row_count, width), f32),
            whole((row_count, width), bf16),
        ),
        in_specs=[SMEM] + [VMEM] * 5 + [ANY] * len(arrays_two),
        out_specs=(VMEM,) * 6,
        scratch_shapes=wide + [pltpu.SemaphoreType.DMA((n_two,))],
        compiler_params=params(),
        cost_estimate=cost(1e9, 1e6),
        name="cross_attention",
    )(ints, coarse_seg, coarse_view, blended, attended, gains, *arrays_two)
    second_near = swap(second, CORE)
    held_mlp, second, second_near, ints_near = fence((held_mlp, second, second_near, ints_near))

    early = dict(held_mlp)
    relay_steps(held_mlp)

    def mlp_call(pieces, last):
        groups = tuple(sorted(pieces))
        count = len(groups)
        fixed = pl.BlockSpec((row_count, width), lambda g: (0, 0))
        moving = pl.BlockSpec((1, 2, up_rows, width), lambda g: (g, 0, 0, 0))
        both = pl.BlockSpec((2, row_count, width), lambda g: (0, 0, 0))
        table = whole((row_count, width), f32)
        out_shape = [whole((count, 2, up_rows, width), bf16), whole((2, row_count, width), bf16)]
        out_specs = [moving, both]
        scratch = [pltpu.VMEM((row_count, width), f32)] * (4 if last else 2)
        if last:
            out_shape.append(whole((2, row_count, width), bf16))
            out_specs.append(both)
        else:
            out_shape += [table, table]
            out_specs += [fixed, fixed]
        made = pl.pallas_call(
            functools.partial(mlp_kernel, (groups, tuple((e, None) for e in groups), up_rows, last)),
            grid=(count,),
            out_shape=tuple(out_shape),
            in_specs=[fixed] * 4 + [ANY] * count,
            out_specs=tuple(out_specs),
            scratch_shapes=scratch
            + [
                pltpu.VMEM((count, up_rows, width), bf16),
                pltpu.VMEM((count, up_rows, width), bf16),
                pltpu.VMEM((2, row_count, up_rows), bf16),
                pltpu.VMEM((2, row_count, up_rows), bf16),
                pltpu.SemaphoreType.DMA((2 * count,)),
            ],
            compiler_params=params(32),
            cost_estimate=cost(1e9, 1e6),
            name="feed_forward",
        )(second, second_near, cotangent, cotangent_near, *[pieces[e] for e in groups])
        return groups, made[0].reshape(count, 2 * up_rows, width), made[1], made[2:]

    groups_a, keep_a, going_a, (mlp_out, grad_second) = mlp_call(early, False)
    late = {e: b for e, b in held_mlp.items() if e not in near_tok}
    late, keep_a, going_a, mlp_out, grad_second = fence((late, keep_a, going_a, mlp_out, grad_second))
    came_a = swap(going_a, CORE)
    groups_b, keep_b, going_b, (own_b,) = mlp_call(late, True)
    came_a, keep_b, going_b, own_b = fence((came_a, keep_b, going_b, own_b))
    came_b = swap(going_b, CORE)
    totals = [None] * pairs
    for groups, keep in ((groups_a, keep_a), (groups_b, keep_b)):
        for i, e in enumerate(groups):
            totals[e // 2] = keep[i]
    totals, came_b = fence((totals, came_b))

    sum_mlp = OuterSum(totals)
    upper, lower = slice(0, up_rows), slice(up_rows, 2 * up_rows)
    sum_mlp.relays()
    sum_mlp.prepare(link_masks()[-1], upper)
    output, grad_joined, grad_cq, grad_ckv, gain_two, keep_two, send_two = pl.pallas_call(
        functools.partial(third_kernel, (blocks, places_two, layout, dp_count, mirrors)),
        out_shape=(
            whole((row_count, width), bf16),
            whole((row_count, width), f32),
            whole((row_count, width), bf16),
            whole((coarse_rows, 2 * width), bf16),
            whole((8, width), f32),
            whole((pairs, rows_two, width), bf16),
            whole((pairs, rows_two, width), bf16),
        ),
        in_specs=[SMEM] + [VMEM] * 12 + [ANY] * len(arrays_two),
        out_specs=(VMEM,) * 5 + (ANY,) * 2,
        scratch_shapes=[
            wide[3],
            wide[3],
            pltpu.VMEM((row_count, width), bf16),
            pltpu.SemaphoreType.DMA((n_two + dp_count,)),
        ],
        compiler_params=params(32),
        cost_estimate=cost(1e9, 1e6),
        name="cross_attention_backward",
    )(ints, coarse_seg, gains, mlp_out, grad_second, own_b, came_a, came_b, joined, cotangent, crossed, cq, ckv, *arrays_two)
    state, grad_joined = fence((sum_mlp.state(), grad_joined))
    sum_mlp.put(state)

    sum_mlp.singles(upper)
    for mask in link_masks():
        sum_mlp.prepare(mask, lower)
    coarse_grad, grad_res, grad_att, gain_grads, keep_two, send_two = pl.pallas_call(
        functools.partial(third_part, (places_two, layout, dp_count, mirrors)),
        out_shape=(
            whole((coarse_rows, width), f32),
            whole((row_count, width), f32),
            whole((row_count, width), bf16),
            whole((8, width), f32),
            whole((pairs, rows_two, width), bf16),
            whole((pairs, rows_two, width), bf16),
        ),
        in_specs=[SMEM] + [VMEM] * 8 + [ANY] * (2 + len(arrays_two)),
        out_specs=(VMEM,) * 4 + (ANY,) * 2,
        scratch_shapes=[
            wide[0],
            wide[1],
            wide[2],
            wide[0],
            wide[1],
            wide[2],
            pltpu.VMEM((row_count, width), bf16),
            pltpu.SemaphoreType.DMA((n_two,)),
        ],
        input_output_aliases={9: 4, 10: 5},
        compiler_params=params(),
        cost_estimate=cost(1e9, 1e6),
        name="cross_attention_weights",
    )(
        ints, coarse_view, gains, gain_two, grad_joined, residual, attended, grad_cq, grad_ckv, keep_two, send_two, *arrays_two
    )

    state, grad_att, keep_two, send_two = fence((sum_mlp.state(), grad_att, keep_two, send_two))
    sum_mlp.put(state)

    sum_mlp.singles(lower)
    came_two = swap(send_two, CORE)
    def attention_back(first, last, held):
        count = last - first
        return pl.pallas_call(
            functools.partial(fourth_kernel, (blocks, first, last)),
            out_shape=whole((row_count, 3 * width), bf16),
            in_specs=[SMEM] + [VMEM] * 3 + [ANY] * len(held),
            out_specs=ANY,
            scratch_shapes=[pltpu.VMEM((row_count, PAIR), bf16)] * (3 * count)
            + [pltpu.VMEM((row_count, PAIR), f32)] * (2 * count)
            + [pltpu.SemaphoreType.DMA((3 * count,))],
            input_output_aliases={4: 0} if held else {},
            compiler_params=params(32),
            cost_estimate=cost(1e9, 1e6),
            name="self_attention_backward",
        )(ints, seg_row, grad_att, qkv, *held)

    inner_mlp = [InnerSum(sum_mlp.result(0).reshape(fsdp_count, up_part, width))]
    inner_mlp[0].step()
    grad_proj = attention_back(0, HEADS // 2, ())
    state, came_two, grad_proj, inner_mlp[0].came = fence((sum_mlp.state(), came_two, grad_proj, inner_mlp[0].came))
    sum_mlp.put(state)

    sum_two = OuterSum(keep_two, came_two)
    sum_two.relays()
    sum_two.singles(masks=link_masks()[-1:])
    inner_mlp.append(InnerSum(sum_mlp.result(1).reshape(fsdp_count, up_part, width)))
    inner_mlp[1].step()
    keep_one, send_one = pl.pallas_call(
        functools.partial(sixth_kernel, (dp_count, places_one, qkv_rows, mirrors)),
        out_shape=(
            whole((pairs, qkv_rows + 16, width), bf16),
            whole((pairs, qkv_rows + 16, width), bf16),
        ),
        in_specs=[SMEM] + [VMEM] * 4 + [ANY] * len(arrays_one),
        out_specs=(ANY,) * 2,
        scratch_shapes=[
            pltpu.VMEM((3 * width, width), bf16),
            pltpu.VMEM((3 * width, width), bf16),
            pltpu.VMEM((16, width), bf16),
            pltpu.SemaphoreType.DMA((len(arrays_one) + 2 * dp_count,)),
        ],
        compiler_params=params(),
        cost_estimate=cost(1e9, 1e6),
        name="self_attention_weights",
    )(ints, gains, gain_grads, blended, grad_proj, *arrays_one)
    state, keep_one, send_one, inner_mlp[1].came = fence((sum_two.state(), keep_one, send_one, inner_mlp[1].came))
    sum_two.put(state)

    sum_two.singles(masks=link_masks()[:-1])
    came_one = swap(send_one, CORE)
    base, going_tok = pl.pallas_call(
        functools.partial(fifth_kernel, (dp_count, blocks, places_one, qkv_rows, mirrors)),
        out_shape=(
            whole((row_count, width), f32),
            whole((row_count, width), bf16),
        ),
        in_specs=[SMEM, SMEM] + [VMEM] * 4 + [ANY] * len(arrays_one),
        out_specs=(VMEM,) * 2,
        scratch_shapes=[
            pltpu.VMEM((3 * width, width), bf16),
            pltpu.SemaphoreType.DMA((len(arrays_one),)),
        ],
        compiler_params=params(),
        cost_estimate=cost(1e9, 1e6),
        name="self_attention_input",
    )(ints, mix_weight, gains, blended, grad_res, grad_proj, *arrays_one)
    state, came_one, going_tok = fence((sum_two.state(), came_one, going_tok))
    sum_two.put(state)

    sum_one = OuterSum(keep_one, came_one)
    sum_one.relays()
    came_tok = swap(going_tok, CORE)
    placed = pl.pallas_call(
        functools.partial(place_kernel, (blocks, mirrors)),
        out_shape=whole((pairs, row_count, width), bf16),
        in_specs=[SMEM, SMEM] + [VMEM] * 2,
        out_specs=VMEM,
        compiler_params=params(32),
        cost_estimate=cost(1e9, 1e6),
        name="place_partner_gradients",
    )(ints, ints_near, going_tok, came_tok)
    mlp_parts = jnp.concatenate([inner_parts(inner) for inner in inner_mlp], axis=1)
    inner_mlp = InnerSum(mlp_parts)
    inner_mlp.finish()
    state, placed, mlp_came = fence((sum_one.state(), placed, inner_mlp.came))
    sum_one.put(state)
    inner_mlp.came = mlp_came

    sum_one.singles()
    sum_tok = OuterSum(placed)
    sum_tok.relays()
    two_sum = sum_two.result()
    two_parts = jnp.concatenate(
        [two_sum[first : first + size].reshape(fsdp_count, size // fsdp_count, width) for first, size in layout], axis=1
    )
    inner_two = InnerSum(two_parts)
    inner_two.step()
    state, state_tok, two_came = fence((sum_one.state(), sum_tok.state(), inner_two.came))
    sum_one.put(state)
    sum_tok.put(state_tok)
    inner_two.came = two_came

    sum_tok.singles()
    one_sum = sum_one.result()
    gain_sum = jnp.broadcast_to(one_sum[qkv_rows : qkv_rows + 8][None], (fsdp_count, 8, width))
    one_parts = jnp.concatenate([one_sum[:qkv_rows].reshape(fsdp_count, qkv_part, width), gain_sum], axis=1)
    inner_one = InnerSum(one_parts)
    inner_one.step()
    one_mine = inner_one.result()
    mlp_mine = inner_mlp.result()
    up_shard, down_shard = mlp_mine[:up_part].T, mlp_mine[up_part:]
    two_mine = inner_two.result()
    found = []
    at = 0
    for size in sizes_two:
        found.append(two_mine[at : at + size])
        at += size
    ckv_shard, out_shard, cq_shard, cout_shard = found[0].T, found[1], found[2], found[3]
    qkv_shard = one_mine[:qkv_part].T
    gain_mine = lax.dynamic_slice(one_mine[qkv_part:], (0, device_me * part), (3, part))
    token_grad = base + sum_tok.result()
    return (
        output,
        token_grad,
        coarse_grad,
        gain_mine[0],
        qkv_shard,
        out_shard,
        gain_mine[1],
        cq_shard,
        ckv_shard,
        cout_shard,
        gain_mine[2],
        up_shard,
        down_shard,
    )


def solution(mesh):
    rows = P(("dp", "fsdp"), None)
    columns = P(None, ("dp", "fsdp"))
    line = P(("dp", "fsdp"))
    in_specs = (
        rows, rows, rows, rows, line, line, line, columns, rows,
        line, rows, columns, rows, line, columns, rows, rows,
    )
    out_specs = (
        rows, rows, rows, line, columns, rows, line, rows, columns, rows, line, columns, rows,
    )
    return jax.shard_map(shards, mesh=mesh, in_specs=in_specs, out_specs=out_specs, check_vma=False)
```

```python
import functools

import jax
import jax.numpy as jnp
from jax import lax
from jax.experimental import pallas as pl
from jax.experimental.pallas import tpu as pltpu
from jax.sharding import PartitionSpec as P

HEADS = 12
HEAD = 64
PAIR = 2 * HEAD
CORE = 1
CLIP = 128
WINDOW = 256
TILE = 256
f32 = jnp.float32
bf16 = jnp.bfloat16
fence = lax.optimization_barrier


def swap(values, mask):
    count = lax.axis_size("dp")
    return lax.ppermute(values, "dp", [(i, i ^ mask) for i in range(count)])


def shift(values, step):
    count = lax.axis_size("fsdp")
    return lax.ppermute(values, "fsdp", [(i, (i + step) % count) for i in range(count)])


def link_masks():
    masks = []
    mask = 2
    while mask < lax.axis_size("dp"):
        masks.append(mask)
        mask *= 2
    return masks


def inner_swap(values, mask):
    count = lax.axis_size("fsdp")
    return lax.ppermute(values, "fsdp", [(i, i ^ mask) for i in range(count)])


def inner_double(held, mask):
    return inner_join(held, inner_swap(held, mask), mask)


def inner_join(held, came, mask):
    high = (lax.axis_index("fsdp") & mask) != 0
    return jnp.concatenate([jnp.where(high, came, held), jnp.where(high, held, came)])


def inner_rest(held):
    while held.shape[0] < lax.axis_size("fsdp"):
        held = inner_double(held, held.shape[0])
    return held


def inner_start(shard):
    return [shard] + [shift(shard, step) for step in range(1, lax.axis_size("fsdp"))]


def inner_order(came):
    count = len(came)
    me = lax.axis_index("fsdp")
    line = [came[count - 1 - k] for k in range(count)] + [came[count - k] for k in range(1, count)]
    return lax.dynamic_slice_in_dim(jnp.stack(line), count - 1 - me, count, 0)


def mirrored(role):
    masks = link_masks()
    return sum(masks[len(masks) - 1 - i] for i, mask in enumerate(masks) if role & mask)


def step_along(values, mask):
    count = lax.axis_size("dp")
    return lax.ppermute(values, "dp", [(i, i ^ (mirrored(mask) if i & CORE else mask)) for i in range(count)])


def top_bit(role):
    return 1 << (role.bit_length() - 1)


def relayed_roles():
    found = [role for role in range(2, lax.axis_size("dp"), 2) if role & (role - 1)]
    return sorted(found, key=lambda role: bin(role).count("1"))


def device_of(me, role, mirrors):
    holder = me ^ (role & CORE)
    link = role & ~CORE
    return holder ^ (link + lax.rem(holder, 2) * (mirrors[link] - link))


def mirror_table():
    return {role: mirrored(role) for role in range(0, lax.axis_size("dp"), 2)}


def single_steps(block):
    return {mask: step_along(block, mask) for mask in link_masks()}


def relay_steps(held):
    for role in relayed_roles():
        held[role] = step_along(held[role ^ top_bit(role)], top_bit(role))


def parts_of(pieces, total):
    return [pieces[e] for e in sorted(pieces)], tuple((e, 0, total) for e in sorted(pieces))


def core_steps(held):
    return {**held, **{e | CORE: swap(block, CORE) for e, block in held.items()}}


def inner_parts(inner):
    inner.add()
    return inner.parts


def add_low(a, b):
    return (a.astype(f32) + b.astype(f32)).astype(bf16)


class OuterSum:
    def __init__(self, *parts):
        self.parts = {2 * g: [part[g] for part in parts] for g in range(lax.axis_size("dp") // 2)}
        self.came = []
        self.ready = {}

    def prepare(self, role, rows=slice(None)):
        self.ready[role, rows.start] = self.value(role, rows).astype(bf16)

    def going(self, role, rows):
        return self.ready[role, rows.start] if (role, rows.start) in self.ready else self.value(role, rows).astype(bf16)

    def value(self, role, rows=slice(None)):
        total = self.parts[role][0][rows].astype(f32)
        for part in self.parts[role][1:]:
            total = total + part[rows].astype(f32)
        return total

    def relays(self):
        for role in relayed_roles()[::-1]:
            came = step_along(self.value(role).astype(bf16), top_bit(role))
            self.parts[role ^ top_bit(role)].append(came)

    def singles(self, rows=slice(None), masks=None):
        self.came.append((rows, [step_along(self.going(mask, rows), mask) for mask in masks or link_masks()]))

    def result(self, index=None):
        found = {}
        for rows, blocks in self.came:
            found.setdefault(rows.start, (rows, []))[1].extend(blocks)
        chosen = list(found.values())
        sums = []
        for rows, blocks in chosen if index is None else [chosen[index]]:
            total = self.value(0, rows)
            for block in blocks:
                total = total + block.astype(f32)
            sums.append(total)
        return sums[0] if len(sums) == 1 else jnp.concatenate(sums)

    def state(self):
        return (self.parts, [blocks for _, blocks in self.came], list(self.ready.values()))

    def put(self, state):
        self.parts = state[0]
        self.ready = dict(zip(self.ready, state[2]))
        self.came = [(rows, blocks) for (rows, _), blocks in zip(self.came, state[1])]


class InnerSum:
    def __init__(self, parts):
        self.parts = parts
        self.came = None
        self.mask = parts.shape[0]

    def step(self):
        self.add()
        self.mask //= 2
        bit = ((lax.axis_index("fsdp") & self.mask) != 0).astype(jnp.int32)
        halves = self.parts.reshape((2, self.mask) + self.parts.shape[1:])
        self.parts = lax.dynamic_index_in_dim(halves, bit, 0, keepdims=False)
        going = lax.dynamic_index_in_dim(halves, 1 - bit, 0, keepdims=False).astype(bf16)
        self.came = inner_swap(going, self.mask)

    def finish(self, steps=None):
        while self.mask > 1:
            self.step()

    def add(self):
        if self.came is not None:
            self.parts = self.parts + self.came.astype(f32)
            self.came = None

    def result(self):
        self.finish()
        self.add()
        return self.parts[0]


def nn(a, b):
    return jnp.dot(a, b, preferred_element_type=f32)


def nt(a, b):
    return lax.dot_general(a, b, (((1,), (1,)), ((), ())), preferred_element_type=f32)


def tn(a, b):
    return lax.dot_general(a, b, (((0,), (0,)), ((), ())), preferred_element_type=f32)


def tiles(size):
    step = TILE if size % TILE == 0 else size
    return [(at, step) for at in range(0, size, step)]


def centred(values):
    centre = jnp.mean(values, axis=-1, keepdims=True)
    shifted = values - centre
    spread = jnp.mean(shifted * shifted, axis=-1, keepdims=True)
    r = lax.rsqrt(spread + 1e-06)
    return shifted * r, r


def norm_back(xhat, r, gain, grad):
    c = grad * gain
    first = jnp.mean(c, axis=-1, keepdims=True)
    second = jnp.mean(c * xhat, axis=-1, keepdims=True)
    return r * (c - first - xhat * second), jnp.sum(grad * xhat, axis=0, keepdims=True)


def lower_half(rows):
    return lax.broadcasted_iota(jnp.int32, (rows, PAIR), 1) < HEAD


def two_heads(rows):
    keep = lower_half(rows.shape[0])
    zero = jnp.zeros_like(rows)
    return jnp.concatenate([jnp.where(keep, rows, zero), jnp.where(keep, zero, rows)], axis=0)


def side_by_side(stacked):
    rows = stacked.shape[0] // 2
    return jnp.where(lower_half(rows), stacked[:rows], stacked[rows:])


def softmax_rows(scores):
    raised = jnp.exp(scores - jnp.max(scores, axis=-1, keepdims=True))
    return raised / jnp.sum(raised, axis=-1, keepdims=True)


def bias_of(key_seg, own_seg):
    return jnp.where(key_seg == own_seg, 0.0, -1e30).astype(f32)


def block_bias(key_seg, ints, blocks):
    return jnp.stack([bias_of(key_seg[...], ints[1 + 3 * blocks + i]) for i in range(blocks)])


def biased(scores, bias):
    blocks, _, keys = bias.shape
    rows = scores.shape[0] // (2 * blocks)
    return (scores.reshape(2, blocks, rows, keys) + bias[None]).reshape(scores.shape)


def copies(jobs, sems, at):
    made = [pltpu.make_async_copy(src, dst, sems.at[at + i]) for i, (src, dst) in enumerate(jobs)]
    for job in made:
        job.start()
    return made


def whole(shape, dtype):
    return jax.ShapeDtypeStruct(shape, dtype)


VMEM = pl.BlockSpec(memory_space=pltpu.VMEM)
SMEM = pl.BlockSpec(memory_space=pltpu.SMEM)
ANY = pl.BlockSpec(memory_space=pl.ANY)


def params(mib=56):
    return pltpu.CompilerParams(vmem_limit_bytes=mib * 1024 * 1024)


def cost(flops, moved, exps=0):
    return pl.CostEstimate(flops=int(flops), bytes_accessed=int(moved), transcendentals=int(exps))


def first_kernel(
    geometry, ints, mix, seg_row, tokens, *refs
):
    dp_count, blocks, token_places, qkv_places, qkv_rows, mirrors = geometry
    n_tok, n_qkv = len(token_places), len(qkv_places)
    token_refs, qkv_refs = refs[:n_tok], refs[n_tok : n_tok + n_qkv]
    blended_ref, qkv_ref, attended_ref, gains_ref, partner, weight, gain_parts, sems = refs[n_tok + n_qkv :]
    me = ints[0]
    width = tokens.shape[1]

    for b in range(blocks):
        holder, slot = ints[1 + b], ints[1 + blocks + b]
        for ref, (role, _, rows) in zip(token_refs, token_places):

            @pl.when(holder == device_of(me, role, mirrors))
            def _(ref=ref, rows=rows, b=b, slot=slot):
                at = pl.multiple_of(slot * CLIP, CLIP)
                pltpu.make_async_copy(ref.at[pl.ds(at, CLIP)], partner.at[b], sems.at[b]).start()

    jobs = []
    for ref, (e, start, rows) in zip(qkv_refs, qkv_places):
        take = min(rows, qkv_rows - start)
        at = pl.multiple_of(device_of(me, e, mirrors) * qkv_rows + start, 16)
        jobs.append((ref.at[pl.ds(0, take)], weight.at[pl.ds(at, take)]))
        if start + rows > qkv_rows:
            jobs.append((ref.at[pl.ds(take, rows - take)], gain_parts.at[e]))
    made = copies(jobs, sems, blocks)
    for b in range(blocks):
        pltpu.make_async_copy(tokens.at[pl.ds(0, CLIP)], partner.at[b], sems.at[b]).wait()
    for b in range(blocks):
        rows = slice(b * CLIP, (b + 1) * CLIP)
        share = mix[b]
        blended_ref[rows, :] = share * tokens[rows, :].astype(f32) + (1.0 - share) * partner[b].astype(f32)
    for job in made:
        job.wait()
    gains = gain_parts[0].astype(f32)
    for e in range(1, dp_count):
        gains = gains + gain_parts[e].astype(f32)
    gains_ref[...] = gains[:8]
    xhat, _ = centred(blended_ref[...])
    normed = (xhat * gains[0:1]).astype(bf16)
    for at, step in tiles(3 * width):
        tile = nt(normed, weight[at : at + step, :])
        if at + step <= width:
            tile = tile * 0.125
        qkv_ref[:, at : at + step] = tile.astype(bf16)

    @pl.loop(0, blocks)
    def _(i):
        window = pl.multiple_of(ints[1 + 2 * blocks + i] * CLIP, CLIP)
        bias = bias_of(seg_row[:, pl.ds(window, WINDOW)], ints[1 + 3 * blocks + i])
        rows = pl.ds(pl.multiple_of(i * CLIP, CLIP), CLIP)
        keys = pl.ds(window, WINDOW)
        for at in range(0, width, PAIR):
            queries = two_heads(qkv_ref[rows, at : at + PAIR])
            probs = softmax_rows(nt(queries, qkv_ref[keys, width + at : width + at + PAIR]) + bias).astype(bf16)
            out = nn(probs, qkv_ref[keys, 2 * width + at : 2 * width + at + PAIR])
            attended_ref[rows, at : at + PAIR] = side_by_side(out).astype(bf16)


def load_cross(me, refs, places, layout, weights, sems, mirrors):
    jobs = []
    for ref, (e, start, rows) in zip(refs, places):
        for (first, size), weight in zip(layout, weights):
            if weight is not None and first >= start and first + size <= start + rows:
                at = pl.multiple_of(device_of(me, e, mirrors) * size, 16)
                jobs.append((ref.at[pl.ds(first - start, size)], weight.at[pl.ds(at, size)]))
    return copies(jobs, sems, 0)


def second_kernel(geometry, ints, coarse_seg, coarse, blended, attended, gains, *refs):
    blocks, places, layout, mirrors = geometry
    weight_refs = refs[: len(places)]
    residual_ref, cq_ref, ckv_ref, crossed_ref, joined_ref, second_ref = refs[len(places) : len(places) + 6]
    w_ckv, w_out, w_cq, w_cout, sems = refs[len(places) + 6 :]
    made = load_cross(ints[0], weight_refs, places, layout, (w_ckv, w_out, w_cq, w_cout), sems, mirrors)
    for job in made:
        job.wait()
    width = blended.shape[1]
    for at, step in tiles(2 * width):
        ckv_ref[:, at : at + step] = nt(coarse[...], w_ckv[at : at + step, :]).astype(bf16)
    for at, step in tiles(width):
        residual_ref[:, at : at + step] = blended[:, at : at + step] + nn(attended[...], w_out[:, at : at + step])
    xhat, _ = centred(residual_ref[...])
    crossed_in = (xhat * gains[1:2]).astype(bf16)
    for at, step in tiles(width):
        cq_ref[:, at : at + step] = (nn(crossed_in, w_cq[:, at : at + step]) * 0.125).astype(bf16)

    bias = block_bias(coarse_seg, ints, blocks)
    for at in range(0, width, PAIR):
        queries = two_heads(cq_ref[:, at : at + PAIR])
        probs = softmax_rows(biased(nt(queries, ckv_ref[:, at : at + PAIR]), bias)).astype(bf16)
        out = nn(probs, ckv_ref[:, width + at : width + at + PAIR])
        crossed_ref[:, at : at + PAIR] = side_by_side(out).astype(bf16)

    for at, step in tiles(width):
        joined_ref[:, at : at + step] = residual_ref[:, at : at + step] + nn(crossed_ref[...], w_cout[:, at : at + step])
    xhat, _ = centred(joined_ref[...])
    second_ref[...] = (xhat * gains[2:3]).astype(bf16)


def mlp_kernel(geometry, second, second_near, cotangent, cotangent_near, *refs):
    groups, places, rows, last = geometry
    weight_refs = refs[: len(places)]
    refs = refs[len(places) :]
    keep_ref, going_ref = refs[:2]
    if last:
        own_ref = refs[2]
        sums = refs[3:7]
        refs = refs[7:]
    else:
        sums = refs[2:6]
        refs = refs[6:]
    w_up, w_down, hidden, grad_pre, sems = refs
    step = pl.program_id(0)

    def jobs_of(group):
        jobs = []
        for ref, (e, which) in zip(weight_refs, places):
            if e == groups[group]:
                for part, weight in ((0, w_up), (1, w_down)):
                    if which is None or which == part:
                        first = part * rows if which is None else 0
                        jobs.append((ref.at[pl.ds(first, rows)], weight.at[group]))
        return jobs

    at = 0
    for group in range(len(groups)):
        jobs = jobs_of(group)
        made = [pltpu.make_async_copy(s, d, sems.at[at + i]) for i, (s, d) in enumerate(jobs)]
        at += len(jobs)

        @pl.when(step == 0)
        def _(made=made):
            for job in made:
                job.start()

        @pl.when(step == group)
        def _(made=made):
            for job in made:
                job.wait()

    @pl.when(step == 0)
    def _():
        for ref in sums:
            ref[...] = jnp.zeros_like(ref)

    up, down = w_up.at[step], w_down.at[step]
    for half, (inputs, upstream) in enumerate(((second, cotangent), (second_near, cotangent_near))):
        pre = nt(inputs[...], up[...])
        grad_hidden = nt(upstream[...], down[...])
        cdf = 0.5 * (1.0 + lax.erf(pre * 0.7071067811865476))
        slope = cdf + pre * (jnp.exp(-0.5 * pre * pre) * 0.3989422804014327)
        hidden[half] = (pre * cdf).astype(bf16)
        grad_pre[half] = (grad_hidden * slope).astype(bf16)
        for first, size in tiles(second.shape[1]):
            columns = slice(first, first + size)
            sums[2 * half][:, columns] += nn(hidden[half], down[:, columns])
            sums[2 * half + 1][:, columns] += nn(grad_pre[half], up[:, columns])
    keep_ref[0, 0] = (tn(grad_pre[0], second[...]) + tn(grad_pre[1], second_near[...])).astype(bf16)
    keep_ref[0, 1] = (tn(hidden[0], cotangent[...]) + tn(hidden[1], cotangent_near[...])).astype(bf16)

    @pl.when(step == len(groups) - 1)
    def _():
        going_ref[0] = sums[2][...].astype(bf16)
        going_ref[1] = sums[3][...].astype(bf16)
        if last:
            own_ref[0] = sums[0][...].astype(bf16)
            own_ref[1] = sums[1][...].astype(bf16)


def grads_out(me, dp_count, layout, sources, keep_ref, send_ref, sems, at, mirrors):
    jobs = []
    for e in range(dp_count):
        target = send_ref if e & CORE else keep_ref
        for (first, size), source in zip(layout, sources):
            if source is None:
                continue
            row = pl.multiple_of(device_of(me, e, mirrors) * size, 16)
            jobs.append((source.at[pl.ds(row, size)], target.at[e // 2, pl.ds(first, size)]))
    return copies(jobs, sems, at)


def third_kernel(
    geometry, ints, coarse_seg, gains, mlp_out, grad_second, own_b, came_a, came_b, joined, cotangent, crossed, cq, ckv, *refs
):
    blocks, places, layout, dp_count, mirrors = geometry
    weight_refs = refs[: len(places)]
    refs = refs[len(places) :]
    output_ref, grad_joined_ref, grad_cq_ref, grad_ckv_ref, gain_grads_ref, keep_ref, send_ref = refs[:7]
    w_cout, g_cout, grad_cross, sems = refs[7:]
    me = ints[0]
    width = joined.shape[1]
    made = load_cross(me, weight_refs, places, layout, (None, None, None, w_cout), sems, mirrors)
    rest = [own_b[i].astype(f32) + came_a[i].astype(f32) + came_b[i].astype(f32) for i in range(2)]
    output_ref[...] = (joined[...] + (mlp_out[...] + rest[0])).astype(bf16)
    xhat, r = centred(joined[...])
    grad_in, gain_two = norm_back(xhat, r, gains[2:3], grad_second[...] + rest[1])
    grad_joined_ref[...] = cotangent[...].astype(f32) + grad_in
    low = grad_joined_ref[...].astype(bf16)
    for job in made:
        job.wait()
    for at, step in tiles(width):
        grad_cross[:, at : at + step] = nt(low, w_cout[at : at + step, :]).astype(bf16)
    for at, step in tiles(width):
        g_cout[at : at + step, :] = tn(crossed[:, at : at + step], low).astype(bf16)
    going = grads_out(me, dp_count, layout, (None, None, None, g_cout), keep_ref, send_ref, sems, len(made), mirrors)
    bias = block_bias(coarse_seg, ints, blocks)
    for at in range(0, width, PAIR):
        lanes = slice(at, at + PAIR)
        queries = two_heads(cq[:, lanes])
        grads = two_heads(grad_cross[:, lanes])
        keys = ckv[:, lanes]
        values = ckv[:, width + at : width + at + PAIR]
        probs = softmax_rows(biased(nt(queries, keys), bias))
        grad_ckv_ref[:, width + at : width + at + PAIR] = tn(probs.astype(bf16), grads).astype(bf16)
        grad_probs = nt(grads, values)
        inner = jnp.sum(probs * grad_probs, axis=-1, keepdims=True)
        scores = (probs * (grad_probs - inner)).astype(bf16)
        part = side_by_side(nn(scores, keys)).astype(bf16)
        grad_cq_ref[:, lanes] = part * jnp.asarray(0.125, bf16)
        grad_ckv_ref[:, lanes] = tn(scores, queries).astype(bf16)

    gain_grads_ref[...] = jnp.concatenate([gain_two] * 8, axis=0)
    for job in going:
        job.wait()


def third_part(geometry, ints, coarse, gains, gain_two, grad_joined, residual, attended, grad_cq, grad_ckv, keep_in, send_in, *refs):
    places, layout, dp_count, mirrors = geometry
    weight_refs = refs[: len(places)]
    refs = refs[len(places) :]
    coarse_ref, grad_res_ref, grad_att_ref, gain_grads_ref, keep_ref, send_ref = refs[:6]
    w_ckv, w_out, w_cq, g_ckv, g_out, g_cq, crossed_in, sems = refs[6:]
    me = ints[0]
    width = residual.shape[1]
    made = load_cross(me, weight_refs, places, layout, (w_ckv, w_out, w_cq, None), sems, mirrors)
    xhat, r = centred(residual[...])
    crossed_in[...] = (xhat * gains[1:2]).astype(bf16)
    for at, step in tiles(width):
        g_cq[at : at + step, :] = tn(crossed_in[:, at : at + step], grad_cq[...]).astype(bf16)
    for at, step in tiles(2 * width):
        g_ckv[at : at + step, :] = tn(grad_ckv[:, at : at + step], coarse[...]).astype(bf16)
    for job in made:
        job.wait()
    going = grads_out(me, dp_count, layout, (g_ckv, None, g_cq, None), keep_ref, send_ref, sems, 0, mirrors)
    for at, step in tiles(width):
        coarse_ref[:, at : at + step] = nn(grad_ckv[:, 0:width], w_ckv[0:width, at : at + step]) + nn(
            grad_ckv[:, width : 2 * width], w_ckv[width : 2 * width, at : at + step]
        )
    pieces = [nt(grad_cq[...], w_cq[at : at + step, :]) for at, step in tiles(width)]
    grad_in, gain_cross = norm_back(xhat, r, gains[1:2], jnp.concatenate(pieces, axis=1))
    grad_res = grad_joined[...] + grad_in
    grad_res_ref[...] = grad_res
    low = grad_res.astype(bf16)
    for at, step in tiles(width):
        g_out[at : at + step, :] = tn(attended[:, at : at + step], low).astype(bf16)
    going += grads_out(me, dp_count, layout, (None, g_out, None, None), keep_ref, send_ref, sems, len(going), mirrors)
    for at, step in tiles(width):
        grad_att_ref[:, at : at + step] = nt(low, w_out[at : at + step, :]).astype(bf16)
    zero = jnp.zeros_like(gain_cross)
    gain_grads_ref[...] = jnp.concatenate([zero, gain_cross, gain_two[0:1]] + [zero] * 5, axis=0)
    for job in going:
        job.wait()


def fourth_kernel(geometry, ints, seg_row, grad_att, qkv, *refs):
    blocks, first, last = geometry
    count = last - first
    grad_proj, sems = refs[-1 - 5 * count - 1], refs[-1]
    scratch = refs[-1 - 5 * count : -1]
    query_part, key_part, value_part, key_sum, value_sum = [scratch[i * count : (i + 1) * count] for i in range(5)]
    width = grad_att.shape[1]
    for ref in key_sum + value_sum:
        ref[...] = jnp.zeros_like(ref)

    @pl.loop(0, blocks)
    def _(i):
        window = pl.multiple_of(ints[1 + 2 * blocks + i] * CLIP, CLIP)
        bias = bias_of(seg_row[:, pl.ds(window, WINDOW)], ints[1 + 3 * blocks + i])
        rows = pl.ds(pl.multiple_of(i * CLIP, CLIP), CLIP)
        near = pl.ds(window, WINDOW)
        for pair in range(count):
            at = (first + pair) * PAIR
            queries = two_heads(qkv[rows, at : at + PAIR])
            grads = two_heads(grad_att[rows, at : at + PAIR])
            keys = qkv[near, width + at : width + at + PAIR]
            values = qkv[near, 2 * width + at : 2 * width + at + PAIR]
            probs = softmax_rows(nt(queries, keys) + bias)
            grad_probs = nt(grads, values)
            inner = jnp.sum(probs * grad_probs, axis=-1, keepdims=True)
            scores = (probs * (grad_probs - inner)).astype(bf16)
            part = side_by_side(nn(scores, keys)).astype(bf16)
            query_part[pair][rows, :] = part * jnp.asarray(0.125, bf16)
            value_sum[pair][near, :] += tn(probs.astype(bf16), grads)
            key_sum[pair][near, :] += tn(scores, queries)

    jobs = []
    for pair in range(count):
        key_part[pair][...] = key_sum[pair][...].astype(bf16)
        value_part[pair][...] = value_sum[pair][...].astype(bf16)
        for i, part in enumerate((query_part, key_part, value_part)):
            jobs.append((part[pair], grad_proj.at[:, pl.ds(i * width + (first + pair) * PAIR, PAIR)]))
    for job in copies(jobs, sems, 0):
        job.wait()


def fifth_kernel(geometry, ints, mix, gains, blended, grad_res, grad_proj, *refs):
    dp_count, blocks, qkv_places, qkv_rows, mirrors = geometry
    weight_refs = refs[: len(qkv_places)]
    refs = refs[len(qkv_places) :]
    base_ref, going_ref = refs[:2]
    weight, sems = refs[2:]
    me = ints[0]
    width = blended.shape[1]
    jobs = []
    for ref, (e, start, rows) in zip(weight_refs, qkv_places):
        take = min(rows, qkv_rows - start)
        at = pl.multiple_of(device_of(me, e, mirrors) * qkv_rows + start, 16)
        jobs.append((ref.at[pl.ds(0, take)], weight.at[pl.ds(at, take)]))
    made = copies(jobs, sems, 0)
    xhat, r = centred(blended[...])
    for job in made:
        job.wait()
    pieces = [nn(grad_proj[...], weight[:, at : at + step]) for at, step in tiles(width)]
    grad_in, _ = norm_back(xhat, r, gains[0:1], jnp.concatenate(pieces, axis=1))
    grad_blend = grad_res[...] + grad_in
    for b in range(blocks):
        rows = slice(b * CLIP, (b + 1) * CLIP)
        share = mix[b]
        part = grad_blend[rows, :]
        base_ref[rows, :] = share * part
        going_ref[rows, :] = ((1.0 - share) * part).astype(bf16)


def place_kernel(geometry, ints, ints_near, blocks_own, blocks_near, out_ref):
    blocks, mirrors = geometry
    me = ints[0]
    out_ref[...] = jnp.zeros_like(out_ref)
    for table, first, source in ((ints, 1, blocks_own), (ints_near, 0, blocks_near)):
        for b in range(blocks):
            holder, slot = table[first + b], table[first + blocks + b]
            group = jnp.int32(0)
            for role in mirrors:
                group = group + jnp.where(device_of(me, role, mirrors) == holder, role // 2, 0)

            @pl.when(lax.rem(holder, 2) == lax.rem(me, 2))
            def _(group=group, slot=slot, source=source, b=b):
                rows = pl.ds(pl.multiple_of(slot * CLIP, CLIP), CLIP)
                part = source[b * CLIP : (b + 1) * CLIP, :].astype(f32)
                out_ref[group, rows, :] = (out_ref[group, rows, :].astype(f32) + part).astype(bf16)


def sixth_kernel(geometry, ints, gains, gain_grads, blended, grad_proj, *refs):
    dp_count, qkv_places, qkv_rows, mirrors = geometry
    weight_refs = refs[: len(qkv_places)]
    keep_ref, send_ref, weight, grad_w, gain_rows, sems = refs[len(qkv_places) :]
    me = ints[0]
    width = blended.shape[1]
    jobs = []
    for ref, (e, start, rows) in zip(weight_refs, qkv_places):
        take = min(rows, qkv_rows - start)
        at = pl.multiple_of(device_of(me, e, mirrors) * qkv_rows + start, 16)
        jobs.append((ref.at[pl.ds(0, take)], weight.at[pl.ds(at, take)]))
    made = copies(jobs, sems, 0)
    xhat, _ = centred(blended[...])
    normed = (xhat * gains[0:1]).astype(bf16)
    for job in made:
        job.wait()
    gain_one = jnp.zeros((1, width), f32)
    for at, step in tiles(3 * width):
        part = tn(grad_proj[:, at : at + step], normed)
        gain_one = gain_one + jnp.sum(part * weight[at : at + step, :].astype(f32), axis=0, keepdims=True)
        grad_w[at : at + step, :] = part.astype(bf16)
    sent = grads_out(me, dp_count, ((0, qkv_rows),), (grad_w,), keep_ref, send_ref, sems, len(jobs), mirrors)
    all_gains = jnp.concatenate([gain_one / gains[0:1], gain_grads[1:8], jnp.zeros((8, width), f32)], axis=0)
    gain_rows[...] = all_gains.astype(bf16)
    last = []
    for e in range(dp_count):
        target = send_ref if e & CORE else keep_ref
        last.append((gain_rows, target.at[e // 2, pl.ds(qkv_rows, 16)]))
    for job in sent + copies(last, sems, len(jobs) + dp_count):
        job.wait()


def shards(
    tokens,
    coarse_view,
    segment_ids,
    partner_device,
    partner_slot,
    mix_weight,
    ln1_gain,
    w_qkv,
    w_out,
    lnx_gain,
    w_cq,
    w_ckv,
    w_cout,
    ln2_gain,
    w_up,
    w_down,
    cotangent,
):
    row_count, width = tokens.shape
    coarse_rows = coarse_view.shape[0]
    blocks = mix_weight.shape[0]
    dp_count, fsdp_count = lax.axis_size("dp"), lax.axis_size("fsdp")
    dp_me, fsdp_me = lax.axis_index("dp"), lax.axis_index("fsdp")
    part = ln1_gain.shape[0]
    device_me = dp_me * fsdp_count + fsdp_me
    pairs = dp_count // 2
    mirrors = mirror_table()

    target = partner_device[:, 0]
    segments = segment_ids[0]
    videos = segments.reshape(blocks, row_count // blocks)[:, 0]
    following = jnp.concatenate([videos[1:] == videos[:-1], jnp.zeros((1,), bool)])
    before = jnp.concatenate([jnp.zeros((1,), bool), videos[1:] == videos[:-1]])
    index = jnp.arange(blocks, dtype=jnp.int32)
    window = jnp.where(following, index, jnp.where(before, index - 1, jnp.minimum(index, blocks - 2)))
    ints = jnp.concatenate(
        [dp_me[None].astype(jnp.int32), target, partner_slot, window, videos]
    )
    ints_near = swap(ints[1 : 1 + 2 * blocks], CORE)
    seg_row = segments[None, :]
    coarse_seg = segments.reshape(coarse_rows, row_count // coarse_rows)[:, 0][None, :]

    gain_rows = lax.dynamic_update_slice(
        jnp.zeros((8, width), bf16), jnp.stack([ln1_gain, lnx_gain, ln2_gain]), (0, device_me * part)
    )
    shard_one = jnp.concatenate([w_qkv.T, gain_rows])
    shard_first = jnp.concatenate([shard_one, w_ckv.T])
    shard_rest = jnp.concatenate([w_out, w_cq, w_cout])
    shard_mlp = jnp.concatenate([w_up.T, w_down])
    sizes_two = (w_ckv.shape[1], w_out.shape[0], w_cq.shape[0], w_cout.shape[0])
    qkv_part, up_part = w_qkv.shape[1], w_up.shape[1]
    qkv_rows, up_rows = qkv_part * fsdp_count, up_part * fsdp_count
    layout = []
    at = 0
    for size in sizes_two:
        layout.append((at * fsdp_count, size * fsdp_count))
        at += size
    layout = tuple(layout)
    rows_two = at * fsdp_count

    held_tok = {0: tokens, **single_steps(tokens)}
    came_first = inner_start(shard_first)
    held_tok, came_first, shard_rest = fence((held_tok, came_first, shard_rest))

    firsts = inner_order(came_first)
    ones = firsts[:, : qkv_part + 8]
    gain_block = jnp.sum(ones[:, qkv_part:].astype(f32), axis=0).astype(bf16)
    block_one = jnp.concatenate(
        [ones[:, :qkv_part].reshape(qkv_rows, width), gain_block, jnp.zeros((8, width), bf16)]
    )
    held_one = {0: block_one, **single_steps(block_one)}
    came_rest = inner_start(shard_rest)
    held_tok, held_one, came_rest, shard_mlp, firsts = fence((held_tok, held_one, came_rest, shard_mlp, firsts))

    near_mlp = inner_swap(shard_mlp, 1)
    core_tok = core_steps(dict(held_tok))
    near_tok = set(held_tok)
    relay_steps(held_tok)
    rests = inner_order(came_rest)
    split = [firsts[:, qkv_part + 8 :].reshape(sizes_two[0] * fsdp_count, width)]
    at = 0
    for size in sizes_two[1:]:
        split.append(rests[:, at : at + size].reshape(size * fsdp_count, width))
        at += size
    block_two = jnp.concatenate(split)
    held_one, core_tok, held_tok, block_two, near_mlp = fence((held_one, core_tok, held_tok, block_two, near_mlp))

    cuts = (0, 5 * up_part // 12, 3 * up_part // 2, 2 * up_part)
    mlp_cut = [
        inner_join(shard_mlp[None, first:last], near_mlp[None, first:last], 1) for first, last in zip(cuts, cuts[1:])
    ]
    mlp_came = [inner_swap(mlp_cut[0], 2)]
    core_one = core_steps(dict(held_one))
    relay_steps(held_one)
    late_tok = core_steps({e: b for e, b in held_tok.items() if e not in near_tok})
    held_one, core_one, late_tok, block_two, mlp_cut, mlp_came = fence(
        (held_one, core_one, late_tok, block_two, mlp_cut, mlp_came)
    )

    held_two = {0: block_two, **single_steps(block_two)}
    cotangent_near = swap(cotangent, CORE)
    mlp_came.append(inner_swap(mlp_cut[1], 2))
    mlp_joined = [inner_rest(inner_join(mlp_cut[0], mlp_came[0], 2))]
    late_one = core_steps({e: b for e, b in held_one.items() if e not in near_tok})
    pieces_tok = {**core_tok, **late_tok}
    pieces_one = {**core_one, **late_one}
    arrays_tok, places_tok = parts_of(pieces_tok, row_count)
    arrays_one, places_one = parts_of(pieces_one, qkv_rows + 16)
    blended, qkv, attended, gains = pl.pallas_call(
        functools.partial(first_kernel, (dp_count, blocks, places_tok, places_one, qkv_rows, mirrors)),
        out_shape=(
            whole((row_count, width), f32),
            whole((row_count, 3 * width), bf16),
            whole((row_count, width), bf16),
            whole((8, width), f32),
        ),
        in_specs=[SMEM, SMEM, VMEM, VMEM] + [ANY] * (len(arrays_tok) + len(arrays_one)),
        out_specs=(VMEM,) * 4,
        scratch_shapes=[
            pltpu.VMEM((blocks, CLIP, width), bf16),
            pltpu.VMEM((3 * width, width), bf16),
            pltpu.VMEM((dp_count, 16, width), bf16),
            pltpu.SemaphoreType.DMA((blocks + len(arrays_one) + dp_count,)),
        ],
        compiler_params=params(),
        cost_estimate=cost(1e9, 1e6),
        name="mix_self_attention",
    )(ints, mix_weight, seg_row, tokens, *arrays_tok, *arrays_one)
    held_two, attended, mlp_came, cotangent_near, mlp_cut, mlp_joined = fence(
        (held_two, attended, mlp_came, cotangent_near, mlp_cut, mlp_joined)
    )

    core_two = core_steps(dict(held_two))
    relay_steps(held_two)
    mlp_came.append(inner_swap(mlp_cut[2], 2))
    mlp_joined.append(inner_rest(inner_join(mlp_cut[1], mlp_came[1], 2)))
    held_two, core_two, mlp_came, mlp_joined = fence((held_two, core_two, mlp_came, mlp_joined))

    mlp_joined.append(inner_rest(inner_join(mlp_cut[2], mlp_came[2], 2)))
    mlp = jnp.concatenate(mlp_joined, axis=1)
    block_mlp = jnp.concatenate([mlp[:, :up_part].reshape(up_rows, width), mlp[:, up_part:].reshape(up_rows, width)])
    held_mlp = {0: block_mlp, **single_steps(block_mlp)}
    late_two = core_steps({e: b for e, b in held_two.items() if e not in near_tok})
    pieces_two = {**core_two, **late_two}
    wide = [pltpu.VMEM((sizes * fsdp_count * dp_count, width), bf16) for sizes in sizes_two]
    n_two = 4 * dp_count
    arrays_two, places_two = parts_of(pieces_two, rows_two)
    wide = [pltpu.VMEM((sizes * fsdp_count * dp_count, width), bf16) for sizes in sizes_two]
    n_two = 4 * dp_count
    residual, cq, ckv, crossed, joined, second = pl.pallas_call(
        functools.partial(second_kernel, (blocks, places_two, layout, mirrors)),
        out_shape=(
            whole((row_count, width), f32),
            whole((row_count, width), bf16),
            whole((coarse_rows, 2 * width), bf16),
            whole((row_count, width), bf16),
            whole((row_count, width), f32),
            whole((row_count, width), bf16),
        ),
        in_specs=[SMEM] + [VMEM] * 5 + [ANY] * len(arrays_two),
        out_specs=(VMEM,) * 6,
        scratch_shapes=wide + [pltpu.SemaphoreType.DMA((n_two,))],
        compiler_params=params(),
        cost_estimate=cost(1e9, 1e6),
        name="cross_attention",
    )(ints, coarse_seg, coarse_view, blended, attended, gains, *arrays_two)
    second_near = swap(second, CORE)
    held_mlp, second, second_near, ints_near = fence((held_mlp, second, second_near, ints_near))

    early = dict(held_mlp)
    relay_steps(held_mlp)

    def mlp_call(pieces, last):
        groups = tuple(sorted(pieces))
        count = len(groups)
        fixed = pl.BlockSpec((row_count, width), lambda g: (0, 0))
        moving = pl.BlockSpec((1, 2, up_rows, width), lambda g: (g, 0, 0, 0))
        both = pl.BlockSpec((2, row_count, width), lambda g: (0, 0, 0))
        table = whole((row_count, width), f32)
        out_shape = [whole((count, 2, up_rows, width), bf16), whole((2, row_count, width), bf16)]
        out_specs = [moving, both]
        scratch = [pltpu.VMEM((row_count, width), f32)] * (4 if last else 2)
        if last:
            out_shape.append(whole((2, row_count, width), bf16))
            out_specs.append(both)
        else:
            out_shape += [table, table]
            out_specs += [fixed, fixed]
        made = pl.pallas_call(
            functools.partial(mlp_kernel, (groups, tuple((e, None) for e in groups), up_rows, last)),
            grid=(count,),
            out_shape=tuple(out_shape),
            in_specs=[fixed] * 4 + [ANY] * count,
            out_specs=tuple(out_specs),
            scratch_shapes=scratch
            + [
                pltpu.VMEM((count, up_rows, width), bf16),
                pltpu.VMEM((count, up_rows, width), bf16),
                pltpu.VMEM((2, row_count, up_rows), bf16),
                pltpu.VMEM((2, row_count, up_rows), bf16),
                pltpu.SemaphoreType.DMA((2 * count,)),
            ],
            compiler_params=params(32),
            cost_estimate=cost(1e9, 1e6),
            name="feed_forward",
        )(second, second_near, cotangent, cotangent_near, *[pieces[e] for e in groups])
        return groups, made[0].reshape(count, 2 * up_rows, width), made[1], made[2:]

    groups_a, keep_a, going_a, (mlp_out, grad_second) = mlp_call(early, False)
    late = {e: b for e, b in held_mlp.items() if e not in near_tok}
    late, keep_a, going_a, mlp_out, grad_second = fence((late, keep_a, going_a, mlp_out, grad_second))
    came_a = swap(going_a, CORE)
    groups_b, keep_b, going_b, (own_b,) = mlp_call(late, True)
    came_a, keep_b, going_b, own_b = fence((came_a, keep_b, going_b, own_b))
    came_b = swap(going_b, CORE)
    totals = [None] * pairs
    for groups, keep in ((groups_a, keep_a), (groups_b, keep_b)):
        for i, e in enumerate(groups):
            totals[e // 2] = keep[i]
    totals, came_b = fence((totals, came_b))

    sum_mlp = OuterSum(totals)
    upper, lower = slice(0, up_rows), slice(up_rows, 2 * up_rows)
    sum_mlp.relays()
    sum_mlp.prepare(link_masks()[-1], upper)
    output, grad_joined, grad_cq, grad_ckv, gain_two, keep_two, send_two = pl.pallas_call(
        functools.partial(third_kernel, (blocks, places_two, layout, dp_count, mirrors)),
        out_shape=(
            whole((row_count, width), bf16),
            whole((row_count, width), f32),
            whole((row_count, width), bf16),
            whole((coarse_rows, 2 * width), bf16),
            whole((8, width), f32),
            whole((pairs, rows_two, width), bf16),
            whole((pairs, rows_two, width), bf16),
        ),
        in_specs=[SMEM] + [VMEM] * 12 + [ANY] * len(arrays_two),
        out_specs=(VMEM,) * 5 + (ANY,) * 2,
        scratch_shapes=[
            wide[3],
            wide[3],
            pltpu.VMEM((row_count, width), bf16),
            pltpu.SemaphoreType.DMA((n_two + dp_count,)),
        ],
        compiler_params=params(32),
        cost_estimate=cost(1e9, 1e6),
        name="cross_attention_backward",
    )(ints, coarse_seg, gains, mlp_out, grad_second, own_b, came_a, came_b, joined, cotangent, crossed, cq, ckv, *arrays_two)
    state, grad_joined = fence((sum_mlp.state(), grad_joined))
    sum_mlp.put(state)

    sum_mlp.singles(upper)
    for mask in link_masks():
        sum_mlp.prepare(mask, lower)
    coarse_grad, grad_res, grad_att, gain_grads, keep_two, send_two = pl.pallas_call(
        functools.partial(third_part, (places_two, layout, dp_count, mirrors)),
        out_shape=(
            whole((coarse_rows, width), f32),
            whole((row_count, width), f32),
            whole((row_count, width), bf16),
            whole((8, width), f32),
            whole((pairs, rows_two, width), bf16),
            whole((pairs, rows_two, width), bf16),
        ),
        in_specs=[SMEM] + [VMEM] * 8 + [ANY] * (2 + len(arrays_two)),
        out_specs=(VMEM,) * 4 + (ANY,) * 2,
        scratch_shapes=[
            wide[0],
            wide[1],
            wide[2],
            wide[0],
            wide[1],
            wide[2],
            pltpu.VMEM((row_count, width), bf16),
            pltpu.SemaphoreType.DMA((n_two,)),
        ],
        input_output_aliases={9: 4, 10: 5},
        compiler_params=params(),
        cost_estimate=cost(1e9, 1e6),
        name="cross_attention_weights",
    )(
        ints, coarse_view, gains, gain_two, grad_joined, residual, attended, grad_cq, grad_ckv, keep_two, send_two, *arrays_two
    )

    state, grad_att, keep_two, send_two = fence((sum_mlp.state(), grad_att, keep_two, send_two))
    sum_mlp.put(state)

    sum_mlp.singles(lower)
    came_two = swap(send_two, CORE)
    def attention_back(first, last, held):
        count = last - first
        return pl.pallas_call(
            functools.partial(fourth_kernel, (blocks, first, last)),
            out_shape=whole((row_count, 3 * width), bf16),
            in_specs=[SMEM] + [VMEM] * 3 + [ANY] * len(held),
            out_specs=ANY,
            scratch_shapes=[pltpu.VMEM((row_count, PAIR), bf16)] * (3 * count)
            + [pltpu.VMEM((row_count, PAIR), f32)] * (2 * count)
            + [pltpu.SemaphoreType.DMA((3 * count,))],
            input_output_aliases={4: 0} if held else {},
            compiler_params=params(32),
            cost_estimate=cost(1e9, 1e6),
            name="self_attention_backward",
        )(ints, seg_row, grad_att, qkv, *held)

    inner_mlp = [InnerSum(sum_mlp.result(0).reshape(fsdp_count, up_part, width))]
    inner_mlp[0].step()
    grad_proj = attention_back(0, HEADS // 2, ())
    state, came_two, grad_proj, inner_mlp[0].came = fence((sum_mlp.state(), came_two, grad_proj, inner_mlp[0].came))
    sum_mlp.put(state)

    sum_two = OuterSum(keep_two, came_two)
    sum_two.relays()
    sum_two.singles(masks=link_masks()[-1:])
    inner_mlp.append(InnerSum(sum_mlp.result(1).reshape(fsdp_count, up_part, width)))
    inner_mlp[1].step()
    keep_one, send_one = pl.pallas_call(
        functools.partial(sixth_kernel, (dp_count, places_one, qkv_rows, mirrors)),
        out_shape=(
            whole((pairs, qkv_rows + 16, width), bf16),
            whole((pairs, qkv_rows + 16, width), bf16),
        ),
        in_specs=[SMEM] + [VMEM] * 4 + [ANY] * len(arrays_one),
        out_specs=(ANY,) * 2,
        scratch_shapes=[
            pltpu.VMEM((3 * width, width), bf16),
            pltpu.VMEM((3 * width, width), bf16),
            pltpu.VMEM((16, width), bf16),
            pltpu.SemaphoreType.DMA((len(arrays_one) + 2 * dp_count,)),
        ],
        compiler_params=params(),
        cost_estimate=cost(1e9, 1e6),
        name="self_attention_weights",
    )(ints, gains, gain_grads, blended, grad_proj, *arrays_one)
    state, keep_one, send_one, inner_mlp[1].came = fence((sum_two.state(), keep_one, send_one, inner_mlp[1].came))
    sum_two.put(state)

    sum_two.singles(masks=link_masks()[:-1])
    came_one = swap(send_one, CORE)
    base, going_tok = pl.pallas_call(
        functools.partial(fifth_kernel, (dp_count, blocks, places_one, qkv_rows, mirrors)),
        out_shape=(
            whole((row_count, width), f32),
            whole((row_count, width), bf16),
        ),
        in_specs=[SMEM, SMEM] + [VMEM] * 4 + [ANY] * len(arrays_one),
        out_specs=(VMEM,) * 2,
        scratch_shapes=[
            pltpu.VMEM((3 * width, width), bf16),
            pltpu.SemaphoreType.DMA((len(arrays_one),)),
        ],
        compiler_params=params(),
        cost_estimate=cost(1e9, 1e6),
        name="self_attention_input",
    )(ints, mix_weight, gains, blended, grad_res, grad_proj, *arrays_one)
    state, came_one, going_tok = fence((sum_two.state(), came_one, going_tok))
    sum_two.put(state)

    sum_one = OuterSum(keep_one, came_one)
    sum_one.relays()
    came_tok = swap(going_tok, CORE)
    placed = pl.pallas_call(
        functools.partial(place_kernel, (blocks, mirrors)),
        out_shape=whole((pairs, row_count, width), bf16),
        in_specs=[SMEM, SMEM] + [VMEM] * 2,
        out_specs=VMEM,
        compiler_params=params(32),
        cost_estimate=cost(1e9, 1e6),
        name="place_partner_gradients",
    )(ints, ints_near, going_tok, came_tok)
    mlp_parts = jnp.concatenate([inner_parts(inner) for inner in inner_mlp], axis=1)
    inner_mlp = InnerSum(mlp_parts)
    inner_mlp.finish()
    state, placed, mlp_came = fence((sum_one.state(), placed, inner_mlp.came))
    sum_one.put(state)
    inner_mlp.came = mlp_came

    sum_one.singles()
    sum_tok = OuterSum(placed)
    sum_tok.relays()
    two_sum = sum_two.result()
    two_parts = jnp.concatenate(
        [two_sum[first : first + size].reshape(fsdp_count, size // fsdp_count, width) for first, size in layout], axis=1
    )
    inner_two = InnerSum(two_parts)
    inner_two.step()
    state, state_tok, two_came = fence((sum_one.state(), sum_tok.state(), inner_two.came))
    sum_one.put(state)
    sum_tok.put(state_tok)
    inner_two.came = two_came

    sum_tok.singles()
    one_sum = sum_one.result()
    gain_sum = jnp.broadcast_to(one_sum[qkv_rows : qkv_rows + 8][None], (fsdp_count, 8, width))
    one_parts = jnp.concatenate([one_sum[:qkv_rows].reshape(fsdp_count, qkv_part, width), gain_sum], axis=1)
    inner_one = InnerSum(one_parts)
    inner_one.step()
    one_mine = inner_one.result()
    mlp_mine = inner_mlp.result()
    up_shard, down_shard = mlp_mine[:up_part].T, mlp_mine[up_part:]
    two_mine = inner_two.result()
    found = []
    at = 0
    for size in sizes_two:
        found.append(two_mine[at : at + size])
        at += size
    ckv_shard, out_shard, cq_shard, cout_shard = found[0].T, found[1], found[2], found[3]
    qkv_shard = one_mine[:qkv_part].T
    gain_mine = lax.dynamic_slice(one_mine[qkv_part:], (0, device_me * part), (3, part))
    token_grad = base + sum_tok.result()
    return (
        output,
        token_grad,
        coarse_grad,
        gain_mine[0],
        qkv_shard,
        out_shard,
        gain_mine[1],
        cq_shard,
        ckv_shard,
        cout_shard,
        gain_mine[2],
        up_shard,
        down_shard,
    )


def solution(mesh):
    rows = P(("dp", "fsdp"), None)
    columns = P(None, ("dp", "fsdp"))
    line = P(("dp", "fsdp"))
    in_specs = (
        rows, rows, rows, rows, line, line, line, columns, rows,
        line, rows, columns, rows, line, columns, rows, rows,
    )
    out_specs = (
        rows, rows, rows, line, columns, rows, line, rows, columns, rows, line, columns, rows,
    )
    return jax.shard_map(shards, mesh=mesh, in_specs=in_specs, out_specs=out_specs, check_vma=False)
```

```python
import functools

import jax
import jax.numpy as jnp
from jax import lax
from jax.experimental import pallas as pl
from jax.experimental.pallas import tpu as pltpu
from jax.sharding import PartitionSpec as P

HEADS = 12
HEAD = 64
PAIR = 2 * HEAD
CORE = 1
CLIP = 128
WINDOW = 256
TILE = 256
f32 = jnp.float32
bf16 = jnp.bfloat16
fence = lax.optimization_barrier


def swap(values, mask):
    count = lax.axis_size("dp")
    return lax.ppermute(values, "dp", [(i, i ^ mask) for i in range(count)])


def shift(values, step):
    count = lax.axis_size("fsdp")
    return lax.ppermute(values, "fsdp", [(i, (i + step) % count) for i in range(count)])


def link_masks():
    masks = []
    mask = 2
    while mask < lax.axis_size("dp"):
        masks.append(mask)
        mask *= 2
    return masks


def inner_swap(values, mask):
    count = lax.axis_size("fsdp")
    return lax.ppermute(values, "fsdp", [(i, i ^ mask) for i in range(count)])


def inner_double(held, mask):
    return inner_join(held, inner_swap(held, mask), mask)


def inner_join(held, came, mask):
    high = (lax.axis_index("fsdp") & mask) != 0
    return jnp.concatenate([jnp.where(high, came, held), jnp.where(high, held, came)])


def inner_rest(held):
    while held.shape[0] < lax.axis_size("fsdp"):
        held = inner_double(held, held.shape[0])
    return held


def inner_start(shard):
    return [shard] + [shift(shard, step) for step in range(1, lax.axis_size("fsdp"))]


def inner_order(came):
    count = len(came)
    me = lax.axis_index("fsdp")
    line = [came[count - 1 - k] for k in range(count)] + [came[count - k] for k in range(1, count)]
    return lax.dynamic_slice_in_dim(jnp.stack(line), count - 1 - me, count, 0)


def mirrored(role):
    masks = link_masks()
    return sum(masks[len(masks) - 1 - i] for i, mask in enumerate(masks) if role & mask)


def step_along(values, mask):
    count = lax.axis_size("dp")
    return lax.ppermute(values, "dp", [(i, i ^ (mirrored(mask) if i & CORE else mask)) for i in range(count)])


def top_bit(role):
    return 1 << (role.bit_length() - 1)


def relayed_roles():
    found = [role for role in range(2, lax.axis_size("dp"), 2) if role & (role - 1)]
    return sorted(found, key=lambda role: bin(role).count("1"))


def device_of(me, role, mirrors):
    holder = me ^ (role & CORE)
    link = role & ~CORE
    return holder ^ (link + lax.rem(holder, 2) * (mirrors[link] - link))


def mirror_table():
    return {role: mirrored(role) for role in range(0, lax.axis_size("dp"), 2)}


def single_steps(block):
    return {mask: step_along(block, mask) for mask in link_masks()}


def relay_steps(held):
    for role in relayed_roles():
        held[role] = step_along(held[role ^ top_bit(role)], top_bit(role))


def parts_of(pieces, total):
    return [pieces[e] for e in sorted(pieces)], tuple((e, 0, total) for e in sorted(pieces))


def core_steps(held):
    return {**held, **{e | CORE: swap(block, CORE) for e, block in held.items()}}


def inner_parts(inner):
    inner.add()
    return inner.parts


def add_low(a, b):
    return (a.astype(f32) + b.astype(f32)).astype(bf16)


class OuterSum:
    def __init__(self, *parts):
        self.parts = {2 * g: [part[g] for part in parts] for g in range(lax.axis_size("dp") // 2)}
        self.came = []
        self.ready = {}

    def prepare(self, role, rows=slice(None)):
        self.ready[role, rows.start] = self.value(role, rows).astype(bf16)

    def going(self, role, rows):
        return self.ready[role, rows.start] if (role, rows.start) in self.ready else self.value(role, rows).astype(bf16)

    def value(self, role, rows=slice(None)):
        total = self.parts[role][0][rows].astype(f32)
        for part in self.parts[role][1:]:
            total = total + part[rows].astype(f32)
        return total

    def relays(self):
        for role in relayed_roles()[::-1]:
            came = step_along(self.value(role).astype(bf16), top_bit(role))
            self.parts[role ^ top_bit(role)].append(came)

    def singles(self, rows=slice(None), masks=None):
        self.came.append((rows, [step_along(self.going(mask, rows), mask) for mask in masks or link_masks()]))

    def result(self, index=None):
        found = {}
        for rows, blocks in self.came:
            found.setdefault(rows.start, (rows, []))[1].extend(blocks)
        chosen = list(found.values())
        sums = []
        for rows, blocks in chosen if index is None else [chosen[index]]:
            total = self.value(0, rows)
            for block in blocks:
                total = total + block.astype(f32)
            sums.append(total)
        return sums[0] if len(sums) == 1 else jnp.concatenate(sums)

    def state(self):
        return (self.parts, [blocks for _, blocks in self.came], list(self.ready.values()))

    def put(self, state):
        self.parts = state[0]
        self.ready = dict(zip(self.ready, state[2]))
        self.came = [(rows, blocks) for (rows, _), blocks in zip(self.came, state[1])]


class InnerSum:
    def __init__(self, parts):
        self.parts = parts
        self.came = None
        self.mask = parts.shape[0]

    def step(self):
        self.add()
        self.mask //= 2
        bit = ((lax.axis_index("fsdp") & self.mask) != 0).astype(jnp.int32)
        halves = self.parts.reshape((2, self.mask) + self.parts.shape[1:])
        self.parts = lax.dynamic_index_in_dim(halves, bit, 0, keepdims=False)
        going = lax.dynamic_index_in_dim(halves, 1 - bit, 0, keepdims=False).astype(bf16)
        self.came = inner_swap(going, self.mask)

    def finish(self, steps=None):
        while self.mask > 1:
            self.step()

    def add(self):
        if self.came is not None:
            self.parts = self.parts + self.came.astype(f32)
            self.came = None

    def result(self):
        self.finish()
        self.add()
        return self.parts[0]


def nn(a, b):
    return jnp.dot(a, b, preferred_element_type=f32)


def nt(a, b):
    return lax.dot_general(a, b, (((1,), (1,)), ((), ())), preferred_element_type=f32)


def tn(a, b):
    return lax.dot_general(a, b, (((0,), (0,)), ((), ())), preferred_element_type=f32)


def tiles(size):
    step = TILE if size % TILE == 0 else size
    return [(at, step) for at in range(0, size, step)]


def centred(values):
    centre = jnp.mean(values, axis=-1, keepdims=True)
    shifted = values - centre
    spread = jnp.mean(shifted * shifted, axis=-1, keepdims=True)
    r = lax.rsqrt(spread + 1e-06)
    return shifted * r, r


def norm_back(xhat, r, gain, grad):
    c = grad * gain
    first = jnp.mean(c, axis=-1, keepdims=True)
    second = jnp.mean(c * xhat, axis=-1, keepdims=True)
    return r * (c - first - xhat * second), jnp.sum(grad * xhat, axis=0, keepdims=True)


def lower_half(rows):
    return lax.broadcasted_iota(jnp.int32, (rows, PAIR), 1) < HEAD


def two_heads(rows):
    keep = lower_half(rows.shape[0])
    zero = jnp.zeros_like(rows)
    return jnp.concatenate([jnp.where(keep, rows, zero), jnp.where(keep, zero, rows)], axis=0)


def side_by_side(stacked):
    rows = stacked.shape[0] // 2
    return jnp.where(lower_half(rows), stacked[:rows], stacked[rows:])


def softmax_rows(scores):
    raised = jnp.exp(scores - jnp.max(scores, axis=-1, keepdims=True))
    return raised / jnp.sum(raised, axis=-1, keepdims=True)


def bias_of(key_seg, own_seg):
    return jnp.where(key_seg == own_seg, 0.0, -1e30).astype(f32)


def block_bias(key_seg, ints, blocks):
    return jnp.stack([bias_of(key_seg[...], ints[1 + 3 * blocks + i]) for i in range(blocks)])


def biased(scores, bias):
    blocks, _, keys = bias.shape
    rows = scores.shape[0] // (2 * blocks)
    return (scores.reshape(2, blocks, rows, keys) + bias[None]).reshape(scores.shape)


def copies(jobs, sems, at):
    made = [pltpu.make_async_copy(src, dst, sems.at[at + i]) for i, (src, dst) in enumerate(jobs)]
    for job in made:
        job.start()
    return made


def whole(shape, dtype):
    return jax.ShapeDtypeStruct(shape, dtype)


VMEM = pl.BlockSpec(memory_space=pltpu.VMEM)
SMEM = pl.BlockSpec(memory_space=pltpu.SMEM)
ANY = pl.BlockSpec(memory_space=pl.ANY)


def params(mib=56):
    return pltpu.CompilerParams(vmem_limit_bytes=mib * 1024 * 1024)


def cost(flops, moved, exps=0):
    return pl.CostEstimate(flops=int(flops), bytes_accessed=int(moved), transcendentals=int(exps))


def first_kernel(
    geometry, ints, mix, seg_row, tokens, *refs
):
    dp_count, blocks, token_places, qkv_places, qkv_rows, mirrors = geometry
    n_tok, n_qkv = len(token_places), len(qkv_places)
    token_refs, qkv_refs = refs[:n_tok], refs[n_tok : n_tok + n_qkv]
    blended_ref, qkv_ref, attended_ref, gains_ref, partner, weight, gain_parts, sems = refs[n_tok + n_qkv :]
    me = ints[0]
    width = tokens.shape[1]

    for b in range(blocks):
        holder, slot = ints[1 + b], ints[1 + blocks + b]
        for ref, (role, _, rows) in zip(token_refs, token_places):

            @pl.when(holder == device_of(me, role, mirrors))
            def _(ref=ref, rows=rows, b=b, slot=slot):
                at = pl.multiple_of(slot * CLIP, CLIP)
                pltpu.make_async_copy(ref.at[pl.ds(at, CLIP)], partner.at[b], sems.at[b]).start()

    jobs = []
    for ref, (e, start, rows) in zip(qkv_refs, qkv_places):
        take = min(rows, qkv_rows - start)
        at = pl.multiple_of(device_of(me, e, mirrors) * qkv_rows + start, 16)
        jobs.append((ref.at[pl.ds(0, take)], weight.at[pl.ds(at, take)]))
        if start + rows > qkv_rows:
            jobs.append((ref.at[pl.ds(take, rows - take)], gain_parts.at[e]))
    made = copies(jobs, sems, blocks)
    for b in range(blocks):
        pltpu.make_async_copy(tokens.at[pl.ds(0, CLIP)], partner.at[b], sems.at[b]).wait()
    for b in range(blocks):
        rows = slice(b * CLIP, (b + 1) * CLIP)
        share = mix[b]
        blended_ref[rows, :] = share * tokens[rows, :].astype(f32) + (1.0 - share) * partner[b].astype(f32)
    for job in made:
        job.wait()
    gains = gain_parts[0].astype(f32)
    for e in range(1, dp_count):
        gains = gains + gain_parts[e].astype(f32)
    gains_ref[...] = gains[:8]
    xhat, _ = centred(blended_ref[...])
    normed = (xhat * gains[0:1]).astype(bf16)
    for at, step in tiles(3 * width):
        tile = nt(normed, weight[at : at + step, :])
        if at + step <= width:
            tile = tile * 0.125
        qkv_ref[:, at : at + step] = tile.astype(bf16)

    @pl.loop(0, blocks)
    def _(i):
        window = pl.multiple_of(ints[1 + 2 * blocks + i] * CLIP, CLIP)
        bias = bias_of(seg_row[:, pl.ds(window, WINDOW)], ints[1 + 3 * blocks + i])
        rows = pl.ds(pl.multiple_of(i * CLIP, CLIP), CLIP)
        keys = pl.ds(window, WINDOW)
        for at in range(0, width, PAIR):
            queries = two_heads(qkv_ref[rows, at : at + PAIR])
            probs = softmax_rows(nt(queries, qkv_ref[keys, width + at : width + at + PAIR]) + bias).astype(bf16)
            out = nn(probs, qkv_ref[keys, 2 * width + at : 2 * width + at + PAIR])
            attended_ref[rows, at : at + PAIR] = side_by_side(out).astype(bf16)


def load_cross(me, refs, places, layout, weights, sems, mirrors):
    jobs = []
    for ref, (e, start, rows) in zip(refs, places):
        for (first, size), weight in zip(layout, weights):
            if weight is not None and first >= start and first + size <= start + rows:
                at = pl.multiple_of(device_of(me, e, mirrors) * size, 16)
                jobs.append((ref.at[pl.ds(first - start, size)], weight.at[pl.ds(at, size)]))
    return copies(jobs, sems, 0)


def second_kernel(geometry, ints, coarse_seg, coarse, blended, attended, gains, *refs):
    blocks, places, layout, mirrors = geometry
    weight_refs = refs[: len(places)]
    residual_ref, cq_ref, ckv_ref, crossed_ref, joined_ref, second_ref = refs[len(places) : len(places) + 6]
    w_ckv, w_out, w_cq, w_cout, sems = refs[len(places) + 6 :]
    made = load_cross(ints[0], weight_refs, places, layout, (w_ckv, w_out, w_cq, w_cout), sems, mirrors)
    for job in made:
        job.wait()
    width = blended.shape[1]
    for at, step in tiles(2 * width):
        ckv_ref[:, at : at + step] = nt(coarse[...], w_ckv[at : at + step, :]).astype(bf16)
    for at, step in tiles(width):
        residual_ref[:, at : at + step] = blended[:, at : at + step] + nn(attended[...], w_out[:, at : at + step])
    xhat, _ = centred(residual_ref[...])
    crossed_in = (xhat * gains[1:2]).astype(bf16)
    for at, step in tiles(width):
        cq_ref[:, at : at + step] = (nn(crossed_in, w_cq[:, at : at + step]) * 0.125).astype(bf16)

    bias = block_bias(coarse_seg, ints, blocks)
    for at in range(0, width, PAIR):
        queries = two_heads(cq_ref[:, at : at + PAIR])
        probs = softmax_rows(biased(nt(queries, ckv_ref[:, at : at + PAIR]), bias)).astype(bf16)
        out = nn(probs, ckv_ref[:, width + at : width + at + PAIR])
        crossed_ref[:, at : at + PAIR] = side_by_side(out).astype(bf16)

    for at, step in tiles(width):
        joined_ref[:, at : at + step] = residual_ref[:, at : at + step] + nn(crossed_ref[...], w_cout[:, at : at + step])
    xhat, _ = centred(joined_ref[...])
    second_ref[...] = (xhat * gains[2:3]).astype(bf16)


def mlp_kernel(geometry, second, second_near, cotangent, cotangent_near, *refs):
    groups, places, rows, last = geometry
    weight_refs = refs[: len(places)]
    refs = refs[len(places) :]
    keep_ref, going_ref = refs[:2]
    if last:
        own_ref = refs[2]
        sums = refs[3:7]
        refs = refs[7:]
    else:
        sums = refs[2:6]
        refs = refs[6:]
    w_up, w_down, hidden, grad_pre, sems = refs
    step = pl.program_id(0)

    def jobs_of(group):
        jobs = []
        for ref, (e, which) in zip(weight_refs, places):
            if e == groups[group]:
                for part, weight in ((0, w_up), (1, w_down)):
                    if which is None or which == part:
                        first = part * rows if which is None else 0
                        jobs.append((ref.at[pl.ds(first, rows)], weight.at[group]))
        return jobs

    at = 0
    for group in range(len(groups)):
        jobs = jobs_of(group)
        made = [pltpu.make_async_copy(s, d, sems.at[at + i]) for i, (s, d) in enumerate(jobs)]
        at += len(jobs)

        @pl.when(step == 0)
        def _(made=made):
            for job in made:
                job.start()

        @pl.when(step == group)
        def _(made=made):
            for job in made:
                job.wait()

    @pl.when(step == 0)
    def _():
        for ref in sums:
            ref[...] = jnp.zeros_like(ref)

    up, down = w_up.at[step], w_down.at[step]
    for half, (inputs, upstream) in enumerate(((second, cotangent), (second_near, cotangent_near))):
        pre = nt(inputs[...], up[...])
        grad_hidden = nt(upstream[...], down[...])
        cdf = 0.5 * (1.0 + lax.erf(pre * 0.7071067811865476))
        slope = cdf + pre * (jnp.exp(-0.5 * pre * pre) * 0.3989422804014327)
        hidden[half] = (pre * cdf).astype(bf16)
        grad_pre[half] = (grad_hidden * slope).astype(bf16)
        for first, size in tiles(second.shape[1]):
            columns = slice(first, first + size)
            sums[2 * half][:, columns] += nn(hidden[half], down[:, columns])
            sums[2 * half + 1][:, columns] += nn(grad_pre[half], up[:, columns])
    keep_ref[0, 0] = (tn(grad_pre[0], second[...]) + tn(grad_pre[1], second_near[...])).astype(bf16)
    keep_ref[0, 1] = (tn(hidden[0], cotangent[...]) + tn(hidden[1], cotangent_near[...])).astype(bf16)

    @pl.when(step == len(groups) - 1)
    def _():
        going_ref[0] = sums[2][...].astype(bf16)
        going_ref[1] = sums[3][...].astype(bf16)
        if last:
            own_ref[0] = sums[0][...].astype(bf16)
            own_ref[1] = sums[1][...].astype(bf16)


def grads_out(me, dp_count, layout, sources, keep_ref, send_ref, sems, at, mirrors):
    jobs = []
    for e in range(dp_count):
        target = send_ref if e & CORE else keep_ref
        for (first, size), source in zip(layout, sources):
            if source is None:
                continue
            row = pl.multiple_of(device_of(me, e, mirrors) * size, 16)
            jobs.append((source.at[pl.ds(row, size)], target.at[e // 2, pl.ds(first, size)]))
    return copies(jobs, sems, at)


def third_kernel(
    geometry, ints, coarse_seg, gains, mlp_out, grad_second, own_b, came_a, came_b, joined, cotangent, crossed, cq, ckv, *refs
):
    blocks, places, layout, dp_count, mirrors = geometry
    weight_refs = refs[: len(places)]
    refs = refs[len(places) :]
    output_ref, grad_joined_ref, grad_cq_ref, grad_ckv_ref, gain_grads_ref, keep_ref, send_ref = refs[:7]
    w_cout, g_cout, grad_cross, sems = refs[7:]
    me = ints[0]
    width = joined.shape[1]
    made = load_cross(me, weight_refs, places, layout, (None, None, None, w_cout), sems, mirrors)
    rest = [own_b[i].astype(f32) + came_a[i].astype(f32) + came_b[i].astype(f32) for i in range(2)]
    output_ref[...] = (joined[...] + (mlp_out[...] + rest[0])).astype(bf16)
    xhat, r = centred(joined[...])
    grad_in, gain_two = norm_back(xhat, r, gains[2:3], grad_second[...] + rest[1])
    grad_joined_ref[...] = cotangent[...].astype(f32) + grad_in
    low = grad_joined_ref[...].astype(bf16)
    for job in made:
        job.wait()
    for at, step in tiles(width):
        grad_cross[:, at : at + step] = nt(low, w_cout[at : at + step, :]).astype(bf16)
    for at, step in tiles(width):
        g_cout[at : at + step, :] = tn(crossed[:, at : at + step], low).astype(bf16)
    going = grads_out(me, dp_count, layout, (None, None, None, g_cout), keep_ref, send_ref, sems, len(made), mirrors)
    bias = block_bias(coarse_seg, ints, blocks)
    for at in range(0, width, PAIR):
        lanes = slice(at, at + PAIR)
        queries = two_heads(cq[:, lanes])
        grads = two_heads(grad_cross[:, lanes])
        keys = ckv[:, lanes]
        values = ckv[:, width + at : width + at + PAIR]
        probs = softmax_rows(biased(nt(queries, keys), bias))
        grad_ckv_ref[:, width + at : width + at + PAIR] = tn(probs.astype(bf16), grads).astype(bf16)
        grad_probs = nt(grads, values)
        inner = jnp.sum(probs * grad_probs, axis=-1, keepdims=True)
        scores = (probs * (grad_probs - inner)).astype(bf16)
        part = side_by_side(nn(scores, keys)).astype(bf16)
        grad_cq_ref[:, lanes] = part * jnp.asarray(0.125, bf16)
        grad_ckv_ref[:, lanes] = tn(scores, queries).astype(bf16)

    gain_grads_ref[...] = jnp.concatenate([gain_two] * 8, axis=0)
    for job in going:
        job.wait()


def third_part(geometry, ints, coarse, gains, gain_two, grad_joined, residual, attended, grad_cq, grad_ckv, keep_in, send_in, *refs):
    places, layout, dp_count, mirrors = geometry
    weight_refs = refs[: len(places)]
    refs = refs[len(places) :]
    coarse_ref, grad_res_ref, grad_att_ref, gain_grads_ref, keep_ref, send_ref = refs[:6]
    w_ckv, w_out, w_cq, g_ckv, g_out, g_cq, crossed_in, sems = refs[6:]
    me = ints[0]
    width = residual.shape[1]
    made = load_cross(me, weight_refs, places, layout, (w_ckv, w_out, w_cq, None), sems, mirrors)
    xhat, r = centred(residual[...])
    crossed_in[...] = (xhat * gains[1:2]).astype(bf16)
    for at, step in tiles(width):
        g_cq[at : at + step, :] = tn(crossed_in[:, at : at + step], grad_cq[...]).astype(bf16)
    for at, step in tiles(2 * width):
        g_ckv[at : at + step, :] = tn(grad_ckv[:, at : at + step], coarse[...]).astype(bf16)
    for job in made:
        job.wait()
    going = grads_out(me, dp_count, layout, (g_ckv, None, g_cq, None), keep_ref, send_ref, sems, 0, mirrors)
    for at, step in tiles(width):
        coarse_ref[:, at : at + step] = nn(grad_ckv[:, 0:width], w_ckv[0:width, at : at + step]) + nn(
            grad_ckv[:, width : 2 * width], w_ckv[width : 2 * width, at : at + step]
        )
    pieces = [nt(grad_cq[...], w_cq[at : at + step, :]) for at, step in tiles(width)]
    grad_in, gain_cross = norm_back(xhat, r, gains[1:2], jnp.concatenate(pieces, axis=1))
    grad_res = grad_joined[...] + grad_in
    grad_res_ref[...] = grad_res
    low = grad_res.astype(bf16)
    for at, step in tiles(width):
        g_out[at : at + step, :] = tn(attended[:, at : at + step], low).astype(bf16)
    going += grads_out(me, dp_count, layout, (None, g_out, None, None), keep_ref, send_ref, sems, len(going), mirrors)
    for at, step in tiles(width):
        grad_att_ref[:, at : at + step] = nt(low, w_out[at : at + step, :]).astype(bf16)
    zero = jnp.zeros_like(gain_cross)
    gain_grads_ref[...] = jnp.concatenate([zero, gain_cross, gain_two[0:1]] + [zero] * 5, axis=0)
    for job in going:
        job.wait()


def fourth_kernel(geometry, ints, seg_row, grad_att, qkv, *refs):
    blocks, first, last = geometry
    count = last - first
    grad_proj, sems = refs[-1 - 5 * count - 1], refs[-1]
    scratch = refs[-1 - 5 * count : -1]
    query_part, key_part, value_part, key_sum, value_sum = [scratch[i * count : (i + 1) * count] for i in range(5)]
    width = grad_att.shape[1]
    for ref in key_sum + value_sum:
        ref[...] = jnp.zeros_like(ref)

    @pl.loop(0, blocks)
    def _(i):
        window = pl.multiple_of(ints[1 + 2 * blocks + i] * CLIP, CLIP)
        bias = bias_of(seg_row[:, pl.ds(window, WINDOW)], ints[1 + 3 * blocks + i])
        rows = pl.ds(pl.multiple_of(i * CLIP, CLIP), CLIP)
        near = pl.ds(window, WINDOW)
        for pair in range(count):
            at = (first + pair) * PAIR
            queries = two_heads(qkv[rows, at : at + PAIR])
            grads = two_heads(grad_att[rows, at : at + PAIR])
            keys = qkv[near, width + at : width + at + PAIR]
            values = qkv[near, 2 * width + at : 2 * width + at + PAIR]
            probs = softmax_rows(nt(queries, keys) + bias)
            grad_probs = nt(grads, values)
            inner = jnp.sum(probs * grad_probs, axis=-1, keepdims=True)
            scores = (probs * (grad_probs - inner)).astype(bf16)
            part = side_by_side(nn(scores, keys)).astype(bf16)
            query_part[pair][rows, :] = part * jnp.asarray(0.125, bf16)
            value_sum[pair][near, :] += tn(probs.astype(bf16), grads)
            key_sum[pair][near, :] += tn(scores, queries)

    jobs = []
    for pair in range(count):
        key_part[pair][...] = key_sum[pair][...].astype(bf16)
        value_part[pair][...] = value_sum[pair][...].astype(bf16)
        for i, part in enumerate((query_part, key_part, value_part)):
            jobs.append((part[pair], grad_proj.at[:, pl.ds(i * width + (first + pair) * PAIR, PAIR)]))
    for job in copies(jobs, sems, 0):
        job.wait()


def fifth_kernel(geometry, ints, mix, gains, blended, grad_res, grad_proj, *refs):
    dp_count, blocks, qkv_places, qkv_rows, mirrors = geometry
    weight_refs = refs[: len(qkv_places)]
    refs = refs[len(qkv_places) :]
    base_ref, going_ref = refs[:2]
    weight, sems = refs[2:]
    me = ints[0]
    width = blended.shape[1]
    jobs = []
    for ref, (e, start, rows) in zip(weight_refs, qkv_places):
        take = min(rows, qkv_rows - start)
        at = pl.multiple_of(device_of(me, e, mirrors) * qkv_rows + start, 16)
        jobs.append((ref.at[pl.ds(0, take)], weight.at[pl.ds(at, take)]))
    made = copies(jobs, sems, 0)
    xhat, r = centred(blended[...])
    for job in made:
        job.wait()
    pieces = [nn(grad_proj[...], weight[:, at : at + step]) for at, step in tiles(width)]
    grad_in, _ = norm_back(xhat, r, gains[0:1], jnp.concatenate(pieces, axis=1))
    grad_blend = grad_res[...] + grad_in
    for b in range(blocks):
        rows = slice(b * CLIP, (b + 1) * CLIP)
        share = mix[b]
        part = grad_blend[rows, :]
        base_ref[rows, :] = share * part
        going_ref[rows, :] = ((1.0 - share) * part).astype(bf16)


def place_kernel(geometry, ints, ints_near, blocks_own, blocks_near, out_ref):
    blocks, mirrors = geometry
    me = ints[0]
    out_ref[...] = jnp.zeros_like(out_ref)
    for table, first, source in ((ints, 1, blocks_own), (ints_near, 0, blocks_near)):
        for b in range(blocks):
            holder, slot = table[first + b], table[first + blocks + b]
            group = jnp.int32(0)
            for role in mirrors:
                group = group + jnp.where(device_of(me, role, mirrors) == holder, role // 2, 0)

            @pl.when(lax.rem(holder, 2) == lax.rem(me, 2))
            def _(group=group, slot=slot, source=source, b=b):
                rows = pl.ds(pl.multiple_of(slot * CLIP, CLIP), CLIP)
                part = source[b * CLIP : (b + 1) * CLIP, :].astype(f32)
                out_ref[group, rows, :] = (out_ref[group, rows, :].astype(f32) + part).astype(bf16)


def sixth_kernel(geometry, ints, gains, gain_grads, blended, grad_proj, *refs):
    dp_count, qkv_places, qkv_rows, mirrors = geometry
    weight_refs = refs[: len(qkv_places)]
    keep_ref, send_ref, weight, grad_w, gain_rows, sems = refs[len(qkv_places) :]
    me = ints[0]
    width = blended.shape[1]
    jobs = []
    for ref, (e, start, rows) in zip(weight_refs, qkv_places):
        take = min(rows, qkv_rows - start)
        at = pl.multiple_of(device_of(me, e, mirrors) * qkv_rows + start, 16)
        jobs.append((ref.at[pl.ds(0, take)], weight.at[pl.ds(at, take)]))
    made = copies(jobs, sems, 0)
    xhat, _ = centred(blended[...])
    normed = (xhat * gains[0:1]).astype(bf16)
    for job in made:
        job.wait()
    gain_one = jnp.zeros((1, width), f32)
    for at, step in tiles(3 * width):
        part = tn(grad_proj[:, at : at + step], normed)
        gain_one = gain_one + jnp.sum(part * weight[at : at + step, :].astype(f32), axis=0, keepdims=True)
        grad_w[at : at + step, :] = part.astype(bf16)
    sent = grads_out(me, dp_count, ((0, qkv_rows),), (grad_w,), keep_ref, send_ref, sems, len(jobs), mirrors)
    all_gains = jnp.concatenate([gain_one / gains[0:1], gain_grads[1:8], jnp.zeros((8, width), f32)], axis=0)
    gain_rows[...] = all_gains.astype(bf16)
    last = []
    for e in range(dp_count):
        target = send_ref if e & CORE else keep_ref
        last.append((gain_rows, target.at[e // 2, pl.ds(qkv_rows, 16)]))
    for job in sent + copies(last, sems, len(jobs) + dp_count):
        job.wait()


def shards(
    tokens,
    coarse_view,
    segment_ids,
    partner_device,
    partner_slot,
    mix_weight,
    ln1_gain,
    w_qkv,
    w_out,
    lnx_gain,
    w_cq,
    w_ckv,
    w_cout,
    ln2_gain,
    w_up,
    w_down,
    cotangent,
):
    row_count, width = tokens.shape
    coarse_rows = coarse_view.shape[0]
    blocks = mix_weight.shape[0]
    dp_count, fsdp_count = lax.axis_size("dp"), lax.axis_size("fsdp")
    dp_me, fsdp_me = lax.axis_index("dp"), lax.axis_index("fsdp")
    part = ln1_gain.shape[0]
    device_me = dp_me * fsdp_count + fsdp_me
    pairs = dp_count // 2
    mirrors = mirror_table()

    target = partner_device[:, 0]
    segments = segment_ids[0]
    videos = segments.reshape(blocks, row_count // blocks)[:, 0]
    following = jnp.concatenate([videos[1:] == videos[:-1], jnp.zeros((1,), bool)])
    before = jnp.concatenate([jnp.zeros((1,), bool), videos[1:] == videos[:-1]])
    index = jnp.arange(blocks, dtype=jnp.int32)
    window = jnp.where(following, index, jnp.where(before, index - 1, jnp.minimum(index, blocks - 2)))
    ints = jnp.concatenate(
        [dp_me[None].astype(jnp.int32), target, partner_slot, window, videos]
    )
    ints_near = swap(ints[1 : 1 + 2 * blocks], CORE)
    seg_row = segments[None, :]
    coarse_seg = segments.reshape(coarse_rows, row_count // coarse_rows)[:, 0][None, :]

    gain_rows = lax.dynamic_update_slice(
        jnp.zeros((8, width), bf16), jnp.stack([ln1_gain, lnx_gain, ln2_gain]), (0, device_me * part)
    )
    shard_one = jnp.concatenate([w_qkv.T, gain_rows])
    shard_first = jnp.concatenate([shard_one, w_ckv.T])
    shard_rest = jnp.concatenate([w_out, w_cq, w_cout])
    shard_mlp = jnp.concatenate([w_up.T, w_down])
    sizes_two = (w_ckv.shape[1], w_out.shape[0], w_cq.shape[0], w_cout.shape[0])
    qkv_part, up_part = w_qkv.shape[1], w_up.shape[1]
    qkv_rows, up_rows = qkv_part * fsdp_count, up_part * fsdp_count
    layout = []
    at = 0
    for size in sizes_two:
        layout.append((at * fsdp_count, size * fsdp_count))
        at += size
    layout = tuple(layout)
    rows_two = at * fsdp_count

    held_tok = {0: tokens, **single_steps(tokens)}
    came_first = inner_start(shard_first)
    held_tok, came_first, shard_rest = fence((held_tok, came_first, shard_rest))

    firsts = inner_order(came_first)
    ones = firsts[:, : qkv_part + 8]
    gain_block = jnp.sum(ones[:, qkv_part:].astype(f32), axis=0).astype(bf16)
    block_one = jnp.concatenate(
        [ones[:, :qkv_part].reshape(qkv_rows, width), gain_block, jnp.zeros((8, width), bf16)]
    )
    held_one = {0: block_one, **single_steps(block_one)}
    came_rest = inner_start(shard_rest)
    held_tok, held_one, came_rest, shard_mlp, firsts = fence((held_tok, held_one, came_rest, shard_mlp, firsts))

    near_mlp = inner_swap(shard_mlp, 1)
    core_tok = core_steps(dict(held_tok))
    near_tok = set(held_tok)
    relay_steps(held_tok)
    rests = inner_order(came_rest)
    split = [firsts[:, qkv_part + 8 :].reshape(sizes_two[0] * fsdp_count, width)]
    at = 0
    for size in sizes_two[1:]:
        split.append(rests[:, at : at + size].reshape(size * fsdp_count, width))
        at += size
    block_two = jnp.concatenate(split)
    held_one, core_tok, held_tok, block_two, near_mlp = fence((held_one, core_tok, held_tok, block_two, near_mlp))

    cuts = (0, 5 * up_part // 12, 3 * up_part // 2, 2 * up_part)
    mlp_cut = [
        inner_join(shard_mlp[None, first:last], near_mlp[None, first:last], 1) for first, last in zip(cuts, cuts[1:])
    ]
    mlp_came = [inner_swap(mlp_cut[0], 2)]
    core_one = core_steps(dict(held_one))
    relay_steps(held_one)
    late_tok = core_steps({e: b for e, b in held_tok.items() if e not in near_tok})
    held_one, core_one, late_tok, block_two, mlp_cut, mlp_came = fence(
        (held_one, core_one, late_tok, block_two, mlp_cut, mlp_came)
    )

    held_two = {0: block_two, **single_steps(block_two)}
    cotangent_near = swap(cotangent, CORE)
    mlp_came.append(inner_swap(mlp_cut[1], 2))
    mlp_joined = [inner_rest(inner_join(mlp_cut[0], mlp_came[0], 2))]
    late_one = core_steps({e: b for e, b in held_one.items() if e not in near_tok})
    pieces_tok = {**core_tok, **late_tok}
    pieces_one = {**core_one, **late_one}
    arrays_tok, places_tok = parts_of(pieces_tok, row_count)
    arrays_one, places_one = parts_of(pieces_one, qkv_rows + 16)
    blended, qkv, attended, gains = pl.pallas_call(
        functools.partial(first_kernel, (dp_count, blocks, places_tok, places_one, qkv_rows, mirrors)),
        out_shape=(
            whole((row_count, width), f32),
            whole((row_count, 3 * width), bf16),
            whole((row_count, width), bf16),
            whole((8, width), f32),
        ),
        in_specs=[SMEM, SMEM, VMEM, VMEM] + [ANY] * (len(arrays_tok) + len(arrays_one)),
        out_specs=(VMEM,) * 4,
        scratch_shapes=[
            pltpu.VMEM((blocks, CLIP, width), bf16),
            pltpu.VMEM((3 * width, width), bf16),
            pltpu.VMEM((dp_count, 16, width), bf16),
            pltpu.SemaphoreType.DMA((blocks + len(arrays_one) + dp_count,)),
        ],
        compiler_params=params(),
        cost_estimate=cost(1e9, 1e6),
        name="mix_self_attention",
    )(ints, mix_weight, seg_row, tokens, *arrays_tok, *arrays_one)
    held_two, attended, mlp_came, cotangent_near, mlp_cut, mlp_joined = fence(
        (held_two, attended, mlp_came, cotangent_near, mlp_cut, mlp_joined)
    )

    core_two = core_steps(dict(held_two))
    relay_steps(held_two)
    mlp_came.append(inner_swap(mlp_cut[2], 2))
    mlp_joined.append(inner_rest(inner_join(mlp_cut[1], mlp_came[1], 2)))
    held_two, core_two, mlp_came, mlp_joined = fence((held_two, core_two, mlp_came, mlp_joined))

    mlp_joined.append(inner_rest(inner_join(mlp_cut[2], mlp_came[2], 2)))
    mlp = jnp.concatenate(mlp_joined, axis=1)
    block_mlp = jnp.concatenate([mlp[:, :up_part].reshape(up_rows, width), mlp[:, up_part:].reshape(up_rows, width)])
    held_mlp = {0: block_mlp, **single_steps(block_mlp)}
    late_two = core_steps({e: b for e, b in held_two.items() if e not in near_tok})
    pieces_two = {**core_two, **late_two}
    wide = [pltpu.VMEM((sizes * fsdp_count * dp_count, width), bf16) for sizes in sizes_two]
    n_two = 4 * dp_count
    arrays_two, places_two = parts_of(pieces_two, rows_two)
    wide = [pltpu.VMEM((sizes * fsdp_count * dp_count, width), bf16) for sizes in sizes_two]
    n_two = 4 * dp_count
    residual, cq, ckv, crossed, joined, second = pl.pallas_call(
        functools.partial(second_kernel, (blocks, places_two, layout, mirrors)),
        out_shape=(
            whole((row_count, width), f32),
            whole((row_count, width), bf16),
            whole((coarse_rows, 2 * width), bf16),
            whole((row_count, width), bf16),
            whole((row_count, width), f32),
            whole((row_count, width), bf16),
        ),
        in_specs=[SMEM] + [VMEM] * 5 + [ANY] * len(arrays_two),
        out_specs=(VMEM,) * 6,
        scratch_shapes=wide + [pltpu.SemaphoreType.DMA((n_two,))],
        compiler_params=params(),
        cost_estimate=cost(1e9, 1e6),
        name="cross_attention",
    )(ints, coarse_seg, coarse_view, blended, attended, gains, *arrays_two)
    second_near = swap(second, CORE)
    held_mlp, second, second_near, ints_near = fence((held_mlp, second, second_near, ints_near))

    early = dict(held_mlp)
    relay_steps(held_mlp)

    def mlp_call(pieces, last):
        groups = tuple(sorted(pieces))
        count = len(groups)
        fixed = pl.BlockSpec((row_count, width), lambda g: (0, 0))
        moving = pl.BlockSpec((1, 2, up_rows, width), lambda g: (g, 0, 0, 0))
        both = pl.BlockSpec((2, row_count, width), lambda g: (0, 0, 0))
        table = whole((row_count, width), f32)
        out_shape = [whole((count, 2, up_rows, width), bf16), whole((2, row_count, width), bf16)]
        out_specs = [moving, both]
        scratch = [pltpu.VMEM((row_count, width), f32)] * (4 if last else 2)
        if last:
            out_shape.append(whole((2, row_count, width), bf16))
            out_specs.append(both)
        else:
            out_shape += [table, table]
            out_specs += [fixed, fixed]
        made = pl.pallas_call(
            functools.partial(mlp_kernel, (groups, tuple((e, None) for e in groups), up_rows, last)),
            grid=(count,),
            out_shape=tuple(out_shape),
            in_specs=[fixed] * 4 + [ANY] * count,
            out_specs=tuple(out_specs),
            scratch_shapes=scratch
            + [
                pltpu.VMEM((count, up_rows, width), bf16),
                pltpu.VMEM((count, up_rows, width), bf16),
                pltpu.VMEM((2, row_count, up_rows), bf16),
                pltpu.VMEM((2, row_count, up_rows), bf16),
                pltpu.SemaphoreType.DMA((2 * count,)),
            ],
            compiler_params=params(32),
            cost_estimate=cost(1e9, 1e6),
            name="feed_forward",
        )(second, second_near, cotangent, cotangent_near, *[pieces[e] for e in groups])
        return groups, made[0].reshape(count, 2 * up_rows, width), made[1], made[2:]

    groups_a, keep_a, going_a, (mlp_out, grad_second) = mlp_call(early, False)
    late = {e: b for e, b in held_mlp.items() if e not in near_tok}
    late, keep_a, going_a, mlp_out, grad_second = fence((late, keep_a, going_a, mlp_out, grad_second))
    came_a = swap(going_a, CORE)
    groups_b, keep_b, going_b, (own_b,) = mlp_call(late, True)
    came_a, keep_b, going_b, own_b = fence((came_a, keep_b, going_b, own_b))
    came_b = swap(going_b, CORE)
    totals = [None] * pairs
    for groups, keep in ((groups_a, keep_a), (groups_b, keep_b)):
        for i, e in enumerate(groups):
            totals[e // 2] = keep[i]
    came_b = fence(came_b)

    sum_mlp = OuterSum(totals)
    upper, lower = slice(0, up_rows), slice(up_rows, 2 * up_rows)
    sum_mlp.relays()
    sum_mlp.prepare(link_masks()[-1], upper)
    output, grad_joined, grad_cq, grad_ckv, gain_two, keep_two, send_two = pl.pallas_call(
        functools.partial(third_kernel, (blocks, places_two, layout, dp_count, mirrors)),
        out_shape=(
            whole((row_count, width), bf16),
            whole((row_count, width), f32),
            whole((row_count, width), bf16),
            whole((coarse_rows, 2 * width), bf16),
            whole((8, width), f32),
            whole((pairs, rows_two, width), bf16),
            whole((pairs, rows_two, width), bf16),
        ),
        in_specs=[SMEM] + [VMEM] * 12 + [ANY] * len(arrays_two),
        out_specs=(VMEM,) * 5 + (ANY,) * 2,
        scratch_shapes=[
            wide[3],
            wide[3],
            pltpu.VMEM((row_count, width), bf16),
            pltpu.SemaphoreType.DMA((n_two + dp_count,)),
        ],
        compiler_params=params(32),
        cost_estimate=cost(1e9, 1e6),
        name="cross_attention_backward",
    )(ints, coarse_seg, gains, mlp_out, grad_second, own_b, came_a, came_b, joined, cotangent, crossed, cq, ckv, *arrays_two)
    state, grad_joined = fence((sum_mlp.state(), grad_joined))
    sum_mlp.put(state)

    sum_mlp.singles(upper)
    for mask in link_masks():
        sum_mlp.prepare(mask, lower)
    coarse_grad, grad_res, grad_att, gain_grads, keep_two, send_two = pl.pallas_call(
        functools.partial(third_part, (places_two, layout, dp_count, mirrors)),
        out_shape=(
            whole((coarse_rows, width), f32),
            whole((row_count, width), f32),
            whole((row_count, width), bf16),
            whole((8, width), f32),
            whole((pairs, rows_two, width), bf16),
            whole((pairs, rows_two, width), bf16),
        ),
        in_specs=[SMEM] + [VMEM] * 8 + [ANY] * (2 + len(arrays_two)),
        out_specs=(VMEM,) * 4 + (ANY,) * 2,
        scratch_shapes=[
            wide[0],
            wide[1],
            wide[2],
            wide[0],
            wide[1],
            wide[2],
            pltpu.VMEM((row_count, width), bf16),
            pltpu.SemaphoreType.DMA((n_two,)),
        ],
        input_output_aliases={9: 4, 10: 5},
        compiler_params=params(),
        cost_estimate=cost(1e9, 1e6),
        name="cross_attention_weights",
    )(
        ints, coarse_view, gains, gain_two, grad_joined, residual, attended, grad_cq, grad_ckv, keep_two, send_two, *arrays_two
    )

    state, grad_att, keep_two, send_two = fence((sum_mlp.state(), grad_att, keep_two, send_two))
    sum_mlp.put(state)

    sum_mlp.singles(lower)
    came_two = swap(send_two, CORE)
    def attention_back(first, last, held):
        count = last - first
        return pl.pallas_call(
            functools.partial(fourth_kernel, (blocks, first, last)),
            out_shape=whole((row_count, 3 * width), bf16),
            in_specs=[SMEM] + [VMEM] * 3 + [ANY] * len(held),
            out_specs=ANY,
            scratch_shapes=[pltpu.VMEM((row_count, PAIR), bf16)] * (3 * count)
            + [pltpu.VMEM((row_count, PAIR), f32)] * (2 * count)
            + [pltpu.SemaphoreType.DMA((3 * count,))],
            input_output_aliases={4: 0} if held else {},
            compiler_params=params(32),
            cost_estimate=cost(1e9, 1e6),
            name="self_attention_backward",
        )(ints, seg_row, grad_att, qkv, *held)

    inner_mlp = [InnerSum(sum_mlp.result(0).reshape(fsdp_count, up_part, width))]
    inner_mlp[0].step()
    grad_proj = attention_back(0, HEADS // 2, ())
    state, came_two, grad_proj, inner_mlp[0].came = fence((sum_mlp.state(), came_two, grad_proj, inner_mlp[0].came))
    sum_mlp.put(state)

    sum_two = OuterSum(keep_two, came_two)
    sum_two.relays()
    sum_two.singles(masks=link_masks()[-1:])
    inner_mlp.append(InnerSum(sum_mlp.result(1).reshape(fsdp_count, up_part, width)))
    inner_mlp[1].step()
    keep_one, send_one = pl.pallas_call(
        functools.partial(sixth_kernel, (dp_count, places_one, qkv_rows, mirrors)),
        out_shape=(
            whole((pairs, qkv_rows + 16, width), bf16),
            whole((pairs, qkv_rows + 16, width), bf16),
        ),
        in_specs=[SMEM] + [VMEM] * 4 + [ANY] * len(arrays_one),
        out_specs=(ANY,) * 2,
        scratch_shapes=[
            pltpu.VMEM((3 * width, width), bf16),
            pltpu.VMEM((3 * width, width), bf16),
            pltpu.VMEM((16, width), bf16),
            pltpu.SemaphoreType.DMA((len(arrays_one) + 2 * dp_count,)),
        ],
        compiler_params=params(),
        cost_estimate=cost(1e9, 1e6),
        name="self_attention_weights",
    )(ints, gains, gain_grads, blended, grad_proj, *arrays_one)
    state, keep_one, send_one, inner_mlp[1].came = fence((sum_two.state(), keep_one, send_one, inner_mlp[1].came))
    sum_two.put(state)

    sum_two.singles(masks=link_masks()[:-1])
    came_one = swap(send_one, CORE)
    base, going_tok = pl.pallas_call(
        functools.partial(fifth_kernel, (dp_count, blocks, places_one, qkv_rows, mirrors)),
        out_shape=(
            whole((row_count, width), f32),
            whole((row_count, width), bf16),
        ),
        in_specs=[SMEM, SMEM] + [VMEM] * 4 + [ANY] * len(arrays_one),
        out_specs=(VMEM,) * 2,
        scratch_shapes=[
            pltpu.VMEM((3 * width, width), bf16),
            pltpu.SemaphoreType.DMA((len(arrays_one),)),
        ],
        compiler_params=params(),
        cost_estimate=cost(1e9, 1e6),
        name="self_attention_input",
    )(ints, mix_weight, gains, blended, grad_res, grad_proj, *arrays_one)
    state, came_one, going_tok = fence((sum_two.state(), came_one, going_tok))
    sum_two.put(state)

    sum_one = OuterSum(keep_one, came_one)
    sum_one.relays()
    came_tok = swap(going_tok, CORE)
    placed = pl.pallas_call(
        functools.partial(place_kernel, (blocks, mirrors)),
        out_shape=whole((pairs, row_count, width), bf16),
        in_specs=[SMEM, SMEM] + [VMEM] * 2,
        out_specs=VMEM,
        compiler_params=params(32),
        cost_estimate=cost(1e9, 1e6),
        name="place_partner_gradients",
    )(ints, ints_near, going_tok, came_tok)
    mlp_parts = jnp.concatenate([inner_parts(inner) for inner in inner_mlp], axis=1)
    inner_mlp = InnerSum(mlp_parts)
    inner_mlp.finish()
    state, placed, mlp_came = fence((sum_one.state(), placed, inner_mlp.came))
    sum_one.put(state)
    inner_mlp.came = mlp_came

    sum_one.singles()
    sum_tok = OuterSum(placed)
    sum_tok.relays()
    two_sum = sum_two.result()
    two_parts = jnp.concatenate(
        [two_sum[first : first + size].reshape(fsdp_count, size // fsdp_count, width) for first, size in layout], axis=1
    )
    inner_two = InnerSum(two_parts)
    inner_two.step()
    state, state_tok, two_came = fence((sum_one.state(), sum_tok.state(), inner_two.came))
    sum_one.put(state)
    sum_tok.put(state_tok)
    inner_two.came = two_came

    for mask in link_masks():
        sum_tok.prepare(mask)
    state, state_tok, inner_two.came = fence((sum_one.state(), sum_tok.state(), inner_two.came))
    sum_one.put(state)
    sum_tok.put(state_tok)
    sum_tok.singles()
    one_sum = sum_one.result()
    gain_sum = jnp.broadcast_to(one_sum[qkv_rows : qkv_rows + 8][None], (fsdp_count, 8, width))
    one_parts = jnp.concatenate([one_sum[:qkv_rows].reshape(fsdp_count, qkv_part, width), gain_sum], axis=1)
    inner_one = InnerSum(one_parts)
    inner_one.step()
    one_mine = inner_one.result()
    mlp_mine = inner_mlp.result()
    up_shard, down_shard = mlp_mine[:up_part].T, mlp_mine[up_part:]
    two_mine = inner_two.result()
    found = []
    at = 0
    for size in sizes_two:
        found.append(two_mine[at : at + size])
        at += size
    ckv_shard, out_shard, cq_shard, cout_shard = found[0].T, found[1], found[2], found[3]
    qkv_shard = one_mine[:qkv_part].T
    gain_mine = lax.dynamic_slice(one_mine[qkv_part:], (0, device_me * part), (3, part))
    token_grad = base + sum_tok.result()
    return (
        output,
        token_grad,
        coarse_grad,
        gain_mine[0],
        qkv_shard,
        out_shard,
        gain_mine[1],
        cq_shard,
        ckv_shard,
        cout_shard,
        gain_mine[2],
        up_shard,
        down_shard,
    )


def solution(mesh):
    rows = P(("dp", "fsdp"), None)
    columns = P(None, ("dp", "fsdp"))
    line = P(("dp", "fsdp"))
    in_specs = (
        rows, rows, rows, rows, line, line, line, columns, rows,
        line, rows, columns, rows, line, columns, rows, rows,
    )
    out_specs = (
        rows, rows, rows, line, columns, rows, line, rows, columns, rows, line, columns, rows,
    )
    return jax.shard_map(shards, mesh=mesh, in_specs=in_specs, out_specs=out_specs, check_vma=False)
```
